32 devices in a mesh: ctx: 8 (over z, x), fsdp: 4 (over y, core).
Axes of the slice: x: 2, y: 2, z: 4, core: 2. Of those that a mesh axis runs over, the one named last changes fastest.
Arguments:
- layer_in: bfloat16 [4, 1024, 4096], P('fsdp', 'ctx'), may hold values from -6 to 6
- w_bc: bfloat16 [4096, 256], P('fsdp'), may hold values from -0.09375 to 0.09375
- conv_w: float32 [4, 256], replicated, may hold values from -3 to 3
- conv_b: float32 [256], replicated, may hold values from -0.5 to 0.5
- ssm_in: bfloat16 [4, 1024, 4096], P('fsdp', 'ctx'), may hold values from -6 to 6
- dt_raw: float32 [4, 1024, 32], P('fsdp', 'ctx'), may hold values from -4 to 4
- dt_bias: float32 [32], replicated, as said below
- a_log: float32 [32], replicated, as said below
- skip_scale: float32 [32], replicated, may hold values from 0.5 to 1.5
- grad_out: bfloat16 [4, 1024, 4096], P('fsdp', 'ctx'), may hold values from -6 to 6
Outputs:
- ssm_out: bfloat16 [4, 1024, 4096], P('fsdp', 'ctx')
- grad_ssm_in: bfloat16 [4, 1024, 4096], P('fsdp', 'ctx')
- grad_layer_in: bfloat16 [4, 1024, 4096], P('fsdp', 'ctx')
- grad_dt_raw: float32 [4, 1024, 32], P('fsdp', 'ctx')
- grad_w_bc: float32 [4096, 256], P('fsdp')
- grad_conv_w: float32 [4, 256], replicated
- grad_conv_b: float32 [256], replicated
- grad_dt_bias: float32 [32], replicated
- grad_a_log: float32 [32], replicated
- grad_skip: float32 [32], replicated
The draws below stay inside these ranges and needn't reach their ends.
Inputs may be any that keep to these rules, and one draw needn't show every extreme that they name: `dt_bias`: drawn together with a_log. `a_log`: drawn together with dt_bias.
All inputs are finite; a program needn't handle non-finite values.
Results may differ from the reference program's by a relative error of at most 0.039.
Values may be sent and summed in bfloat16 or wider, within the bound.
No kernel may reach another device: no remote copies, remote signals or barrier semaphores. Data moves between devices by JAX's collectives and lax.ppermute only.
A program may use at most 320 MiB of HBM per device.

```python
import math
import jax
import jax.numpy as jnp
from jax import lax

D = 4096
H = 32
P_SIZE = 128
N = 128
SPAN = 128
KW = 4
TOK_DEV = 128
TOKENS = 1024
SEQS = 4


def head_tables(key):
    head_key = jax.random.fold_in(key, 101)
    lowest = math.log(30.0)
    highest = math.log(40.0 * TOKENS)
    memory = jnp.exp(jax.random.uniform(head_key, (H,), jnp.float32, lowest, highest))
    step_level = 0.1 / jnp.sqrt(jnp.minimum(memory, float(TOKENS)))
    rate = 1.0 / (memory * step_level)
    return (jnp.log(jnp.expm1(step_level)), jnp.log(rate))


def draw_dt_bias(key, part):
    return head_tables(key)[0]


def draw_a_log(key, part):
    return head_tables(key)[1]


def draw_dt_raw(key, part):
    offset_key = jax.random.fold_in(key, 5)
    rough_key = jax.random.fold_in(key, 6)
    blocks = TOKENS // TOK_DEV
    offsets = jax.random.uniform(offset_key, (SEQS, blocks, 1, H), jnp.float32, -0.8, 0.8)
    rough = 0.5 * jax.random.normal(rough_key, (SEQS, blocks, TOK_DEV, H), jnp.float32)
    return jnp.clip((offsets + rough).reshape(SEQS, TOKENS, H), -4.0, 4.0)


def with_spikes(values, rng, source, target, parts, factor):
    def block_of(position):
        return (jnp.arange(values.shape[position]) // (values.shape[position] // parts)).reshape((-1,) + (1,) * (values.ndim - 1 - position))

    near = jax.random.permutation(rng, parts)[block_of(target)]
    other_side = (block_of(target) + parts // 2) % parts
    return jnp.where((block_of(source) == near) | (block_of(source) == other_side), factor * values, values)


def steps_of(rng, dims, pieces, low, top_value):
    level = 1.0
    for axis_at, parts in pieces:
        draws = jax.random.uniform(jax.random.fold_in(jax.random.fold_in(rng, 6), axis_at), (parts,), jnp.float32, low / len(pieces), top_value / len(pieces))
        level = level * jnp.repeat(jnp.exp(draws), dims[axis_at] // parts).reshape((-1,) + (1,) * (len(dims) - 1 - axis_at))
    return level


def scatter_about(rng, shape, deviation, reach, shards=(), kind=jnp.bfloat16):
    level = steps_of(rng, shape, shards, -0.22, 0.18) if shards else 1.0
    values = jax.random.normal(rng, shape, jnp.float32) * deviation * level
    return jnp.minimum(jnp.maximum(values, -reach), reach).astype(kind)


def gaussian_with(rng, extent, spread, limit, split, heavy, kind=jnp.bfloat16):
    drawn = spread * jax.random.normal(rng, extent, jnp.float32)
    if split:
        drawn = drawn * steps_of(rng, extent, split, -0.22, 0.18)
    return jnp.clip(with_spikes(drawn, jax.random.fold_in(rng, 3), *heavy), -limit, limit).astype(kind)


def setup_inputs(seed: int = 0) -> dict:
    key_list = jax.random.split(jax.random.key(seed), 11)
    return {
        "layer_in": gaussian_with(key_list[0], (SEQS, TOKENS, D), 1.0, 6.0, ((0, 4), (1, 8)), (0, 2, 4, 2.0)),
        "w_bc": scatter_about(key_list[1], (D, 2 * N), D ** -0.5, 0.09375, ((0, 4),)),
        "conv_w": scatter_about(key_list[2], (KW, 2 * N), KW ** -0.5, 3.0, (), jnp.float32),
        "conv_b": jnp.clip(jax.random.uniform(key_list[3], (2 * N,), jnp.float32, -0.5, 0.5), -0.5, 0.5),
        "ssm_in": scatter_about(key_list[4], (SEQS, TOKENS, H * P_SIZE), 1.0, 6.0, ((0, 4), (1, 8))),
        "dt_raw": draw_dt_raw(jax.random.fold_in(key_list[10], 71), 0),
        "dt_bias": draw_dt_bias(jax.random.fold_in(key_list[10], 71), 0),
        "a_log": draw_a_log(jax.random.fold_in(key_list[10], 71), 0),
        "skip_scale": jnp.clip(jax.random.uniform(key_list[8], (H,), jnp.float32, 0.5, 1.5), 0.5, 1.5),
        "grad_out": scatter_about(key_list[9], (SEQS, TOKENS, H * P_SIZE), 1.0, 6.0, ((0, 4), (1, 8))),
    }


def prepare(padded, conv_w, conv_b, dt_raw, dt_bias, a_log):
    row_count = dt_raw.shape[0]
    conv_width = conv_w.shape[0]
    conv_sum = conv_b[None, :] + conv_w[0][None, :] * padded[0:row_count]
    for offset in range(1, conv_width):
        conv_sum = conv_sum + conv_w[offset][None, :] * padded[offset:offset + row_count]
    activated = jax.nn.silu(conv_sum)
    half_width = activated.shape[1] // 2
    b_in = activated[:, :half_width].astype(jnp.bfloat16)
    c_out = activated[:, half_width:].astype(jnp.bfloat16)
    step_size = jax.nn.softplus(dt_raw + dt_bias[None, :])
    log_decay = -step_size * jnp.exp(a_log)[None, :]
    return (b_in, c_out, step_size, log_decay)

def span_local(b_in, c_out, step_size, log_decay, values, skip_scale):
    span_len = step_size.shape[0]
    cumulated = jnp.cumsum(log_decay, axis=0)
    scores = jnp.dot(c_out, b_in.T, preferred_element_type=jnp.float32)
    per_head = cumulated.T
    gap_log = per_head[:, :, None] - per_head[:, None, :]
    row_ids = lax.broadcasted_iota(jnp.int32, (span_len, span_len), 0)
    col_ids = lax.broadcasted_iota(jnp.int32, (span_len, span_len), 1)
    causal_mask = (row_ids >= col_ids)[None, :, :]
    decay_grid = jnp.where(causal_mask, jnp.exp(jnp.where(causal_mask, gap_log, 0.0)), 0.0)
    mixing = (scores[None, :, :] * decay_grid * step_size.T[:, None, :]).astype(jnp.bfloat16)
    mixing = lax.optimization_barrier(mixing)
    inside_out = jnp.einsum('hij,jhp->ihp', mixing.astype(jnp.float32), values.astype(jnp.float32))
    local_out = inside_out + skip_scale[None, :, None] * values.astype(jnp.float32)
    end_weight = jnp.exp(per_head[:, -1:] - per_head) * step_size.T
    deposit = (end_weight[:, :, None] * b_in.astype(jnp.float32)[None, :, :]).astype(jnp.bfloat16)
    deposit = lax.optimization_barrier(deposit)
    span_state = jnp.einsum('hjn,jhp->hnp', deposit.astype(jnp.float32), values.astype(jnp.float32))
    return (local_out, span_state, jnp.exp(per_head[:, -1]), jnp.exp(cumulated))

def span_output(local_out, growth, c_out, state):
    stored = lax.optimization_barrier(state.astype(jnp.bfloat16))
    carried_out = jnp.einsum('in,hnp->ihp', c_out.astype(jnp.float32), stored.astype(jnp.float32))
    return local_out + growth[:, :, None] * carried_out

def sequence_forward(projected, conv_w, conv_b, values, dt_raw, dt_bias, a_log, skip_scale):
    conv_width = conv_w.shape[0]
    padded = jnp.concatenate([jnp.zeros((conv_width - 1, projected.shape[1]), projected.dtype), projected], 0)
    b_in, c_out, step_size, log_decay = prepare(padded, conv_w, conv_b, dt_raw, dt_bias, a_log)
    span_count = step_size.shape[0] // SPAN
    head_count = step_size.shape[1]
    head_size = values.shape[1] // head_count
    state_size = b_in.shape[1]
    items = (b_in.reshape(span_count, SPAN, state_size), c_out.reshape(span_count, SPAN, state_size), step_size.reshape(span_count, SPAN, head_count), log_decay.reshape(span_count, SPAN, head_count), values.reshape(span_count, SPAN, head_count, head_size))

    def advance(state, item):
        b_part, c_part, step_part, decay_part, value_part = item
        local_out, span_state, span_decay, growth = span_local(b_part, c_part, step_part, decay_part, value_part, skip_scale)
        result = span_output(local_out, growth, c_part, state).astype(jnp.bfloat16)
        return (span_decay[:, None, None] * state + span_state, result.reshape(SPAN, head_count * head_size))
    start_state = jnp.zeros((head_count, state_size, head_size), jnp.float32)
    final_state, outputs = lax.scan(jax.checkpoint(advance), start_state, items)
    return outputs.reshape(span_count * SPAN, head_count * head_size)

def reference(layer_in, w_bc, conv_w, conv_b, ssm_in, dt_raw, dt_bias, a_log, skip_scale, grad_out):

    def one_sequence(totals, item):
        tokens_in, values_in, raw_steps, upstream = item
        projected = jnp.dot(tokens_in, w_bc, preferred_element_type=jnp.float32)
        result, backward = jax.vjp(sequence_forward, projected, conv_w, conv_b, values_in, raw_steps, dt_bias, a_log, skip_scale)
        grad_proj, grad_cw, grad_cb, grad_values, grad_raw, grad_bias, grad_log, grad_skip_one = backward(upstream)
        grad_rounded = grad_proj.astype(jnp.bfloat16)
        grad_tokens = jnp.dot(grad_rounded, w_bc.T, preferred_element_type=jnp.float32).astype(jnp.bfloat16)
        grad_weight = jnp.dot(tokens_in.T, grad_rounded, preferred_element_type=jnp.float32)
        terms = (grad_weight, grad_cw, grad_cb, grad_bias, grad_log, grad_skip_one)
        totals = tuple((first + second for first, second in zip(totals, terms)))
        return (totals, (result, grad_values, grad_tokens, grad_raw))
    start = (jnp.zeros(w_bc.shape, jnp.float32), jnp.zeros(conv_w.shape, jnp.float32), jnp.zeros(conv_b.shape, jnp.float32), jnp.zeros(dt_bias.shape, jnp.float32), jnp.zeros(a_log.shape, jnp.float32), jnp.zeros(skip_scale.shape, jnp.float32))
    totals, stacked = lax.scan(one_sequence, start, (layer_in, ssm_in, dt_raw, grad_out))
    ssm_out, grad_ssm_in, grad_layer_in, grad_dt_raw = stacked
    grad_w_bc, grad_conv_w, grad_conv_b, grad_dt_bias, grad_a_log, grad_skip = totals
    return (ssm_out, grad_ssm_in, grad_layer_in, grad_dt_raw, grad_w_bc, grad_conv_w, grad_conv_b, grad_dt_bias, grad_a_log, grad_skip)
```

```python
import functools

import jax
import jax.numpy as jnp
from jax import lax
from jax.experimental import pallas as pl
from jax.experimental.pallas import tpu as pltpu
from jax.sharding import PartitionSpec as P

F32 = jnp.float32
BF16 = jnp.bfloat16
LANES = 128
HALO = 16
LIMIT = 40 * 1024 * 1024


def dot(a, b, dims=((1,), (0,)), precision=None):
    return lax.dot_general(
        a, b, (dims, ((), ())), precision=precision, preferred_element_type=F32
    )


TN = ((0,), (0,))
NT = ((1,), (1,))


def params():
    return pltpu.CompilerParams(vmem_limit_bytes=LIMIT)


def vmem(count):
    return [pl.BlockSpec(memory_space=pltpu.VMEM)] * count


def smem(count):
    return [pl.BlockSpec(memory_space=pltpu.SMEM)] * count


def shape(dims, dtype):
    return jax.ShapeDtypeStruct(dims, dtype)


def triangle(n):
    rows = lax.broadcasted_iota(jnp.int32, (n, n), 0)
    cols = lax.broadcasted_iota(jnp.int32, (n, n), 1)
    return rows >= cols


def vectors_kernel(dt_ref, bias_ref, alog_ref, step_ref, cum_ref, cumt_ref, grow_ref, endw_ref):
    raw = dt_ref[...] + bias_ref[...]
    step = jnp.maximum(raw, 0.0) + jnp.log1p(jnp.exp(-jnp.abs(raw)))
    log_decay = -step * jnp.exp(alog_ref[...])
    n = raw.shape[0]
    lower = jnp.where(triangle(n), 1.0, 0.0).astype(F32)
    cum = dot(lower, log_decay, precision=lax.Precision.HIGHEST)
    step_ref[...] = step
    cum_ref[...] = cum
    cumt_ref[...] = cum.T
    grow_ref[...] = jnp.exp(cum)
    endw_ref[...] = jnp.exp(cum[n - 1 : n, :] - cum)


def project_kernel(count, offs_ref, layer_ref, halo_ref, *refs):
    pieces = refs[:count]
    cw_ref, cb_ref, ext_ref, pre_ref, bc_ref = refs[count:]
    rows = pieces[0].shape[0]
    taps = cw_ref.shape[0]
    tokens = layer_ref.shape[0]
    total = jnp.zeros((tokens, pieces[0].shape[1]), F32)
    rim = jnp.zeros((HALO, pieces[0].shape[1]), F32)
    for k in range(count):
        at = pl.ds(pl.multiple_of(offs_ref[k], LANES), rows)
        w = pieces[k][...]
        total += dot(layer_ref[:, at], w)
        rim += dot(halo_ref[:, at], w)
    ext_ref[0:HALO, :] = rim
    ext_ref[HALO:, :] = total
    first = HALO - taps + 1
    pre = cb_ref[...] + cw_ref[0:1, :] * ext_ref[first : first + tokens, :]
    for k in range(1, taps):
        pre = pre + cw_ref[k : k + 1, :] * ext_ref[first + k : first + k + tokens, :]
    pre_ref[...] = pre
    bc_ref[...] = (pre * jax.nn.sigmoid(pre)).astype(BF16)


def widen(row, lane, heads):
    return jnp.concatenate(
        [jnp.broadcast_to(row[:, lane + h : lane + h + 1], (1, LANES)) for h in range(heads)], 1
    )


def states_kernel(
    heads, chunks, idx_ref, x0_ref, x1_ref, g0_ref, g1_ref, bc0_ref, bc1_ref, step_ref, grow_ref,
    endw_ref, *refs
):
    p_refs, q_refs = refs[:chunks], refs[chunks : 2 * chunks]
    sf_ref, ds_ref, dec_ref, s_scr, d_scr, dec_scr, xe_scr, ge_scr = refs[2 * chunks :]
    n = step_ref.shape[0]
    r = idx_ref[0]
    for slot, (x_ref, g_ref, bc_ref) in enumerate(
        ((x0_ref, g0_ref, bc0_ref), (x1_ref, g1_ref, bc1_ref))
    ):
        for h in range(heads):
            lane = slot * heads + h
            at = slice(h * LANES, (h + 1) * LANES)
            weight = step_ref[:, lane : lane + 1] * endw_ref[:, lane : lane + 1]
            xe_scr[:, at] = (x_ref[:, at].astype(F32) * weight).astype(BF16)
            ge_scr[:, at] = (g_ref[:, at].astype(F32) * grow_ref[:, lane : lane + 1]).astype(BF16)
        b = bc_ref[:, :LANES]
        c = bc_ref[:, LANES:]
        s_scr[slot] = dot(b, xe_scr[...], TN)
        d_scr[slot] = dot(c, ge_scr[...], TN)
        dec_scr[slot] = widen(grow_ref[n - 1 : n, :], slot * heads, heads)
    dec_first, dec_second = dec_scr[r], dec_scr[1 - r]
    s_first, d_second = s_scr[r], d_scr[1 - r]
    sf_ref[...] = s_first.astype(BF16)
    ds_ref[...] = d_second.astype(BF16)
    p = (dec_second * s_first + s_scr[1 - r]).astype(BF16)
    q = (dec_first * d_second + d_scr[r]).astype(BF16)
    width = p_refs[0].shape[1]
    for i in range(chunks):
        p_refs[i][...] = p[:, i * width : (i + 1) * width]
        q_refs[i][...] = q[:, i * width : (i + 1) * width]
    dec_ref[0:1, :] = dec_first * dec_second
    dec_ref[1:2, :] = dec_first
    dec_ref[2:3, :] = dec_second
    dec_ref[3:8, :] = jnp.zeros((5, dec_first.shape[1]), F32)


def final_kernel(
    heads, chunks, hops, idx_ref, x0_ref, x1_ref, g0_ref, g1_ref, bc0_ref, bc1_ref, step_ref,
    cum_ref, cumt_ref, grow_ref, endw_ref, dt_ref, bias_ref, alog_ref, skip_ref, sf_ref, ds_ref,
    dec_ref, *refs
):
    p_refs = refs[:chunks]
    e_refs = refs[chunks : chunks + chunks * hops]
    r_refs = refs[chunks + chunks * hops : chunks + 2 * chunks * hops]
    (
        y0_ref, y1_ref, dx0_ref, dx1_ref, dbc0_ref, dbc1_ref, draw_ref, sums_ref,
        e_scr, r_scr, n_scr, ce_scr, br_scr, xe_scr, ge_scr, gy_scr, ds_scr, re_scr,
    ) = refs[chunks + 2 * chunks * hops :]
    n = step_ref.shape[0]
    r = idx_ref[0]

    def whole(parts):
        columns = []
        for i in range(chunks):
            total = parts[i * hops][...].astype(F32)
            for k in range(1, hops):
                total = total + parts[i * hops + k][...].astype(F32)
            columns.append(total)
        return jnp.concatenate(columns, 1)

    dec_pair, dec_first, dec_second = dec_ref[0:1, :], dec_ref[1:2, :], dec_ref[2:3, :]
    entering = whole(e_refs)
    e_scr[r] = entering.astype(BF16)
    middle = dec_first * entering + sf_ref[...].astype(F32)
    e_scr[1 - r] = middle.astype(BF16)
    leaving = dec_pair * entering + jnp.concatenate([p[...] for p in p_refs], 1).astype(F32)
    later = whole(r_refs)
    r_scr[1 - r] = later.astype(BF16)
    earlier = dec_second * later + ds_ref[...].astype(F32)
    r_scr[r] = earlier.astype(BF16)
    n_scr[1 - r] = jnp.sum(later * leaving, axis=0, keepdims=True)
    n_scr[r] = jnp.sum(earlier * middle, axis=0, keepdims=True)

    mask = triangle(n)
    gy_scr[...] = jnp.zeros_like(gy_scr)
    ds_scr[...] = jnp.zeros_like(ds_scr)
    re_scr[...] = jnp.zeros_like(re_scr)
    for slot, (x_ref, g_ref, bc_ref, y_ref, dx_ref, dbc_ref) in enumerate(
        (
            (x0_ref, g0_ref, bc0_ref, y0_ref, dx0_ref, dbc0_ref),
            (x1_ref, g1_ref, bc1_ref, y1_ref, dx1_ref, dbc1_ref),
        )
    ):
        b = bc_ref[:, :LANES]
        c = bc_ref[:, LANES:]
        scores = dot(c, b, NT)
        e_all = e_scr[slot]
        r_all = r_scr[slot]
        ce_scr[...] = dot(c, e_all)
        br_scr[...] = dot(b, r_all)
        dscores = jnp.zeros((n, n), F32)
        for h in range(heads):
            lane = slot * heads + h
            at = slice(h * LANES, (h + 1) * LANES)
            step = step_ref[:, lane : lane + 1]
            grow = grow_ref[:, lane : lane + 1]
            endw = endw_ref[:, lane : lane + 1]
            gap = cum_ref[:, lane : lane + 1] - cumt_ref[lane : lane + 1, :]
            decay = jnp.exp(jnp.where(mask, gap, -jnp.inf))
            mixing = (scores * decay).astype(BF16)
            x = x_ref[:, at].astype(F32)
            g = g_ref[:, at]
            gf = g.astype(F32)
            xs = x * step
            xsb = xs.astype(BF16)
            xe_scr[:, at] = (xs * endw).astype(BF16)
            ge_scr[:, at] = (gf * grow).astype(BF16)
            skip = skip_ref[r * heads + h]
            y = dot(mixing, xsb) + grow * ce_scr[:, at]
            dxs = dot(mixing, g, TN) + endw * br_scr[:, at]
            dscores += dot(g, xsb, NT) * decay
            y_ref[:, at] = (y + skip * x).astype(BF16)
            dx_ref[:, at] = (dxs * step + skip * gf).astype(BF16)
            gy_scr[:, lane : lane + 1] = jnp.sum(gf * y, axis=1, keepdims=True)
            ds_scr[:, lane : lane + 1] = jnp.sum(x * dxs, axis=1, keepdims=True)
            re_scr[0:1, lane : lane + 1] = jnp.sum(n_scr[slot][:, at], axis=1, keepdims=True)
            re_scr[1:2, lane : lane + 1] = jnp.sum(
                jnp.sum(gf * x, axis=0, keepdims=True), axis=1, keepdims=True
            )
        dsb = dscores.astype(BF16)
        dbc_ref[:, :LANES] = dot(xe_scr[...], r_all, NT) + dot(dsb, c, TN)
        dbc_ref[:, LANES:] = dot(ge_scr[...], e_all, NT) + dot(dsb, b)

    step = step_ref[...]
    ds = ds_scr[...]
    rate = jnp.exp(alog_ref[...])
    last = lax.broadcasted_iota(jnp.int32, (n, LANES), 0) == n - 1
    dcum = gy_scr[...] - step * ds + jnp.where(last, re_scr[0:1, :], 0.0)
    lower = jnp.where(mask, 1.0, 0.0).astype(F32)
    dlog = dot(lower, dcum, TN, precision=lax.Precision.HIGHEST)
    draw = (ds - rate * dlog) * jax.nn.sigmoid(dt_ref[...] + bias_ref[...])
    draw_ref[...] = draw
    sums_ref[0:1, :] = jnp.sum(draw, axis=0, keepdims=True)
    sums_ref[1:2, :] = jnp.sum(dlog * (-step * rate), axis=0, keepdims=True)
    sums_ref[2:3, :] = re_scr[1:2, :]
    sums_ref[3:8, :] = jnp.zeros((5, LANES), F32)


def conv_back_kernel(own_ref, ret_ref, pre_ref, ext_ref, cw_ref, grad_ref, gradb_ref, sums_ref, z_scr):
    tokens = pre_ref.shape[0]
    taps = cw_ref.shape[0]
    pre = pre_ref[...]
    sig = jax.nn.sigmoid(pre)
    dconv = (own_ref[...] + ret_ref[...].astype(F32)) * sig * (1.0 + pre * (1.0 - sig))
    z_scr[...] = jnp.zeros_like(z_scr)
    z_scr[HALO : HALO + tokens, :] = dconv
    grad = cw_ref[0:1, :] * z_scr[taps - 1 : taps - 1 + tokens + HALO, :]
    for k in range(1, taps):
        grad = grad + cw_ref[k : k + 1, :] * z_scr[taps - 1 - k : taps - 1 - k + tokens + HALO, :]
    grad_ref[...] = grad
    gradb_ref[...] = grad.astype(BF16)
    sums_ref[...] = jnp.zeros_like(sums_ref)
    first = HALO - taps + 1
    for k in range(taps):
        sums_ref[k : k + 1, :] = jnp.sum(
            dconv * ext_ref[first + k : first + k + tokens, :], axis=0, keepdims=True
        )
    sums_ref[taps : taps + 1, :] = jnp.sum(dconv, axis=0, keepdims=True)


def pack_kernel(count, offs_ref, layer_ref, halo_ref, *outs):
    for k in range(count):
        rows = outs[k].shape[1]
        at = pl.ds(pl.multiple_of(offs_ref[k], LANES), rows)
        outs[k][0:HALO, :] = halo_ref[:, at]
        outs[k][HALO:, :] = layer_ref[:, at]


def weight_kernel(count, size, offs_ref, *refs):
    lefts, rights = refs[:count], refs[count : 2 * count]
    outs, total = refs[2 * count : 2 * count + size], refs[2 * count + size]
    acc = dot(lefts[0][...], rights[0][...], TN)
    for k in range(1, count):
        acc = acc + dot(lefts[k][...], rights[k][...], TN)
    total[...] = acc
    chunk = outs[0].shape[0]
    for k in range(size):
        at = pl.ds(pl.multiple_of(offs_ref[k], chunk), chunk)
        outs[k][...] = total[at, :].astype(BF16)


def place_rows_kernel(count, offs_ref, *refs):
    out = refs[count]
    chunk = refs[0].shape[0]
    for k in range(count):
        at = pl.ds(pl.multiple_of(offs_ref[k], chunk), chunk)
        out[at, :] = refs[k][...].astype(F32)


def tokens_kernel(count, offs_ref, grad_ref, rim_ref, *refs):
    pieces, out = refs[:count], refs[count]
    own = grad_ref[HALO:, :]
    tail = rim_ref.shape[0]
    g = jnp.concatenate([own[:-tail], own[-tail:] + rim_ref[...]], 0).astype(BF16)
    rows = pieces[0].shape[0]
    for k in range(count):
        at = pl.ds(pl.multiple_of(offs_ref[k], LANES), rows)
        out[:, at] = dot(g, pieces[k][...], NT).astype(BF16)


def toggled(x, axis, bits):
    size = lax.axis_size(axis)
    return lax.ppermute(x, axis, [(i, i ^ bits) for i in range(size)])


def everyone_sums(x, axis):
    bits = 1
    while bits < lax.axis_size(axis):
        x = x + toggled(x, axis, bits)
        bits *= 2
    return x


def chain(parts, decay, axis, forward):
    size = lax.axis_size(axis)
    pairs = size // 2
    received = [[] for _ in parts]
    width = parts[0].shape[1]
    for hop in range(pairs - 1):
        source = hop if forward else pairs - 1 - hop
        target = source + 1 if forward else source - 1
        lanes = [(2 * source + i, 2 * target + i) for i in range(2)]
        for i, part in enumerate(parts):
            value = part
            if hop:
                scale = decay[:, i * width : (i + 1) * width]
                value = (scale * received[i][-1].astype(F32) + part.astype(F32)).astype(BF16)
            received[i].append(lax.ppermute(value, axis, lanes))
    return received


def body(layer_in, w_bc, conv_w, conv_b, ssm_in, dt_raw, dt_bias, a_log, skip_scale, grad_out):
    ctx, fsdp = lax.axis_size("ctx"), lax.axis_size("fsdp")
    d, f = lax.axis_index("ctx"), lax.axis_index("fsdp")
    r = d % 2
    tokens_in, x, g, dt = layer_in[0], ssm_in[0], grad_out[0], dt_raw[0]
    tokens, width = x.shape
    total_heads = dt_bias.shape[0]
    heads = total_heads // 2
    half = width // 2
    state = w_bc.shape[1] // 2
    taps = conv_w.shape[0]
    rows = w_bc.shape[0]
    chunks = 2
    hops = ctx // 2 - 1
    idx = jnp.reshape(r, (1,)).astype(jnp.int32)
    column_offs = (jnp.arange(fsdp, dtype=jnp.int32) ^ f.astype(jnp.int32)) * rows
    chunk_rows = rows // ctx
    row_offs = (jnp.arange(ctx, dtype=jnp.int32) ^ d.astype(jnp.int32)) * chunk_rows

    def mine(a, axis=-1):
        n = a.shape[axis] // 2
        return jnp.where(
            r == 0, lax.slice_in_dim(a, 0, n, axis=axis), lax.slice_in_dim(a, n, 2 * n, axis=axis)
        )

    def other(a, axis=-1):
        n = a.shape[axis] // 2
        return jnp.where(
            r == 0, lax.slice_in_dim(a, n, 2 * n, axis=axis), lax.slice_in_dim(a, 0, n, axis=axis)
        )

    def joined(own, returned, axis=-1):
        return jnp.where(
            r == 0,
            jnp.concatenate([own, returned], axis),
            jnp.concatenate([returned, own], axis),
        )

    pieces = {0: w_bc}
    bit = fsdp // 2
    while bit:
        for k in list(pieces):
            pieces[k | bit] = toggled(pieces[k], "fsdp", bit)
        bit //= 2
    pieces = [pieces[k] for k in range(fsdp)]
    halo = lax.ppermute(tokens_in[tokens - HALO :], "ctx", [(i, i + 1) for i in range(ctx - 1)])
    x_recv = toggled(other(x), "ctx", 1)
    g_recv = toggled(other(g), "ctx", 1)
    dt_recv = toggled(other(dt), "ctx", 1)

    def lanes_of(a):
        return jnp.pad(a, ((0, 0), (0, LANES - a.shape[1])))

    def twice(a):
        m = mine(a)[None, :]
        return lanes_of(jnp.concatenate([m, m], 1))

    dt2 = lanes_of(jnp.concatenate([mine(dt), dt_recv], 1))
    bias2, alog2 = twice(dt_bias), twice(a_log)
    square = shape((tokens, LANES), F32)
    step, cum, cumt, grow, endw = pl.pallas_call(
        vectors_kernel,
        out_shape=[square] * 5,
        in_specs=vmem(3),
        out_specs=vmem(5),
        compiler_params=params(),
        name="vectors",
    )(dt2, bias2, alog2)

    ext, pre, bc = pl.pallas_call(
        functools.partial(project_kernel, fsdp),
        out_shape=[
            shape((tokens + HALO, 2 * state), F32),
            shape((tokens, 2 * state), F32),
            shape((tokens, 2 * state), BF16),
        ],
        in_specs=smem(1) + vmem(4 + fsdp),
        out_specs=vmem(3),
        compiler_params=params(),
        name="project",
    )(column_offs, tokens_in, halo, *pieces, conv_w, conv_b[None, :])
    bc_recv = toggled(bc, "ctx", 1)

    own_half = pl.BlockSpec((tokens, half), lambda i, at: (0, at[0]))

    def full(a):
        rank = len(a.shape)
        return pl.BlockSpec(a.shape, lambda i, at: (0,) * rank)

    part = shape((state, half // chunks), BF16)
    flat = shape((state, half), BF16)
    out_shape = [part] * (2 * chunks) + [flat, flat, shape((8, half), F32)]
    operands = (x, x_recv, g, g_recv, bc, bc_recv, step, grow, endw)
    in_specs = [own_half, full(x_recv), own_half, full(g_recv)] + [full(a) for a in operands[4:]]
    results = pl.pallas_call(
        functools.partial(states_kernel, heads, chunks),
        out_shape=out_shape,
        grid_spec=pltpu.PrefetchScalarGridSpec(
            num_scalar_prefetch=1,
            grid=(1,),
            in_specs=in_specs,
            out_specs=[full(a) for a in out_shape],
            scratch_shapes=[
                pltpu.VMEM((2, state, half), F32),
                pltpu.VMEM((2, state, half), F32),
                pltpu.VMEM((2, 1, half), F32),
                pltpu.VMEM((tokens, half), BF16),
                pltpu.VMEM((tokens, half), BF16),
            ],
        ),
        compiler_params=params(),
        name="states",
    )(idx, *operands)
    p_parts, q_parts = results[:chunks], results[chunks : 2 * chunks]
    s_first, d_second, decays = results[2 * chunks :]
    pair_decay = decays[0:1]
    received_e = chain(p_parts, pair_decay, "ctx", True)
    received_r = chain(q_parts, pair_decay, "ctx", False)

    late_tokens, late_halo, _ = lax.optimization_barrier((tokens_in, halo, bc))
    packs = pl.pallas_call(
        functools.partial(pack_kernel, fsdp),
        out_shape=[shape((tokens + HALO, rows), BF16)] * fsdp,
        in_specs=smem(1) + vmem(2),
        out_specs=vmem(fsdp),
        compiler_params=params(),
        name="pack",
    )(column_offs, late_tokens, late_halo)
    lefts = [packs[0]] + [toggled(packs[k], "fsdp", k) for k in range(1, fsdp)]

    out_shape = [shape((tokens, half), BF16)] * 4 + [shape((tokens, 2 * state), F32)] * 2
    out_shape += [square, shape((8, LANES), F32)]
    operands = (
        x, x_recv, g, g_recv, bc, bc_recv, step, cum, cumt, grow, endw, dt2, bias2, alog2,
        skip_scale, s_first, d_second, decays, *p_parts,
        *[a for group in received_e for a in group], *[a for group in received_r for a in group],
    )
    in_specs = [own_half, full(x_recv), own_half, full(g_recv)] + [full(a) for a in operands[4:]]
    in_specs[14] = pl.BlockSpec(memory_space=pltpu.SMEM)
    y_own, y_send, dx_own, dx_send, dbc_own, dbc_send, draw, head_sums = pl.pallas_call(
        functools.partial(final_kernel, heads, chunks, hops),
        out_shape=out_shape,
        grid_spec=pltpu.PrefetchScalarGridSpec(
            num_scalar_prefetch=1,
            grid=(1,),
            in_specs=in_specs,
            out_specs=[full(a) for a in out_shape],
            scratch_shapes=[
                pltpu.VMEM((2, state, half), BF16),
                pltpu.VMEM((2, state, half), BF16),
                pltpu.VMEM((2, 1, half), F32),
                pltpu.VMEM((tokens, half), F32),
                pltpu.VMEM((tokens, half), F32),
                pltpu.VMEM((tokens, half), BF16),
                pltpu.VMEM((tokens, half), BF16),
                pltpu.VMEM((tokens, LANES), F32),
                pltpu.VMEM((tokens, LANES), F32),
                pltpu.VMEM((8, LANES), F32),
            ],
        ),
        compiler_params=params(),
        name="final",
    )(idx, *operands)

    dbc_ret = toggled(dbc_send.astype(BF16), "ctx", 1)
    grad, grad_b, conv_sums = pl.pallas_call(
        conv_back_kernel,
        out_shape=[
            shape((tokens + HALO, 2 * state), F32),
            shape((tokens + HALO, 2 * state), BF16),
            shape((8, 2 * state), F32),
        ],
        in_specs=vmem(5),
        out_specs=vmem(3),
        scratch_shapes=[pltpu.VMEM((tokens + 2 * HALO, 2 * state), F32)],
        compiler_params=params(),
        name="conv_back",
    )(dbc_own, dbc_ret, pre, ext, conv_w)

    rights = [grad_b] + [toggled(grad_b, "fsdp", k) for k in range(1, fsdp)]
    terms = pl.pallas_call(
        functools.partial(weight_kernel, fsdp, ctx),
        out_shape=[shape((chunk_rows, 2 * state), BF16)] * ctx,
        in_specs=smem(1) + vmem(2 * fsdp),
        out_specs=vmem(ctx),
        scratch_shapes=[pltpu.VMEM((rows, 2 * state), F32)],
        compiler_params=params(),
        name="weight",
    )(row_offs, *lefts, *rights)
    total = terms[0].astype(F32)
    for k in range(1, ctx):
        total = total + toggled(terms[k], "ctx", k).astype(F32)
    total = total.astype(BF16)
    everyones = [total] + [toggled(total, "ctx", k) for k in range(1, ctx)]
    grad_weight = pl.pallas_call(
        functools.partial(place_rows_kernel, ctx),
        out_shape=shape((rows, 2 * state), F32),
        in_specs=smem(1) + vmem(ctx),
        out_specs=vmem(1)[0],
        compiler_params=params(),
        name="place_rows",
    )(row_offs, *everyones)

    both = head_sums[:3, :heads] + head_sums[:3, heads : 2 * heads]
    both = joined(both, jnp.zeros_like(both))
    both = jnp.pad(both.reshape(1, -1), ((0, 0), (0, 2 * state - 3 * total_heads)))
    small = jnp.concatenate([conv_sums[: taps + 1], both], 0)
    small = everyone_sums(everyone_sums(small, "fsdp"), "ctx")
    per_head = small[taps + 1, : 3 * total_heads].reshape(3, total_heads)

    rim = lax.ppermute(grad[HALO - 8 : HALO], "ctx", [(i + 1, i) for i in range(ctx - 1)])
    grad_tokens = pl.pallas_call(
        functools.partial(tokens_kernel, fsdp),
        out_shape=shape((tokens, fsdp * rows), BF16),
        in_specs=smem(1) + vmem(2 + fsdp),
        out_specs=vmem(1)[0],
        compiler_params=params(),
        name="grad_tokens",
    )(column_offs, grad, rim, *pieces)
    ssm_out = joined(y_own, toggled(y_send, "ctx", 1))
    grad_values = joined(dx_own, toggled(dx_send, "ctx", 1))
    grad_raw = joined(draw[:, :heads], toggled(draw[:, heads : 2 * heads], "ctx", 1))
    return (
        ssm_out[None],
        grad_values[None],
        grad_tokens[None],
        grad_raw[None],
        grad_weight,
        small[:taps],
        small[taps],
        per_head[0],
        per_head[1],
        per_head[2],
    )


def solution(mesh):
    tokens = P("fsdp", "ctx", None)
    in_specs = (tokens, P("fsdp", None), P(), P(), tokens, tokens, P(), P(), P(), tokens)
    out_specs = (tokens, tokens, tokens, tokens, P("fsdp", None), P(), P(), P(), P(), P())
    return jax.shard_map(body, mesh=mesh, in_specs=in_specs, out_specs=out_specs, check_vma=False)
```

```python
import functools

import jax
import jax.numpy as jnp
from jax import lax
from jax.experimental import pallas as pl
from jax.experimental.pallas import tpu as pltpu
from jax.sharding import PartitionSpec as P

F32 = jnp.float32
BF16 = jnp.bfloat16
LANES = 128
HALO = 16
GROUPS = 2
CHUNKS = 1
LIMIT = 16 * 1024 * 1024
HIGHEST = lax.Precision.HIGHEST
TN = ((0,), (0,))
NT = ((1,), (1,))


def dot(a, b, dims=((1,), (0,)), precision=None):
    return lax.dot_general(
        a, b, (dims, ((), ())), precision=precision, preferred_element_type=F32
    )


def shape(dims, dtype):
    return jax.ShapeDtypeStruct(dims, dtype)


def call(kernel, name, out_shape, smem, *operands, scratch=(), flops=0):
    single = not isinstance(out_shape, list)
    outs = [out_shape] if single else out_shape
    moved = sum(a.size * a.dtype.itemsize for a in [*operands, *outs])
    result = pl.pallas_call(
        kernel,
        out_shape=outs,
        in_specs=[pl.BlockSpec(memory_space=pltpu.SMEM)] * len(smem)
        + [pl.BlockSpec(memory_space=pltpu.VMEM)] * len(operands),
        out_specs=[pl.BlockSpec(memory_space=pltpu.VMEM)] * len(outs),
        scratch_shapes=list(scratch),
        compiler_params=pltpu.CompilerParams(vmem_limit_bytes=LIMIT),
        cost_estimate=pl.CostEstimate(flops=flops, bytes_accessed=moved, transcendentals=0),
        name=name,
    )(*smem, *operands)
    return result[0] if single else result


def aligned(at, size):
    return pl.ds(pl.multiple_of(at, LANES), size)


def triangle(n):
    rows = lax.broadcasted_iota(jnp.int32, (n, n), 0)
    cols = lax.broadcasted_iota(jnp.int32, (n, n), 1)
    return rows >= cols


def split(value):
    high = value.astype(BF16)
    return high, (value - high.astype(F32)).astype(BF16)


def swap_kernel(offs_ref, x_ref, g_ref, *refs):
    outs, sems = refs[:GROUPS], refs[GROUPS]
    width = outs[0].shape[1] // 2
    copies = []
    for i in range(GROUPS):
        for j, source in enumerate((x_ref, g_ref)):
            copies.append(
                pltpu.make_async_copy(
                    source.at[:, aligned(offs_ref[0] + i * width, width)],
                    outs[i].at[:, j * width : (j + 1) * width],
                    sems.at[2 * i + j],
                )
            )
    for copy in copies:
        copy.start()
    for copy in copies:
        copy.wait()


def vectors_kernel(dt_ref, bias_ref, alog_ref, step_ref, cum_ref, cumt_ref, grow_ref, endw_ref):
    raw = dt_ref[...] + bias_ref[...]
    step = jnp.maximum(raw, 0.0) + jnp.log1p(jnp.exp(-jnp.abs(raw)))
    log_decay = -step * jnp.exp(alog_ref[...])
    n = raw.shape[0]
    lower = jnp.where(triangle(n), 1.0, 0.0).astype(F32)
    cum = dot(lower, log_decay, precision=HIGHEST)
    step_ref[...] = step
    cum_ref[...] = cum
    cumt_ref[...] = cum.T
    grow_ref[...] = jnp.exp(cum)
    endw_ref[...] = jnp.exp(cum[n - 1 : n, :] - cum)


def project_kernel(count, offs_ref, layer_ref, halo_ref, *refs):
    pieces = refs[:count]
    cw_ref, cb_ref, ext_ref, pre_ref, bc_ref = refs[count:]
    rows = pieces[0].shape[0]
    taps = cw_ref.shape[0]
    tokens = layer_ref.shape[0]
    total = jnp.zeros((tokens, pieces[0].shape[1]), F32)
    rim = jnp.zeros((HALO, pieces[0].shape[1]), F32)
    for k in range(count):
        at = aligned(offs_ref[k], rows)
        w = pieces[k][...]
        total += dot(layer_ref[:, at], w)
        rim += dot(halo_ref[:, at], w)
    ext_ref[0:HALO, :] = rim
    ext_ref[HALO:, :] = total
    first = HALO - taps + 1
    pre = cb_ref[...] + cw_ref[0:1, :] * ext_ref[first : first + tokens, :]
    for k in range(1, taps):
        pre = pre + cw_ref[k : k + 1, :] * ext_ref[first + k : first + k + tokens, :]
    pre_ref[...] = pre
    bc_ref[...] = (pre * jax.nn.sigmoid(pre)).astype(BF16)


def scale_kernel(heads, lane, offs_ref, x_ref, g_ref, step_ref, grow_ref, endw_ref, xe_ref, ge_ref):
    for h in range(heads):
        at = slice(h * LANES, (h + 1) * LANES)
        one = slice(lane + h, lane + h + 1)
        x = x_ref[:, aligned(offs_ref[0] + h * LANES, LANES)].astype(F32)
        g = g_ref[:, aligned(offs_ref[1] + h * LANES, LANES)].astype(F32)
        xe_ref[:, at] = (x * (step_ref[:, one] * endw_ref[:, one])).astype(BF16)
        ge_ref[:, at] = (g * grow_ref[:, one]).astype(BF16)


def widen(row, lane, heads):
    return jnp.concatenate(
        [jnp.broadcast_to(row[:, lane + h : lane + h + 1], (1, LANES)) for h in range(heads)], 1
    )


def states_kernel(
    heads, lanes, idx_ref, bc0_ref, bc1_ref, xe0_ref, ge0_ref, xe1_ref, ge1_ref, grow_ref,
    p_ref, q_ref, sf_ref, ds_ref, dec_ref, s_scr, d_scr, dec_scr,
):
    n = grow_ref.shape[0]
    r = idx_ref[0]
    for slot, (bc_ref, xe_ref, ge_ref) in enumerate(
        ((bc0_ref, xe0_ref, ge0_ref), (bc1_ref, xe1_ref, ge1_ref))
    ):
        s_scr[slot] = dot(bc_ref[:, :LANES], xe_ref[...], TN)
        d_scr[slot] = dot(bc_ref[:, LANES:], ge_ref[...], TN)
        dec_scr[slot] = widen(grow_ref[n - 1 : n, :], lanes[slot], heads)
    dec_first, dec_second = dec_scr[r], dec_scr[1 - r]
    s_first, d_second = s_scr[r], d_scr[1 - r]
    sf_ref[...] = s_first.astype(BF16)
    ds_ref[...] = d_second.astype(BF16)
    p_ref[...] = (dec_second * s_first + s_scr[1 - r]).astype(BF16)
    q_ref[...] = (dec_first * d_second + d_scr[r]).astype(BF16)
    dec_ref[0:1, :] = dec_first * dec_second
    dec_ref[1:2, :] = dec_first
    dec_ref[2:3, :] = dec_second
    dec_ref[3:8, :] = jnp.zeros((5, dec_first.shape[1]), F32)


def inside_kernel(
    heads, lane, skip_at, idx_ref, offs_ref, skip_ref, x_ref, g_ref, bc_ref, step_ref, cum_ref,
    cumt_ref, y_ref, dx_ref, dscores_ref, gy_ref, ds_ref, gx_ref,
):
    n = step_ref.shape[0]
    mask = triangle(n)
    scores = jnp.where(mask, dot(bc_ref[:, LANES:], bc_ref[:, :LANES], NT), 0.0)
    gy_ref[...] = jnp.zeros_like(gy_ref)
    ds_ref[...] = jnp.zeros_like(ds_ref)
    gx_ref[...] = jnp.zeros_like(gx_ref)
    dscores = jnp.zeros((n, n), F32)
    for h in range(heads):
        at = slice(h * LANES, (h + 1) * LANES)
        one = slice(lane + h, lane + h + 1)
        step = step_ref[:, one]
        gap = cum_ref[:, one] - cumt_ref[one, :]
        decay = jnp.exp(jnp.where(mask, gap, 0.0))
        mixing = (scores * decay).astype(BF16)
        x = x_ref[:, aligned(offs_ref[0] + h * LANES, LANES)].astype(F32)
        g = g_ref[:, aligned(offs_ref[1] + h * LANES, LANES)]
        gf = g.astype(F32)
        xs = (x * step).astype(BF16)
        skip = skip_ref[idx_ref[0] * GROUPS * heads + skip_at + h]
        y = dot(mixing, xs)
        dxs = dot(mixing, g, TN)
        dscores += dot(g, xs, NT) * decay
        y_ref[:, at] = y + skip * x
        dx_ref[:, at] = dxs * step + skip * gf
        gy_ref[:, one] = jnp.sum(gf * y, axis=1, keepdims=True)
        ds_ref[:, one] = jnp.sum(x * dxs, axis=1, keepdims=True)
        gx_ref[0:1, one] = jnp.sum(jnp.sum(gf * x, axis=0, keepdims=True), axis=1, keepdims=True)
    dscores_ref[...] = jnp.where(mask, dscores, 0.0)


def inside_bc_kernel(bc0_ref, bc1_ref, *refs):
    parts, outs = refs[: 2 * GROUPS], refs[2 * GROUPS :]
    for slot, bc_ref in enumerate((bc0_ref, bc1_ref)):
        total = parts[slot * GROUPS][...]
        for i in range(1, GROUPS):
            total = total + parts[slot * GROUPS + i][...]
        ds = total.astype(BF16)
        outs[slot][:, :LANES] = dot(ds, bc_ref[:, LANES:], TN)
        outs[slot][:, LANES:] = dot(ds, bc_ref[:, :LANES])


def across_kernel(
    heads, lanes, hops, idx_ref, offs_ref, x0_ref, g0_ref, back_ref, bc0_ref, bc1_ref, xe0_ref,
    ge0_ref, xe1_ref, ge1_ref, step_ref, grow_ref, endw_ref, dec_ref, p_ref, sf_ref, ds_ref,
    y0_ref, dx0_ref, y1_ref, dx1_ref, dbc0_ref, dbc1_ref, *refs
):
    received = refs[: hops * CHUNKS]
    (
        yo_ref, dxo_ref, send_ref, dbco0_ref, dbco1_ref, u_ref, t_ref, re_ref,
        e_in, r_in, e_scr, r_scr, n_scr,
    ) = refs[hops * CHUNKS :]
    r, pos = idx_ref[0], idx_ref[1]
    width = back_ref.shape[1] // 2
    part = width // CHUNKS
    e_in[...] = jnp.zeros_like(e_in)
    r_in[...] = jnp.zeros_like(r_in)
    for k in range(hops):
        for i in range(CHUNKS):
            at = slice(i * part, (i + 1) * part)

            @pl.when(pos - 1 == k)
            def _(k=k, i=i, at=at):
                e_in[:, at] = received[k * CHUNKS + i][...]

            @pl.when(hops - 1 - pos == k)
            def _(k=k, i=i, at=at):
                r_in[:, at] = received[k * CHUNKS + i][...]

    dec_pair, dec_first, dec_second = dec_ref[0:1, :], dec_ref[1:2, :], dec_ref[2:3, :]
    entering = e_in[...].astype(F32)
    later = r_in[...].astype(F32)
    middle = dec_first * entering + sf_ref[...].astype(F32)
    leaving = dec_pair * entering + p_ref[...].astype(F32)
    earlier = dec_second * later + ds_ref[...].astype(F32)
    e_scr[r] = e_in[...]
    e_scr[1 - r] = middle.astype(BF16)
    r_scr[1 - r] = r_in[...]
    r_scr[r] = earlier.astype(BF16)
    n_scr[1 - r] = jnp.sum(later * leaving, axis=0, keepdims=True)
    n_scr[r] = jnp.sum(earlier * middle, axis=0, keepdims=True)

    u_ref[...] = jnp.zeros_like(u_ref)
    t_ref[...] = jnp.zeros_like(t_ref)
    re_ref[...] = jnp.zeros_like(re_ref)
    for slot, (bc_ref, xe_ref, ge_ref, y_ref, dx_ref, dbc_ref, dbco_ref) in enumerate(
        (
            (bc0_ref, xe0_ref, ge0_ref, y0_ref, dx0_ref, dbc0_ref, dbco0_ref),
            (bc1_ref, xe1_ref, ge1_ref, y1_ref, dx1_ref, dbc1_ref, dbco1_ref),
        )
    ):
        e_all = e_scr[slot]
        r_all = r_scr[slot]
        dbco_ref[:, :LANES] = dbc_ref[:, :LANES] + dot(xe_ref[...], r_all, NT)
        dbco_ref[:, LANES:] = dbc_ref[:, LANES:] + dot(ge_ref[...], e_all, NT)
        ce_all = dot(bc_ref[:, LANES:], e_all)
        br_all = dot(bc_ref[:, :LANES], r_all)
        for h in range(heads):
            at = slice(h * LANES, (h + 1) * LANES)
            lane = lanes[slot] + h
            one = slice(lane, lane + 1)
            ce, br = ce_all[:, at], br_all[:, at]
            y = (y_ref[:, at] + grow_ref[:, one] * ce).astype(BF16)
            dx = (dx_ref[:, at] + (step_ref[:, one] * endw_ref[:, one]) * br).astype(BF16)
            if slot == 0:
                yo_ref[:, at] = y
                dxo_ref[:, at] = dx
                x = x0_ref[:, aligned(offs_ref[0] + h * LANES, LANES)].astype(F32)
                g = g0_ref[:, aligned(offs_ref[1] + h * LANES, LANES)].astype(F32)
            else:
                send_ref[:, at] = y
                send_ref[:, width + h * LANES : width + (h + 1) * LANES] = dx
                x = back_ref[:, at].astype(F32)
                g = back_ref[:, width + h * LANES : width + (h + 1) * LANES].astype(F32)
            u_ref[:, one] = jnp.sum(g * ce, axis=1, keepdims=True)
            t_ref[:, one] = jnp.sum(x * br, axis=1, keepdims=True)
            re_ref[0:1, one] = jnp.sum(n_scr[slot][:, at], axis=1, keepdims=True)


def steps_kernel(dt_ref, bias_ref, alog_ref, step_ref, grow_ref, endw_ref, *refs):
    count = 2 * GROUPS
    gys, dss, gxs = refs[:count], refs[count : 2 * count], refs[2 * count : 3 * count]
    refs = refs[3 * count :]
    us, ts, res = refs[:GROUPS], refs[GROUPS : 2 * GROUPS], refs[2 * GROUPS : 3 * GROUPS]
    draw_ref, sums_ref = refs[3 * GROUPS :]

    def total(parts):
        value = parts[0][...]
        for a in parts[1:]:
            value = value + a[...]
        return value

    n = step_ref.shape[0]
    step = step_ref[...]
    ds = total(dss) + endw_ref[...] * total(ts)
    gy = total(gys) + grow_ref[...] * total(us)
    rate = jnp.exp(alog_ref[...])
    last = lax.broadcasted_iota(jnp.int32, (n, LANES), 0) == n - 1
    dcum = gy - step * ds + jnp.where(last, total(res)[0:1, :], 0.0)
    lower = jnp.where(triangle(n), 1.0, 0.0).astype(F32)
    dlog = dot(lower, dcum, TN, precision=HIGHEST)
    draw = (ds - rate * dlog) * jax.nn.sigmoid(dt_ref[...] + bias_ref[...])
    draw_ref[...] = draw
    sums_ref[0:1, :] = jnp.sum(draw, axis=0, keepdims=True)
    sums_ref[1:2, :] = jnp.sum(dlog * (-step * rate), axis=0, keepdims=True)
    sums_ref[2:3, :] = total(gxs)[0:1, :]
    sums_ref[3:8, :] = jnp.zeros((5, LANES), F32)


def conv_back_kernel(
    idx_ref, own_ref, ret_ref, pre_ref, ext_ref, cw_ref, heads_ref, grad_ref, message_ref, z_scr, sum_scr
):
    tokens = pre_ref.shape[0]
    taps = cw_ref.shape[0]
    pre = pre_ref[...]
    sig = jax.nn.sigmoid(pre)
    dconv = (own_ref[...] + ret_ref[...].astype(F32)) * sig * (1.0 + pre * (1.0 - sig))
    z_scr[...] = jnp.zeros_like(z_scr)
    z_scr[HALO : HALO + tokens, :] = dconv
    grad = cw_ref[0:1, :] * z_scr[taps - 1 : taps - 1 + tokens + HALO, :]
    for k in range(1, taps):
        grad = grad + cw_ref[k : k + 1, :] * z_scr[taps - 1 - k : taps - 1 - k + tokens + HALO, :]
    grad_ref[...] = grad
    first = HALO - taps + 1
    sum_scr[...] = jnp.zeros_like(sum_scr)
    for k in range(taps):
        sum_scr[k : k + 1, :] = jnp.sum(
            dconv * ext_ref[first + k : first + k + tokens, :], axis=0, keepdims=True
        )
    sum_scr[taps : taps + 1, :] = jnp.sum(dconv, axis=0, keepdims=True)
    sum_scr[8:11, aligned(idx_ref[0] * LANES, LANES)] = heads_ref[0:3, :]
    high, low = split(sum_scr[...])
    message_ref[0 : tokens + HALO, :] = grad.astype(BF16)
    message_ref[tokens + HALO : tokens + HALO + 16, :] = high
    message_ref[tokens + HALO + 16 :, :] = low


def pack_kernel(count, offs_ref, layer_ref, halo_ref, *outs):
    for k in range(count):
        at = aligned(offs_ref[k], outs[k].shape[1])
        outs[k][0:HALO, :] = halo_ref[:, at]
        outs[k][HALO:, :] = layer_ref[:, at]


def turn_kernel(count, *refs):
    out = refs[count]
    tokens = refs[0].shape[0] - HALO
    for k in range(count):
        out[:, k * tokens : (k + 1) * tokens] = refs[k][HALO:, :].T
    halos = jnp.concatenate([refs[k][0:HALO, :] for k in range(count)], 0)
    out[:, count * tokens :] = halos.T


def weight_kernel(count, size, offs_ref, left_ref, *refs):
    rights, outs, total = refs[:count], refs[count : count + size], refs[count + size]
    tokens = (left_ref.shape[1] // count) - HALO
    right = jnp.concatenate(
        [a[HALO : HALO + tokens, :] for a in rights] + [a[0:HALO, :] for a in rights], 0
    )
    total[...] = dot(left_ref[...], right)
    at = tokens + HALO
    small = jnp.zeros((16, right.shape[1]), F32)
    for a in rights:
        small += a[at : at + 16, :].astype(F32) + a[at + 16 : at + 32, :].astype(F32)
    high, low = split(small)
    chunk = outs[0].shape[0] - 32
    for k in range(size):
        outs[k][0:chunk, :] = total[pl.ds(pl.multiple_of(offs_ref[k], chunk), chunk), :].astype(BF16)
        outs[k][chunk : chunk + 16, :] = high
        outs[k][chunk + 16 :, :] = low


def reduce_kernel(count, *refs):
    total_ref, small_ref = refs[count:]
    chunk = total_ref.shape[0]
    total = refs[0][...].astype(F32)
    for k in range(1, count):
        total = total + refs[k][...].astype(F32)
    total_ref[...] = total[0:chunk].astype(BF16)
    small_ref[...] = total[chunk : chunk + 16] + total[chunk + 16 :]


def place_rows_kernel(count, offs_ref, *refs):
    out = refs[count]
    chunk = refs[0].shape[0]
    for k in range(count):
        out[pl.ds(pl.multiple_of(offs_ref[k], chunk), chunk), :] = refs[k][...].astype(F32)


def tokens_kernel(count, offs_ref, grad_ref, rim_ref, *refs):
    pieces, out = refs[:count], refs[count]
    own = grad_ref[HALO:, :]
    tail = rim_ref.shape[0]
    g = jnp.concatenate([own[:-tail], own[-tail:] + rim_ref[...]], 0).astype(BF16)
    rows = pieces[0].shape[0]
    for k in range(count):
        out[:, aligned(offs_ref[k], rows)] = dot(g, pieces[k][...], NT).astype(BF16)


def join_kernel(offs_ref, *refs):
    own_y, own_dx, back = refs[:GROUPS], refs[GROUPS : 2 * GROUPS], refs[2 * GROUPS : 3 * GROUPS]
    y_ref, dx_ref = refs[3 * GROUPS :]
    width = own_y[0].shape[1]
    for i in range(GROUPS):
        mine, others = (aligned(offs_ref[j] + i * width, width) for j in range(2))
        y_ref[:, mine] = own_y[i][...]
        dx_ref[:, mine] = own_dx[i][...]
        y_ref[:, others] = back[i][:, :width]
        dx_ref[:, others] = back[i][:, width:]


def toggled(x, axis, bits):
    size = lax.axis_size(axis)
    return lax.ppermute(x, axis, [(i, i ^ bits) for i in range(size)])


def chain(p, q, decay, axis):
    pairs = lax.axis_size(axis) // 2
    pos = lax.axis_index(axis) // 2
    received = []
    for hop in range(pairs - 1):
        value = jnp.where(pos == hop, p, q)
        if hop:
            value = decay * received[-1].astype(F32) + value.astype(F32)
        lanes = [(hop, hop + 1), (pairs - 1 - hop, pairs - 2 - hop)]
        lanes = [(2 * a + i, 2 * b + i) for a, b in lanes for i in range(2)]
        received.append(lax.ppermute(value.astype(BF16), axis, lanes))
    return received


def body(layer_in, w_bc, conv_w, conv_b, ssm_in, dt_raw, dt_bias, a_log, skip_scale, grad_out):
    ctx, fsdp = lax.axis_size("ctx"), lax.axis_size("fsdp")
    d, f = lax.axis_index("ctx").astype(jnp.int32), lax.axis_index("fsdp").astype(jnp.int32)
    r = d % 2
    layer, x, g, dt = layer_in[0], ssm_in[0], grad_out[0], dt_raw[0]
    tokens, width = x.shape
    total_heads = dt_bias.shape[0]
    heads = total_heads // 2
    half = width // 2
    hg, gw = heads // GROUPS, half // GROUPS
    state = w_bc.shape[1] // 2
    taps = conv_w.shape[0]
    rows = w_bc.shape[0]
    chunk_rows = rows // ctx
    hops = ctx // 2 - 1
    idx = jnp.stack([r, d // 2])
    own_at, other_at = r * half, (1 - r) * half
    column_offs = (jnp.arange(fsdp, dtype=jnp.int32) ^ f) * rows
    row_offs = (jnp.arange(ctx, dtype=jnp.int32) ^ d) * chunk_rows
    square = shape((tokens, LANES), F32)

    def mine(a):
        n = a.shape[-1] // 2
        return jnp.where(r == 0, a[..., :n], a[..., n:])

    halo = lax.ppermute(layer[tokens - HALO :], "ctx", [(i, i + 1) for i in range(ctx - 1)])
    pieces = {0: w_bc}
    bit = fsdp // 2
    while bit:
        for k in list(pieces):
            pieces[k | bit] = toggled(pieces[k], "fsdp", bit)
        bit //= 2
    pieces = [pieces[k] for k in range(fsdp)]
    n = dt.shape[1] // 2
    dt_recv = toggled(jnp.where(r == 0, dt[:, n:], dt[:, :n]), "ctx", 1)
    swaps = pl.pallas_call(
        swap_kernel,
        out_shape=[shape((tokens, 2 * gw), BF16)] * GROUPS,
        in_specs=[pl.BlockSpec(memory_space=pltpu.SMEM)] + [pl.BlockSpec(memory_space=pl.ANY)] * 2,
        out_specs=[pl.BlockSpec(memory_space=pltpu.VMEM)] * GROUPS,
        scratch_shapes=[pltpu.SemaphoreType.DMA((2 * GROUPS,))],
        compiler_params=pltpu.CompilerParams(vmem_limit_bytes=LIMIT),
        name="swap",
    )(other_at[None], x, g)
    swapped = [toggled(a, "ctx", 1) for a in swaps]

    def lanes_of(a):
        return jnp.pad(a, ((0, 0), (0, LANES - a.shape[1])))

    def twice(a):
        m = mine(a)[None, :]
        return lanes_of(jnp.concatenate([m, m], 1))

    dt2 = lanes_of(jnp.concatenate([mine(dt), dt_recv], 1))
    bias2, alog2 = twice(dt_bias), twice(a_log)
    step, cum, cumt, grow, endw = call(vectors_kernel, "vectors", [square] * 5, (), dt2, bias2, alog2)

    def source(slot, i):
        if slot == 0:
            at = own_at + i * gw
            return jnp.stack([at, at]), x, g
        return jnp.array([0, gw], jnp.int32), swapped[i], swapped[i]

    flat = shape((tokens, gw), BF16)
    scaled = {}
    for slot in range(2):
        for i in range(GROUPS):
            offs, xa, ga = source(slot, i)
            scaled[slot, i] = call(
                functools.partial(scale_kernel, hg, slot * heads + i * hg), "scale", [flat, flat],
                (offs,), xa, ga, step, grow, endw,
            )

    ext, pre, bc = call(
        functools.partial(project_kernel, fsdp), "project",
        [
            shape((tokens + HALO, 2 * state), F32),
            shape((tokens, 2 * state), F32),
            shape((tokens, 2 * state), BF16),
        ],
        (column_offs,), layer, halo, *pieces, conv_w, conv_b[None, :],
    )
    bcs = [bc, toggled(bc, "ctx", 1)]

    states, received = [], []
    for i in range(GROUPS):
        lanes = (i * hg, heads + i * hg)
        wide = shape((state, gw), BF16)
        p, q, s_first, d_second, decays = call(
            functools.partial(states_kernel, hg, lanes), "states",
            [wide] * 4 + [shape((8, gw), F32)],
            (idx,), *bcs, *scaled[0, i], *scaled[1, i], grow,
            scratch=[pltpu.VMEM((2, state, gw), F32)] * 2 + [pltpu.VMEM((2, 1, gw), F32)],
        )
        states.append((decays, p, s_first, d_second))
        part = gw // CHUNKS
        cut = [slice(k * part, (k + 1) * part) for k in range(CHUNKS)]
        links = [chain(p[:, a], q[:, a], decays[0:1, a], "ctx") for a in cut]
        received.append([links[k][hop] for hop in range(hops) for k in range(CHUNKS)])

    inside = {}
    for slot in range(2):
        for i in range(GROUPS):
            offs, xa, ga = source(slot, i)
            inside[slot, i] = call(
                functools.partial(inside_kernel, hg, slot * heads + i * hg, i * hg), "inside",
                [shape((tokens, gw), F32)] * 2 + [shape((tokens, tokens), F32), square, square]
                + [shape((8, LANES), F32)],
                (idx, offs, skip_scale), xa, ga, bcs[slot], step, cum, cumt,
            )
    order = [(slot, i) for slot in range(2) for i in range(GROUPS)]
    dbcs = call(
        inside_bc_kernel, "inside_bc", [shape((tokens, 2 * state), F32)] * 2, (),
        *bcs, *[inside[key][2] for key in order],
    )

    late_layer, late_halo, _ = lax.optimization_barrier((layer, halo, bc))
    packs = call(
        functools.partial(pack_kernel, fsdp), "pack", [shape((tokens + HALO, rows), BF16)] * fsdp,
        (column_offs,), late_layer, late_halo,
    )
    lefts = [packs[0]] + [toggled(packs[k], "fsdp", k) for k in range(1, fsdp)]
    left = call(
        functools.partial(turn_kernel, fsdp), "turn", shape((rows, fsdp * (tokens + HALO)), BF16),
        (), *lefts,
    )

    own_y, own_dx, sends, us, ts, res = [], [], [], [], [], []
    for i in range(GROUPS):
        offs, xa, ga = source(0, i)
        lanes = (i * hg, heads + i * hg)
        y, dx, send, *dbcs, u, t, re = call(
            functools.partial(across_kernel, hg, lanes, hops), "across",
            [flat, flat, shape((tokens, 2 * gw), BF16)] + [shape((tokens, 2 * state), F32)] * 2
            + [square, square, shape((8, LANES), F32)],
            (idx, offs), xa, ga, swapped[i], *bcs, *scaled[0, i], *scaled[1, i], step, grow, endw,
            *states[i], *inside[0, i][:2], *inside[1, i][:2], *dbcs, *received[i],
            scratch=[pltpu.VMEM((state, gw), BF16)] * 2 + [pltpu.VMEM((2, state, gw), BF16)] * 2
            + [pltpu.VMEM((2, 1, gw), F32)],
        )
        own_y.append(y)
        own_dx.append(dx)
        sends.append(send)
        us.append(u)
        ts.append(t)
        res.append(re)

    dbc_ret = toggled(dbcs[1].astype(BF16), "ctx", 1)
    draw, head_sums = call(
        steps_kernel, "steps", [square, shape((8, LANES), F32)], (), dt2, bias2, alog2, step, grow,
        endw, *[inside[key][j] for j in (3, 4, 5) for key in order], *us, *ts, *res,
    )
    grad, message = call(
        conv_back_kernel, "conv_back",
        [
            shape((tokens + HALO, 2 * state), F32),
            shape((tokens + HALO + 32, 2 * state), BF16),
        ],
        (idx,), dbcs[0], dbc_ret, pre, ext, conv_w, head_sums,
        scratch=[
            pltpu.VMEM((tokens + 2 * HALO, 2 * state), F32),
            pltpu.VMEM((16, 2 * state), F32),
        ],
    )

    rights = [message] + [toggled(message, "fsdp", k) for k in range(1, fsdp)]
    terms = call(
        functools.partial(weight_kernel, fsdp, ctx), "weight",
        [shape((chunk_rows + 32, 2 * state), BF16)] * ctx,
        (row_offs,), left, *rights,
        scratch=[pltpu.VMEM((rows, 2 * state), F32)],
    )
    arrived = [terms[0]] + [toggled(terms[k], "ctx", k) for k in range(1, ctx)]
    total, small = call(
        functools.partial(reduce_kernel, ctx), "reduce",
        [shape((chunk_rows, 2 * state), BF16), shape((16, 2 * state), F32)], (), *arrived,
    )
    everyones = [total] + [toggled(total, "ctx", k) for k in range(1, ctx)]
    grad_weight = call(
        functools.partial(place_rows_kernel, ctx), "place_rows", shape((rows, 2 * state), F32),
        (row_offs,), *everyones,
    )
    folded = small[8:11].reshape(3, 2, LANES)
    per_head = (folded[:, :, :heads] + folded[:, :, heads : 2 * heads]).reshape(3, total_heads)

    rim = lax.ppermute(grad[HALO - 8 : HALO], "ctx", [(i + 1, i) for i in range(ctx - 1)])
    grad_tokens = call(
        functools.partial(tokens_kernel, fsdp), "grad_tokens", shape((tokens, fsdp * rows), BF16),
        (column_offs,), grad, rim, *pieces,
    )
    backs = [toggled(a, "ctx", 1) for a in sends]
    ssm_out, grad_values = call(
        join_kernel, "join", [shape((tokens, width), BF16)] * 2, (jnp.stack([own_at, other_at]),),
        *own_y, *own_dx, *backs,
    )
    own_raw, back_raw = draw[:, :heads], toggled(draw[:, heads : 2 * heads], "ctx", 1)
    grad_raw = jnp.where(
        r == 0,
        jnp.concatenate([own_raw, back_raw], 1),
        jnp.concatenate([back_raw, own_raw], 1),
    )
    return (
        ssm_out[None],
        grad_values[None],
        grad_tokens[None],
        grad_raw[None],
        grad_weight,
        small[:taps],
        small[taps],
        per_head[0],
        per_head[1],
        per_head[2],
    )


def solution(mesh):
    tokens = P("fsdp", "ctx", None)
    in_specs = (tokens, P("fsdp", None), P(), P(), tokens, tokens, P(), P(), P(), tokens)
    out_specs = (tokens, tokens, tokens, tokens, P("fsdp", None), P(), P(), P(), P(), P())
    return jax.shard_map(body, mesh=mesh, in_specs=in_specs, out_specs=out_specs, check_vma=False)
```

```python
import functools

import jax
import jax.numpy as jnp
from jax import lax
from jax.experimental import pallas as pl
from jax.experimental.pallas import tpu as pltpu
from jax.sharding import PartitionSpec as P

F32 = jnp.float32
BF16 = jnp.bfloat16
LANES = 128
HALO = 16
GROUPS = 2
LIMIT = 16 * 1024 * 1024
HIGHEST = lax.Precision.HIGHEST
TN = ((0,), (0,))
NT = ((1,), (1,))


def dot(a, b, dims=((1,), (0,)), precision=None):
    return lax.dot_general(
        a, b, (dims, ((), ())), precision=precision, preferred_element_type=F32
    )


def shape(dims, dtype):
    return jax.ShapeDtypeStruct(dims, dtype)


def call(kernel, name, out_shape, smem, *operands, hbm=(), hbm_outs=0, scratch=(), aliases=None):
    single = not isinstance(out_shape, list)
    outs = [out_shape] if single else out_shape
    spaces = [pltpu.SMEM] * len(smem) + [pltpu.HBM] * len(hbm) + [pltpu.VMEM] * len(operands)
    out_spaces = [pltpu.HBM] * hbm_outs + [pltpu.VMEM] * (len(outs) - hbm_outs)
    result = pl.pallas_call(
        kernel,
        out_shape=outs,
        in_specs=[pl.BlockSpec(memory_space=a) for a in spaces],
        out_specs=[pl.BlockSpec(memory_space=a) for a in out_spaces],
        scratch_shapes=list(scratch),
        compiler_params=pltpu.CompilerParams(vmem_limit_bytes=LIMIT),
        input_output_aliases=aliases or {},
        name=name,
    )(*smem, *hbm, *operands)
    return result[0] if single else result


def copy_all(pairs, sems):
    copies = [pltpu.make_async_copy(a, b, sems.at[i]) for i, (a, b) in enumerate(pairs)]
    for copy in copies:
        copy.start()
    return copies


def aligned(at, size):
    return pl.ds(pl.multiple_of(at, LANES), size)


def triangle(n):
    rows = lax.broadcasted_iota(jnp.int32, (n, n), 0)
    cols = lax.broadcasted_iota(jnp.int32, (n, n), 1)
    return rows >= cols


def split(value):
    high = value.astype(BF16)
    return high, (value - high.astype(F32)).astype(BF16)


def swap_kernel(offs_ref, layer_ref, x_ref, g_ref, *refs):
    halo_ref, outs, sems = refs[0], refs[1 : 1 + GROUPS], refs[1 + GROUPS]
    width = outs[0].shape[1] // 2
    tokens = layer_ref.shape[0]
    pairs = [(layer_ref.at[tokens - HALO : tokens, :], halo_ref)]
    for i in range(GROUPS):
        for j, source in enumerate((x_ref, g_ref)):
            at = aligned(offs_ref[0] + i * width, width)
            pairs.append((source.at[:, at], outs[i].at[:, j * width : (j + 1) * width]))
    for copy in copy_all(pairs, sems):
        copy.wait()


def vectors_kernel(dt_ref, bias_ref, alog_ref, step_ref, cum_ref, cumt_ref, grow_ref, endw_ref):
    raw = dt_ref[...] + bias_ref[...]
    step = jnp.maximum(raw, 0.0) + jnp.log1p(jnp.exp(-jnp.abs(raw)))
    log_decay = -step * jnp.exp(alog_ref[...])
    n = raw.shape[0]
    lower = jnp.where(triangle(n), 1.0, 0.0).astype(F32)
    cum = dot(lower, log_decay, precision=HIGHEST)
    step_ref[...] = step
    cum_ref[...] = cum
    cumt_ref[...] = cum.T
    grow_ref[...] = jnp.exp(cum)
    endw_ref[...] = jnp.exp(cum[n - 1 : n, :] - cum)


def project_kernel(count, offs_ref, layer_ref, *refs):
    pieces = refs[:count]
    halo_ref, cw_ref, cb_ref, kept_ref, bc_ref, layer_scr, w_scr, sems = refs[count:]
    rows = pieces[0].shape[0]
    taps = cw_ref.shape[0]
    tokens = layer_ref.shape[0]
    pairs = [(layer_ref, layer_scr)] + [(pieces[k], w_scr.at[k]) for k in range(count)]
    copies = copy_all(pairs, sems)
    total = jnp.zeros((tokens, pieces[0].shape[1]), F32)
    rim = jnp.zeros((HALO, pieces[0].shape[1]), F32)
    copies[0].wait()
    for k in range(count):
        copies[k + 1].wait()
        at = aligned(offs_ref[k], rows)
        w = w_scr[k]
        total += dot(layer_scr[:, at], w)
        rim += dot(halo_ref[:, at], w)
    kept_ref[0:HALO, :] = rim
    kept_ref[HALO : HALO + tokens, :] = total
    first = HALO - taps + 1
    pre = cb_ref[...] + cw_ref[0:1, :] * kept_ref[first : first + tokens, :]
    for k in range(1, taps):
        pre = pre + cw_ref[k : k + 1, :] * kept_ref[first + k : first + k + tokens, :]
    kept_ref[HALO + tokens :, :] = pre
    bc_ref[...] = (pre * jax.nn.sigmoid(pre)).astype(BF16)


def scale_kernel(heads, lane, offs_ref, x_ref, g_ref, step_ref, grow_ref, endw_ref, xe_ref, ge_ref):
    for h in range(heads):
        at = slice(h * LANES, (h + 1) * LANES)
        one = slice(lane + h, lane + h + 1)
        x = x_ref[:, aligned(offs_ref[0] + h * LANES, LANES)].astype(F32)
        g = g_ref[:, aligned(offs_ref[1] + h * LANES, LANES)].astype(F32)
        xe_ref[:, at] = (x * (step_ref[:, one] * endw_ref[:, one])).astype(BF16)
        ge_ref[:, at] = (g * grow_ref[:, one]).astype(BF16)


def widen(row, lane, heads):
    return jnp.concatenate(
        [jnp.broadcast_to(row[:, lane + h : lane + h + 1], (1, LANES)) for h in range(heads)], 1
    )


def states_kernel(
    heads, lanes, idx_ref, bc0_ref, bc1_ref, xe0_ref, ge0_ref, xe1_ref, ge1_ref, grow_ref,
    first_ref, p_ref, q_ref, sf_ref, ds_ref, dec_ref, s_scr, d_scr, dec_scr,
):
    n = grow_ref.shape[0]
    r = idx_ref[0]
    for slot, (bc_ref, xe_ref, ge_ref) in enumerate(
        ((bc0_ref, xe0_ref, ge0_ref), (bc1_ref, xe1_ref, ge1_ref))
    ):
        s_scr[slot] = dot(bc_ref[:, :LANES], xe_ref[...], TN)
        d_scr[slot] = dot(bc_ref[:, LANES:], ge_ref[...], TN)
        dec_scr[slot] = widen(grow_ref[n - 1 : n, :], lanes[slot], heads)
    dec_first, dec_second = dec_scr[r], dec_scr[1 - r]
    s_first, d_second = s_scr[r], d_scr[1 - r]
    sf_ref[...] = s_first.astype(BF16)
    ds_ref[...] = d_second.astype(BF16)
    p = (dec_second * s_first + s_scr[1 - r]).astype(BF16)
    q = (dec_first * d_second + d_scr[r]).astype(BF16)
    p_ref[...] = p
    q_ref[...] = q

    @pl.when(idx_ref[1] == 0)
    def _():
        first_ref[...] = p

    @pl.when(idx_ref[1] != 0)
    def _():
        first_ref[...] = q

    dec_ref[0:1, :] = dec_first * dec_second
    dec_ref[1:2, :] = dec_first
    dec_ref[2:3, :] = dec_second
    dec_ref[3:8, :] = jnp.zeros((5, dec_first.shape[1]), F32)


def hop_kernel(hop, idx_ref, received_ref, p_ref, q_ref, dec_ref, out_ref):
    carried = dec_ref[0:1, :] * received_ref[...].astype(F32)

    @pl.when(idx_ref[1] == hop)
    def _():
        out_ref[...] = (carried + p_ref[...].astype(F32)).astype(BF16)

    @pl.when(idx_ref[1] != hop)
    def _():
        out_ref[...] = (carried + q_ref[...].astype(F32)).astype(BF16)


def inside_kernel(
    heads, lane, skip_at, idx_ref, offs_ref, skip_ref, x_ref, g_ref, bc_ref, step_ref, cum_ref,
    cumt_ref, y_ref, dx_ref, dscores_ref, gy_ref, ds_ref, gx_ref,
):
    n = step_ref.shape[0]
    mask = triangle(n)
    scores = jnp.where(mask, dot(bc_ref[:, LANES:], bc_ref[:, :LANES], NT), 0.0)
    gy_ref[...] = jnp.zeros_like(gy_ref)
    ds_ref[...] = jnp.zeros_like(ds_ref)
    gx_ref[...] = jnp.zeros_like(gx_ref)
    dscores = jnp.zeros((n, n), F32)
    for h in range(heads):
        at = slice(h * LANES, (h + 1) * LANES)
        one = slice(lane + h, lane + h + 1)
        step = step_ref[:, one]
        gap = cum_ref[:, one] - cumt_ref[one, :]
        decay = jnp.exp(jnp.where(mask, gap, 0.0))
        mixing = (scores * decay).astype(BF16)
        x = x_ref[:, aligned(offs_ref[0] + h * LANES, LANES)].astype(F32)
        g = g_ref[:, aligned(offs_ref[1] + h * LANES, LANES)]
        gf = g.astype(F32)
        xs = (x * step).astype(BF16)
        skip = skip_ref[idx_ref[0] * GROUPS * heads + skip_at + h]
        y = dot(mixing, xs)
        dxs = dot(mixing, g, TN)
        dscores += dot(g, xs, NT) * decay
        y_ref[:, at] = y + skip * x
        dx_ref[:, at] = dxs * step + skip * gf
        gy_ref[:, one] = jnp.sum(gf * y, axis=1, keepdims=True)
        ds_ref[:, one] = jnp.sum(x * dxs, axis=1, keepdims=True)
        gx_ref[0:1, one] = jnp.sum(jnp.sum(gf * x, axis=0, keepdims=True), axis=1, keepdims=True)
    dscores_ref[...] = jnp.where(mask, dscores, 0.0)


def inside_bc_kernel(bc0_ref, bc1_ref, *refs):
    parts, outs = refs[: 2 * GROUPS], refs[2 * GROUPS :]
    for slot, bc_ref in enumerate((bc0_ref, bc1_ref)):
        total = parts[slot * GROUPS][...]
        for i in range(1, GROUPS):
            total = total + parts[slot * GROUPS + i][...]
        ds = total.astype(BF16)
        outs[slot][:, :LANES] = dot(ds, bc_ref[:, LANES:], TN)
        outs[slot][:, LANES:] = dot(ds, bc_ref[:, :LANES])


def across_kernel(
    heads, lanes, hops, filled, idx_ref, offs_ref, *refs
):
    refs = refs[2 * filled :]
    across_block(heads, lanes, hops, idx_ref, offs_ref, *refs)


def across_block(
    heads, lanes, hops, idx_ref, offs_ref, x0_ref, g0_ref, back_ref, bc0_ref, bc1_ref, xe0_ref,
    ge0_ref, xe1_ref, ge1_ref, step_ref, grow_ref, endw_ref, dec_ref, p_ref, sf_ref, ds_ref,
    y0_ref, dx0_ref, y1_ref, dx1_ref, dbc0_ref, dbc1_ref, *refs
):
    received = refs[:hops]
    (
        yf_ref, dxf_ref, send_ref, dbco0_ref, dbco1_ref, u_ref, t_ref, re_ref,
        e_in, r_in, e_scr, r_scr, n_scr, yo_ref, dxo_ref, sems,
    ) = refs[hops:]
    r, pos = idx_ref[0], idx_ref[1]
    width = back_ref.shape[1] // 2
    e_in[...] = jnp.zeros_like(e_in)
    r_in[...] = jnp.zeros_like(r_in)
    for k in range(hops):

        @pl.when(pos - 1 == k)
        def _(k=k):
            e_in[...] = received[k][...]

        @pl.when(hops - 1 - pos == k)
        def _(k=k):
            r_in[...] = received[k][...]

    dec_pair, dec_first, dec_second = dec_ref[0:1, :], dec_ref[1:2, :], dec_ref[2:3, :]
    entering = e_in[...].astype(F32)
    later = r_in[...].astype(F32)
    middle = dec_first * entering + sf_ref[...].astype(F32)
    leaving = dec_pair * entering + p_ref[...].astype(F32)
    earlier = dec_second * later + ds_ref[...].astype(F32)
    e_scr[r] = e_in[...]
    e_scr[1 - r] = middle.astype(BF16)
    r_scr[1 - r] = r_in[...]
    r_scr[r] = earlier.astype(BF16)
    n_scr[1 - r] = jnp.sum(later * leaving, axis=0, keepdims=True)
    n_scr[r] = jnp.sum(earlier * middle, axis=0, keepdims=True)

    u_ref[...] = jnp.zeros_like(u_ref)
    t_ref[...] = jnp.zeros_like(t_ref)
    re_ref[...] = jnp.zeros_like(re_ref)
    for slot, (bc_ref, xe_ref, ge_ref, y_ref, dx_ref, dbc_ref, dbco_ref) in enumerate(
        (
            (bc0_ref, xe0_ref, ge0_ref, y0_ref, dx0_ref, dbc0_ref, dbco0_ref),
            (bc1_ref, xe1_ref, ge1_ref, y1_ref, dx1_ref, dbc1_ref, dbco1_ref),
        )
    ):
        e_all = e_scr[slot]
        r_all = r_scr[slot]
        dbco_ref[:, :LANES] = dbc_ref[:, :LANES] + dot(xe_ref[...], r_all, NT)
        dbco_ref[:, LANES:] = dbc_ref[:, LANES:] + dot(ge_ref[...], e_all, NT)
        ce_all = dot(bc_ref[:, LANES:], e_all)
        br_all = dot(bc_ref[:, :LANES], r_all)
        for h in range(heads):
            at = slice(h * LANES, (h + 1) * LANES)
            lane = lanes[slot] + h
            one = slice(lane, lane + 1)
            ce, br = ce_all[:, at], br_all[:, at]
            y = (y_ref[:, at] + grow_ref[:, one] * ce).astype(BF16)
            dx = (dx_ref[:, at] + (step_ref[:, one] * endw_ref[:, one]) * br).astype(BF16)
            if slot == 0:
                yo_ref[:, at] = y
                dxo_ref[:, at] = dx
                x = x0_ref[:, aligned(offs_ref[0] + h * LANES, LANES)].astype(F32)
                g = g0_ref[:, aligned(offs_ref[1] + h * LANES, LANES)].astype(F32)
            else:
                send_ref[:, at] = y
                send_ref[:, width + h * LANES : width + (h + 1) * LANES] = dx
                x = back_ref[:, at].astype(F32)
                g = back_ref[:, width + h * LANES : width + (h + 1) * LANES].astype(F32)
            u_ref[:, one] = jnp.sum(g * ce, axis=1, keepdims=True)
            t_ref[:, one] = jnp.sum(x * br, axis=1, keepdims=True)
            re_ref[0:1, one] = jnp.sum(n_scr[slot][:, at], axis=1, keepdims=True)
        if slot == 0:
            columns = aligned(offs_ref[0], width)
            pairs = [(yo_ref, yf_ref.at[:, columns]), (dxo_ref, dxf_ref.at[:, columns])]
            copies = copy_all(pairs, sems)
    for copy in copies:
        copy.wait()


def steps_kernel(dt_ref, bias_ref, alog_ref, step_ref, grow_ref, endw_ref, *refs):
    count = 2 * GROUPS
    gys, dss, gxs = refs[:count], refs[count : 2 * count], refs[2 * count : 3 * count]
    refs = refs[3 * count :]
    us, ts, res = refs[:GROUPS], refs[GROUPS : 2 * GROUPS], refs[2 * GROUPS : 3 * GROUPS]
    own_ref, send_ref, sums_ref = refs[3 * GROUPS :]

    def total(parts):
        value = parts[0][...]
        for a in parts[1:]:
            value = value + a[...]
        return value

    n = step_ref.shape[0]
    step = step_ref[...]
    ds = total(dss) + endw_ref[...] * total(ts)
    gy = total(gys) + grow_ref[...] * total(us)
    rate = jnp.exp(alog_ref[...])
    last = lax.broadcasted_iota(jnp.int32, (n, LANES), 0) == n - 1
    dcum = gy - step * ds + jnp.where(last, total(res)[0:1, :], 0.0)
    lower = jnp.where(triangle(n), 1.0, 0.0).astype(F32)
    dlog = dot(lower, dcum, TN, precision=HIGHEST)
    draw = (ds - rate * dlog) * jax.nn.sigmoid(dt_ref[...] + bias_ref[...])
    turned = draw.T
    heads = own_ref.shape[0]
    own_ref[...] = turned[:heads, :]
    send_ref[...] = turned[heads : 2 * heads, :]
    sums_ref[0:1, :] = jnp.sum(draw, axis=0, keepdims=True)
    sums_ref[1:2, :] = jnp.sum(dlog * (-step * rate), axis=0, keepdims=True)
    sums_ref[2:3, :] = total(gxs)[0:1, :]
    sums_ref[3:8, :] = jnp.zeros((5, LANES), F32)


def conv_back_kernel(
    idx_ref, own_ref, ret_ref, kept_ref, cw_ref, heads_ref, grad_ref, rim_ref, message_ref, z_scr, sum_scr
):
    tokens = own_ref.shape[0]
    taps = cw_ref.shape[0]
    pre = kept_ref[HALO + tokens :, :]
    sig = jax.nn.sigmoid(pre)
    dconv = (own_ref[...] + ret_ref[...].astype(F32)) * sig * (1.0 + pre * (1.0 - sig))
    z_scr[...] = jnp.zeros_like(z_scr)
    z_scr[HALO : HALO + tokens, :] = dconv
    grad = cw_ref[0:1, :] * z_scr[taps - 1 : taps - 1 + tokens + HALO, :]
    for k in range(1, taps):
        grad = grad + cw_ref[k : k + 1, :] * z_scr[taps - 1 - k : taps - 1 - k + tokens + HALO, :]
    grad_ref[...] = grad[HALO:, :]
    rim_ref[...] = grad[HALO - 8 : HALO, :]
    first = HALO - taps + 1
    sum_scr[...] = jnp.zeros_like(sum_scr)
    for k in range(taps):
        sum_scr[k : k + 1, :] = jnp.sum(
            dconv * kept_ref[first + k : first + k + tokens, :], axis=0, keepdims=True
        )
    sum_scr[taps : taps + 1, :] = jnp.sum(dconv, axis=0, keepdims=True)
    sum_scr[8:11, aligned(idx_ref[0] * LANES, LANES)] = heads_ref[0:3, :]
    high, low = split(sum_scr[...])
    grad = grad.astype(BF16)
    for k in range(message_ref.shape[0]):
        message_ref[k, 0 : tokens + HALO, :] = grad
        message_ref[k, tokens + HALO : tokens + HALO + 16, :] = high
        message_ref[k, tokens + HALO + 16 :, :] = low


def pack_kernel(layer_ref, halo_ref, out_ref, sems):
    count, _, rows = out_ref.shape
    pairs = []
    for k in range(count):
        at = slice(k * rows, (k + 1) * rows)
        pairs.append((halo_ref.at[:, at], out_ref.at[k, 0:HALO, :]))
        pairs.append((layer_ref.at[:, at], out_ref.at[k, HALO:, :]))
    for copy in copy_all(pairs, sems):
        copy.wait()


def turn_kernel(parts_ref, out_ref):
    count, tokens, _ = parts_ref.shape
    tokens -= HALO
    for k in range(count):
        out_ref[:, k * tokens : (k + 1) * tokens] = parts_ref[k, HALO:, :].T
    halos = jnp.concatenate([parts_ref[k, 0:HALO, :] for k in range(count)], 0)
    out_ref[:, count * tokens :] = halos.T


def weight_kernel(left_ref, rights_ref, out_ref):
    count = rights_ref.shape[0]
    tokens = (left_ref.shape[1] // count) - HALO
    right = jnp.concatenate(
        [rights_ref[k, HALO : HALO + tokens, :] for k in range(count)]
        + [rights_ref[k, 0:HALO, :] for k in range(count)],
        0,
    )
    at = tokens + HALO
    small = jnp.zeros((16, right.shape[1]), F32)
    for k in range(count):
        small += rights_ref[k, at : at + 16, :].astype(F32)
        small += rights_ref[k, at + 16 : at + 32, :].astype(F32)
    high, low = split(small)
    chunk = out_ref.shape[1] - 32
    for k in range(out_ref.shape[0]):
        term = dot(left_ref[k * chunk : (k + 1) * chunk, :], right)
        out_ref[k, 0:chunk, :] = term.astype(BF16)
        out_ref[k, chunk : chunk + 16, :] = high
        out_ref[k, chunk + 16 :, :] = low


def reduce_kernel(heads, terms_ref, total_ref, cw_ref, cb_ref, *head_refs):
    chunk = total_ref.shape[1]
    total = terms_ref[0].astype(F32)
    for k in range(1, terms_ref.shape[0]):
        total = total + terms_ref[k].astype(F32)
    for k in range(total_ref.shape[0]):
        total_ref[k] = total[0:chunk].astype(BF16)
    small = total[chunk : chunk + 16] + total[chunk + 16 :]
    taps = cw_ref.shape[0]
    cw_ref[...] = small[0:taps, :]
    cb_ref[...] = small[taps : taps + 1, :]
    for i, ref in enumerate(head_refs):
        row = small[8 + i : 9 + i, :]
        ref[:, :heads] = row[:, :heads] + row[:, heads : 2 * heads]
        row = row[:, LANES:]
        ref[:, heads:] = row[:, :heads] + row[:, heads : 2 * heads]


def place_rows_kernel(parts_ref, out_ref):
    chunk = parts_ref.shape[1]
    for k in range(parts_ref.shape[0]):
        out_ref[k * chunk : (k + 1) * chunk, :] = parts_ref[k].astype(F32)


def tokens_kernel(count, offs_ref, *refs):
    pieces = refs[:count]
    grad_ref, rim_ref, out_ref, w_scr, sems = refs[count:]
    copies = copy_all([(pieces[k], w_scr.at[k]) for k in range(count)], sems)
    tail = rim_ref.shape[0]
    own = grad_ref[...]
    g = jnp.concatenate([own[:-tail], own[-tail:] + rim_ref[...]], 0).astype(BF16)
    rows = pieces[0].shape[0]
    for k in range(count):
        copies[k].wait()
        out_ref[:, aligned(offs_ref[k], rows)] = dot(g, w_scr[k], NT).astype(BF16)


def join_kernel(offs_ref, *refs):
    backs = refs[2 : 2 + GROUPS]
    own_ref, back_ref, y_ref, dx_ref, raw_ref, sems = refs[2 + GROUPS :]
    width = backs[0].shape[1] // 2
    pairs = []
    for i in range(GROUPS):
        at = aligned(offs_ref[0] + i * width, width)
        pairs.append((backs[i].at[:, :width], y_ref.at[:, at]))
        pairs.append((backs[i].at[:, width:], dx_ref.at[:, at]))
    copies = copy_all(pairs, sems)
    heads = own_ref.shape[0]
    r = offs_ref[1]
    raw_ref[pl.ds(pl.multiple_of(r * heads, 8), heads), :] = own_ref[...]
    raw_ref[pl.ds(pl.multiple_of((1 - r) * heads, 8), heads), :] = back_ref[...]
    for copy in copies:
        copy.wait()


def toggled(x, axis, bits):
    size = lax.axis_size(axis)
    return lax.ppermute(x, axis, [(i, i ^ bits) for i in range(size)])


def exchanged(x, axis):
    return lax.all_to_all(x, axis, 0, 0)


def after(x, *others):
    return lax.optimization_barrier((x, *others))[0]


def body(layer_in, w_bc, conv_w, conv_b, ssm_in, dt_raw, dt_bias, a_log, skip_scale, grad_out):
    ctx, fsdp = lax.axis_size("ctx"), lax.axis_size("fsdp")
    d, f = lax.axis_index("ctx").astype(jnp.int32), lax.axis_index("fsdp").astype(jnp.int32)
    r = d % 2
    layer, x, g, dt = layer_in[0], ssm_in[0], grad_out[0], dt_raw[0]
    tokens, width = x.shape
    total_heads = dt_bias.shape[0]
    heads = total_heads // 2
    half = width // 2
    hg, gw = heads // GROUPS, half // GROUPS
    state = w_bc.shape[1] // 2
    taps = conv_w.shape[0]
    rows = w_bc.shape[0]
    chunk_rows = rows // ctx
    pairs = ctx // 2
    hops = pairs - 1
    idx = jnp.stack([r, d // 2])
    own_at, other_at = r * half, (1 - r) * half
    column_offs = (jnp.arange(fsdp, dtype=jnp.int32) ^ f) * rows
    square = shape((tokens, LANES), F32)
    both_bc = [shape((tokens, 2 * state), F32)] * 2

    def mine(a):
        n = a.shape[-1] // 2
        return jnp.where(r == 0, a[..., :n], a[..., n:])

    pieces = {0: w_bc}
    bit = fsdp // 2
    while bit:
        for k in list(pieces):
            pieces[k | bit] = toggled(pieces[k], "fsdp", bit)
        bit //= 2
    pieces = [pieces[k] for k in range(fsdp)]
    halo_send, *swaps = call(
        swap_kernel, "swap",
        [shape((HALO, layer.shape[1]), BF16)] + [shape((tokens, 2 * gw), BF16)] * GROUPS,
        (other_at[None],), hbm=(layer, x, g),
        scratch=[pltpu.SemaphoreType.DMA((1 + 2 * GROUPS,))],
    )
    halo = lax.ppermute(halo_send, "ctx", [(i, i + 1) for i in range(ctx - 1)])
    n = dt.shape[1] // 2
    dt_recv = toggled(jnp.where(r == 0, dt[:, n:], dt[:, :n]), "ctx", 1)
    swapped = [toggled(after(a, halo, dt_recv), "ctx", 1) for a in swaps]

    def lanes_of(a):
        return jnp.pad(a, ((0, 0), (0, LANES - a.shape[1])))

    def twice(a):
        m = mine(a)[None, :]
        return lanes_of(jnp.concatenate([m, m], 1))

    dt2 = lanes_of(jnp.concatenate([mine(dt), dt_recv], 1))
    bias2, alog2 = twice(dt_bias), twice(a_log)
    step, cum, cumt, grow, endw = call(vectors_kernel, "vectors", [square] * 5, (), dt2, bias2, alog2)

    def source(slot, i):
        if slot == 0:
            at = own_at + i * gw
            return jnp.stack([at, at]), x, g
        return jnp.array([0, gw], jnp.int32), swapped[i], swapped[i]

    flat = shape((tokens, gw), BF16)

    def scale(slot, i):
        offs, xa, ga = source(slot, i)
        return call(
            functools.partial(scale_kernel, hg, slot * heads + i * hg), "scale", [flat, flat],
            (offs,), xa, ga, step, grow, endw,
        )

    scaled = {(0, i): scale(0, i) for i in range(GROUPS)}
    kept, bc = call(
        functools.partial(project_kernel, fsdp), "project",
        [
            shape((2 * tokens + HALO, 2 * state), F32),
            shape((tokens, 2 * state), BF16),
        ],
        (column_offs,), after(halo, *[scaled[0, i][0] for i in range(GROUPS)]), conv_w,
        conv_b[None, :], hbm=(layer, *pieces),
        scratch=[
            pltpu.VMEM(layer.shape, BF16),
            pltpu.VMEM((fsdp, *w_bc.shape), BF16),
            pltpu.SemaphoreType.DMA((1 + fsdp,)),
        ],
    )
    bcs = [bc, toggled(bc, "ctx", 1)]

    wide = shape((state, gw), BF16)
    states, received = [], []
    for i in range(GROUPS):
        lanes = (i * hg, heads + i * hg)
        scaled[1, i] = scale(1, i)
        first, p, q, s_first, d_second, decays = call(
            functools.partial(states_kernel, hg, lanes), "states",
            [wide] * 5 + [shape((8, gw), F32)],
            (idx,), *bcs, *scaled[0, i], *scaled[1, i], grow,
            scratch=[pltpu.VMEM((2, state, gw), F32)] * 2 + [pltpu.VMEM((2, 1, gw), F32)],
        )
        states.append((decays, p, s_first, d_second, q))
        received.append([first])

    def within(slot, i):
        offs, xa, ga = source(slot, i)
        return call(
            functools.partial(inside_kernel, hg, slot * heads + i * hg, i * hg), "inside",
            [shape((tokens, gw), F32)] * 2 + [shape((tokens, tokens), F32), square, square]
            + [shape((8, LANES), F32)],
            (idx, offs, skip_scale), xa, ga, bcs[slot], step, cum, cumt,
        )

    order = [(slot, i) for slot in range(2) for i in range(GROUPS)]
    inside = {}
    waiting = list(order)
    for hop in range(hops):
        moves = [(hop, hop + 1), (pairs - 1 - hop, pairs - 2 - hop)]
        moves = [(2 * a + i, 2 * b + i) for a, b in moves for i in range(2)]
        for i in range(GROUPS):
            value = received[i][-1]
            if hop:
                decays, p, _, _, q = states[i]
                if waiting:
                    key = waiting.pop(0)
                    inside[key] = within(*key)
                    value = after(value, inside[key][2])
                value = call(
                    functools.partial(hop_kernel, hop), "hop", wide, (idx,), value, p, q, decays
                )
            received[i].append(lax.ppermute(value, "ctx", moves))
    for key in waiting:
        inside[key] = within(*key)
    dbcs = call(inside_bc_kernel, "inside_bc", both_bc, (), *bcs, *[inside[key][2] for key in order])

    packs = call(
        pack_kernel, "pack", shape((fsdp, tokens + HALO, rows), BF16), (),
        hbm=(layer, after(halo, bc)), scratch=[pltpu.SemaphoreType.DMA((2 * fsdp,))],
    )
    left = call(
        turn_kernel, "turn", shape((rows, fsdp * (tokens + HALO)), BF16), (),
        exchanged(packs, "fsdp"),
    )

    full = shape((tokens, width), BF16)
    finals, sends, us, ts, res = (), [], [], [], []
    for i in range(GROUPS):
        offs, xa, ga = source(0, i)
        lanes = (i * hg, heads + i * hg)
        y, dx, send, *dbcs, u, t, re = call(
            functools.partial(across_kernel, hg, lanes, hops, len(finals) // 2), "across",
            [full, full, shape((tokens, 2 * gw), BF16)] + both_bc
            + [square, square, shape((8, LANES), F32)],
            (idx, offs), xa, ga, swapped[i], *bcs, *scaled[0, i], *scaled[1, i], step, grow, endw,
            *states[i][:4], *inside[0, i][:2], *inside[1, i][:2], *dbcs, *received[i][1:],
            hbm=finals, hbm_outs=2, aliases={2: 0, 3: 1} if finals else None,
            scratch=[pltpu.VMEM((state, gw), BF16)] * 2 + [pltpu.VMEM((2, state, gw), BF16)] * 2
            + [pltpu.VMEM((2, 1, gw), F32)] + [pltpu.VMEM((tokens, gw), BF16)] * 2
            + [pltpu.SemaphoreType.DMA((2,))],
        )
        finals = (y, dx)
        sends.append(send)
        us.append(u)
        ts.append(t)
        res.append(re)

    dbc_ret = toggled(dbcs[1].astype(BF16), "ctx", 1)
    backs = [toggled(a, "ctx", 1) for a in sends[:-1]]
    raw_own, raw_send, head_sums = call(
        steps_kernel, "steps", [shape((heads, tokens), F32)] * 2 + [shape((8, LANES), F32)], (),
        dt2, bias2, alog2, step, grow, endw, *[inside[key][j] for j in (3, 4, 5) for key in order],
        *us, *ts, *res,
    )
    raw_back = toggled(raw_send, "ctx", 1)
    grad, rim_send, message = call(
        conv_back_kernel, "conv_back",
        [
            shape((tokens, 2 * state), F32),
            shape((8, 2 * state), F32),
            shape((fsdp, tokens + HALO + 32, 2 * state), BF16),
        ],
        (idx,), dbcs[0], dbc_ret, kept, conv_w, head_sums,
        scratch=[
            pltpu.VMEM((tokens + 2 * HALO, 2 * state), F32),
            pltpu.VMEM((16, 2 * state), F32),
        ],
    )
    rim = lax.ppermute(rim_send, "ctx", [(i + 1, i) for i in range(ctx - 1)])
    backs.append(toggled(after(sends[-1], rim), "ctx", 1))

    rights = exchanged(message, "fsdp")
    terms = call(
        weight_kernel, "weight", shape((ctx, chunk_rows + 32, 2 * state), BF16), (),
        left, after(rights, rim, raw_back, *backs[:-1]),
    )
    total, grad_cw, grad_cb, *per_head = call(
        functools.partial(reduce_kernel, heads), "reduce",
        [
            shape((ctx, chunk_rows, 2 * state), BF16),
            shape((taps, 2 * state), F32),
            shape((1, 2 * state), F32),
        ]
        + [shape((1, total_heads), F32)] * 3,
        (), after(exchanged(terms, "ctx"), backs[-1]),
    )
    grad_weight = call(
        place_rows_kernel, "place_rows", shape((rows, 2 * state), F32), (), exchanged(total, "ctx")
    )
    grad_tokens = call(
        functools.partial(tokens_kernel, fsdp), "grad_tokens", shape((tokens, fsdp * rows), BF16),
        (column_offs,), grad, rim, hbm=pieces,
        scratch=[pltpu.VMEM((fsdp, *w_bc.shape), BF16), pltpu.SemaphoreType.DMA((fsdp,))],
    )
    ssm_out, grad_values, grad_raw = call(
        join_kernel, "join", [full, full, shape((total_heads, tokens), F32)],
        (jnp.stack([other_at, r]),), raw_own, raw_back, hbm=(*finals, *backs), hbm_outs=2,
        aliases={1: 0, 2: 1}, scratch=[pltpu.SemaphoreType.DMA((2 * GROUPS,))],
    )
    return (
        ssm_out[None],
        grad_values[None],
        grad_tokens[None],
        grad_raw.T[None],
        grad_weight,
        grad_cw,
        grad_cb[0],
        *[a[0] for a in per_head],
    )


def solution(mesh):
    tokens = P("fsdp", "ctx", None)
    in_specs = (tokens, P("fsdp", None), P(), P(), tokens, tokens, P(), P(), P(), tokens)
    out_specs = (tokens, tokens, tokens, tokens, P("fsdp", None), P(), P(), P(), P(), P())
    return jax.shard_map(body, mesh=mesh, in_specs=in_specs, out_specs=out_specs, check_vma=False)
```

```python
import functools

import jax
import jax.numpy as jnp
from jax import lax
from jax.experimental import pallas as pl
from jax.experimental.pallas import tpu as pltpu
from jax.sharding import PartitionSpec as P

F32 = jnp.float32
BF16 = jnp.bfloat16
LANES = 128
HALO = 16
GROUPS = 2
LIMIT = 16 * 1024 * 1024
HIGHEST = lax.Precision.HIGHEST
TN = ((0,), (0,))
NT = ((1,), (1,))


def dot(a, b, dims=((1,), (0,)), precision=None):
    return lax.dot_general(
        a, b, (dims, ((), ())), precision=precision, preferred_element_type=F32
    )


def shape(dims, dtype):
    return jax.ShapeDtypeStruct(dims, dtype)


def call(kernel, name, out_shape, smem, *operands, hbm=(), hbm_outs=0, scratch=(), aliases=None):
    single = not isinstance(out_shape, list)
    outs = [out_shape] if single else out_shape
    spaces = [pltpu.SMEM] * len(smem) + [pltpu.HBM] * len(hbm) + [pltpu.VMEM] * len(operands)
    out_spaces = [pltpu.HBM] * hbm_outs + [pltpu.VMEM] * (len(outs) - hbm_outs)
    result = pl.pallas_call(
        kernel,
        out_shape=outs,
        in_specs=[pl.BlockSpec(memory_space=a) for a in spaces],
        out_specs=[pl.BlockSpec(memory_space=a) for a in out_spaces],
        scratch_shapes=list(scratch),
        compiler_params=pltpu.CompilerParams(vmem_limit_bytes=LIMIT),
        input_output_aliases=aliases or {},
        name=name,
    )(*smem, *[pltpu.with_memory_space_constraint(a, pltpu.HBM) for a in hbm], *operands)
    return result[0] if single else result


def copy_all(pairs, sems):
    copies = [pltpu.make_async_copy(a, b, sems.at[i]) for i, (a, b) in enumerate(pairs)]
    for copy in copies:
        copy.start()
    return copies


def side():
    return lax.rem(lax.axis_index("ctx"), 2)


def place():
    return lax.div(lax.axis_index("ctx"), 2)


def peer_columns(k, rows):
    return aligned((lax.axis_index("fsdp") ^ k) * rows, rows)


def aligned(at, size):
    return pl.ds(pl.multiple_of(at, LANES), size)


def triangle(n):
    rows = lax.broadcasted_iota(jnp.int32, (n, n), 0)
    cols = lax.broadcasted_iota(jnp.int32, (n, n), 1)
    return rows >= cols


def split(value):
    high = value.astype(BF16)
    return high, (value - high.astype(F32)).astype(BF16)


def swap_kernel(layer_ref, dt_ref, x_ref, g_ref, halo_ref, dt_out_ref, first_ref, x_out_ref, g_out_ref, sems):
    width = x_out_ref.shape[1]
    tokens = layer_ref.shape[0]
    heads = dt_out_ref.shape[0]
    other = 1 - side()
    base = other * (GROUPS * width)
    rows = pl.ds(pl.multiple_of(other * heads, 8), heads)
    pairs = [
        (layer_ref.at[tokens - HALO : tokens, :], halo_ref),
        (dt_ref.at[rows, :], dt_out_ref),
        (x_ref.at[:, aligned(base, width)], first_ref.at[:, :width]),
        (g_ref.at[:, aligned(base, width)], first_ref.at[:, width:]),
        (x_ref.at[:, aligned(base + width, width)], x_out_ref),
        (g_ref.at[:, aligned(base + width, width)], g_out_ref),
    ]
    for copy in copy_all(pairs, sems):
        copy.wait()


def vectors_kernel(
    dt_ref, back_ref, bias_ref, alog_ref, step_ref, cum_ref, cumt_ref, grow_ref, endw_ref, sig_ref,
    rate_ref, turned, rows,
):
    heads, n = back_ref.shape
    r = side()
    turned[...] = jnp.zeros_like(turned)
    turned[0:heads, :] = dt_ref[pl.ds(pl.multiple_of(r * heads, 8), heads), :]
    turned[heads : 2 * heads, :] = back_ref[...]
    rows[...] = jnp.zeros_like(rows)
    for i, ref in enumerate((bias_ref, alog_ref)):
        half = jnp.where(r == 0, ref[:, :heads], ref[:, heads:])
        rows[i : i + 1, 0:heads] = half
        rows[i : i + 1, heads : 2 * heads] = half
    raw = turned[...].T + rows[0:1, :]
    step = jnp.maximum(raw, 0.0) + jnp.log1p(jnp.exp(-jnp.abs(raw)))
    rate = jnp.exp(rows[1:2, :])
    log_decay = -step * rate
    lower = jnp.where(triangle(n), 1.0, 0.0).astype(F32)
    cum = dot(lower, log_decay, precision=HIGHEST)
    step_ref[...] = step
    cum_ref[...] = cum
    cumt_ref[...] = cum.T
    grow_ref[...] = jnp.exp(cum)
    endw_ref[...] = jnp.exp(cum[n - 1 : n, :] - cum)
    sig_ref[...] = jax.nn.sigmoid(raw)
    rate_ref[...] = jnp.broadcast_to(rate, rate_ref.shape)


def project_kernel(count, layer_ref, *refs):
    pieces = refs[:count]
    halo_ref, cw_ref, cb_ref, kept_ref, bc_ref, layer_scr, w_scr, sems = refs[count:]
    rows = pieces[0].shape[0]
    taps = cw_ref.shape[0]
    tokens = layer_ref.shape[0]
    pairs = [(layer_ref, layer_scr)] + [(pieces[k], w_scr.at[k]) for k in range(count)]
    copies = copy_all(pairs, sems)
    total = jnp.zeros((tokens, pieces[0].shape[1]), F32)
    rim = jnp.zeros((HALO, pieces[0].shape[1]), F32)
    copies[0].wait()
    for k in range(count):
        copies[k + 1].wait()
        at = peer_columns(k, rows)
        w = w_scr[k]
        total += dot(layer_scr[:, at], w)
        rim += dot(halo_ref[:, at], w)
    kept_ref[0:HALO, :] = rim
    kept_ref[HALO : HALO + tokens, :] = total
    first = HALO - taps + 1
    pre = cb_ref[...] + cw_ref[0:1, :] * kept_ref[first : first + tokens, :]
    for k in range(1, taps):
        pre = pre + cw_ref[k : k + 1, :] * kept_ref[first + k : first + k + tokens, :]
    kept_ref[HALO + tokens :, :] = pre
    bc_ref[...] = (pre * jax.nn.sigmoid(pre)).astype(BF16)


def head_columns(at, h):
    first, more = at
    return aligned(first + side() * more + h * LANES, LANES)


def scale_kernel(heads, lane, x_at, g_at, x_ref, g_ref, step_ref, grow_ref, endw_ref, xe_ref, ge_ref):
    for h in range(heads):
        at = slice(h * LANES, (h + 1) * LANES)
        one = slice(lane + h, lane + h + 1)
        x = x_ref[:, head_columns(x_at, h)].astype(F32)
        g = g_ref[:, head_columns(g_at, h)].astype(F32)
        xe_ref[:, at] = (x * (step_ref[:, one] * endw_ref[:, one])).astype(BF16)
        ge_ref[:, at] = (g * grow_ref[:, one]).astype(BF16)


def widen(row, lane, heads):
    return jnp.concatenate(
        [jnp.broadcast_to(row[:, lane + h : lane + h + 1], (1, LANES)) for h in range(heads)], 1
    )


def states_kernel(
    heads, lanes, bc0_ref, bc1_ref, xe0_ref, ge0_ref, xe1_ref, ge1_ref, grow_ref,
    first_ref, p_ref, q_ref, sf_ref, ds_ref, dec_ref, s_scr, d_scr, dec_scr,
):
    n = grow_ref.shape[0]
    r = side()
    for slot, (bc_ref, xe_ref, ge_ref) in enumerate(
        ((bc0_ref, xe0_ref, ge0_ref), (bc1_ref, xe1_ref, ge1_ref))
    ):
        s_scr[slot] = dot(bc_ref[:, :LANES], xe_ref[...], TN)
        d_scr[slot] = dot(bc_ref[:, LANES:], ge_ref[...], TN)
        dec_scr[slot] = widen(grow_ref[n - 1 : n, :], lanes[slot], heads)
    dec_first, dec_second = dec_scr[r], dec_scr[1 - r]
    s_first, d_second = s_scr[r], d_scr[1 - r]
    sf_ref[...] = s_first.astype(BF16)
    ds_ref[...] = d_second.astype(BF16)
    p = (dec_second * s_first + s_scr[1 - r]).astype(BF16)
    q = (dec_first * d_second + d_scr[r]).astype(BF16)
    p_ref[...] = p
    q_ref[...] = q

    @pl.when(place() == 0)
    def _():
        first_ref[...] = p

    @pl.when(place() != 0)
    def _():
        first_ref[...] = q

    dec_ref[0:1, :] = dec_first * dec_second
    dec_ref[1:2, :] = dec_first
    dec_ref[2:3, :] = dec_second
    dec_ref[3:8, :] = jnp.zeros((5, dec_first.shape[1]), F32)


def hop_kernel(hop, received_ref, p_ref, q_ref, dec_ref, out_ref):
    carried = dec_ref[0:1, :] * received_ref[...].astype(F32)

    @pl.when(place() == hop)
    def _():
        out_ref[...] = (carried + p_ref[...].astype(F32)).astype(BF16)

    @pl.when(place() != hop)
    def _():
        out_ref[...] = (carried + q_ref[...].astype(F32)).astype(BF16)


def inside_kernel(
    heads, lane, skip_at, x_at, g_at, skip_ref, x_ref, g_ref, bc_ref, step_ref, cum_ref,
    cumt_ref, y_ref, dx_ref, dscores_ref, gy_ref, ds_ref, gx_ref,
):
    n = step_ref.shape[0]
    mask = triangle(n)
    scores = jnp.where(mask, dot(bc_ref[:, LANES:], bc_ref[:, :LANES], NT), 0.0)
    gy_ref[...] = jnp.zeros_like(gy_ref)
    ds_ref[...] = jnp.zeros_like(ds_ref)
    gx_ref[...] = jnp.zeros_like(gx_ref)
    dscores = jnp.zeros((n, n), F32)
    for h in range(heads):
        at = slice(h * LANES, (h + 1) * LANES)
        one = slice(lane + h, lane + h + 1)
        step = step_ref[:, one]
        gap = cum_ref[:, one] - cumt_ref[one, :]
        decay = jnp.exp(jnp.where(mask, gap, 0.0))
        mixing = (scores * decay).astype(BF16)
        x = x_ref[:, head_columns(x_at, h)].astype(F32)
        g = g_ref[:, head_columns(g_at, h)]
        gf = g.astype(F32)
        xs = (x * step).astype(BF16)
        skip = skip_ref[side() * GROUPS * heads + skip_at + h]
        y = dot(mixing, xs)
        dxs = dot(mixing, g, TN)
        dscores += dot(g, xs, NT) * decay
        y_ref[:, at] = y + skip * x
        dx_ref[:, at] = dxs * step + skip * gf
        gy_ref[:, one] = jnp.sum(gf * y, axis=1, keepdims=True)
        ds_ref[:, one] = jnp.sum(x * dxs, axis=1, keepdims=True)
        gx_ref[0:1, one] = jnp.sum(jnp.sum(gf * x, axis=0, keepdims=True), axis=1, keepdims=True)
    dscores_ref[...] = jnp.where(mask, dscores, 0.0)


def inside_bc_kernel(bc0_ref, bc1_ref, *refs):
    parts, outs = refs[: 2 * GROUPS], refs[2 * GROUPS :]
    for slot, bc_ref in enumerate((bc0_ref, bc1_ref)):
        total = parts[slot * GROUPS][...]
        for i in range(1, GROUPS):
            total = total + parts[slot * GROUPS + i][...]
        ds = total.astype(BF16)
        outs[slot][:, :LANES] = dot(ds, bc_ref[:, LANES:], TN)
        outs[slot][:, LANES:] = dot(ds, bc_ref[:, :LANES])


def across_kernel(heads, lanes, hops, filled, own_at, columns, *refs):
    refs = refs[2 * filled :]
    across_block(heads, lanes, hops, own_at, columns, *refs)


def across_block(
    heads, lanes, hops, own_at, columns, x0_ref, g0_ref, x1_ref, g1_ref, bc0_ref, bc1_ref, xe0_ref,
    ge0_ref, xe1_ref, ge1_ref, step_ref, grow_ref, endw_ref, dec_ref, p_ref, sf_ref, ds_ref,
    y0_ref, dx0_ref, y1_ref, dx1_ref, dbc0_ref, dbc1_ref, *refs
):
    received = refs[:hops]
    (
        yf_ref, dxf_ref, send_ref, dbco0_ref, dbco1_ref, u_ref, t_ref, re_ref,
        e_in, r_in, e_scr, r_scr, n_scr, yo_ref, dxo_ref, sems,
    ) = refs[hops:]
    r, pos = side(), place()
    width = yo_ref.shape[1]
    e_in[...] = jnp.zeros_like(e_in)
    r_in[...] = jnp.zeros_like(r_in)
    for k in range(hops):

        @pl.when(pos - 1 == k)
        def _(k=k):
            e_in[...] = received[k][...]

        @pl.when(hops - 1 - pos == k)
        def _(k=k):
            r_in[...] = received[k][...]

    dec_pair, dec_first, dec_second = dec_ref[0:1, :], dec_ref[1:2, :], dec_ref[2:3, :]
    entering = e_in[...].astype(F32)
    later = r_in[...].astype(F32)
    middle = dec_first * entering + sf_ref[...].astype(F32)
    leaving = dec_pair * entering + p_ref[...].astype(F32)
    earlier = dec_second * later + ds_ref[...].astype(F32)
    e_scr[r] = e_in[...]
    e_scr[1 - r] = middle.astype(BF16)
    r_scr[1 - r] = r_in[...]
    r_scr[r] = earlier.astype(BF16)
    n_scr[1 - r] = jnp.sum(later * leaving, axis=0, keepdims=True)
    n_scr[r] = jnp.sum(earlier * middle, axis=0, keepdims=True)

    u_ref[...] = jnp.zeros_like(u_ref)
    t_ref[...] = jnp.zeros_like(t_ref)
    re_ref[...] = jnp.zeros_like(re_ref)
    for slot, (bc_ref, xe_ref, ge_ref, y_ref, dx_ref, dbc_ref, dbco_ref) in enumerate(
        (
            (bc0_ref, xe0_ref, ge0_ref, y0_ref, dx0_ref, dbc0_ref, dbco0_ref),
            (bc1_ref, xe1_ref, ge1_ref, y1_ref, dx1_ref, dbc1_ref, dbco1_ref),
        )
    ):
        e_all = e_scr[slot]
        r_all = r_scr[slot]
        db = dbc_ref[:, :LANES] + dot(xe_ref[...], r_all, NT)
        dc = dbc_ref[:, LANES:] + dot(ge_ref[...], e_all, NT)
        dbco_ref[:, :LANES] = db.astype(dbco_ref.dtype)
        dbco_ref[:, LANES:] = dc.astype(dbco_ref.dtype)
        ce_all = dot(bc_ref[:, LANES:], e_all)
        br_all = dot(bc_ref[:, :LANES], r_all)
        for h in range(heads):
            at = slice(h * LANES, (h + 1) * LANES)
            lane = lanes[slot] + h
            one = slice(lane, lane + 1)
            ce, br = ce_all[:, at], br_all[:, at]
            y = (y_ref[:, at] + grow_ref[:, one] * ce).astype(BF16)
            dx = (dx_ref[:, at] + (step_ref[:, one] * endw_ref[:, one]) * br).astype(BF16)
            if slot == 0:
                yo_ref[:, at] = y
                dxo_ref[:, at] = dx
                x = x0_ref[:, head_columns(own_at, h)].astype(F32)
                g = g0_ref[:, head_columns(own_at, h)].astype(F32)
            else:
                send_ref[:, at] = y
                send_ref[:, width + h * LANES : width + (h + 1) * LANES] = dx
                x = x1_ref[:, head_columns(columns[0], h)].astype(F32)
                g = g1_ref[:, head_columns(columns[1], h)].astype(F32)
            u_ref[:, one] = jnp.sum(g * ce, axis=1, keepdims=True)
            t_ref[:, one] = jnp.sum(x * br, axis=1, keepdims=True)
            re_ref[0:1, one] = jnp.sum(n_scr[slot][:, at], axis=1, keepdims=True)
        if slot == 0:
            final = aligned(own_at[0] + r * own_at[1], width)
            pairs = [(yo_ref, yf_ref.at[:, final]), (dxo_ref, dxf_ref.at[:, final])]
            copies = copy_all(pairs, sems)
    for copy in copies:
        copy.wait()


def steps_kernel(sig_ref, rate_ref, step_ref, grow_ref, endw_ref, *refs):
    count = 2 * GROUPS
    gys, dss, gxs = refs[:count], refs[count : 2 * count], refs[2 * count : 3 * count]
    refs = refs[3 * count :]
    us, ts, res = refs[:GROUPS], refs[GROUPS : 2 * GROUPS], refs[2 * GROUPS : 3 * GROUPS]
    own_ref, send_ref, sums_ref = refs[3 * GROUPS :]

    def total(parts):
        value = parts[0][...]
        for a in parts[1:]:
            value = value + a[...]
        return value

    n = step_ref.shape[0]
    step = step_ref[...]
    ds = total(dss) + endw_ref[...] * total(ts)
    gy = total(gys) + grow_ref[...] * total(us)
    rate = rate_ref[0:1, :]
    last = lax.broadcasted_iota(jnp.int32, (n, LANES), 0) == n - 1
    dcum = gy - step * ds + jnp.where(last, total(res)[0:1, :], 0.0)
    lower = jnp.where(triangle(n), 1.0, 0.0).astype(F32)
    dlog = dot(lower, dcum, TN, precision=HIGHEST)
    draw = (ds - rate * dlog) * sig_ref[...]
    turned = draw.T
    heads = own_ref.shape[0]
    own_ref[...] = turned[:heads, :]
    send_ref[...] = turned[heads : 2 * heads, :]
    sums_ref[0:1, :] = jnp.sum(draw, axis=0, keepdims=True)
    sums_ref[1:2, :] = jnp.sum(dlog * (-step * rate), axis=0, keepdims=True)
    sums_ref[2:3, :] = total(gxs)[0:1, :]
    sums_ref[3:8, :] = jnp.zeros((5, LANES), F32)


def conv_back_kernel(
    own_ref, ret_ref, kept_ref, cw_ref, heads_ref, grad_ref, rim_ref, message_ref, z_scr, sum_scr
):
    tokens = own_ref.shape[0]
    taps = cw_ref.shape[0]
    pre = kept_ref[HALO + tokens :, :]
    sig = jax.nn.sigmoid(pre)
    dconv = (own_ref[...] + ret_ref[...].astype(F32)) * sig * (1.0 + pre * (1.0 - sig))
    z_scr[...] = jnp.zeros_like(z_scr)
    z_scr[HALO : HALO + tokens, :] = dconv
    grad = cw_ref[0:1, :] * z_scr[taps - 1 : taps - 1 + tokens + HALO, :]
    for k in range(1, taps):
        grad = grad + cw_ref[k : k + 1, :] * z_scr[taps - 1 - k : taps - 1 - k + tokens + HALO, :]
    grad_ref[...] = grad[HALO:, :]
    rim_ref[...] = grad[HALO - 8 : HALO, :]
    first = HALO - taps + 1
    sum_scr[...] = jnp.zeros_like(sum_scr)
    for k in range(taps):
        sum_scr[k : k + 1, :] = jnp.sum(
            dconv * kept_ref[first + k : first + k + tokens, :], axis=0, keepdims=True
        )
    sum_scr[taps : taps + 1, :] = jnp.sum(dconv, axis=0, keepdims=True)
    sum_scr[8:11, aligned(side() * LANES, LANES)] = heads_ref[0:3, :]
    high, low = split(sum_scr[...])
    grad = grad.astype(BF16)
    for k in range(message_ref.shape[0]):
        message_ref[k, 0 : tokens + HALO, :] = grad
        message_ref[k, tokens + HALO : tokens + HALO + 16, :] = high
        message_ref[k, tokens + HALO + 16 :, :] = low


def pack_kernel(count, layer_ref, halo_ref, *refs):
    outs, sems = refs[:count], refs[count]
    pairs = []
    for k in range(count):
        at = peer_columns(k, outs[k].shape[1])
        pairs.append((halo_ref.at[:, at], outs[k].at[0:HALO, :]))
        pairs.append((layer_ref.at[:, at], outs[k].at[HALO:, :]))
    for copy in copy_all(pairs, sems):
        copy.wait()


def turn_kernel(count, *refs):
    parts, out_ref = refs[:count], refs[count]
    tokens = parts[0].shape[0] - HALO
    f = lax.axis_index("fsdp")
    for k in range(count):
        out_ref[:, aligned((f ^ k) * tokens, tokens)] = parts[k][HALO:, :].T
    halos = jnp.concatenate([parts[k][0:HALO, :] for k in range(count)], 0)
    out_ref[:, count * tokens :] = halos.T


def weight_kernel(left_ref, rights_ref, out_ref):
    count = rights_ref.shape[0]
    tokens = (left_ref.shape[1] // count) - HALO
    right = jnp.concatenate(
        [rights_ref[k, HALO : HALO + tokens, :] for k in range(count)]
        + [rights_ref[lax.axis_index("fsdp") ^ k, 0:HALO, :] for k in range(count)],
        0,
    )
    at = tokens + HALO
    small = jnp.zeros((16, right.shape[1]), F32)
    for k in range(count):
        small += rights_ref[k, at : at + 16, :].astype(F32)
        small += rights_ref[k, at + 16 : at + 32, :].astype(F32)
    high, low = split(small)
    chunk = out_ref.shape[1] - 32
    for k in range(out_ref.shape[0]):
        term = dot(left_ref[k * chunk : (k + 1) * chunk, :], right)
        out_ref[k, 0:chunk, :] = term.astype(BF16)
        out_ref[k, chunk : chunk + 16, :] = high
        out_ref[k, chunk + 16 :, :] = low


def reduce_kernel(heads, terms_ref, total_ref, cw_ref, cb_ref, *head_refs):
    chunk = total_ref.shape[1]
    total = terms_ref[0].astype(F32)
    for k in range(1, terms_ref.shape[0]):
        total = total + terms_ref[k].astype(F32)
    for k in range(total_ref.shape[0]):
        total_ref[k] = total[0:chunk].astype(BF16)
    small = total[chunk : chunk + 16] + total[chunk + 16 :]
    taps = cw_ref.shape[0]
    cw_ref[...] = small[0:taps, :]
    cb_ref[...] = small[taps : taps + 1, :]
    for i, ref in enumerate(head_refs):
        row = small[8 + i : 9 + i, :]
        ref[:, :heads] = row[:, :heads] + row[:, heads : 2 * heads]
        row = row[:, LANES:]
        ref[:, heads:] = row[:, :heads] + row[:, heads : 2 * heads]


def place_rows_kernel(parts_ref, out_ref):
    chunk = parts_ref.shape[1]
    for k in range(parts_ref.shape[0]):
        out_ref[k * chunk : (k + 1) * chunk, :] = parts_ref[k].astype(F32)


def tokens_kernel(count, *refs):
    pieces = refs[:count]
    grad_ref, rim_ref, out_ref, w_scr, sems = refs[count:]
    copies = copy_all([(pieces[k], w_scr.at[k]) for k in range(count)], sems)
    tail = rim_ref.shape[0]
    own = grad_ref[...]
    g = jnp.concatenate([own[:-tail], own[-tail:] + rim_ref[...]], 0).astype(BF16)
    rows = pieces[0].shape[0]
    for k in range(count):
        copies[k].wait()
        out_ref[:, peer_columns(k, rows)] = dot(g, w_scr[k], NT).astype(BF16)


def join_kernel(*refs):
    backs = refs[2 : 2 + GROUPS]
    own_ref, back_ref, y_ref, dx_ref, raw_ref, sems = refs[2 + GROUPS :]
    width = backs[0].shape[1] // 2
    r = side()
    pairs = []
    for i in range(GROUPS):
        at = aligned(((1 - r) * GROUPS + i) * width, width)
        pairs.append((backs[i].at[:, :width], y_ref.at[:, at]))
        pairs.append((backs[i].at[:, width:], dx_ref.at[:, at]))
    copies = copy_all(pairs, sems)
    heads = own_ref.shape[0]
    raw_ref[pl.ds(pl.multiple_of(r * heads, 8), heads), :] = own_ref[...]
    raw_ref[pl.ds(pl.multiple_of((1 - r) * heads, 8), heads), :] = back_ref[...]
    for copy in copies:
        copy.wait()


def toggled(x, axis, bits):
    size = lax.axis_size(axis)
    return lax.ppermute(x, axis, [(i, i ^ bits) for i in range(size)])


def exchanged(x, axis):
    return lax.all_to_all(x, axis, 0, 0)


def after(x, *others):
    return lax.optimization_barrier((x, *others))[0]


def body(layer_in, w_bc, conv_w, conv_b, ssm_in, dt_raw, dt_bias, a_log, skip_scale, grad_out):
    ctx, fsdp = lax.axis_size("ctx"), lax.axis_size("fsdp")
    layer, x, g, dt = layer_in[0], ssm_in[0], grad_out[0], dt_raw[0].T
    tokens, width = x.shape
    total_heads = dt_bias.shape[0]
    heads = total_heads // 2
    half = width // 2
    hg, gw = heads // GROUPS, half // GROUPS
    state = w_bc.shape[1] // 2
    taps = conv_w.shape[0]
    rows = w_bc.shape[0]
    chunk_rows = rows // ctx
    pairs = ctx // 2
    hops = pairs - 1
    square = shape((tokens, LANES), F32)
    flat = shape((tokens, gw), BF16)
    turned = shape((heads, tokens), F32)
    both_bc = [shape((tokens, 2 * state), F32)] * 2

    halo_send, dt_send, *swaps = call(
        swap_kernel, "swap",
        [shape((HALO, layer.shape[1]), BF16), turned, shape((tokens, 2 * gw), BF16), flat, flat], (),
        hbm=(layer, dt, x, g), scratch=[pltpu.SemaphoreType.DMA((6,))],
    )
    halo = lax.ppermute(halo_send, "ctx", [(i, i + 1) for i in range(ctx - 1)])
    dt_back = toggled(dt_send, "ctx", 1)
    pieces = {0: w_bc}
    bit = fsdp // 2
    while bit:
        for k in list(pieces):
            pieces[k | bit] = toggled(pieces[k], "fsdp", bit)
        bit //= 2
    pieces = [pieces[k] for k in range(fsdp)]
    swapped_first, swapped_x = [toggled(after(a, halo, dt_back), "ctx", 1) for a in swaps[:2]]

    step, cum, cumt, grow, endw, sig, rate = call(
        vectors_kernel, "vectors", [square] * 6 + [shape((8, LANES), F32)], (), dt, dt_back,
        dt_bias[None, :], a_log[None, :],
        scratch=[pltpu.VMEM((tokens, tokens), F32), pltpu.VMEM((8, LANES), F32)],
    )

    def source(slot, i):
        if slot == 0:
            return (i * gw, half), (i * gw, half), x, g
        if i == 0:
            return (0, 0), (gw, 0), swapped_first, swapped_first
        return (0, 0), (0, 0), swapped_x, swapped_g

    def scale(slot, i):
        x_at, g_at, xa, ga = source(slot, i)
        return call(
            functools.partial(scale_kernel, hg, slot * heads + i * hg, x_at, g_at), "scale",
            [flat, flat], (), xa, ga, step, grow, endw,
        )

    packs = call(
        functools.partial(pack_kernel, fsdp), "pack", [shape((tokens + HALO, rows), BF16)] * fsdp,
        (), hbm=(layer, halo), scratch=[pltpu.SemaphoreType.DMA((2 * fsdp,))],
    )
    lefts = [packs[0]] + [toggled(packs[k], "fsdp", k) for k in range(1, fsdp)]

    scaled = {(0, i): scale(0, i) for i in range(GROUPS)}
    kept, bc = call(
        functools.partial(project_kernel, fsdp), "project",
        [
            shape((2 * tokens + HALO, 2 * state), F32),
            shape((tokens, 2 * state), BF16),
        ],
        (), after(halo, *[scaled[0, i][0] for i in range(GROUPS)]), conv_w,
        conv_b[None, :], hbm=(layer, *pieces),
        scratch=[
            pltpu.VMEM(layer.shape, BF16),
            pltpu.VMEM((fsdp, *w_bc.shape), BF16),
            pltpu.SemaphoreType.DMA((1 + fsdp,)),
        ],
    )
    bcs = [bc, toggled(bc, "ctx", 1)]
    swapped_g = toggled(after(swaps[2], bcs[1]), "ctx", 1)

    wide = shape((state, gw), BF16)
    states, received = [], []
    for i in range(GROUPS):
        lanes = (i * hg, heads + i * hg)
        scaled[1, i] = scale(1, i)
        first, p, q, s_first, d_second, decays = call(
            functools.partial(states_kernel, hg, lanes), "states",
            [wide] * 5 + [shape((8, gw), F32)],
            (), *bcs, *scaled[0, i], *scaled[1, i], grow,
            scratch=[pltpu.VMEM((2, state, gw), F32)] * 2 + [pltpu.VMEM((2, 1, gw), F32)],
        )
        states.append((decays, p, s_first, d_second, q))
        received.append([first])

    def within(slot, i):
        x_at, g_at, xa, ga = source(slot, i)
        return call(
            functools.partial(inside_kernel, hg, slot * heads + i * hg, i * hg, x_at, g_at), "inside",
            [shape((tokens, gw), F32)] * 2 + [shape((tokens, tokens), F32), square, square]
            + [shape((8, LANES), F32)],
            (skip_scale,), xa, ga, bcs[slot], step, cum, cumt,
        )

    order = [(slot, i) for slot in range(2) for i in range(GROUPS)]
    inside = {}
    waiting = list(order)
    for hop in range(hops):
        moves = [(hop, hop + 1), (pairs - 1 - hop, pairs - 2 - hop)]
        moves = [(2 * a + i, 2 * b + i) for a, b in moves for i in range(2)]
        for i in range(GROUPS):
            value = received[i][-1]
            if hop:
                decays, p, _, _, q = states[i]
                if waiting:
                    key = waiting.pop(0)
                    inside[key] = within(*key)
                    value = after(value, inside[key][2])
                value = call(
                    functools.partial(hop_kernel, hop), "hop", wide, (), value, p, q, decays
                )
            received[i].append(lax.ppermute(value, "ctx", moves))
    for key in waiting:
        inside[key] = within(*key)
    dbcs = call(inside_bc_kernel, "inside_bc", both_bc, (), *bcs, *[inside[key][2] for key in order])

    left = call(
        functools.partial(turn_kernel, fsdp), "turn", shape((rows, fsdp * (tokens + HALO)), BF16),
        (), *lefts,
    )

    full = shape((tokens, width), BF16)
    finals, sends, us, ts, res = (), [], [], [], []
    for i in range(GROUPS):
        last = i == GROUPS - 1
        own_at, _, xa, ga = source(0, i)
        x_at, g_at, xb, gb = source(1, i)
        lanes = (i * hg, heads + i * hg)
        y, dx, send, *dbcs, u, t, re = call(
            functools.partial(
                across_kernel, hg, lanes, hops, len(finals) // 2, own_at, (x_at, g_at)
            ),
            "across",
            [full, full, shape((tokens, 2 * gw), BF16)]
            + [both_bc[0], shape((tokens, 2 * state), BF16 if last else F32)]
            + [square, square, shape((8, LANES), F32)],
            (), xa, ga, xb, gb, *bcs, *scaled[0, i], *scaled[1, i], step, grow, endw,
            *states[i][:4], *inside[0, i][:2], *inside[1, i][:2], *dbcs, *received[i][1:],
            hbm=finals, hbm_outs=2, aliases={0: 0, 1: 1} if finals else None,
            scratch=[pltpu.VMEM((state, gw), BF16)] * 2 + [pltpu.VMEM((2, state, gw), BF16)] * 2
            + [pltpu.VMEM((2, 1, gw), F32)] + [pltpu.VMEM((tokens, gw), BF16)] * 2
            + [pltpu.SemaphoreType.DMA((2,))],
        )
        finals = (y, dx)
        sends.append(send)
        us.append(u)
        ts.append(t)
        res.append(re)

    dbc_ret = toggled(dbcs[1], "ctx", 1)
    raw_own, raw_send, head_sums = call(
        steps_kernel, "steps", [turned] * 2 + [shape((8, LANES), F32)], (),
        sig, rate, step, grow, endw, *[inside[key][j] for j in (3, 4, 5) for key in order],
        *us, *ts, *res,
    )
    raw_back = toggled(raw_send, "ctx", 1)
    grad, rim_send, message = call(
        conv_back_kernel, "conv_back",
        [
            shape((tokens, 2 * state), F32),
            shape((8, 2 * state), F32),
            shape((fsdp, tokens + HALO + 32, 2 * state), BF16),
        ],
        (), dbcs[0], dbc_ret, kept, conv_w, head_sums,
        scratch=[
            pltpu.VMEM((tokens + 2 * HALO, 2 * state), F32),
            pltpu.VMEM((16, 2 * state), F32),
        ],
    )
    rim = lax.ppermute(rim_send, "ctx", [(i + 1, i) for i in range(ctx - 1)])
    backs = [toggled(after(a, rim), "ctx", 1) for a in sends[:-1]]

    rights = exchanged(message, "fsdp")
    terms = call(
        weight_kernel, "weight", shape((ctx, chunk_rows + 32, 2 * state), BF16), (),
        left, after(rights, rim, raw_back),
    )
    backs.append(toggled(after(sends[-1], terms), "ctx", 1))
    total, grad_cw, grad_cb, *per_head = call(
        functools.partial(reduce_kernel, heads), "reduce",
        [
            shape((ctx, chunk_rows, 2 * state), BF16),
            shape((taps, 2 * state), F32),
            shape((1, 2 * state), F32),
        ]
        + [shape((1, total_heads), F32)] * 3,
        (), exchanged(terms, "ctx"),
    )
    grad_weight = call(
        place_rows_kernel, "place_rows", shape((rows, 2 * state), F32), (), exchanged(total, "ctx")
    )
    grad_tokens = call(
        functools.partial(tokens_kernel, fsdp), "grad_tokens", shape((tokens, fsdp * rows), BF16),
        (), grad, rim, hbm=pieces,
        scratch=[pltpu.VMEM((fsdp, *w_bc.shape), BF16), pltpu.SemaphoreType.DMA((fsdp,))],
    )
    ssm_out, grad_values, grad_raw = call(
        join_kernel, "join", [full, full, shape((total_heads, tokens), F32)],
        (), raw_own, raw_back, hbm=(*finals, *backs), hbm_outs=2,
        aliases={0: 0, 1: 1}, scratch=[pltpu.SemaphoreType.DMA((2 * GROUPS,))],
    )
    return (
        ssm_out[None],
        grad_values[None],
        grad_tokens[None],
        grad_raw.T[None],
        grad_weight,
        grad_cw,
        grad_cb[0],
        *[a[0] for a in per_head],
    )


def solution(mesh):
    tokens = P("fsdp", "ctx", None)
    in_specs = (tokens, P("fsdp", None), P(), P(), tokens, tokens, P(), P(), P(), tokens)
    out_specs = (tokens, tokens, tokens, tokens, P("fsdp", None), P(), P(), P(), P(), P())
    return jax.shard_map(body, mesh=mesh, in_specs=in_specs, out_specs=out_specs, check_vma=False)
```

```python
import functools

import jax
import jax.numpy as jnp
from jax import lax
from jax.experimental import pallas as pl
from jax.experimental.pallas import tpu as pltpu
from jax.sharding import PartitionSpec as P

F32 = jnp.float32
BF16 = jnp.bfloat16
LANES = 128
HALO = 16
GROUPS = 2
LIMIT = 16 * 1024 * 1024
HIGHEST = lax.Precision.HIGHEST
TN = ((0,), (0,))
NT = ((1,), (1,))


def dot(a, b, dims=((1,), (0,)), precision=None):
    return lax.dot_general(
        a, b, (dims, ((), ())), precision=precision, preferred_element_type=F32
    )


def shape(dims, dtype):
    return jax.ShapeDtypeStruct(dims, dtype)


def call(kernel, name, out_shape, smem, *operands, hbm=(), hbm_outs=0, scratch=(), aliases=None):
    single = not isinstance(out_shape, list)
    outs = [out_shape] if single else out_shape
    spaces = [pltpu.SMEM] * len(smem) + [pltpu.HBM] * len(hbm) + [pltpu.VMEM] * len(operands)
    out_spaces = [pltpu.HBM] * hbm_outs + [pltpu.VMEM] * (len(outs) - hbm_outs)
    result = pl.pallas_call(
        kernel,
        out_shape=outs,
        in_specs=[pl.BlockSpec(memory_space=a) for a in spaces],
        out_specs=[pl.BlockSpec(memory_space=a) for a in out_spaces],
        scratch_shapes=list(scratch),
        compiler_params=pltpu.CompilerParams(vmem_limit_bytes=LIMIT),
        input_output_aliases=aliases or {},
        name=name,
    )(*smem, *[pltpu.with_memory_space_constraint(a, pltpu.HBM) for a in hbm], *operands)
    return result[0] if single else result


def copy_all(pairs, sems):
    copies = [pltpu.make_async_copy(a, b, sems.at[i]) for i, (a, b) in enumerate(pairs)]
    for copy in copies:
        copy.start()
    return copies


def side():
    return lax.rem(lax.axis_index("ctx"), 2)


def place():
    return lax.div(lax.axis_index("ctx"), 2)


def peer_columns(k, rows):
    return aligned((lax.axis_index("fsdp") ^ k) * rows, rows)


def aligned(at, size):
    return pl.ds(pl.multiple_of(at, LANES), size)


def triangle(n):
    rows = lax.broadcasted_iota(jnp.int32, (n, n), 0)
    cols = lax.broadcasted_iota(jnp.int32, (n, n), 1)
    return rows >= cols


def split(value):
    high = value.astype(BF16).astype(F32)
    return jnp.concatenate([high, value - high], 0).astype(BF16)


def swap_kernel(layer_ref, dt_ref, x_ref, g_ref, halo_ref, dt_out_ref, first_ref, x_out_ref, g_out_ref, sems):
    width = x_out_ref.shape[1]
    tokens = layer_ref.shape[0]
    heads = dt_out_ref.shape[0]
    other = 1 - side()
    base = other * (GROUPS * width)
    rows = pl.ds(pl.multiple_of(other * heads, 8), heads)
    pairs = [
        (layer_ref.at[tokens - HALO : tokens, :], halo_ref),
        (dt_ref.at[rows, :], dt_out_ref),
        (x_ref.at[:, aligned(base, width)], first_ref.at[:, :width]),
        (g_ref.at[:, aligned(base, width)], first_ref.at[:, width:]),
        (x_ref.at[:, aligned(base + width, width)], x_out_ref),
        (g_ref.at[:, aligned(base + width, width)], g_out_ref),
    ]
    for copy in copy_all(pairs, sems):
        copy.wait()


def vectors_kernel(
    dt_ref, back_ref, bias_ref, alog_ref, step_ref, cum_ref, cumt_ref, grow_ref, endw_ref, sig_ref,
    rate_ref, turned, rows,
):
    heads, n = back_ref.shape
    r = side()
    turned[...] = jnp.zeros_like(turned)
    turned[0:heads, :] = dt_ref[pl.ds(pl.multiple_of(r * heads, 8), heads), :]
    turned[heads : 2 * heads, :] = back_ref[...]
    rows[...] = jnp.zeros_like(rows)
    for i, ref in enumerate((bias_ref, alog_ref)):
        half = jnp.where(r == 0, ref[:, :heads], ref[:, heads:])
        rows[i : i + 1, 0:heads] = half
        rows[i : i + 1, heads : 2 * heads] = half
    raw = turned[...].T + rows[0:1, :]
    step = jnp.maximum(raw, 0.0) + jnp.log1p(jnp.exp(-jnp.abs(raw)))
    rate = jnp.exp(rows[1:2, :])
    log_decay = -step * rate
    lower = jnp.where(triangle(n), 1.0, 0.0).astype(F32)
    cum = dot(lower, log_decay, precision=HIGHEST)
    step_ref[...] = step
    cum_ref[...] = cum
    cumt_ref[...] = cum.T
    grow_ref[...] = jnp.exp(cum)
    endw_ref[...] = jnp.exp(cum[n - 1 : n, :] - cum)
    sig_ref[...] = jax.nn.sigmoid(raw)
    rate_ref[...] = jnp.broadcast_to(rate, rate_ref.shape)


def project_kernel(count, layer_ref, *refs):
    pieces = refs[:count]
    halo_ref, cw_ref, cb_ref, kept_ref, bc_ref, layer_scr, w_scr, sems = refs[count:]
    rows = pieces[0].shape[0]
    taps = cw_ref.shape[0]
    tokens = layer_ref.shape[0]
    pairs = [(layer_ref, layer_scr)] + [(pieces[k], w_scr.at[k]) for k in range(count)]
    copies = copy_all(pairs, sems)
    total = jnp.zeros((tokens, pieces[0].shape[1]), F32)
    rim = jnp.zeros((HALO, pieces[0].shape[1]), F32)
    copies[0].wait()
    for k in range(count):
        copies[k + 1].wait()
        at = peer_columns(k, rows)
        w = w_scr[k]
        total += dot(layer_scr[:, at], w)
        rim += dot(halo_ref[:, at], w)
    kept_ref[0:HALO, :] = rim
    kept_ref[HALO : HALO + tokens, :] = total
    first = HALO - taps + 1
    pre = cb_ref[...] + cw_ref[0:1, :] * kept_ref[first : first + tokens, :]
    for k in range(1, taps):
        pre = pre + cw_ref[k : k + 1, :] * kept_ref[first + k : first + k + tokens, :]
    kept_ref[HALO + tokens :, :] = pre
    bc_ref[...] = (pre * jax.nn.sigmoid(pre)).astype(BF16)


def head_columns(at, h):
    first, more = at
    return aligned(first + side() * more + h * LANES, LANES)


def scale_kernel(heads, lane, x_at, g_at, x_ref, g_ref, step_ref, grow_ref, endw_ref, xe_ref, ge_ref):
    for h in range(heads):
        at = slice(h * LANES, (h + 1) * LANES)
        one = slice(lane + h, lane + h + 1)
        x = x_ref[:, head_columns(x_at, h)].astype(F32)
        g = g_ref[:, head_columns(g_at, h)].astype(F32)
        xe_ref[:, at] = (x * (step_ref[:, one] * endw_ref[:, one])).astype(BF16)
        ge_ref[:, at] = (g * grow_ref[:, one]).astype(BF16)


def widen(row, lane, heads):
    return jnp.concatenate(
        [jnp.broadcast_to(row[:, lane + h : lane + h + 1], (1, LANES)) for h in range(heads)], 1
    )


def states_kernel(
    heads, lanes, bc0_ref, bc1_ref, xe0_ref, ge0_ref, xe1_ref, ge1_ref, grow_ref,
    first_ref, p_ref, q_ref, sf_ref, ds_ref, dec_ref, s_scr, d_scr, dec_scr,
):
    n = grow_ref.shape[0]
    r = side()
    for slot, (bc_ref, xe_ref, ge_ref) in enumerate(
        ((bc0_ref, xe0_ref, ge0_ref), (bc1_ref, xe1_ref, ge1_ref))
    ):
        s_scr[slot] = dot(bc_ref[:, :LANES], xe_ref[...], TN)
        d_scr[slot] = dot(bc_ref[:, LANES:], ge_ref[...], TN)
        dec_scr[slot] = widen(grow_ref[n - 1 : n, :], lanes[slot], heads)
    dec_first, dec_second = dec_scr[r], dec_scr[1 - r]
    s_first, d_second = s_scr[r], d_scr[1 - r]
    sf_ref[...] = s_first.astype(BF16)
    ds_ref[...] = d_second.astype(BF16)
    p = (dec_second * s_first + s_scr[1 - r]).astype(BF16)
    q = (dec_first * d_second + d_scr[r]).astype(BF16)
    p_ref[...] = p
    q_ref[...] = q

    @pl.when(place() == 0)
    def _():
        first_ref[...] = p

    @pl.when(place() != 0)
    def _():
        first_ref[...] = q

    dec_ref[0:1, :] = dec_first * dec_second
    dec_ref[1:2, :] = dec_first
    dec_ref[2:3, :] = dec_second
    dec_ref[3:8, :] = jnp.zeros((5, dec_first.shape[1]), F32)


def hop_kernel(hop, received_ref, p_ref, q_ref, dec_ref, out_ref):
    carried = dec_ref[0:1, :] * received_ref[...].astype(F32)

    @pl.when(place() == hop)
    def _():
        out_ref[...] = (carried + p_ref[...].astype(F32)).astype(BF16)

    @pl.when(place() != hop)
    def _():
        out_ref[...] = (carried + q_ref[...].astype(F32)).astype(BF16)


def inside_kernel(
    heads, lane, skip_at, x_at, g_at, skip_ref, x_ref, g_ref, bc_ref, step_ref, cum_ref,
    cumt_ref, y_ref, dx_ref, dscores_ref, gy_ref, ds_ref, gx_ref,
):
    n = step_ref.shape[0]
    mask = triangle(n)
    scores = jnp.where(mask, dot(bc_ref[:, LANES:], bc_ref[:, :LANES], NT), 0.0)
    gy_ref[...] = jnp.zeros_like(gy_ref)
    ds_ref[...] = jnp.zeros_like(ds_ref)
    gx_ref[...] = jnp.zeros_like(gx_ref)
    dscores = jnp.zeros((n, n), F32)
    for h in range(heads):
        at = slice(h * LANES, (h + 1) * LANES)
        one = slice(lane + h, lane + h + 1)
        step = step_ref[:, one]
        gap = cum_ref[:, one] - cumt_ref[one, :]
        decay = jnp.exp(jnp.where(mask, gap, 0.0))
        mixing = (scores * decay).astype(BF16)
        x = x_ref[:, head_columns(x_at, h)].astype(F32)
        g = g_ref[:, head_columns(g_at, h)]
        gf = g.astype(F32)
        xs = (x * step).astype(BF16)
        skip = skip_ref[side() * GROUPS * heads + skip_at + h]
        y = dot(mixing, xs)
        dxs = dot(mixing, g, TN)
        dscores += dot(g, xs, NT) * decay
        y_ref[:, at] = y + skip * x
        dx_ref[:, at] = dxs * step + skip * gf
        gy_ref[:, one] = jnp.sum(gf * y, axis=1, keepdims=True)
        ds_ref[:, one] = jnp.sum(x * dxs, axis=1, keepdims=True)
        gx_ref[0:1, one] = jnp.sum(jnp.sum(gf * x, axis=0, keepdims=True), axis=1, keepdims=True)
    dscores_ref[...] = jnp.where(mask, dscores, 0.0)


def inside_bc_kernel(bc0_ref, bc1_ref, *refs):
    parts, outs = refs[: 2 * GROUPS], refs[2 * GROUPS :]
    for slot, bc_ref in enumerate((bc0_ref, bc1_ref)):
        total = parts[slot * GROUPS][...]
        for i in range(1, GROUPS):
            total = total + parts[slot * GROUPS + i][...]
        ds = total.astype(BF16)
        outs[slot][:, :LANES] = dot(ds, bc_ref[:, LANES:], TN)
        outs[slot][:, LANES:] = dot(ds, bc_ref[:, :LANES])


def across_kernel(heads, lanes, hops, filled, own_at, columns, *refs):
    refs = refs[2 * filled :]
    across_block(heads, lanes, hops, own_at, columns, *refs)


def across_block(
    heads, lanes, hops, own_at, columns, x0_ref, g0_ref, x1_ref, g1_ref, bc0_ref, bc1_ref, xe0_ref,
    ge0_ref, xe1_ref, ge1_ref, step_ref, grow_ref, endw_ref, dec_ref, p_ref, sf_ref, ds_ref,
    y0_ref, dx0_ref, y1_ref, dx1_ref, dbc0_ref, dbc1_ref, *refs
):
    received = refs[:hops]
    (
        yf_ref, dxf_ref, send_ref, dbco0_ref, dbco1_ref, u_ref, t_ref, re_ref,
        e_in, r_in, e_scr, r_scr, n_scr, yo_ref, dxo_ref, sems,
    ) = refs[hops:]
    r, pos = side(), place()
    width = yo_ref.shape[1]
    e_in[...] = jnp.zeros_like(e_in)
    r_in[...] = jnp.zeros_like(r_in)
    for k in range(hops):

        @pl.when(pos - 1 == k)
        def _(k=k):
            e_in[...] = received[k][...]

        @pl.when(hops - 1 - pos == k)
        def _(k=k):
            r_in[...] = received[k][...]

    dec_pair, dec_first, dec_second = dec_ref[0:1, :], dec_ref[1:2, :], dec_ref[2:3, :]
    entering = e_in[...].astype(F32)
    later = r_in[...].astype(F32)
    middle = dec_first * entering + sf_ref[...].astype(F32)
    leaving = dec_pair * entering + p_ref[...].astype(F32)
    earlier = dec_second * later + ds_ref[...].astype(F32)
    e_scr[r] = e_in[...]
    e_scr[1 - r] = middle.astype(BF16)
    r_scr[1 - r] = r_in[...]
    r_scr[r] = earlier.astype(BF16)
    n_scr[1 - r] = jnp.sum(later * leaving, axis=0, keepdims=True)
    n_scr[r] = jnp.sum(earlier * middle, axis=0, keepdims=True)

    u_ref[...] = jnp.zeros_like(u_ref)
    t_ref[...] = jnp.zeros_like(t_ref)
    re_ref[...] = jnp.zeros_like(re_ref)
    for slot, (bc_ref, xe_ref, ge_ref, y_ref, dx_ref, dbc_ref, dbco_ref) in enumerate(
        (
            (bc0_ref, xe0_ref, ge0_ref, y0_ref, dx0_ref, dbc0_ref, dbco0_ref),
            (bc1_ref, xe1_ref, ge1_ref, y1_ref, dx1_ref, dbc1_ref, dbco1_ref),
        )
    ):
        e_all = e_scr[slot]
        r_all = r_scr[slot]
        db = dbc_ref[:, :LANES] + dot(xe_ref[...], r_all, NT)
        dc = dbc_ref[:, LANES:] + dot(ge_ref[...], e_all, NT)
        dbco_ref[:, :LANES] = db.astype(dbco_ref.dtype)
        dbco_ref[:, LANES:] = dc.astype(dbco_ref.dtype)
        ce_all = dot(bc_ref[:, LANES:], e_all)
        br_all = dot(bc_ref[:, :LANES], r_all)
        for h in range(heads):
            at = slice(h * LANES, (h + 1) * LANES)
            lane = lanes[slot] + h
            one = slice(lane, lane + 1)
            ce, br = ce_all[:, at], br_all[:, at]
            y = (y_ref[:, at] + grow_ref[:, one] * ce).astype(BF16)
            dx = (dx_ref[:, at] + (step_ref[:, one] * endw_ref[:, one]) * br).astype(BF16)
            if slot == 0:
                yo_ref[:, at] = y
                dxo_ref[:, at] = dx
                x = x0_ref[:, head_columns(own_at, h)].astype(F32)
                g = g0_ref[:, head_columns(own_at, h)].astype(F32)
            else:
                send_ref[:, at] = y
                send_ref[:, width + h * LANES : width + (h + 1) * LANES] = dx
                x = x1_ref[:, head_columns(columns[0], h)].astype(F32)
                g = g1_ref[:, head_columns(columns[1], h)].astype(F32)
            u_ref[:, one] = jnp.sum(g * ce, axis=1, keepdims=True)
            t_ref[:, one] = jnp.sum(x * br, axis=1, keepdims=True)
            re_ref[0:1, one] = jnp.sum(n_scr[slot][:, at], axis=1, keepdims=True)
        if slot == 0:
            final = aligned(own_at[0] + r * own_at[1], width)
            pairs = [(yo_ref, yf_ref.at[:, final]), (dxo_ref, dxf_ref.at[:, final])]
            copies = copy_all(pairs, sems)
    for copy in copies:
        copy.wait()


def steps_kernel(sig_ref, rate_ref, step_ref, grow_ref, endw_ref, *refs):
    count = 2 * GROUPS
    gys, dss, gxs = refs[:count], refs[count : 2 * count], refs[2 * count : 3 * count]
    refs = refs[3 * count :]
    us, ts, res = refs[:GROUPS], refs[GROUPS : 2 * GROUPS], refs[2 * GROUPS : 3 * GROUPS]
    own_ref, send_ref, sums_ref = refs[3 * GROUPS :]

    def total(parts):
        value = parts[0][...]
        for a in parts[1:]:
            value = value + a[...]
        return value

    n = step_ref.shape[0]
    step = step_ref[...]
    ds = total(dss) + endw_ref[...] * total(ts)
    gy = total(gys) + grow_ref[...] * total(us)
    rate = rate_ref[0:1, :]
    last = lax.broadcasted_iota(jnp.int32, (n, LANES), 0) == n - 1
    dcum = gy - step * ds + jnp.where(last, total(res)[0:1, :], 0.0)
    lower = jnp.where(triangle(n), 1.0, 0.0).astype(F32)
    dlog = dot(lower, dcum, TN, precision=HIGHEST)
    draw = (ds - rate * dlog) * sig_ref[...]
    turned = draw.T
    heads = own_ref.shape[0]
    own_ref[...] = turned[:heads, :]
    send_ref[...] = turned[heads : 2 * heads, :]
    sums_ref[0:1, :] = jnp.sum(draw, axis=0, keepdims=True)
    sums_ref[1:2, :] = jnp.sum(dlog * (-step * rate), axis=0, keepdims=True)
    sums_ref[2:3, :] = total(gxs)[0:1, :]
    sums_ref[3:8, :] = jnp.zeros((5, LANES), F32)


def conv_back_kernel(
    own_ref, ret_ref, kept_ref, cw_ref, heads_ref, grad_ref, rim_ref, message_ref, z_scr, sum_scr
):
    tokens = own_ref.shape[0]
    taps = cw_ref.shape[0]
    pre = kept_ref[HALO + tokens :, :]
    sig = jax.nn.sigmoid(pre)
    dconv = (own_ref[...] + ret_ref[...].astype(F32)) * sig * (1.0 + pre * (1.0 - sig))
    z_scr[...] = jnp.zeros_like(z_scr)
    z_scr[HALO : HALO + tokens, :] = dconv
    grad = cw_ref[0:1, :] * z_scr[taps - 1 : taps - 1 + tokens + HALO, :]
    for k in range(1, taps):
        grad = grad + cw_ref[k : k + 1, :] * z_scr[taps - 1 - k : taps - 1 - k + tokens + HALO, :]
    grad_ref[...] = grad[HALO:, :]
    rim_ref[...] = grad[HALO - 8 : HALO, :]
    first = HALO - taps + 1
    sum_scr[...] = jnp.zeros_like(sum_scr)
    for k in range(taps):
        sum_scr[k : k + 1, :] = jnp.sum(
            dconv * kept_ref[first + k : first + k + tokens, :], axis=0, keepdims=True
        )
    sum_scr[taps : taps + 1, :] = jnp.sum(dconv, axis=0, keepdims=True)
    sum_scr[5:8, aligned(side() * LANES, LANES)] = heads_ref[0:3, :]
    small = split(sum_scr[...])
    grad = grad.astype(BF16)
    for k in range(message_ref.shape[0]):
        message_ref[k, 0 : tokens + HALO, :] = grad
        message_ref[k, tokens + HALO :, :] = small


def pack_kernel(count, layer_ref, halo_ref, *refs):
    outs, sems = refs[:count], refs[count]
    pairs = []
    for k in range(count):
        at = peer_columns(k, outs[k].shape[1])
        pairs.append((halo_ref.at[:, at], outs[k].at[0:HALO, :]))
        pairs.append((layer_ref.at[:, at], outs[k].at[HALO:, :]))
    for copy in copy_all(pairs, sems):
        copy.wait()


def turn_kernel(count, *refs):
    parts, out_ref = refs[:count], refs[count]
    tokens = parts[0].shape[0] - HALO
    f = lax.axis_index("fsdp")
    for k in range(count):
        out_ref[:, aligned((f ^ k) * tokens, tokens)] = parts[k][HALO:, :].T
    halos = jnp.concatenate([parts[k][0:HALO, :] for k in range(count)], 0)
    out_ref[:, count * tokens :] = halos.T


def weight_kernel(left_ref, rights_ref, out_ref):
    count = rights_ref.shape[0]
    tokens = (left_ref.shape[1] // count) - HALO
    right = jnp.concatenate(
        [rights_ref[k, HALO : HALO + tokens, :] for k in range(count)]
        + [rights_ref[lax.axis_index("fsdp") ^ k, 0:HALO, :] for k in range(count)],
        0,
    )
    at = tokens + HALO
    both = jnp.zeros((16, right.shape[1]), F32)
    for k in range(count):
        both += rights_ref[k, at : at + 16, :].astype(F32)
    small = split(both[0:8, :] + both[8:16, :])
    chunk = out_ref.shape[1] - 16
    for k in range(out_ref.shape[0]):
        term = dot(left_ref[k * chunk : (k + 1) * chunk, :], right)
        out_ref[k, 0:chunk, :] = term.astype(BF16)
        out_ref[k, chunk:, :] = small


def reduce_kernel(heads, terms_ref, total_ref, cw_ref, cb_ref, *head_refs):
    chunk = total_ref.shape[1]
    total = terms_ref[0].astype(F32)
    for k in range(1, terms_ref.shape[0]):
        total = total + terms_ref[k].astype(F32)
    for k in range(total_ref.shape[0]):
        total_ref[k] = total[0:chunk].astype(BF16)
    small = total[chunk : chunk + 8] + total[chunk + 8 :]
    taps = cw_ref.shape[0]
    cw_ref[...] = small[0:taps, :]
    cb_ref[...] = small[taps : taps + 1, :]
    for i, ref in enumerate(head_refs):
        row = small[5 + i : 6 + i, :]
        ref[:, :heads] = row[:, :heads] + row[:, heads : 2 * heads]
        row = row[:, LANES:]
        ref[:, heads:] = row[:, :heads] + row[:, heads : 2 * heads]


def place_rows_kernel(parts_ref, out_ref):
    chunk = parts_ref.shape[1]
    for k in range(parts_ref.shape[0]):
        out_ref[k * chunk : (k + 1) * chunk, :] = parts_ref[k].astype(F32)


def tokens_kernel(count, *refs):
    pieces = refs[:count]
    grad_ref, rim_ref, out_ref, w_scr, sems = refs[count:]
    copies = copy_all([(pieces[k], w_scr.at[k]) for k in range(count)], sems)
    tail = rim_ref.shape[0]
    own = grad_ref[...]
    g = jnp.concatenate([own[:-tail], own[-tail:] + rim_ref[...]], 0).astype(BF16)
    rows = pieces[0].shape[0]
    for k in range(count):
        copies[k].wait()
        out_ref[:, peer_columns(k, rows)] = dot(g, w_scr[k], NT).astype(BF16)


def join_kernel(*refs):
    own_ref, back_ref = refs[2:4]
    backs = refs[4 : 4 + GROUPS]
    y_ref, dx_ref, raw_ref, sems = refs[4 + GROUPS :]
    width = backs[0].shape[1] // 2
    r = side()
    pairs = []
    for i in range(GROUPS):
        at = aligned(((1 - r) * GROUPS + i) * width, width)
        pairs.append((backs[i].at[:, :width], y_ref.at[:, at]))
        pairs.append((backs[i].at[:, width:], dx_ref.at[:, at]))
    copies = copy_all(pairs, sems)
    heads = own_ref.shape[0]
    raw_ref[pl.ds(pl.multiple_of(r * heads, 8), heads), :] = own_ref[...]
    raw_ref[pl.ds(pl.multiple_of((1 - r) * heads, 8), heads), :] = back_ref[...]
    for copy in copies:
        copy.wait()


def toggled(x, axis, bits):
    size = lax.axis_size(axis)
    return lax.ppermute(x, axis, [(i, i ^ bits) for i in range(size)])


def exchanged(x, axis):
    return lax.all_to_all(x, axis, 0, 0)


def after(x, *others):
    return lax.optimization_barrier((x, *others))[0]


def body(layer_in, w_bc, conv_w, conv_b, ssm_in, dt_raw, dt_bias, a_log, skip_scale, grad_out):
    ctx, fsdp = lax.axis_size("ctx"), lax.axis_size("fsdp")
    layer, x, g, dt = layer_in[0], ssm_in[0], grad_out[0], dt_raw[0].T
    tokens, width = x.shape
    total_heads = dt_bias.shape[0]
    heads = total_heads // 2
    half = width // 2
    hg, gw = heads // GROUPS, half // GROUPS
    state = w_bc.shape[1] // 2
    taps = conv_w.shape[0]
    rows = w_bc.shape[0]
    chunk_rows = rows // ctx
    pairs = ctx // 2
    hops = pairs - 1
    square = shape((tokens, LANES), F32)
    flat = shape((tokens, gw), BF16)
    turned = shape((heads, tokens), F32)
    both_bc = [shape((tokens, 2 * state), F32)] * 2

    halo_send, dt_send, *swaps = call(
        swap_kernel, "swap",
        [shape((HALO, layer.shape[1]), BF16), turned, shape((tokens, 2 * gw), BF16), flat, flat], (),
        hbm=(layer, dt, x, g), scratch=[pltpu.SemaphoreType.DMA((6,))],
    )
    halo = lax.ppermute(halo_send, "ctx", [(i, i + 1) for i in range(ctx - 1)])
    dt_back = toggled(dt_send, "ctx", 1)
    swapped_first = toggled(swaps[0], "ctx", 1)
    swapped_x = toggled(after(swaps[1], halo, dt_back), "ctx", 1)

    step, cum, cumt, grow, endw, sig, rate = call(
        vectors_kernel, "vectors", [square] * 6 + [shape((8, LANES), F32)], (), dt, dt_back,
        dt_bias[None, :], a_log[None, :],
        scratch=[pltpu.VMEM((tokens, tokens), F32), pltpu.VMEM((8, LANES), F32)],
    )

    def source(slot, i):
        if slot == 0:
            return (i * gw, half), (i * gw, half), x, g
        if i == 0:
            return (0, 0), (gw, 0), swapped_first, swapped_first
        return (0, 0), (0, 0), swapped_x, swapped_g

    def scale(slot, i):
        x_at, g_at, xa, ga = source(slot, i)
        return call(
            functools.partial(scale_kernel, hg, slot * heads + i * hg, x_at, g_at), "scale",
            [flat, flat], (), xa, ga, step, grow, endw,
        )

    scaled = {(0, i): scale(0, i) for i in range(GROUPS)}
    pieces = {0: w_bc}
    bit = fsdp // 2
    while bit:
        for k in list(pieces):
            piece = pieces[k]
            if k:
                piece = after(piece, halo, *[scaled[0, i][0] for i in range(GROUPS)])
            pieces[k | bit] = toggled(piece, "fsdp", bit)
        bit //= 2
    pieces = [pieces[k] for k in range(fsdp)]
    kept, bc = call(
        functools.partial(project_kernel, fsdp), "project",
        [
            shape((2 * tokens + HALO, 2 * state), F32),
            shape((tokens, 2 * state), BF16),
        ],
        (), halo, conv_w, conv_b[None, :], hbm=(layer, *pieces),
        scratch=[
            pltpu.VMEM(layer.shape, BF16),
            pltpu.VMEM((fsdp, *w_bc.shape), BF16),
            pltpu.SemaphoreType.DMA((1 + fsdp,)),
        ],
    )
    bcs = [bc, toggled(bc, "ctx", 1)]
    swapped_g = toggled(after(swaps[2], bcs[1]), "ctx", 1)

    wide = shape((state, gw), BF16)
    states, received = [], []
    for i in range(GROUPS):
        lanes = (i * hg, heads + i * hg)
        scaled[1, i] = scale(1, i)
        first, p, q, s_first, d_second, decays = call(
            functools.partial(states_kernel, hg, lanes), "states",
            [wide] * 5 + [shape((8, gw), F32)],
            (), *bcs, *scaled[0, i], *scaled[1, i], grow,
            scratch=[pltpu.VMEM((2, state, gw), F32)] * 2 + [pltpu.VMEM((2, 1, gw), F32)],
        )
        states.append((decays, p, s_first, d_second, q))
        received.append([first])

    def within(slot, i, *earlier):
        x_at, g_at, xa, ga = source(slot, i)
        return call(
            functools.partial(inside_kernel, hg, slot * heads + i * hg, i * hg, x_at, g_at), "inside",
            [shape((tokens, gw), F32)] * 2 + [shape((tokens, tokens), F32), square, square]
            + [shape((8, LANES), F32)],
            (skip_scale,), xa, ga, after(bcs[slot], *earlier), step, cum, cumt,
        )

    order = [(slot, i) for slot in range(2) for i in range(GROUPS)]
    inside = {}
    waiting = list(order)
    value = received[-1][0]
    for hop in range(hops):
        moves = [(hop, hop + 1), (pairs - 1 - hop, pairs - 2 - hop)]
        moves = [(2 * a + i, 2 * b + i) for a, b in moves for i in range(2)]
        for i in range(GROUPS):
            earlier, value = value, received[i][-1]
            if hop:
                decays, p, _, _, q = states[i]
                if waiting:
                    key = waiting.pop(0)
                    inside[key] = within(*key, earlier)
                    value = after(value, inside[key][2])
                value = call(
                    functools.partial(hop_kernel, hop), "hop", wide, (), value, p, q, decays
                )
            received[i].append(lax.ppermute(value, "ctx", moves))
    for key in waiting:
        inside[key] = within(*key)
    dbcs = call(inside_bc_kernel, "inside_bc", both_bc, (), *bcs, *[inside[key][2] for key in order])

    packs = call(
        functools.partial(pack_kernel, fsdp), "pack", [shape((tokens + HALO, rows), BF16)] * fsdp,
        (), hbm=(layer, after(halo, value)), scratch=[pltpu.SemaphoreType.DMA((2 * fsdp,))],
    )
    lefts = [packs[0]] + [toggled(packs[k], "fsdp", k) for k in range(1, fsdp)]
    left = call(
        functools.partial(turn_kernel, fsdp), "turn", shape((rows, fsdp * (tokens + HALO)), BF16),
        (), *lefts,
    )

    full = shape((tokens, width), BF16)
    finals, sends, us, ts, res = (), [], [], [], []
    for i in range(GROUPS):
        last = i == GROUPS - 1
        own_at, _, xa, ga = source(0, i)
        x_at, g_at, xb, gb = source(1, i)
        lanes = (i * hg, heads + i * hg)
        y, dx, send, *dbcs, u, t, re = call(
            functools.partial(
                across_kernel, hg, lanes, hops, len(finals) // 2, own_at, (x_at, g_at)
            ),
            "across",
            [full, full, shape((tokens, 2 * gw), BF16)]
            + [both_bc[0], shape((tokens, 2 * state), BF16 if last else F32)]
            + [square, square, shape((8, LANES), F32)],
            (), xa, ga, xb, gb, *bcs, *scaled[0, i], *scaled[1, i], step, grow, endw,
            *states[i][:4], *inside[0, i][:2], *inside[1, i][:2], *dbcs, *received[i][1:],
            hbm=finals, hbm_outs=2, aliases={0: 0, 1: 1} if finals else None,
            scratch=[pltpu.VMEM((state, gw), BF16)] * 2 + [pltpu.VMEM((2, state, gw), BF16)] * 2
            + [pltpu.VMEM((2, 1, gw), F32)] + [pltpu.VMEM((tokens, gw), BF16)] * 2
            + [pltpu.SemaphoreType.DMA((2,))],
        )
        finals = (y, dx)
        sends.append(send)
        us.append(u)
        ts.append(t)
        res.append(re)

    dbc_ret = toggled(dbcs[1], "ctx", 1)
    raw_own, raw_send, head_sums = call(
        steps_kernel, "steps", [turned] * 2 + [shape((8, LANES), F32)], (),
        sig, rate, step, grow, endw, *[inside[key][j] for j in (3, 4, 5) for key in order],
        *us, *ts, *res,
    )
    raw_back = toggled(raw_send, "ctx", 1)
    grad, rim_send, message = call(
        conv_back_kernel, "conv_back",
        [
            shape((tokens, 2 * state), F32),
            shape((8, 2 * state), F32),
            shape((fsdp, tokens + HALO + 16, 2 * state), BF16),
        ],
        (), after(dbcs[0], left), dbc_ret, kept, conv_w, head_sums,
        scratch=[
            pltpu.VMEM((tokens + 2 * HALO, 2 * state), F32),
            pltpu.VMEM((8, 2 * state), F32),
        ],
    )
    rim = lax.ppermute(rim_send, "ctx", [(i + 1, i) for i in range(ctx - 1)])
    backs = [toggled(after(a, rim), "ctx", 1) for a in sends[:-1]]

    rights = exchanged(message, "fsdp")
    terms = call(
        weight_kernel, "weight", shape((ctx, chunk_rows + 16, 2 * state), BF16), (),
        left, after(rights, rim, raw_back),
    )
    backs.append(toggled(after(sends[-1], terms), "ctx", 1))
    total, grad_cw, grad_cb, *per_head = call(
        functools.partial(reduce_kernel, heads), "reduce",
        [
            shape((ctx, chunk_rows, 2 * state), BF16),
            shape((taps, 2 * state), F32),
            shape((1, 2 * state), F32),
        ]
        + [shape((1, total_heads), F32)] * 3,
        (), after(exchanged(terms, "ctx"), *backs),
    )
    grad_weight = call(
        place_rows_kernel, "place_rows", shape((rows, 2 * state), F32), (), exchanged(total, "ctx")
    )
    grad_tokens = call(
        functools.partial(tokens_kernel, fsdp), "grad_tokens", shape((tokens, fsdp * rows), BF16),
        (), grad, rim, hbm=pieces,
        scratch=[pltpu.VMEM((fsdp, *w_bc.shape), BF16), pltpu.SemaphoreType.DMA((fsdp,))],
    )
    ssm_out, grad_values, grad_raw = call(
        join_kernel, "join", [full, full, shape((total_heads, tokens), F32)],
        (), raw_own, raw_back, *backs, hbm=finals, hbm_outs=2,
        aliases={0: 0, 1: 1}, scratch=[pltpu.SemaphoreType.DMA((2 * GROUPS,))],
    )
    return (
        ssm_out[None],
        grad_values[None],
        grad_tokens[None],
        grad_raw.T[None],
        grad_weight,
        grad_cw,
        grad_cb[0],
        *[a[0] for a in per_head],
    )


def solution(mesh):
    tokens = P("fsdp", "ctx", None)
    in_specs = (tokens, P("fsdp", None), P(), P(), tokens, tokens, P(), P(), P(), tokens)
    out_specs = (tokens, tokens, tokens, tokens, P("fsdp", None), P(), P(), P(), P(), P())
    return jax.shard_map(body, mesh=mesh, in_specs=in_specs, out_specs=out_specs, check_vma=False)
```

```python
import functools

import jax
import jax.numpy as jnp
from jax import lax
from jax.experimental import pallas as pl
from jax.experimental.pallas import tpu as pltpu
from jax.sharding import PartitionSpec as P

F32 = jnp.float32
BF16 = jnp.bfloat16
LANES = 128
HALO = 16
GROUPS = 2
LIMIT = 16 * 1024 * 1024
HIGHEST = lax.Precision.HIGHEST
TN = ((0,), (0,))
NT = ((1,), (1,))


def dot(a, b, dims=((1,), (0,)), precision=None):
    return lax.dot_general(
        a, b, (dims, ((), ())), precision=precision, preferred_element_type=F32
    )


def shape(dims, dtype):
    return jax.ShapeDtypeStruct(dims, dtype)


def call(kernel, name, out_shape, smem, *operands, hbm=(), hbm_outs=0, scratch=(), aliases=None):
    single = not isinstance(out_shape, list)
    outs = [out_shape] if single else out_shape
    spaces = [pltpu.SMEM] * len(smem) + [pltpu.HBM] * len(hbm) + [pltpu.VMEM] * len(operands)
    out_spaces = [pltpu.HBM] * hbm_outs + [pltpu.VMEM] * (len(outs) - hbm_outs)
    result = pl.pallas_call(
        kernel,
        out_shape=outs,
        in_specs=[pl.BlockSpec(memory_space=a) for a in spaces],
        out_specs=[pl.BlockSpec(memory_space=a) for a in out_spaces],
        scratch_shapes=list(scratch),
        compiler_params=pltpu.CompilerParams(vmem_limit_bytes=LIMIT),
        input_output_aliases=aliases or {},
        name=name,
    )(*smem, *[pltpu.with_memory_space_constraint(a, pltpu.HBM) for a in hbm], *operands)
    return result[0] if single else result


def copy_all(pairs, sems):
    copies = [pltpu.make_async_copy(a, b, sems.at[i]) for i, (a, b) in enumerate(pairs)]
    for copy in copies:
        copy.start()
    return copies


def side():
    return lax.rem(lax.axis_index("ctx"), 2)


def place():
    return lax.div(lax.axis_index("ctx"), 2)


def peer_columns(k, rows):
    return aligned((lax.axis_index("fsdp") ^ k) * rows, rows)


def aligned(at, size):
    return pl.ds(pl.multiple_of(at, LANES), size)


def triangle(n):
    rows = lax.broadcasted_iota(jnp.int32, (n, n), 0)
    cols = lax.broadcasted_iota(jnp.int32, (n, n), 1)
    return rows >= cols


def split(value):
    high = value.astype(BF16).astype(F32)
    return jnp.concatenate([high, value - high], 0).astype(BF16)


def swap_kernel(layer_ref, dt_ref, x_ref, g_ref, halo_ref, dt_out_ref, first_ref, x_out_ref, g_out_ref, sems):
    width = x_out_ref.shape[1]
    tokens = layer_ref.shape[0]
    heads = dt_out_ref.shape[0]
    other = 1 - side()
    base = other * (GROUPS * width)
    rows = pl.ds(pl.multiple_of(other * heads, 8), heads)
    pairs = [
        (layer_ref.at[tokens - HALO : tokens, :], halo_ref),
        (dt_ref.at[rows, :], dt_out_ref),
        (x_ref.at[:, aligned(base, width)], first_ref.at[:, :width]),
        (g_ref.at[:, aligned(base, width)], first_ref.at[:, width:]),
        (x_ref.at[:, aligned(base + width, width)], x_out_ref),
        (g_ref.at[:, aligned(base + width, width)], g_out_ref),
    ]
    for copy in copy_all(pairs, sems):
        copy.wait()


def vectors_kernel(
    dt_ref, back_ref, bias_ref, alog_ref, step_ref, cum_ref, cumt_ref, grow_ref, endw_ref, sig_ref,
    rate_ref, turned, rows,
):
    heads, n = back_ref.shape
    r = side()
    turned[...] = jnp.zeros_like(turned)
    turned[0:heads, :] = dt_ref[pl.ds(pl.multiple_of(r * heads, 8), heads), :]
    turned[heads : 2 * heads, :] = back_ref[...]
    rows[...] = jnp.zeros_like(rows)
    for i, ref in enumerate((bias_ref, alog_ref)):
        half = jnp.where(r == 0, ref[:, :heads], ref[:, heads:])
        rows[i : i + 1, 0:heads] = half
        rows[i : i + 1, heads : 2 * heads] = half
    raw = turned[...].T + rows[0:1, :]
    step = jnp.maximum(raw, 0.0) + jnp.log1p(jnp.exp(-jnp.abs(raw)))
    rate = jnp.exp(rows[1:2, :])
    log_decay = -step * rate
    lower = jnp.where(triangle(n), 1.0, 0.0).astype(F32)
    cum = dot(lower, log_decay, precision=HIGHEST)
    step_ref[...] = step
    cum_ref[...] = cum
    cumt_ref[...] = cum.T
    grow_ref[...] = jnp.exp(cum)
    endw_ref[...] = jnp.exp(cum[n - 1 : n, :] - cum)
    sig_ref[...] = jax.nn.sigmoid(raw)
    rate_ref[...] = jnp.broadcast_to(rate, rate_ref.shape)


def early_kernel(count, layer_ref, *refs):
    pieces = refs[:count]
    halo_ref, out_ref, layer_scr, w_scr, sems = refs[count:]
    copies = copy_all(
        [(layer_ref, layer_scr)] + [(pieces[k], w_scr.at[k]) for k in range(count)], sems
    )
    copies[0].wait()
    add_products(0, copies[1:], layer_scr, w_scr, halo_ref, out_ref, False)


def add_products(base, copies, layer_scr, w_scr, halo_ref, out_ref, more):
    rows = w_scr.shape[1]
    total, rim = (out_ref[HALO:, :], out_ref[0:HALO, :]) if more else (0.0, 0.0)
    for k, copy in enumerate(copies):
        copy.wait()
        at = peer_columns(base + k, rows)
        w = w_scr[k]
        total += dot(layer_scr[:, at], w)
        rim += dot(halo_ref[:, at], w)
    out_ref[0:HALO, :] = rim
    out_ref[HALO:, :] = total


def project_kernel(base, count, layer_ref, *refs):
    pieces = refs[:count]
    halo_ref, early_ref, cw_ref, cb_ref, kept_ref, bc_ref, layer_scr, w_scr, ext_scr, sems = refs[count:]
    copies = copy_all(
        [(layer_ref, layer_scr)] + [(pieces[k], w_scr.at[k]) for k in range(count)], sems
    )
    taps = cw_ref.shape[0]
    tokens = layer_ref.shape[0]
    ext_scr[...] = early_ref[...]
    copies[0].wait()
    add_products(base, copies[1:], layer_scr, w_scr, halo_ref, ext_scr, True)
    kept_ref[0 : HALO + tokens, :] = ext_scr[...]
    first = HALO - taps + 1
    pre = cb_ref[...] + cw_ref[0:1, :] * ext_scr[first : first + tokens, :]
    for k in range(1, taps):
        pre = pre + cw_ref[k : k + 1, :] * ext_scr[first + k : first + k + tokens, :]
    kept_ref[HALO + tokens :, :] = pre
    bc_ref[...] = (pre * jax.nn.sigmoid(pre)).astype(BF16)


def head_columns(at, h):
    first, more = at
    return aligned(first + side() * more + h * LANES, LANES)


def scale_kernel(heads, lane, x_at, g_at, x_ref, g_ref, step_ref, grow_ref, endw_ref, xe_ref, ge_ref):
    for h in range(heads):
        at = slice(h * LANES, (h + 1) * LANES)
        one = slice(lane + h, lane + h + 1)
        x = x_ref[:, head_columns(x_at, h)].astype(F32)
        g = g_ref[:, head_columns(g_at, h)].astype(F32)
        xe_ref[:, at] = (x * (step_ref[:, one] * endw_ref[:, one])).astype(BF16)
        ge_ref[:, at] = (g * grow_ref[:, one]).astype(BF16)


def widen(row, lane, heads):
    return jnp.concatenate(
        [jnp.broadcast_to(row[:, lane + h : lane + h + 1], (1, LANES)) for h in range(heads)], 1
    )


def states_kernel(
    heads, lanes, bc0_ref, bc1_ref, xe0_ref, ge0_ref, xe1_ref, ge1_ref, grow_ref,
    first_ref, p_ref, q_ref, sf_ref, ds_ref, dec_ref, s_scr, d_scr, dec_scr,
):
    n = grow_ref.shape[0]
    r = side()
    for slot, (bc_ref, xe_ref, ge_ref) in enumerate(
        ((bc0_ref, xe0_ref, ge0_ref), (bc1_ref, xe1_ref, ge1_ref))
    ):
        s_scr[slot] = dot(bc_ref[:, :LANES], xe_ref[...], TN)
        d_scr[slot] = dot(bc_ref[:, LANES:], ge_ref[...], TN)
        dec_scr[slot] = widen(grow_ref[n - 1 : n, :], lanes[slot], heads)
    dec_first, dec_second = dec_scr[r], dec_scr[1 - r]
    s_first, d_second = s_scr[r], d_scr[1 - r]
    sf_ref[...] = s_first.astype(BF16)
    ds_ref[...] = d_second.astype(BF16)
    p = (dec_second * s_first + s_scr[1 - r]).astype(BF16)
    q = (dec_first * d_second + d_scr[r]).astype(BF16)
    p_ref[...] = p
    q_ref[...] = q

    @pl.when(place() == 0)
    def _():
        first_ref[...] = p

    @pl.when(place() != 0)
    def _():
        first_ref[...] = q

    dec_ref[0:1, :] = dec_first * dec_second
    dec_ref[1:2, :] = dec_first
    dec_ref[2:3, :] = dec_second
    dec_ref[3:8, :] = jnp.zeros((5, dec_first.shape[1]), F32)


def hop_kernel(hop, received_ref, p_ref, q_ref, dec_ref, out_ref):
    carried = dec_ref[0:1, :] * received_ref[...].astype(F32)

    @pl.when(place() == hop)
    def _():
        out_ref[...] = (carried + p_ref[...].astype(F32)).astype(BF16)

    @pl.when(place() != hop)
    def _():
        out_ref[...] = (carried + q_ref[...].astype(F32)).astype(BF16)


def inside_kernel(
    heads, lane, skip_at, x_at, g_at, skip_ref, x_ref, g_ref, bc_ref, step_ref, cum_ref,
    cumt_ref, y_ref, dx_ref, dscores_ref, gy_ref, ds_ref, gx_ref,
):
    n = step_ref.shape[0]
    mask = triangle(n)
    scores = jnp.where(mask, dot(bc_ref[:, LANES:], bc_ref[:, :LANES], NT), 0.0)
    gy_ref[...] = jnp.zeros_like(gy_ref)
    ds_ref[...] = jnp.zeros_like(ds_ref)
    gx_ref[...] = jnp.zeros_like(gx_ref)
    dscores = jnp.zeros((n, n), F32)
    for h in range(heads):
        at = slice(h * LANES, (h + 1) * LANES)
        one = slice(lane + h, lane + h + 1)
        step = step_ref[:, one]
        gap = cum_ref[:, one] - cumt_ref[one, :]
        decay = jnp.exp(jnp.where(mask, gap, 0.0))
        mixing = (scores * decay).astype(BF16)
        x = x_ref[:, head_columns(x_at, h)].astype(F32)
        g = g_ref[:, head_columns(g_at, h)]
        gf = g.astype(F32)
        xs = (x * step).astype(BF16)
        skip = skip_ref[side() * GROUPS * heads + skip_at + h]
        y = dot(mixing, xs)
        dxs = dot(mixing, g, TN)
        dscores += dot(g, xs, NT) * decay
        y_ref[:, at] = y + skip * x
        dx_ref[:, at] = dxs * step + skip * gf
        gy_ref[:, one] = jnp.sum(gf * y, axis=1, keepdims=True)
        ds_ref[:, one] = jnp.sum(x * dxs, axis=1, keepdims=True)
        gx_ref[0:1, one] = jnp.sum(jnp.sum(gf * x, axis=0, keepdims=True), axis=1, keepdims=True)
    dscores_ref[...] = jnp.where(mask, dscores, 0.0)


def inside_bc_kernel(bc0_ref, bc1_ref, *refs):
    parts, outs = refs[: 2 * GROUPS], refs[2 * GROUPS :]
    for slot, bc_ref in enumerate((bc0_ref, bc1_ref)):
        total = parts[slot * GROUPS][...]
        for i in range(1, GROUPS):
            total = total + parts[slot * GROUPS + i][...]
        ds = total.astype(BF16)
        outs[slot][:, :LANES] = dot(ds, bc_ref[:, LANES:], TN)
        outs[slot][:, LANES:] = dot(ds, bc_ref[:, :LANES])


def across_kernel(heads, lanes, hops, filled, own_at, columns, *refs):
    refs = refs[2 * filled :]
    across_block(heads, lanes, hops, own_at, columns, *refs)


def across_block(
    heads, lanes, hops, own_at, columns, x0_ref, g0_ref, x1_ref, g1_ref, bc0_ref, bc1_ref, xe0_ref,
    ge0_ref, xe1_ref, ge1_ref, step_ref, grow_ref, endw_ref, dec_ref, p_ref, sf_ref, ds_ref,
    y0_ref, dx0_ref, y1_ref, dx1_ref, dbc0_ref, dbc1_ref, *refs
):
    received = refs[:hops]
    (
        yf_ref, dxf_ref, ys_ref, dxs_ref, dbco0_ref, dbco1_ref, u_ref, t_ref, re_ref,
        e_in, r_in, e_scr, r_scr, n_scr, yo_ref, dxo_ref, sems,
    ) = refs[hops:]
    r, pos = side(), place()
    width = yo_ref.shape[1]
    e_in[...] = jnp.zeros_like(e_in)
    r_in[...] = jnp.zeros_like(r_in)
    for k in range(hops):

        @pl.when(pos - 1 == k)
        def _(k=k):
            e_in[...] = received[k][...]

        @pl.when(hops - 1 - pos == k)
        def _(k=k):
            r_in[...] = received[k][...]

    dec_pair, dec_first, dec_second = dec_ref[0:1, :], dec_ref[1:2, :], dec_ref[2:3, :]
    entering = e_in[...].astype(F32)
    later = r_in[...].astype(F32)
    middle = dec_first * entering + sf_ref[...].astype(F32)
    leaving = dec_pair * entering + p_ref[...].astype(F32)
    earlier = dec_second * later + ds_ref[...].astype(F32)
    e_scr[r] = e_in[...]
    e_scr[1 - r] = middle.astype(BF16)
    r_scr[1 - r] = r_in[...]
    r_scr[r] = earlier.astype(BF16)
    n_scr[1 - r] = jnp.sum(later * leaving, axis=0, keepdims=True)
    n_scr[r] = jnp.sum(earlier * middle, axis=0, keepdims=True)

    u_ref[...] = jnp.zeros_like(u_ref)
    t_ref[...] = jnp.zeros_like(t_ref)
    re_ref[...] = jnp.zeros_like(re_ref)
    for slot, (bc_ref, xe_ref, ge_ref, y_ref, dx_ref, dbc_ref, dbco_ref) in enumerate(
        (
            (bc0_ref, xe0_ref, ge0_ref, y0_ref, dx0_ref, dbc0_ref, dbco0_ref),
            (bc1_ref, xe1_ref, ge1_ref, y1_ref, dx1_ref, dbc1_ref, dbco1_ref),
        )
    ):
        e_all = e_scr[slot]
        r_all = r_scr[slot]
        db = dbc_ref[:, :LANES] + dot(xe_ref[...], r_all, NT)
        dc = dbc_ref[:, LANES:] + dot(ge_ref[...], e_all, NT)
        dbco_ref[:, :LANES] = db.astype(dbco_ref.dtype)
        dbco_ref[:, LANES:] = dc.astype(dbco_ref.dtype)
        ce_all = dot(bc_ref[:, LANES:], e_all)
        br_all = dot(bc_ref[:, :LANES], r_all)
        for h in range(heads):
            at = slice(h * LANES, (h + 1) * LANES)
            lane = lanes[slot] + h
            one = slice(lane, lane + 1)
            ce, br = ce_all[:, at], br_all[:, at]
            y = (y_ref[:, at] + grow_ref[:, one] * ce).astype(BF16)
            dx = (dx_ref[:, at] + (step_ref[:, one] * endw_ref[:, one]) * br).astype(BF16)
            if slot == 0:
                yo_ref[:, at] = y
                dxo_ref[:, at] = dx
                x = x0_ref[:, head_columns(own_at, h)].astype(F32)
                g = g0_ref[:, head_columns(own_at, h)].astype(F32)
            else:
                ys_ref[:, at] = y
                dxs_ref[:, at] = dx
                x = x1_ref[:, head_columns(columns[0], h)].astype(F32)
                g = g1_ref[:, head_columns(columns[1], h)].astype(F32)
            u_ref[:, one] = jnp.sum(g * ce, axis=1, keepdims=True)
            t_ref[:, one] = jnp.sum(x * br, axis=1, keepdims=True)
            re_ref[0:1, one] = jnp.sum(n_scr[slot][:, at], axis=1, keepdims=True)
        if slot == 0:
            final = aligned(own_at[0] + r * own_at[1], width)
            pairs = [(yo_ref, yf_ref.at[:, final]), (dxo_ref, dxf_ref.at[:, final])]
            copies = copy_all(pairs, sems)
    for copy in copies:
        copy.wait()


def steps_kernel(sig_ref, rate_ref, step_ref, grow_ref, endw_ref, *refs):
    count = 2 * GROUPS
    gys, dss, gxs = refs[:count], refs[count : 2 * count], refs[2 * count : 3 * count]
    refs = refs[3 * count :]
    us, ts, res = refs[:GROUPS], refs[GROUPS : 2 * GROUPS], refs[2 * GROUPS : 3 * GROUPS]
    own_ref, send_ref, sums_ref = refs[3 * GROUPS :]

    def total(parts):
        value = parts[0][...]
        for a in parts[1:]:
            value = value + a[...]
        return value

    n = step_ref.shape[0]
    step = step_ref[...]
    ds = total(dss) + endw_ref[...] * total(ts)
    gy = total(gys) + grow_ref[...] * total(us)
    rate = rate_ref[0:1, :]
    last = lax.broadcasted_iota(jnp.int32, (n, LANES), 0) == n - 1
    dcum = gy - step * ds + jnp.where(last, total(res)[0:1, :], 0.0)
    lower = jnp.where(triangle(n), 1.0, 0.0).astype(F32)
    dlog = dot(lower, dcum, TN, precision=HIGHEST)
    draw = (ds - rate * dlog) * sig_ref[...]
    turned = draw.T
    heads = own_ref.shape[0]
    own_ref[...] = turned[:heads, :]
    send_ref[...] = turned[heads : 2 * heads, :]
    sums_ref[0:1, :] = jnp.sum(draw, axis=0, keepdims=True)
    sums_ref[1:2, :] = jnp.sum(dlog * (-step * rate), axis=0, keepdims=True)
    sums_ref[2:3, :] = total(gxs)[0:1, :]
    sums_ref[3:8, :] = jnp.zeros((5, LANES), F32)


def conv_back_kernel(
    own_ref, ret_ref, kept_ref, cw_ref, heads_ref, grad_ref, rim_ref, message_ref, z_scr, sum_scr
):
    tokens = own_ref.shape[0]
    taps = cw_ref.shape[0]
    pre = kept_ref[HALO + tokens :, :]
    sig = jax.nn.sigmoid(pre)
    dconv = (own_ref[...] + ret_ref[...].astype(F32)) * sig * (1.0 + pre * (1.0 - sig))
    z_scr[...] = jnp.zeros_like(z_scr)
    z_scr[HALO : HALO + tokens, :] = dconv
    grad = cw_ref[0:1, :] * z_scr[taps - 1 : taps - 1 + tokens + HALO, :]
    for k in range(1, taps):
        grad = grad + cw_ref[k : k + 1, :] * z_scr[taps - 1 - k : taps - 1 - k + tokens + HALO, :]
    grad_ref[...] = grad[HALO:, :]
    rim_ref[...] = grad[HALO - 8 : HALO, :]
    first = HALO - taps + 1
    sum_scr[...] = jnp.zeros_like(sum_scr)
    for k in range(taps):
        sum_scr[k : k + 1, :] = jnp.sum(
            dconv * kept_ref[first + k : first + k + tokens, :], axis=0, keepdims=True
        )
    sum_scr[taps : taps + 1, :] = jnp.sum(dconv, axis=0, keepdims=True)
    sum_scr[5:8, aligned(side() * LANES, LANES)] = heads_ref[0:3, :]
    small = split(sum_scr[...])
    grad = grad.astype(BF16)
    for k in range(message_ref.shape[0]):
        message_ref[k, 0 : tokens + HALO, :] = grad
        message_ref[k, tokens + HALO :, :] = small


def pack_kernel(count, layer_ref, halo_ref, *refs):
    outs, sems = refs[:count], refs[count]
    pairs = []
    for k in range(count):
        at = peer_columns(k, outs[k].shape[1])
        pairs.append((halo_ref.at[:, at], outs[k].at[0:HALO, :]))
        pairs.append((layer_ref.at[:, at], outs[k].at[HALO:, :]))
    for copy in copy_all(pairs, sems):
        copy.wait()


def turn_kernel(count, *refs):
    parts, out_ref = refs[:count], refs[count]
    tokens = parts[0].shape[0] - HALO
    f = lax.axis_index("fsdp")
    for k in range(count):
        out_ref[:, aligned((f ^ k) * tokens, tokens)] = parts[k][HALO:, :].T
    halos = jnp.concatenate([parts[k][0:HALO, :] for k in range(count)], 0)
    out_ref[:, count * tokens :] = halos.T


def weight_kernel(left_ref, rights_ref, out_ref):
    count = rights_ref.shape[0]
    tokens = (left_ref.shape[1] // count) - HALO
    right = jnp.concatenate(
        [rights_ref[k, HALO : HALO + tokens, :] for k in range(count)]
        + [rights_ref[lax.axis_index("fsdp") ^ k, 0:HALO, :] for k in range(count)],
        0,
    )
    at = tokens + HALO
    both = jnp.zeros((16, right.shape[1]), F32)
    for k in range(count):
        both += rights_ref[k, at : at + 16, :].astype(F32)
    small = split(both[0:8, :] + both[8:16, :])
    chunk = out_ref.shape[1] - 16
    for k in range(out_ref.shape[0]):
        term = dot(left_ref[k * chunk : (k + 1) * chunk, :], right)
        out_ref[k, 0:chunk, :] = term.astype(BF16)
        out_ref[k, chunk:, :] = small


def reduce_kernel(heads, terms_ref, total_ref, cw_ref, cb_ref, *head_refs):
    chunk = total_ref.shape[1]
    total = terms_ref[0].astype(F32)
    for k in range(1, terms_ref.shape[0]):
        total = total + terms_ref[k].astype(F32)
    for k in range(total_ref.shape[0]):
        total_ref[k] = total[0:chunk].astype(BF16)
    small = total[chunk : chunk + 8] + total[chunk + 8 :]
    taps = cw_ref.shape[0]
    cw_ref[...] = small[0:taps, :]
    cb_ref[...] = small[taps : taps + 1, :]
    for i, ref in enumerate(head_refs):
        row = small[5 + i : 6 + i, :]
        ref[:, :heads] = row[:, :heads] + row[:, heads : 2 * heads]
        row = row[:, LANES:]
        ref[:, heads:] = row[:, :heads] + row[:, heads : 2 * heads]


def place_rows_kernel(parts_ref, out_ref):
    chunk = parts_ref.shape[1]
    for k in range(parts_ref.shape[0]):
        out_ref[k * chunk : (k + 1) * chunk, :] = parts_ref[k].astype(F32)


def tokens_kernel(count, *refs):
    pieces = refs[:count]
    grad_ref, rim_ref, out_ref, w_scr, sems = refs[count:]
    copies = copy_all([(pieces[k], w_scr.at[k]) for k in range(count)], sems)
    tail = rim_ref.shape[0]
    own = grad_ref[...]
    g = jnp.concatenate([own[:-tail], own[-tail:] + rim_ref[...]], 0).astype(BF16)
    rows = pieces[0].shape[0]
    for k in range(count):
        copies[k].wait()
        out_ref[:, peer_columns(k, rows)] = dot(g, w_scr[k], NT).astype(BF16)


def join_kernel(*refs):
    own_ref, back_ref = refs[2:4]
    backs = refs[4 : 4 + 2 * GROUPS]
    y_ref, dx_ref, raw_ref, sems = refs[4 + 2 * GROUPS :]
    width = backs[0].shape[1]
    r = side()
    pairs = []
    for i in range(GROUPS):
        at = aligned(((1 - r) * GROUPS + i) * width, width)
        pairs.append((backs[2 * i], y_ref.at[:, at]))
        pairs.append((backs[2 * i + 1], dx_ref.at[:, at]))
    copies = copy_all(pairs, sems)
    heads = own_ref.shape[0]
    raw_ref[pl.ds(pl.multiple_of(r * heads, 8), heads), :] = own_ref[...]
    raw_ref[pl.ds(pl.multiple_of((1 - r) * heads, 8), heads), :] = back_ref[...]
    for copy in copies:
        copy.wait()


def toggled(x, axis, bits):
    size = lax.axis_size(axis)
    return lax.ppermute(x, axis, [(i, i ^ bits) for i in range(size)])


def exchanged(x, axis):
    return lax.all_to_all(x, axis, 0, 0)


def after(x, *others):
    return lax.optimization_barrier((x, *others))[0]


def body(layer_in, w_bc, conv_w, conv_b, ssm_in, dt_raw, dt_bias, a_log, skip_scale, grad_out):
    ctx, fsdp = lax.axis_size("ctx"), lax.axis_size("fsdp")
    layer, x, g, dt = layer_in[0], ssm_in[0], grad_out[0], dt_raw[0].T
    tokens, width = x.shape
    total_heads = dt_bias.shape[0]
    heads = total_heads // 2
    half = width // 2
    hg, gw = heads // GROUPS, half // GROUPS
    state = w_bc.shape[1] // 2
    taps = conv_w.shape[0]
    rows = w_bc.shape[0]
    chunk_rows = rows // ctx
    pairs = ctx // 2
    hops = pairs - 1
    square = shape((tokens, LANES), F32)
    flat = shape((tokens, gw), BF16)
    turned = shape((heads, tokens), F32)
    both_bc = [shape((tokens, 2 * state), F32)] * 2

    halo_send, dt_send, *swaps = call(
        swap_kernel, "swap",
        [shape((HALO, layer.shape[1]), BF16), turned, shape((tokens, 2 * gw), BF16), flat, flat], (),
        hbm=(layer, dt, x, g), scratch=[pltpu.SemaphoreType.DMA((6,))],
    )
    halo = lax.ppermute(halo_send, "ctx", [(i, i + 1) for i in range(ctx - 1)])
    dt_back = toggled(dt_send, "ctx", 1)
    swapped_first = toggled(swaps[0], "ctx", 1)
    swapped_x = toggled(after(swaps[1], halo, dt_back), "ctx", 1)

    step, cum, cumt, grow, endw, sig, rate = call(
        vectors_kernel, "vectors", [square] * 6 + [shape((8, LANES), F32)], (), dt, dt_back,
        dt_bias[None, :], a_log[None, :],
        scratch=[pltpu.VMEM((tokens, tokens), F32), pltpu.VMEM((8, LANES), F32)],
    )

    def source(slot, i):
        if slot == 0:
            return (i * gw, half), (i * gw, half), x, g
        if i == 0:
            return (0, 0), (gw, 0), swapped_first, swapped_first
        return (0, 0), (0, 0), swapped_x, swapped_g

    def scale(slot, i):
        x_at, g_at, xa, ga = source(slot, i)
        return call(
            functools.partial(scale_kernel, hg, slot * heads + i * hg, x_at, g_at), "scale",
            [flat, flat], (), xa, ga, step, grow, endw,
        )

    scaled = {(0, i): scale(0, i) for i in range(GROUPS)}
    scaled[1, 0] = scale(1, 0)
    packs = call(
        functools.partial(pack_kernel, fsdp), "pack", [shape((tokens + HALO, rows), BF16)] * fsdp,
        (), hbm=(layer, halo), scratch=[pltpu.SemaphoreType.DMA((2 * fsdp,))],
    )

    pieces = {0: w_bc}
    bit = fsdp // 2
    while bit:
        for k in list(pieces):
            piece = pieces[k]
            if k:
                piece = after(piece, scaled[1, 0][0], *[scaled[0, i][0] for i in range(GROUPS)])
            pieces[k | bit] = toggled(piece, "fsdp", bit)
        bit //= 2
    pieces = [pieces[k] for k in range(fsdp)]
    near, far = pieces[: fsdp // 2], pieces[fsdp // 2 :]

    def landing(count):
        return [
            pltpu.VMEM(layer.shape, BF16),
            pltpu.VMEM((count, *w_bc.shape), BF16),
            pltpu.SemaphoreType.DMA((1 + count,)),
        ]

    ext = shape((tokens + HALO, 2 * state), F32)
    early = call(
        functools.partial(early_kernel, len(near)), "project_early", ext, (), halo,
        hbm=(layer, *near), scratch=landing(len(near)),
    )
    layer_scr, w_scr, sems = landing(len(far))
    kept, bc = call(
        functools.partial(project_kernel, len(near), len(far)), "project",
        [
            shape((2 * tokens + HALO, 2 * state), F32),
            shape((tokens, 2 * state), BF16),
        ],
        (), halo, early, conv_w, conv_b[None, :], hbm=(layer, *far),
        scratch=[layer_scr, w_scr, pltpu.VMEM(ext.shape, F32), sems],
    )
    bcs = [bc, toggled(bc, "ctx", 1)]
    swapped_g = toggled(after(swaps[2], bcs[1]), "ctx", 1)

    wide = shape((state, gw), BF16)
    states, received = [], []
    for i in range(GROUPS):
        lanes = (i * hg, heads + i * hg)
        if i:
            scaled[1, i] = scale(1, i)
        first, p, q, s_first, d_second, decays = call(
            functools.partial(states_kernel, hg, lanes), "states",
            [wide] * 5 + [shape((8, gw), F32)],
            (), *bcs, *scaled[0, i], *scaled[1, i], after(grow, swapped_x, packs[0]),
            scratch=[pltpu.VMEM((2, state, gw), F32)] * 2 + [pltpu.VMEM((2, 1, gw), F32)],
        )
        states.append((decays, p, s_first, d_second, q))
        received.append([first])

    def within(slot, i, *earlier):
        x_at, g_at, xa, ga = source(slot, i)
        return call(
            functools.partial(inside_kernel, hg, slot * heads + i * hg, i * hg, x_at, g_at), "inside",
            [shape((tokens, gw), F32)] * 2 + [shape((tokens, tokens), F32), square, square]
            + [shape((8, LANES), F32)],
            (skip_scale,), xa, ga, after(bcs[slot], *earlier), step, cum, cumt,
        )

    order = [(slot, i) for slot in range(2) for i in range(GROUPS)]
    inside = {}
    waiting = list(order)
    value = received[-1][0]
    for hop in range(hops):
        moves = [(hop, hop + 1), (pairs - 1 - hop, pairs - 2 - hop)]
        moves = [(2 * a + i, 2 * b + i) for a, b in moves for i in range(2)]
        for i in range(GROUPS):
            earlier, value = value, received[i][-1]
            if hop:
                decays, p, _, _, q = states[i]
                if waiting:
                    key = waiting.pop(0)
                    inside[key] = within(*key, earlier)
                    value = after(value, inside[key][2])
                value = call(
                    functools.partial(hop_kernel, hop), "hop", wide, (), value, p, q, decays
                )
            received[i].append(lax.ppermute(value, "ctx", moves))
    for key in waiting:
        inside[key] = within(*key)
    lefts = [packs[0]] + [toggled(packs[k], "fsdp", k) for k in range(1, fsdp)]
    left = call(
        functools.partial(turn_kernel, fsdp), "turn", shape((rows, fsdp * (tokens + HALO)), BF16),
        (), *lefts,
    )

    dbcs = call(inside_bc_kernel, "inside_bc", both_bc, (), after(bcs[0], left), bcs[1], *[inside[key][2] for key in order])

    full = shape((tokens, width), BF16)
    finals, sends, us, ts, res = (), [], [], [], []
    for i in range(GROUPS):
        last = i == GROUPS - 1
        own_at, _, xa, ga = source(0, i)
        x_at, g_at, xb, gb = source(1, i)
        lanes = (i * hg, heads + i * hg)
        y, dx, y_send, dx_send, *dbcs, u, t, re = call(
            functools.partial(
                across_kernel, hg, lanes, hops, len(finals) // 2, own_at, (x_at, g_at)
            ),
            "across",
            [full, full, flat, flat]
            + [both_bc[0], shape((tokens, 2 * state), BF16 if last else F32)]
            + [square, square, shape((8, LANES), F32)],
            (), xa, ga, xb, gb, *bcs, *scaled[0, i], *scaled[1, i], step, grow, endw,
            *states[i][:4], *inside[0, i][:2], *inside[1, i][:2], *dbcs, *received[i][1:],
            hbm=finals, hbm_outs=2, aliases={0: 0, 1: 1} if finals else None,
            scratch=[pltpu.VMEM((state, gw), BF16)] * 2 + [pltpu.VMEM((2, state, gw), BF16)] * 2
            + [pltpu.VMEM((2, 1, gw), F32)] + [pltpu.VMEM((tokens, gw), BF16)] * 2
            + [pltpu.SemaphoreType.DMA((2,))],
        )
        finals = (y, dx)
        sends += [y_send, dx_send]
        us.append(u)
        ts.append(t)
        res.append(re)

    dbc_ret = toggled(dbcs[1], "ctx", 1)
    raw_own, raw_send, head_sums = call(
        steps_kernel, "steps", [turned] * 2 + [shape((8, LANES), F32)], (),
        sig, rate, step, grow, endw, *[inside[key][j] for j in (3, 4, 5) for key in order],
        *us, *ts, *res,
    )
    raw_back = toggled(raw_send, "ctx", 1)
    grad, rim_send, message = call(
        conv_back_kernel, "conv_back",
        [
            shape((tokens, 2 * state), F32),
            shape((8, 2 * state), F32),
            shape((fsdp, tokens + HALO + 16, 2 * state), BF16),
        ],
        (), dbcs[0], dbc_ret, kept, conv_w, head_sums,
        scratch=[
            pltpu.VMEM((tokens + 2 * HALO, 2 * state), F32),
            pltpu.VMEM((8, 2 * state), F32),
        ],
    )
    rim = lax.ppermute(rim_send, "ctx", [(i + 1, i) for i in range(ctx - 1)])
    backs = [toggled(after(sends[0], dbc_ret, raw_send), "ctx", 1)]

    rights = exchanged(message, "fsdp")
    terms = call(
        weight_kernel, "weight", shape((ctx, chunk_rows + 16, 2 * state), BF16), (),
        left, after(rights, *backs),
    )
    backs += [toggled(after(a, terms), "ctx", 1) for a in sends[1:]]
    total, grad_cw, grad_cb, *per_head = call(
        functools.partial(reduce_kernel, heads), "reduce",
        [
            shape((ctx, chunk_rows, 2 * state), BF16),
            shape((taps, 2 * state), F32),
            shape((1, 2 * state), F32),
        ]
        + [shape((1, total_heads), F32)] * 3,
        (), after(exchanged(terms, "ctx"), raw_back, rim, *backs[:-1]),
    )
    grad_weight = call(
        place_rows_kernel, "place_rows", shape((rows, 2 * state), F32), (), exchanged(total, "ctx")
    )
    grad_tokens = call(
        functools.partial(tokens_kernel, fsdp), "grad_tokens", shape((tokens, fsdp * rows), BF16),
        (), after(grad, terms), rim, hbm=pieces,
        scratch=[pltpu.VMEM((fsdp, *w_bc.shape), BF16), pltpu.SemaphoreType.DMA((fsdp,))],
    )
    ssm_out, grad_values, grad_raw = call(
        join_kernel, "join", [full, full, shape((total_heads, tokens), F32)],
        (), raw_own, raw_back, *backs, hbm=finals, hbm_outs=2,
        aliases={0: 0, 1: 1}, scratch=[pltpu.SemaphoreType.DMA((2 * GROUPS,))],
    )
    return (
        ssm_out[None],
        grad_values[None],
        grad_tokens[None],
        grad_raw.T[None],
        grad_weight,
        grad_cw,
        grad_cb[0],
        *[a[0] for a in per_head],
    )


def solution(mesh):
    tokens = P("fsdp", "ctx", None)
    in_specs = (tokens, P("fsdp", None), P(), P(), tokens, tokens, P(), P(), P(), tokens)
    out_specs = (tokens, tokens, tokens, tokens, P("fsdp", None), P(), P(), P(), P(), P())
    return jax.shard_map(body, mesh=mesh, in_specs=in_specs, out_specs=out_specs, check_vma=False)
```

```python
import functools

import jax
import jax.numpy as jnp
from jax import lax
from jax.experimental import pallas as pl
from jax.experimental.pallas import tpu as pltpu
from jax.sharding import PartitionSpec as P

F32 = jnp.float32
BF16 = jnp.bfloat16
LANES = 128
HALO = 16
GROUPS = 2
LIMIT = 16 * 1024 * 1024
HIGHEST = lax.Precision.HIGHEST
TN = ((0,), (0,))
NT = ((1,), (1,))


def dot(a, b, dims=((1,), (0,)), precision=None):
    return lax.dot_general(
        a, b, (dims, ((), ())), precision=precision, preferred_element_type=F32
    )


def shape(dims, dtype):
    return jax.ShapeDtypeStruct(dims, dtype)


def call(kernel, name, out_shape, smem, *operands, hbm=(), hbm_outs=0, scratch=(), aliases=None):
    single = not isinstance(out_shape, list)
    outs = [out_shape] if single else out_shape
    spaces = [pltpu.SMEM] * len(smem) + [pl.ANY] * len(hbm) + [pltpu.VMEM] * len(operands)
    out_spaces = [pltpu.HBM] * hbm_outs + [pltpu.VMEM] * (len(outs) - hbm_outs)
    result = pl.pallas_call(
        kernel,
        out_shape=outs,
        in_specs=[pl.BlockSpec(memory_space=a) for a in spaces],
        out_specs=[pl.BlockSpec(memory_space=a) for a in out_spaces],
        scratch_shapes=list(scratch),
        compiler_params=pltpu.CompilerParams(vmem_limit_bytes=LIMIT),
        input_output_aliases=aliases or {},
        name=name,
    )(*smem, *hbm, *operands)
    return result[0] if single else result


def copy_all(pairs, sems):
    copies = [pltpu.make_async_copy(a, b, sems.at[i]) for i, (a, b) in enumerate(pairs)]
    for copy in copies:
        copy.start()
    return copies


def side():
    return lax.rem(lax.axis_index("ctx"), 2)


def place():
    return lax.div(lax.axis_index("ctx"), 2)


def peer_columns(k, rows):
    return aligned((lax.axis_index("fsdp") ^ k) * rows, rows)


def aligned(at, size):
    return pl.ds(pl.multiple_of(at, LANES), size)


def triangle(n):
    rows = lax.broadcasted_iota(jnp.int32, (n, n), 0)
    cols = lax.broadcasted_iota(jnp.int32, (n, n), 1)
    return rows >= cols


def split(value):
    high = value.astype(BF16).astype(F32)
    return jnp.concatenate([high, value - high], 0).astype(BF16)


def swap_kernel(layer_ref, x_ref, g_ref, halo_ref, first_ref, x_out_ref, g_out_ref, sems):
    width = x_out_ref.shape[1]
    tokens = layer_ref.shape[0]
    base = (1 - side()) * (GROUPS * width)
    pairs = [
        (layer_ref.at[tokens - HALO : tokens, :], halo_ref),
        (x_ref.at[:, aligned(base, width)], first_ref.at[:, :width]),
        (g_ref.at[:, aligned(base, width)], first_ref.at[:, width:]),
        (x_ref.at[:, aligned(base + width, width)], x_out_ref),
        (g_ref.at[:, aligned(base + width, width)], g_out_ref),
    ]
    for copy in copy_all(pairs, sems):
        copy.wait()


def vectors_kernel(
    dt_ref, back_ref, bias_ref, alog_ref, step_ref, cum_ref, cumt_ref, grow_ref, endw_ref, sig_ref,
    rate_ref, turned, rows,
):
    n = back_ref.shape[1]
    heads = back_ref.shape[0] // 2
    r = side()
    mine = pl.ds(pl.multiple_of(r * heads, 8), heads)
    turned[...] = jnp.zeros_like(turned)
    turned[0:heads, :] = dt_ref[mine, :]
    turned[heads : 2 * heads, :] = back_ref[mine, :]
    rows[...] = jnp.zeros_like(rows)
    for i, ref in enumerate((bias_ref, alog_ref)):
        half = jnp.where(r == 0, ref[:, :heads], ref[:, heads:])
        rows[i : i + 1, 0:heads] = half
        rows[i : i + 1, heads : 2 * heads] = half
    raw = turned[...].T + rows[0:1, :]
    step = jnp.maximum(raw, 0.0) + jnp.log1p(jnp.exp(-jnp.abs(raw)))
    rate = jnp.exp(rows[1:2, :])
    log_decay = -step * rate
    lower = jnp.where(triangle(n), 1.0, 0.0).astype(F32)
    cum = dot(lower, log_decay, precision=HIGHEST)
    step_ref[...] = step
    cum_ref[...] = cum
    cumt_ref[...] = cum.T
    grow_ref[...] = jnp.exp(cum)
    endw_ref[...] = jnp.exp(cum[n - 1 : n, :] - cum)
    sig_ref[...] = jax.nn.sigmoid(raw)
    rate_ref[...] = jnp.broadcast_to(rate, rate_ref.shape)


def early_kernel(count, layer_ref, *refs):
    pieces = refs[:count]
    out_ref, layer_scr, w_scr, sems = refs[count:]
    copies = copy_all(
        [(layer_ref, layer_scr)] + [(pieces[k], w_scr.at[k]) for k in range(count)], sems
    )
    copies[0].wait()
    total = 0.0
    for k in range(count):
        copies[k + 1].wait()
        total += dot(layer_scr[:, peer_columns(k, w_scr.shape[1])], w_scr[k])
    out_ref[...] = total


def project_kernel(done, count, layer_ref, *refs):
    pieces = refs[:count]
    halo_ref, early_ref, cw_ref, cb_ref, kept_ref, bc_ref, layer_scr, w_scr, ext_scr, sems = refs[count:]
    copies = copy_all(
        [(layer_ref, layer_scr)] + [(pieces[k], w_scr.at[k]) for k in range(count)], sems
    )
    taps = cw_ref.shape[0]
    tokens = layer_ref.shape[0]
    copies[0].wait()
    total, rim = early_ref[...], 0.0
    for k in range(count):
        copies[k + 1].wait()
        at = peer_columns(k, w_scr.shape[1])
        rim += dot(halo_ref[:, at], w_scr[k])
        if k >= done:
            total += dot(layer_scr[:, at], w_scr[k])
    ext_scr[0:HALO, :] = rim
    ext_scr[HALO:, :] = total
    kept_ref[0 : HALO + tokens, :] = ext_scr[...]
    first = HALO - taps + 1
    pre = cb_ref[...] + cw_ref[0:1, :] * ext_scr[first : first + tokens, :]
    for k in range(1, taps):
        pre = pre + cw_ref[k : k + 1, :] * ext_scr[first + k : first + k + tokens, :]
    kept_ref[HALO + tokens :, :] = pre
    bc_ref[...] = (pre * jax.nn.sigmoid(pre)).astype(BF16)


def head_columns(at, h):
    first, more = at
    return aligned(first + side() * more + h * LANES, LANES)


def scale_kernel(heads, lane, x_at, g_at, x_ref, g_ref, step_ref, grow_ref, endw_ref, xe_ref, ge_ref):
    for h in range(heads):
        at = slice(h * LANES, (h + 1) * LANES)
        one = slice(lane + h, lane + h + 1)
        x = x_ref[:, head_columns(x_at, h)].astype(F32)
        g = g_ref[:, head_columns(g_at, h)].astype(F32)
        xe_ref[:, at] = (x * (step_ref[:, one] * endw_ref[:, one])).astype(BF16)
        ge_ref[:, at] = (g * grow_ref[:, one]).astype(BF16)


def widen(row, lane, heads):
    return jnp.concatenate(
        [jnp.broadcast_to(row[:, lane + h : lane + h + 1], (1, LANES)) for h in range(heads)], 1
    )


def states_kernel(
    heads, lanes, bc0_ref, bc1_ref, xe0_ref, ge0_ref, xe1_ref, ge1_ref, grow_ref,
    first_ref, p_ref, q_ref, sf_ref, ds_ref, dec_ref, s_scr, d_scr, dec_scr,
):
    n = grow_ref.shape[0]
    r = side()
    for slot, (bc_ref, xe_ref, ge_ref) in enumerate(
        ((bc0_ref, xe0_ref, ge0_ref), (bc1_ref, xe1_ref, ge1_ref))
    ):
        s_scr[slot] = dot(bc_ref[:, :LANES], xe_ref[...], TN)
        d_scr[slot] = dot(bc_ref[:, LANES:], ge_ref[...], TN)
        dec_scr[slot] = widen(grow_ref[n - 1 : n, :], lanes[slot], heads)
    dec_first, dec_second = dec_scr[r], dec_scr[1 - r]
    s_first, d_second = s_scr[r], d_scr[1 - r]
    sf_ref[...] = s_first.astype(BF16)
    ds_ref[...] = d_second.astype(BF16)
    p = (dec_second * s_first + s_scr[1 - r]).astype(BF16)
    q = (dec_first * d_second + d_scr[r]).astype(BF16)
    p_ref[...] = p
    q_ref[...] = q

    @pl.when(place() == 0)
    def _():
        first_ref[...] = p

    @pl.when(place() != 0)
    def _():
        first_ref[...] = q

    dec_ref[0:1, :] = dec_first * dec_second
    dec_ref[1:2, :] = dec_first
    dec_ref[2:3, :] = dec_second
    dec_ref[3:8, :] = jnp.zeros((5, dec_first.shape[1]), F32)


def hop_kernel(hop, received_ref, p_ref, q_ref, dec_ref, out_ref):
    carried = dec_ref[0:1, :] * received_ref[...].astype(F32)

    @pl.when(place() == hop)
    def _():
        out_ref[...] = (carried + p_ref[...].astype(F32)).astype(BF16)

    @pl.when(place() != hop)
    def _():
        out_ref[...] = (carried + q_ref[...].astype(F32)).astype(BF16)


def inside_kernel(
    heads, lane, skip_at, x_at, g_at, skip_ref, x_ref, g_ref, bc_ref, step_ref, cum_ref,
    cumt_ref, y_ref, dx_ref, dscores_ref, gy_ref, ds_ref, gx_ref,
):
    n = step_ref.shape[0]
    mask = triangle(n)
    scores = jnp.where(mask, dot(bc_ref[:, LANES:], bc_ref[:, :LANES], NT), 0.0)
    gy_ref[...] = jnp.zeros_like(gy_ref)
    ds_ref[...] = jnp.zeros_like(ds_ref)
    gx_ref[...] = jnp.zeros_like(gx_ref)
    dscores = jnp.zeros((n, n), F32)
    for h in range(heads):
        at = slice(h * LANES, (h + 1) * LANES)
        one = slice(lane + h, lane + h + 1)
        step = step_ref[:, one]
        gap = cum_ref[:, one] - cumt_ref[one, :]
        decay = jnp.exp(jnp.where(mask, gap, 0.0))
        mixing = (scores * decay).astype(BF16)
        x = x_ref[:, head_columns(x_at, h)].astype(F32)
        g = g_ref[:, head_columns(g_at, h)]
        gf = g.astype(F32)
        xs = (x * step).astype(BF16)
        skip = skip_ref[side() * GROUPS * heads + skip_at + h]
        y = dot(mixing, xs)
        dxs = dot(mixing, g, TN)
        dscores += dot(g, xs, NT) * decay
        y_ref[:, at] = y + skip * x
        dx_ref[:, at] = dxs * step + skip * gf
        gy_ref[:, one] = jnp.sum(gf * y, axis=1, keepdims=True)
        ds_ref[:, one] = jnp.sum(x * dxs, axis=1, keepdims=True)
        gx_ref[0:1, one] = jnp.sum(jnp.sum(gf * x, axis=0, keepdims=True), axis=1, keepdims=True)
    dscores_ref[...] = jnp.where(mask, dscores, 0.0)


def inside_bc_kernel(bc0_ref, bc1_ref, *refs):
    parts, outs = refs[: 2 * GROUPS], refs[2 * GROUPS :]
    for slot, bc_ref in enumerate((bc0_ref, bc1_ref)):
        total = parts[slot * GROUPS][...]
        for i in range(1, GROUPS):
            total = total + parts[slot * GROUPS + i][...]
        ds = total.astype(BF16)
        outs[slot][:, :LANES] = dot(ds, bc_ref[:, LANES:], TN)
        outs[slot][:, LANES:] = dot(ds, bc_ref[:, :LANES])


def across_kernel(heads, lanes, hops, filled, own_at, columns, *refs):
    refs = refs[2 * filled :]
    across_block(heads, lanes, hops, own_at, columns, *refs)


def across_block(
    heads, lanes, hops, own_at, columns, x0_ref, g0_ref, x1_ref, g1_ref, bc0_ref, bc1_ref, xe0_ref,
    ge0_ref, xe1_ref, ge1_ref, step_ref, grow_ref, endw_ref, dec_ref, p_ref, sf_ref, ds_ref,
    y0_ref, dx0_ref, y1_ref, dx1_ref, dbc0_ref, dbc1_ref, *refs
):
    received = refs[:hops]
    (
        yf_ref, dxf_ref, ys_ref, dxs_ref, dbco0_ref, dbco1_ref, u_ref, t_ref, re_ref,
        e_in, r_in, e_scr, r_scr, n_scr, yo_ref, dxo_ref, sems,
    ) = refs[hops:]
    r, pos = side(), place()
    width = yo_ref.shape[1]
    e_in[...] = jnp.zeros_like(e_in)
    r_in[...] = jnp.zeros_like(r_in)
    for k in range(hops):

        @pl.when(pos - 1 == k)
        def _(k=k):
            e_in[...] = received[k][...]

        @pl.when(hops - 1 - pos == k)
        def _(k=k):
            r_in[...] = received[k][...]

    dec_pair, dec_first, dec_second = dec_ref[0:1, :], dec_ref[1:2, :], dec_ref[2:3, :]
    entering = e_in[...].astype(F32)
    later = r_in[...].astype(F32)
    middle = dec_first * entering + sf_ref[...].astype(F32)
    leaving = dec_pair * entering + p_ref[...].astype(F32)
    earlier = dec_second * later + ds_ref[...].astype(F32)
    e_scr[r] = e_in[...]
    e_scr[1 - r] = middle.astype(BF16)
    r_scr[1 - r] = r_in[...]
    r_scr[r] = earlier.astype(BF16)
    n_scr[1 - r] = jnp.sum(later * leaving, axis=0, keepdims=True)
    n_scr[r] = jnp.sum(earlier * middle, axis=0, keepdims=True)

    u_ref[...] = jnp.zeros_like(u_ref)
    t_ref[...] = jnp.zeros_like(t_ref)
    re_ref[...] = jnp.zeros_like(re_ref)
    for slot, (bc_ref, xe_ref, ge_ref, y_ref, dx_ref, dbc_ref, dbco_ref) in enumerate(
        (
            (bc0_ref, xe0_ref, ge0_ref, y0_ref, dx0_ref, dbc0_ref, dbco0_ref),
            (bc1_ref, xe1_ref, ge1_ref, y1_ref, dx1_ref, dbc1_ref, dbco1_ref),
        )
    ):
        e_all = e_scr[slot]
        r_all = r_scr[slot]
        db = dbc_ref[:, :LANES] + dot(xe_ref[...], r_all, NT)
        dc = dbc_ref[:, LANES:] + dot(ge_ref[...], e_all, NT)
        dbco_ref[:, :LANES] = db.astype(dbco_ref.dtype)
        dbco_ref[:, LANES:] = dc.astype(dbco_ref.dtype)
        ce_all = dot(bc_ref[:, LANES:], e_all)
        br_all = dot(bc_ref[:, :LANES], r_all)
        for h in range(heads):
            at = slice(h * LANES, (h + 1) * LANES)
            lane = lanes[slot] + h
            one = slice(lane, lane + 1)
            ce, br = ce_all[:, at], br_all[:, at]
            y = (y_ref[:, at] + grow_ref[:, one] * ce).astype(BF16)
            dx = (dx_ref[:, at] + (step_ref[:, one] * endw_ref[:, one]) * br).astype(BF16)
            if slot == 0:
                yo_ref[:, at] = y
                dxo_ref[:, at] = dx
                x = x0_ref[:, head_columns(own_at, h)].astype(F32)
                g = g0_ref[:, head_columns(own_at, h)].astype(F32)
            else:
                ys_ref[:, at] = y
                dxs_ref[:, at] = dx
                x = x1_ref[:, head_columns(columns[0], h)].astype(F32)
                g = g1_ref[:, head_columns(columns[1], h)].astype(F32)
            u_ref[:, one] = jnp.sum(g * ce, axis=1, keepdims=True)
            t_ref[:, one] = jnp.sum(x * br, axis=1, keepdims=True)
            re_ref[0:1, one] = jnp.sum(n_scr[slot][:, at], axis=1, keepdims=True)
        if slot == 0:
            final = aligned(own_at[0] + r * own_at[1], width)
            pairs = [(yo_ref, yf_ref.at[:, final]), (dxo_ref, dxf_ref.at[:, final])]
            copies = copy_all(pairs, sems)
    for copy in copies:
        copy.wait()


def steps_kernel(sig_ref, rate_ref, step_ref, grow_ref, endw_ref, *refs):
    count = 2 * GROUPS
    gys, dss, gxs = refs[:count], refs[count : 2 * count], refs[2 * count : 3 * count]
    refs = refs[3 * count :]
    us, ts, res = refs[:GROUPS], refs[GROUPS : 2 * GROUPS], refs[2 * GROUPS : 3 * GROUPS]
    own_ref, send_ref, sums_ref = refs[3 * GROUPS :]

    def total(parts):
        value = parts[0][...]
        for a in parts[1:]:
            value = value + a[...]
        return value

    n = step_ref.shape[0]
    step = step_ref[...]
    ds = total(dss) + endw_ref[...] * total(ts)
    gy = total(gys) + grow_ref[...] * total(us)
    rate = rate_ref[0:1, :]
    last = lax.broadcasted_iota(jnp.int32, (n, LANES), 0) == n - 1
    dcum = gy - step * ds + jnp.where(last, total(res)[0:1, :], 0.0)
    lower = jnp.where(triangle(n), 1.0, 0.0).astype(F32)
    dlog = dot(lower, dcum, TN, precision=HIGHEST)
    draw = (ds - rate * dlog) * sig_ref[...]
    turned = draw.T
    heads = own_ref.shape[0]
    own_ref[...] = turned[:heads, :]
    send_ref[...] = turned[heads : 2 * heads, :]
    sums_ref[0:1, :] = jnp.sum(draw, axis=0, keepdims=True)
    sums_ref[1:2, :] = jnp.sum(dlog * (-step * rate), axis=0, keepdims=True)
    sums_ref[2:3, :] = total(gxs)[0:1, :]
    sums_ref[3:8, :] = jnp.zeros((5, LANES), F32)


def conv_back_kernel(
    own_ref, ret_ref, kept_ref, cw_ref, heads_ref, grad_ref, rim_ref, message_ref, z_scr, sum_scr
):
    tokens = own_ref.shape[0]
    taps = cw_ref.shape[0]
    pre = kept_ref[HALO + tokens :, :]
    sig = jax.nn.sigmoid(pre)
    dconv = (own_ref[...] + ret_ref[...].astype(F32)) * sig * (1.0 + pre * (1.0 - sig))
    z_scr[...] = jnp.zeros_like(z_scr)
    z_scr[HALO : HALO + tokens, :] = dconv
    grad = cw_ref[0:1, :] * z_scr[taps - 1 : taps - 1 + tokens + HALO, :]
    for k in range(1, taps):
        grad = grad + cw_ref[k : k + 1, :] * z_scr[taps - 1 - k : taps - 1 - k + tokens + HALO, :]
    grad_ref[...] = grad[HALO:, :]
    rim_ref[...] = grad[HALO - 8 : HALO, :]
    first = HALO - taps + 1
    sum_scr[...] = jnp.zeros_like(sum_scr)
    for k in range(taps):
        sum_scr[k : k + 1, :] = jnp.sum(
            dconv * kept_ref[first + k : first + k + tokens, :], axis=0, keepdims=True
        )
    sum_scr[taps : taps + 1, :] = jnp.sum(dconv, axis=0, keepdims=True)
    sum_scr[5:8, aligned(side() * LANES, LANES)] = heads_ref[0:3, :]
    small = split(sum_scr[...])
    message_ref[0 : tokens + HALO, :] = grad.astype(BF16)
    message_ref[tokens + HALO :, :] = small


def pack_kernel(count, layer_ref, halo_ref, *refs):
    outs, sems = refs[:count], refs[count]
    pairs = []
    for k in range(count):
        at = peer_columns(k, outs[k].shape[1])
        pairs.append((halo_ref.at[:, at], outs[k].at[0:HALO, :]))
        pairs.append((layer_ref.at[:, at], outs[k].at[HALO:, :]))
    for copy in copy_all(pairs, sems):
        copy.wait()


def turn_kernel(count, *refs):
    parts, out_ref = refs[:count], refs[count]
    tokens = parts[0].shape[0] - HALO
    for k in range(count):
        out_ref[:, k * tokens : (k + 1) * tokens] = parts[k][HALO:, :].T
    halos = jnp.concatenate([parts[k][0:HALO, :] for k in range(count)], 0)
    out_ref[:, count * tokens :] = halos.T


def weight_kernel(count, left_ref, *refs):
    rights, out_ref = refs[:count], refs[count]
    tokens = (left_ref.shape[1] // count) - HALO
    right = jnp.concatenate(
        [a[HALO : HALO + tokens, :] for a in rights] + [a[0:HALO, :] for a in rights], 0
    )
    at = tokens + HALO
    both = jnp.zeros((16, right.shape[1]), F32)
    for a in rights:
        both += a[at : at + 16, :].astype(F32)
    small = split(both[0:8, :] + both[8:16, :])
    chunk = out_ref.shape[1] - 16
    for k in range(out_ref.shape[0]):
        term = dot(left_ref[k * chunk : (k + 1) * chunk, :], right)
        out_ref[k, 0:chunk, :] = term.astype(BF16)
        out_ref[k, chunk:, :] = small


def reduce_kernel(heads, terms_ref, total_ref, cw_ref, cb_ref, *head_refs):
    chunk = total_ref.shape[1]
    total = terms_ref[0].astype(F32)
    for k in range(1, terms_ref.shape[0]):
        total = total + terms_ref[k].astype(F32)
    for k in range(total_ref.shape[0]):
        total_ref[k] = total[0:chunk].astype(BF16)
    small = total[chunk : chunk + 8] + total[chunk + 8 :]
    taps = cw_ref.shape[0]
    cw_ref[...] = small[0:taps, :]
    cb_ref[...] = small[taps : taps + 1, :]
    for i, ref in enumerate(head_refs):
        row = small[5 + i : 6 + i, :]
        ref[:, :heads] = row[:, :heads] + row[:, heads : 2 * heads]
        row = row[:, LANES:]
        ref[:, heads:] = row[:, :heads] + row[:, heads : 2 * heads]


def place_rows_kernel(parts_ref, out_ref):
    chunk = parts_ref.shape[1]
    for k in range(parts_ref.shape[0]):
        out_ref[k * chunk : (k + 1) * chunk, :] = parts_ref[k].astype(F32)


def tokens_kernel(count, *refs):
    pieces = refs[:count]
    grad_ref, rim_ref, out_ref, w_scr, sems = refs[count:]
    copies = copy_all([(pieces[k], w_scr.at[k]) for k in range(count)], sems)
    tail = rim_ref.shape[0]
    own = grad_ref[...]
    g = jnp.concatenate([own[:-tail], own[-tail:] + rim_ref[...]], 0).astype(BF16)
    rows = pieces[0].shape[0]
    for k in range(count):
        copies[k].wait()
        out_ref[:, peer_columns(k, rows)] = dot(g, w_scr[k], NT).astype(BF16)


def join_kernel(*refs):
    own_ref, back_ref = refs[2:4]
    backs = refs[4 : 4 + 2 * GROUPS]
    y_ref, dx_ref, raw_ref, sems = refs[4 + 2 * GROUPS :]
    width = backs[0].shape[1]
    r = side()
    pairs = []
    for i in range(GROUPS):
        at = aligned(((1 - r) * GROUPS + i) * width, width)
        pairs.append((backs[2 * i], y_ref.at[:, at]))
        pairs.append((backs[2 * i + 1], dx_ref.at[:, at]))
    copies = copy_all(pairs, sems)
    heads = own_ref.shape[0]
    raw_ref[pl.ds(pl.multiple_of(r * heads, 8), heads), :] = own_ref[...]
    raw_ref[pl.ds(pl.multiple_of((1 - r) * heads, 8), heads), :] = back_ref[...]
    for copy in copies:
        copy.wait()


def pinned(x):
    return pltpu.with_memory_space_constraint(x, pltpu.HBM)


def toggled(x, axis, bits):
    size = lax.axis_size(axis)
    return lax.ppermute(x, axis, [(i, i ^ bits) for i in range(size)])


def exchanged(x, axis):
    return lax.all_to_all(x, axis, 0, 0)


def after(x, *others):
    return lax.optimization_barrier((x, *others))[0]


def body(layer_in, w_bc, conv_w, conv_b, ssm_in, dt_raw, dt_bias, a_log, skip_scale, grad_out):
    ctx, fsdp = lax.axis_size("ctx"), lax.axis_size("fsdp")
    layer, x, g, dt = layer_in[0], ssm_in[0], grad_out[0], dt_raw[0].T
    tokens, width = x.shape
    total_heads = dt_bias.shape[0]
    heads = total_heads // 2
    half = width // 2
    hg, gw = heads // GROUPS, half // GROUPS
    state = w_bc.shape[1] // 2
    taps = conv_w.shape[0]
    rows = w_bc.shape[0]
    chunk_rows = rows // ctx
    pairs = ctx // 2
    hops = pairs - 1
    square = shape((tokens, LANES), F32)
    flat = shape((tokens, gw), BF16)
    turned = shape((heads, tokens), F32)
    both_bc = [shape((tokens, 2 * state), F32)] * 2

    dt_back = toggled(dt, "ctx", 1)
    halo_send, *swaps = call(
        swap_kernel, "swap",
        [shape((HALO, layer.shape[1]), BF16), shape((tokens, 2 * gw), BF16), flat, flat], (),
        hbm=(pinned(layer), pinned(x), pinned(g)), scratch=[pltpu.SemaphoreType.DMA((5,))],
    )
    halo = lax.ppermute(halo_send, "ctx", [(i, i + 1) for i in range(ctx - 1)])
    swapped_first = toggled(after(swaps[0], dt_back), "ctx", 1)
    swapped_x = toggled(after(swaps[1], halo), "ctx", 1)

    step, cum, cumt, grow, endw, sig, rate = call(
        vectors_kernel, "vectors", [square] * 6 + [shape((8, LANES), F32)], (), dt, dt_back,
        dt_bias[None, :], a_log[None, :],
        scratch=[pltpu.VMEM((tokens, tokens), F32), pltpu.VMEM((8, LANES), F32)],
    )

    def source(slot, i):
        if slot == 0:
            return (i * gw, half), (i * gw, half), x, g
        if i == 0:
            return (0, 0), (gw, 0), swapped_first, swapped_first
        return (0, 0), (0, 0), swapped_x, swapped_g

    def scale(slot, i):
        x_at, g_at, xa, ga = source(slot, i)
        return call(
            functools.partial(scale_kernel, hg, slot * heads + i * hg, x_at, g_at), "scale",
            [flat, flat], (), xa, ga, step, grow, endw,
        )

    scaled = {(0, i): scale(0, i) for i in range(GROUPS)}
    scaled[1, 0] = scale(1, 0)
    packs = call(
        functools.partial(pack_kernel, fsdp), "pack", [shape((tokens + HALO, rows), BF16)] * fsdp,
        (), hbm=(pinned(layer), halo), scratch=[pltpu.SemaphoreType.DMA((2 * fsdp,))],
    )

    pieces = {0: w_bc}
    bit = fsdp // 2
    while bit:
        for k in list(pieces):
            piece = pieces[k]
            if k:
                piece = after(piece, halo, scaled[1, 0][0], *[scaled[0, i][0] for i in range(GROUPS)])
            pieces[k | bit] = toggled(piece, "fsdp", bit)
        bit //= 2
    pieces = [pieces[k] for k in range(fsdp)]
    near = pieces[: fsdp // 2]

    def landing(count):
        return [
            pltpu.VMEM(layer.shape, BF16),
            pltpu.VMEM((count, *w_bc.shape), BF16),
            pltpu.SemaphoreType.DMA((1 + count,)),
        ]

    early = call(
        functools.partial(early_kernel, len(near)), "project_early",
        shape((tokens, 2 * state), F32), (), hbm=(pinned(layer), *near), scratch=landing(len(near)),
    )
    layer_scr, w_scr, sems = landing(fsdp)
    kept, bc = call(
        functools.partial(project_kernel, len(near), fsdp), "project",
        [
            shape((2 * tokens + HALO, 2 * state), F32),
            shape((tokens, 2 * state), BF16),
        ],
        (), halo, early, conv_w, conv_b[None, :], hbm=(pinned(layer), *pieces),
        scratch=[layer_scr, w_scr, pltpu.VMEM((tokens + HALO, 2 * state), F32), sems],
    )
    bcs = [bc, toggled(bc, "ctx", 1)]
    swapped_g = toggled(after(swaps[2], bcs[1]), "ctx", 1)

    wide = shape((state, gw), BF16)
    states, received = [], []
    for i in range(GROUPS):
        lanes = (i * hg, heads + i * hg)
        if i:
            scaled[1, i] = scale(1, i)
        first, p, q, s_first, d_second, decays = call(
            functools.partial(states_kernel, hg, lanes), "states",
            [wide] * 5 + [shape((8, gw), F32)],
            (), *bcs, *scaled[0, i], *scaled[1, i], after(grow, packs[0]) if i else grow,
            scratch=[pltpu.VMEM((2, state, gw), F32)] * 2 + [pltpu.VMEM((2, 1, gw), F32)],
        )
        states.append((decays, p, s_first, d_second, q))
        received.append([first])

    def within(slot, i, *earlier):
        x_at, g_at, xa, ga = source(slot, i)
        return call(
            functools.partial(inside_kernel, hg, slot * heads + i * hg, i * hg, x_at, g_at), "inside",
            [shape((tokens, gw), F32)] * 2 + [shape((tokens, tokens), F32), square, square]
            + [shape((8, LANES), F32)],
            (skip_scale,), xa, ga, after(bcs[slot], *earlier), step, cum, cumt,
        )

    order = [(slot, i) for slot in range(2) for i in range(GROUPS)]
    inside = {}
    waiting = list(order)
    value = received[-1][0]
    for hop in range(hops):
        moves = [(hop, hop + 1), (pairs - 1 - hop, pairs - 2 - hop)]
        moves = [(2 * a + i, 2 * b + i) for a, b in moves for i in range(2)]
        for i in range(GROUPS):
            earlier, value = value, received[i][-1]
            if hop:
                decays, p, _, _, q = states[i]
                if waiting:
                    key = waiting.pop(0)
                    inside[key] = within(*key, earlier)
                    value = after(value, inside[key][2])
                value = call(
                    functools.partial(hop_kernel, hop), "hop", wide, (), value, p, q, decays
                )
            received[i].append(lax.ppermute(value, "ctx", moves))
    for key in waiting:
        inside[key] = within(*key)
    lefts = [packs[0]] + [toggled(packs[k], "fsdp", k) for k in range(1, fsdp)]
    dbcs = call(inside_bc_kernel, "inside_bc", both_bc, (), *bcs, *[inside[key][2] for key in order])

    full = shape((tokens, width), BF16)
    finals, sends, us, ts, res = (), [], [], [], []
    for i in range(GROUPS):
        last = i == GROUPS - 1
        own_at, _, xa, ga = source(0, i)
        x_at, g_at, xb, gb = source(1, i)
        if last:
            left = call(
                functools.partial(turn_kernel, fsdp), "turn",
                shape((rows, fsdp * (tokens + HALO)), BF16), (), after(lefts[0], *sends), *lefts[1:],
            )
        lanes = (i * hg, heads + i * hg)
        y, dx, y_send, dx_send, *dbcs, u, t, re = call(
            functools.partial(
                across_kernel, hg, lanes, hops, len(finals) // 2, own_at, (x_at, g_at)
            ),
            "across",
            [full, full, flat, flat]
            + [both_bc[0], shape((tokens, 2 * state), BF16 if last else F32)]
            + [square, square, shape((8, LANES), F32)],
            (), xa, ga, xb, gb, after(bcs[0], left) if last else bcs[0], bcs[1], *scaled[0, i], *scaled[1, i], step, grow, endw,
            *states[i][:4], *inside[0, i][:2], *inside[1, i][:2], *dbcs, *received[i][1:],
            hbm=finals, hbm_outs=2, aliases={0: 0, 1: 1} if finals else None,
            scratch=[pltpu.VMEM((state, gw), BF16)] * 2 + [pltpu.VMEM((2, state, gw), BF16)] * 2
            + [pltpu.VMEM((2, 1, gw), F32)] + [pltpu.VMEM((tokens, gw), BF16)] * 2
            + [pltpu.SemaphoreType.DMA((2,))],
        )
        finals = (y, dx)
        sends += [y_send, dx_send]
        us.append(u)
        ts.append(t)
        res.append(re)

    dbc_ret = toggled(dbcs[1], "ctx", 1)
    raw_own, raw_send, head_sums = call(
        steps_kernel, "steps", [turned] * 2 + [shape((8, LANES), F32)], (),
        sig, rate, step, grow, endw, *[inside[key][j] for j in (3, 4, 5) for key in order],
        *us, *ts, *res,
    )
    raw_back = toggled(raw_send, "ctx", 1)
    grad, rim_send, message = call(
        conv_back_kernel, "conv_back",
        [
            shape((tokens, 2 * state), F32),
            shape((8, 2 * state), F32),
            shape((tokens + HALO + 16, 2 * state), BF16),
        ],
        (), dbcs[0], dbc_ret, kept, conv_w, head_sums,
        scratch=[
            pltpu.VMEM((tokens + 2 * HALO, 2 * state), F32),
            pltpu.VMEM((8, 2 * state), F32),
        ],
    )
    rim = lax.ppermute(rim_send, "ctx", [(i + 1, i) for i in range(ctx - 1)])
    backs = [toggled(after(sends[0], dbc_ret, raw_send), "ctx", 1)]

    rights = [message] + [toggled(message, "fsdp", k) for k in range(fsdp - 1, 0, -1)][::-1]
    terms = call(
        functools.partial(weight_kernel, fsdp), "weight",
        shape((ctx, chunk_rows + 16, 2 * state), BF16), (), left, after(message, *backs), *rights[1:],
    )
    backs += [toggled(after(a, terms), "ctx", 1) for a in sends[1:]]
    total, grad_cw, grad_cb, *per_head = call(
        functools.partial(reduce_kernel, heads), "reduce",
        [
            shape((ctx, chunk_rows, 2 * state), BF16),
            shape((taps, 2 * state), F32),
            shape((1, 2 * state), F32),
        ]
        + [shape((1, total_heads), F32)] * 3,
        (), after(exchanged(terms, "ctx"), raw_back, rim, *backs[:-2]),
    )
    grad_weight = call(
        place_rows_kernel, "place_rows", shape((rows, 2 * state), F32), (), exchanged(total, "ctx")
    )
    grad_tokens = call(
        functools.partial(tokens_kernel, fsdp), "grad_tokens", shape((tokens, fsdp * rows), BF16),
        (), after(grad, terms, *backs[:-1]), rim, hbm=pieces,
        scratch=[pltpu.VMEM((fsdp, *w_bc.shape), BF16), pltpu.SemaphoreType.DMA((fsdp,))],
    )
    ssm_out, grad_values, grad_raw = call(
        join_kernel, "join", [full, full, shape((total_heads, tokens), F32)],
        (), raw_own, raw_back, *backs, hbm=finals, hbm_outs=2,
        aliases={0: 0, 1: 1}, scratch=[pltpu.SemaphoreType.DMA((2 * GROUPS,))],
    )
    return (
        ssm_out[None],
        grad_values[None],
        grad_tokens[None],
        grad_raw.T[None],
        grad_weight,
        grad_cw,
        grad_cb[0],
        *[a[0] for a in per_head],
    )


def solution(mesh):
    tokens = P("fsdp", "ctx", None)
    in_specs = (tokens, P("fsdp", None), P(), P(), tokens, tokens, P(), P(), P(), tokens)
    out_specs = (tokens, tokens, tokens, tokens, P("fsdp", None), P(), P(), P(), P(), P())
    return jax.shard_map(body, mesh=mesh, in_specs=in_specs, out_specs=out_specs, check_vma=False)
```

```python
import functools

import jax
import jax.numpy as jnp
from jax import lax
from jax.experimental import pallas as pl
from jax.experimental.pallas import tpu as pltpu
from jax.sharding import PartitionSpec as P

F32 = jnp.float32
BF16 = jnp.bfloat16
LANES = 128
HALO = 16
PARTS = (2, 4, 4)
GROUPS = len(PARTS)
LIMIT = 16 * 1024 * 1024
HIGHEST = lax.Precision.HIGHEST
TN = ((0,), (0,))
NT = ((1,), (1,))


def dot(a, b, dims=((1,), (0,)), precision=None):
    return lax.dot_general(
        a, b, (dims, ((), ())), precision=precision, preferred_element_type=F32
    )


def shape(dims, dtype):
    return jax.ShapeDtypeStruct(dims, dtype)


def call(kernel, name, out_shape, smem, *operands, hbm=(), hbm_outs=0, scratch=(), aliases=None):
    single = not isinstance(out_shape, list)
    outs = [out_shape] if single else out_shape
    spaces = [pltpu.SMEM] * len(smem) + [pl.ANY] * len(hbm) + [pltpu.VMEM] * len(operands)
    out_spaces = [pltpu.HBM] * hbm_outs + [pltpu.VMEM] * (len(outs) - hbm_outs)
    result = pl.pallas_call(
        kernel,
        out_shape=outs,
        in_specs=[pl.BlockSpec(memory_space=a) for a in spaces],
        out_specs=[pl.BlockSpec(memory_space=a) for a in out_spaces],
        scratch_shapes=list(scratch),
        compiler_params=pltpu.CompilerParams(vmem_limit_bytes=LIMIT),
        input_output_aliases=aliases or {},
        name=name,
    )(*smem, *hbm, *operands)
    return result[0] if single else result


def copy_all(pairs, sems):
    copies = [pltpu.make_async_copy(a, b, sems.at[i]) for i, (a, b) in enumerate(pairs)]
    for copy in copies:
        copy.start()
    return copies


def side():
    return lax.rem(lax.axis_index("ctx"), 2)


def place():
    return lax.div(lax.axis_index("ctx"), 2)


def peer_columns(k, rows):
    return aligned((lax.axis_index("fsdp") ^ k) * rows, rows)


def aligned(at, size):
    return pl.ds(pl.multiple_of(at, LANES), size)


def triangle(n):
    rows = lax.broadcasted_iota(jnp.int32, (n, n), 0)
    cols = lax.broadcasted_iota(jnp.int32, (n, n), 1)
    return rows >= cols


def split(value):
    high = value.astype(BF16).astype(F32)
    return jnp.concatenate([high, value - high], 0).astype(BF16)


def swap_kernel(layer_ref, x_ref, g_ref, halo_ref, first_ref, x_out_ref, g_out_ref, sems):
    width = first_ref.shape[1] // 2
    more = x_out_ref.shape[1]
    tokens = layer_ref.shape[0]
    base = (1 - side()) * (width + more)
    pairs = [
        (layer_ref.at[tokens - HALO : tokens, :], halo_ref),
        (x_ref.at[:, aligned(base, width)], first_ref.at[:, :width]),
        (g_ref.at[:, aligned(base, width)], first_ref.at[:, width:]),
        (x_ref.at[:, aligned(base + width, more)], x_out_ref),
        (g_ref.at[:, aligned(base + width, more)], g_out_ref),
    ]
    for copy in copy_all(pairs, sems):
        copy.wait()


def vectors_kernel(
    dt_ref, back_ref, bias_ref, alog_ref, step_ref, cum_ref, cumt_ref, grow_ref, endw_ref, sig_ref,
    rate_ref, turned, rows,
):
    n = back_ref.shape[1]
    heads = back_ref.shape[0] // 2
    r = side()
    mine = pl.ds(pl.multiple_of(r * heads, 8), heads)
    turned[...] = jnp.zeros_like(turned)
    turned[0:heads, :] = dt_ref[mine, :]
    turned[heads : 2 * heads, :] = back_ref[mine, :]
    rows[...] = jnp.zeros_like(rows)
    for i, ref in enumerate((bias_ref, alog_ref)):
        half = jnp.where(r == 0, ref[:, :heads], ref[:, heads:])
        rows[i : i + 1, 0:heads] = half
        rows[i : i + 1, heads : 2 * heads] = half
    raw = turned[...].T + rows[0:1, :]
    step = jnp.maximum(raw, 0.0) + jnp.log1p(jnp.exp(-jnp.abs(raw)))
    rate = jnp.exp(rows[1:2, :])
    log_decay = -step * rate
    lower = jnp.where(triangle(n), 1.0, 0.0).astype(F32)
    cum = dot(lower, log_decay, precision=HIGHEST)
    step_ref[...] = step
    cum_ref[...] = cum
    cumt_ref[...] = cum.T
    grow_ref[...] = jnp.exp(cum)
    endw_ref[...] = jnp.exp(cum[n - 1 : n, :] - cum)
    sig_ref[...] = jax.nn.sigmoid(raw)
    rate_ref[...] = jnp.broadcast_to(rate, rate_ref.shape)


def early_kernel(count, layer_ref, *refs):
    pieces = refs[:count]
    out_ref, layer_scr, w_scr, sems = refs[count:]
    copies = copy_all(
        [(layer_ref, layer_scr)] + [(pieces[k], w_scr.at[k]) for k in range(count)], sems
    )
    copies[0].wait()
    total = 0.0
    for k in range(count):
        copies[k + 1].wait()
        total += dot(layer_scr[:, peer_columns(k, w_scr.shape[1])], w_scr[k])
    out_ref[...] = total


def project_kernel(done, count, layer_ref, *refs):
    pieces = refs[:count]
    halo_ref, early_ref, cw_ref, cb_ref, kept_ref, bc_ref, layer_scr, w_scr, ext_scr, sems = refs[count:]
    copies = copy_all(
        [(layer_ref, layer_scr)] + [(pieces[k], w_scr.at[k]) for k in range(count)], sems
    )
    taps = cw_ref.shape[0]
    tokens = layer_ref.shape[0]
    copies[0].wait()
    total, rim = early_ref[...], 0.0
    for k in range(count):
        copies[k + 1].wait()
        at = peer_columns(k, w_scr.shape[1])
        rim += dot(halo_ref[:, at], w_scr[k])
        if k >= done:
            total += dot(layer_scr[:, at], w_scr[k])
    ext_scr[0:HALO, :] = rim
    ext_scr[HALO:, :] = total
    kept_ref[0 : HALO + tokens, :] = ext_scr[...]
    first = HALO - taps + 1
    pre = cb_ref[...] + cw_ref[0:1, :] * ext_scr[first : first + tokens, :]
    for k in range(1, taps):
        pre = pre + cw_ref[k : k + 1, :] * ext_scr[first + k : first + k + tokens, :]
    kept_ref[HALO + tokens :, :] = pre
    bc_ref[...] = (pre * jax.nn.sigmoid(pre)).astype(BF16)


def head_columns(at, h):
    first, more = at
    return aligned(first + side() * more + h * LANES, LANES)


def scale_kernel(heads, lane, x_at, g_at, x_ref, g_ref, step_ref, grow_ref, endw_ref, xe_ref, ge_ref):
    for h in range(heads):
        at = slice(h * LANES, (h + 1) * LANES)
        one = slice(lane + h, lane + h + 1)
        x = x_ref[:, head_columns(x_at, h)].astype(F32)
        g = g_ref[:, head_columns(g_at, h)].astype(F32)
        xe_ref[:, at] = (x * (step_ref[:, one] * endw_ref[:, one])).astype(BF16)
        ge_ref[:, at] = (g * grow_ref[:, one]).astype(BF16)


def widen(row, lane, heads):
    return jnp.concatenate(
        [jnp.broadcast_to(row[:, lane + h : lane + h + 1], (1, LANES)) for h in range(heads)], 1
    )


def states_kernel(
    heads, lanes, bc0_ref, bc1_ref, xe0_ref, ge0_ref, xe1_ref, ge1_ref, grow_ref,
    first_ref, p_ref, q_ref, sf_ref, ds_ref, dec_ref, s_scr, d_scr, dec_scr,
):
    n = grow_ref.shape[0]
    r = side()
    for slot, (bc_ref, xe_ref, ge_ref) in enumerate(
        ((bc0_ref, xe0_ref, ge0_ref), (bc1_ref, xe1_ref, ge1_ref))
    ):
        s_scr[slot] = dot(bc_ref[:, :LANES], xe_ref[...], TN)
        d_scr[slot] = dot(bc_ref[:, LANES:], ge_ref[...], TN)
        dec_scr[slot] = widen(grow_ref[n - 1 : n, :], lanes[slot], heads)
    dec_first, dec_second = dec_scr[r], dec_scr[1 - r]
    s_first, d_second = s_scr[r], d_scr[1 - r]
    sf_ref[...] = s_first.astype(BF16)
    ds_ref[...] = d_second.astype(BF16)
    p = (dec_second * s_first + s_scr[1 - r]).astype(BF16)
    q = (dec_first * d_second + d_scr[r]).astype(BF16)
    p_ref[...] = p
    q_ref[...] = q

    @pl.when(place() == 0)
    def _():
        first_ref[...] = p

    @pl.when(place() != 0)
    def _():
        first_ref[...] = q

    dec_ref[0:1, :] = dec_first * dec_second
    dec_ref[1:2, :] = dec_first
    dec_ref[2:3, :] = dec_second
    dec_ref[3:8, :] = jnp.zeros((5, dec_first.shape[1]), F32)


def hop_kernel(hop, received_ref, p_ref, q_ref, dec_ref, out_ref):
    carried = dec_ref[0:1, :] * received_ref[...].astype(F32)

    @pl.when(place() == hop)
    def _():
        out_ref[...] = (carried + p_ref[...].astype(F32)).astype(BF16)

    @pl.when(place() != hop)
    def _():
        out_ref[...] = (carried + q_ref[...].astype(F32)).astype(BF16)


def inside_kernel(
    heads, lane, skip_at, all_heads, x_at, g_at, skip_ref, x_ref, g_ref, bc_ref, step_ref, cum_ref,
    cumt_ref, y_ref, dx_ref, dscores_ref, gy_ref, ds_ref, gx_ref,
):
    n = step_ref.shape[0]
    mask = triangle(n)
    scores = jnp.where(mask, dot(bc_ref[:, LANES:], bc_ref[:, :LANES], NT), 0.0)
    gy_ref[...] = jnp.zeros_like(gy_ref)
    ds_ref[...] = jnp.zeros_like(ds_ref)
    gx_ref[...] = jnp.zeros_like(gx_ref)
    dscores = jnp.zeros((n, n), F32)
    for h in range(heads):
        at = slice(h * LANES, (h + 1) * LANES)
        one = slice(lane + h, lane + h + 1)
        step = step_ref[:, one]
        gap = cum_ref[:, one] - cumt_ref[one, :]
        decay = jnp.exp(jnp.where(mask, gap, 0.0))
        mixing = (scores * decay).astype(BF16)
        x = x_ref[:, head_columns(x_at, h)].astype(F32)
        g = g_ref[:, head_columns(g_at, h)]
        gf = g.astype(F32)
        xs = (x * step).astype(BF16)
        skip = skip_ref[side() * all_heads + skip_at + h]
        y = dot(mixing, xs)
        dxs = dot(mixing, g, TN)
        dscores += dot(g, xs, NT) * decay
        y_ref[:, at] = y + skip * x
        dx_ref[:, at] = dxs * step + skip * gf
        gy_ref[:, one] = jnp.sum(gf * y, axis=1, keepdims=True)
        ds_ref[:, one] = jnp.sum(x * dxs, axis=1, keepdims=True)
        gx_ref[0:1, one] = jnp.sum(jnp.sum(gf * x, axis=0, keepdims=True), axis=1, keepdims=True)
    dscores_ref[...] = jnp.where(mask, dscores, 0.0)


def inside_bc_kernel(bc0_ref, bc1_ref, *refs):
    parts, outs = refs[: 2 * GROUPS], refs[2 * GROUPS :]
    for slot, bc_ref in enumerate((bc0_ref, bc1_ref)):
        total = parts[slot * GROUPS][...]
        for i in range(1, GROUPS):
            total = total + parts[slot * GROUPS + i][...]
        ds = total.astype(BF16)
        outs[slot][:, :LANES] = dot(ds, bc_ref[:, LANES:], TN)
        outs[slot][:, LANES:] = dot(ds, bc_ref[:, :LANES])


def across_kernel(heads, lanes, hops, filled, own_at, columns, *refs):
    refs = refs[2 * filled :]
    across_block(heads, lanes, hops, own_at, columns, *refs)


def across_block(
    heads, lanes, hops, own_at, columns, x0_ref, g0_ref, x1_ref, g1_ref, bc0_ref, bc1_ref, xe0_ref,
    ge0_ref, xe1_ref, ge1_ref, step_ref, grow_ref, endw_ref, dec_ref, p_ref, sf_ref, ds_ref,
    y0_ref, dx0_ref, y1_ref, dx1_ref, dbc0_ref, dbc1_ref, *refs
):
    received = refs[:hops]
    (
        yf_ref, dxf_ref, *send_refs, dbco0_ref, dbco1_ref, u_ref, t_ref, re_ref,
        e_in, r_in, e_scr, r_scr, n_scr, yo_ref, dxo_ref, sems,
    ) = refs[hops:]
    ys_ref, dxs_ref = send_refs if len(send_refs) == 2 else (send_refs[0].at[0], send_refs[0].at[1])
    r, pos = side(), place()
    width = yo_ref.shape[1]
    e_in[...] = jnp.zeros_like(e_in)
    r_in[...] = jnp.zeros_like(r_in)
    for k in range(hops):

        @pl.when(pos - 1 == k)
        def _(k=k):
            e_in[...] = received[k][...]

        @pl.when(hops - 1 - pos == k)
        def _(k=k):
            r_in[...] = received[k][...]

    dec_pair, dec_first, dec_second = dec_ref[0:1, :], dec_ref[1:2, :], dec_ref[2:3, :]
    entering = e_in[...].astype(F32)
    later = r_in[...].astype(F32)
    middle = dec_first * entering + sf_ref[...].astype(F32)
    leaving = dec_pair * entering + p_ref[...].astype(F32)
    earlier = dec_second * later + ds_ref[...].astype(F32)
    e_scr[r] = e_in[...]
    e_scr[1 - r] = middle.astype(BF16)
    r_scr[1 - r] = r_in[...]
    r_scr[r] = earlier.astype(BF16)
    n_scr[1 - r] = jnp.sum(later * leaving, axis=0, keepdims=True)
    n_scr[r] = jnp.sum(earlier * middle, axis=0, keepdims=True)

    u_ref[...] = jnp.zeros_like(u_ref)
    t_ref[...] = jnp.zeros_like(t_ref)
    re_ref[...] = jnp.zeros_like(re_ref)
    for slot, (bc_ref, xe_ref, ge_ref, y_ref, dx_ref, dbc_ref, dbco_ref) in enumerate(
        (
            (bc0_ref, xe0_ref, ge0_ref, y0_ref, dx0_ref, dbc0_ref, dbco0_ref),
            (bc1_ref, xe1_ref, ge1_ref, y1_ref, dx1_ref, dbc1_ref, dbco1_ref),
        )
    ):
        e_all = e_scr[slot]
        r_all = r_scr[slot]
        db = dbc_ref[:, :LANES] + dot(xe_ref[...], r_all, NT)
        dc = dbc_ref[:, LANES:] + dot(ge_ref[...], e_all, NT)
        dbco_ref[:, :LANES] = db.astype(dbco_ref.dtype)
        dbco_ref[:, LANES:] = dc.astype(dbco_ref.dtype)
        ce_all = dot(bc_ref[:, LANES:], e_all)
        br_all = dot(bc_ref[:, :LANES], r_all)
        for h in range(heads):
            at = slice(h * LANES, (h + 1) * LANES)
            lane = lanes[slot] + h
            one = slice(lane, lane + 1)
            ce, br = ce_all[:, at], br_all[:, at]
            y = (y_ref[:, at] + grow_ref[:, one] * ce).astype(BF16)
            dx = (dx_ref[:, at] + (step_ref[:, one] * endw_ref[:, one]) * br).astype(BF16)
            if slot == 0:
                yo_ref[:, at] = y
                dxo_ref[:, at] = dx
                x = x0_ref[:, head_columns(own_at, h)].astype(F32)
                g = g0_ref[:, head_columns(own_at, h)].astype(F32)
            else:
                ys_ref[:, at] = y
                dxs_ref[:, at] = dx
                x = x1_ref[:, head_columns(columns[0], h)].astype(F32)
                g = g1_ref[:, head_columns(columns[1], h)].astype(F32)
            u_ref[:, one] = jnp.sum(g * ce, axis=1, keepdims=True)
            t_ref[:, one] = jnp.sum(x * br, axis=1, keepdims=True)
            re_ref[0:1, one] = jnp.sum(n_scr[slot][:, at], axis=1, keepdims=True)
        if slot == 0:
            final = aligned(own_at[0] + r * own_at[1], width)
            pairs = [(yo_ref, yf_ref.at[:, final]), (dxo_ref, dxf_ref.at[:, final])]
            copies = copy_all(pairs, sems)
    for copy in copies:
        copy.wait()


def steps_kernel(sig_ref, rate_ref, step_ref, grow_ref, endw_ref, *refs):
    count = 2 * GROUPS
    gys, dss, gxs = refs[:count], refs[count : 2 * count], refs[2 * count : 3 * count]
    refs = refs[3 * count :]
    us, ts, res = refs[:GROUPS], refs[GROUPS : 2 * GROUPS], refs[2 * GROUPS : 3 * GROUPS]
    dbc_ref, own_ref, send_ref, sums_ref = refs[3 * GROUPS :]

    def total(parts):
        value = parts[0][...]
        for a in parts[1:]:
            value = value + a[...]
        return value

    n = step_ref.shape[0]
    step = step_ref[...]
    ds = total(dss) + endw_ref[...] * total(ts)
    gy = total(gys) + grow_ref[...] * total(us)
    rate = rate_ref[0:1, :]
    last = lax.broadcasted_iota(jnp.int32, (n, LANES), 0) == n - 1
    dcum = gy - step * ds + jnp.where(last, total(res)[0:1, :], 0.0)
    lower = jnp.where(triangle(n), 1.0, 0.0).astype(F32)
    dlog = dot(lower, dcum, TN, precision=HIGHEST)
    draw = (ds - rate * dlog) * sig_ref[...]
    turned = draw.T
    heads = own_ref.shape[0]
    own_ref[...] = turned[:heads, :]
    both = split(turned[heads : 2 * heads, :])
    send_ref[0:n, :] = dbc_ref[...]
    send_ref[n:, :LANES] = both[:heads]
    send_ref[n:, LANES:] = both[heads:]
    sums_ref[0:1, :] = jnp.sum(draw, axis=0, keepdims=True)
    sums_ref[1:2, :] = jnp.sum(dlog * (-step * rate), axis=0, keepdims=True)
    sums_ref[2:3, :] = total(gxs)[0:1, :]
    sums_ref[3:8, :] = jnp.zeros((5, LANES), F32)


def conv_back_kernel(
    own_ref, ret_ref, kept_ref, cw_ref, heads_ref, grad_ref, rim_ref, message_ref, z_scr, sum_scr
):
    tokens = own_ref.shape[0]
    taps = cw_ref.shape[0]
    pre = kept_ref[HALO + tokens :, :]
    sig = jax.nn.sigmoid(pre)
    dconv = (own_ref[...] + ret_ref[0:tokens, :].astype(F32)) * sig * (1.0 + pre * (1.0 - sig))
    z_scr[...] = jnp.zeros_like(z_scr)
    z_scr[HALO : HALO + tokens, :] = dconv
    grad = cw_ref[0:1, :] * z_scr[taps - 1 : taps - 1 + tokens + HALO, :]
    for k in range(1, taps):
        grad = grad + cw_ref[k : k + 1, :] * z_scr[taps - 1 - k : taps - 1 - k + tokens + HALO, :]
    grad_ref[...] = grad[HALO:, :]
    rim_ref[...] = grad[HALO - 8 : HALO, :]
    first = HALO - taps + 1
    sum_scr[...] = jnp.zeros_like(sum_scr)
    for k in range(taps):
        sum_scr[k : k + 1, :] = jnp.sum(
            dconv * kept_ref[first + k : first + k + tokens, :], axis=0, keepdims=True
        )
    sum_scr[taps : taps + 1, :] = jnp.sum(dconv, axis=0, keepdims=True)
    sum_scr[5:8, aligned(side() * LANES, LANES)] = heads_ref[0:3, :]
    small = split(sum_scr[...])
    message_ref[0 : tokens + HALO, :] = grad.astype(BF16)
    message_ref[tokens + HALO :, :] = small


def pack_kernel(layer_ref, halo_ref, keep_ref, send_ref, sems):
    half, _, rows = keep_ref.shape
    pairs = []
    for k in range(2 * half):
        out = keep_ref.at[k] if k < half else send_ref.at[k - half]
        at = peer_columns(k, rows)
        pairs.append((halo_ref.at[:, at], out.at[0:HALO, :]))
        pairs.append((layer_ref.at[:, at], out.at[HALO:, :]))
    for copy in copy_all(pairs, sems):
        copy.wait()


def relay_kernel(picks, *refs):
    out_ref = refs[-1]
    for j, (ref, at) in enumerate(picks):
        out_ref[j] = refs[ref][at]


def turn_kernel(picks, *refs):
    out_ref = refs[-1]
    parts = [refs[ref].at[at] for ref, at in picks]
    tokens = parts[0].shape[0] - HALO
    for k, part in enumerate(parts):
        out_ref[:, k * tokens : (k + 1) * tokens] = part[HALO:, :].T
    halos = jnp.concatenate([part[0:HALO, :] for part in parts], 0)
    out_ref[:, len(parts) * tokens :] = halos.T


def weight_kernel(count, left_ref, *refs):
    rights, out_ref = refs[:count], refs[count]
    tokens = (left_ref.shape[1] // count) - HALO
    right = jnp.concatenate(
        [a[HALO : HALO + tokens, :] for a in rights] + [a[0:HALO, :] for a in rights], 0
    )
    at = tokens + HALO
    both = jnp.zeros((16, right.shape[1]), F32)
    for a in rights:
        both += a[at : at + 16, :].astype(F32)
    small = split(both[0:8, :] + both[8:16, :])
    chunk = out_ref.shape[1] - 16
    for k in range(out_ref.shape[0]):
        term = dot(left_ref[k * chunk : (k + 1) * chunk, :], right)
        out_ref[k, 0:chunk, :] = term.astype(BF16)
        out_ref[k, chunk:, :] = small


def reduce_kernel(heads, terms_ref, total_ref, cw_ref, cb_ref, *head_refs):
    chunk = total_ref.shape[1]
    total = terms_ref[0].astype(F32)
    for k in range(1, terms_ref.shape[0]):
        total = total + terms_ref[k].astype(F32)
    for k in range(total_ref.shape[0]):
        total_ref[k] = total[0:chunk].astype(BF16)
    small = total[chunk : chunk + 8] + total[chunk + 8 :]
    taps = cw_ref.shape[0]
    cw_ref[...] = small[0:taps, :]
    cb_ref[...] = small[taps : taps + 1, :]
    for i, ref in enumerate(head_refs):
        row = small[5 + i : 6 + i, :]
        ref[:, :heads] = row[:, :heads] + row[:, heads : 2 * heads]
        row = row[:, LANES:]
        ref[:, heads:] = row[:, :heads] + row[:, heads : 2 * heads]


def place_rows_kernel(parts_ref, out_ref):
    chunk = parts_ref.shape[1]
    for k in range(parts_ref.shape[0]):
        out_ref[k * chunk : (k + 1) * chunk, :] = parts_ref[k].astype(F32)


def tokens_kernel(count, *refs):
    pieces = refs[:count]
    grad_ref, rim_ref, out_ref, w_scr, sems = refs[count:]
    copies = copy_all([(pieces[k], w_scr.at[k]) for k in range(count)], sems)
    tail = rim_ref.shape[0]
    own = grad_ref[...]
    g = jnp.concatenate([own[:-tail], own[-tail:] + rim_ref[...]], 0).astype(BF16)
    rows = pieces[0].shape[0]
    for k in range(count):
        copies[k].wait()
        out_ref[:, peer_columns(k, rows)] = dot(g, w_scr[k], NT).astype(BF16)


def join_kernel(*refs):
    own_ref, back_ref = refs[2:4]
    backs = refs[4 : 5 + GROUPS]
    y_ref, dx_ref, raw_ref, sems = refs[5 + GROUPS :]
    r = side()
    at = (1 - r) * (y_ref.shape[1] // 2)
    pairs = []
    for i in range(GROUPS):
        y, dx = (backs[0], backs[1]) if i == 0 else (backs[i + 1].at[0], backs[i + 1].at[1])
        columns = aligned(at, y.shape[1])
        at += y.shape[1]
        pairs.append((y, y_ref.at[:, columns]))
        pairs.append((dx, dx_ref.at[:, columns]))
    copies = copy_all(pairs, sems)
    heads = own_ref.shape[0]
    raw_ref[pl.ds(pl.multiple_of(r * heads, 8), heads), :] = own_ref[...]
    back = back_ref[back_ref.shape[0] - heads :, :].astype(F32)
    raw_ref[pl.ds(pl.multiple_of((1 - r) * heads, 8), heads), :] = back[:, :LANES] + back[:, LANES:]
    for copy in copies:
        copy.wait()


def pinned(x):
    return pltpu.with_memory_space_constraint(x, pltpu.HBM)


def toggled(x, axis, bits):
    size = lax.axis_size(axis)
    return lax.ppermute(x, axis, [(i, i ^ bits) for i in range(size)])


def exchanged(x, axis):
    return lax.all_to_all(x, axis, 0, 0)


def after(x, *others):
    return lax.optimization_barrier((x, *others))[0]


def body(layer_in, w_bc, conv_w, conv_b, ssm_in, dt_raw, dt_bias, a_log, skip_scale, grad_out):
    ctx, fsdp = lax.axis_size("ctx"), lax.axis_size("fsdp")
    layer, x, g, dt = layer_in[0], ssm_in[0], grad_out[0], dt_raw[0].T
    tokens, width = x.shape
    total_heads = dt_bias.shape[0]
    heads = total_heads // 2
    half = width // 2
    counts = [heads // part for part in PARTS]
    starts = [sum(counts[:i]) for i in range(GROUPS)]
    widths = [half // part for part in PARTS]
    ats = [sum(widths[:i]) for i in range(GROUPS)]
    state = w_bc.shape[1] // 2
    taps = conv_w.shape[0]
    rows = w_bc.shape[0]
    chunk_rows = rows // ctx
    pairs = ctx // 2
    hops = pairs - 1
    square = shape((tokens, LANES), F32)
    flats = [shape((tokens, a), BF16) for a in widths]
    more = shape((tokens, half - widths[0]), BF16)
    turned = shape((heads, tokens), F32)
    both_bc = [shape((tokens, 2 * state), F32)] * 2

    dt_back = toggled(dt, "ctx", 1)
    halo_send, *swaps = call(
        swap_kernel, "swap",
        [shape((HALO, layer.shape[1]), BF16), shape((tokens, 2 * widths[0]), BF16), more, more],
        (),
        hbm=(pinned(layer), pinned(x), pinned(g)), scratch=[pltpu.SemaphoreType.DMA((5,))],
    )
    halo = lax.ppermute(halo_send, "ctx", [(i, i + 1) for i in range(ctx - 1)])
    swapped_first = toggled(after(swaps[0], dt_back), "ctx", 1)
    swapped_x = toggled(after(swaps[1], halo), "ctx", 1)

    step, cum, cumt, grow, endw, sig, rate = call(
        vectors_kernel, "vectors", [square] * 6 + [shape((8, LANES), F32)], (), dt, dt_back,
        dt_bias[None, :], a_log[None, :],
        scratch=[pltpu.VMEM((tokens, tokens), F32), pltpu.VMEM((8, LANES), F32)],
    )

    def source(slot, i):
        if slot == 0:
            return (ats[i], half), (ats[i], half), x, g
        if i == 0:
            return (0, 0), (widths[0], 0), swapped_first, swapped_first
        at = (ats[i] - ats[1], 0)
        return at, at, swapped_x, swapped_g

    def scale(slot, i):
        x_at, g_at, xa, ga = source(slot, i)
        return call(
            functools.partial(scale_kernel, counts[i], slot * heads + starts[i], x_at, g_at), "scale",
            [flats[i]] * 2, (), xa, ga, step, grow, endw,
        )

    scaled = {(0, i): scale(0, i) for i in range(GROUPS)}
    scaled[1, 0] = scale(1, 0)
    parts = shape((fsdp // 2, tokens + HALO, rows), BF16)
    packs = call(
        pack_kernel, "pack", [parts, parts], (), hbm=(pinned(layer), halo),
        scratch=[pltpu.SemaphoreType.DMA((2 * fsdp,))],
    )

    pieces = {0: w_bc}
    bit = fsdp // 2
    while bit:
        for k in list(pieces):
            piece = pieces[k]
            if k:
                piece = after(piece, halo, scaled[1, 0][0], *[scaled[0, i][0] for i in range(GROUPS)])
            pieces[k | bit] = toggled(piece, "fsdp", bit)
        bit //= 2
    pieces = [pieces[k] for k in range(fsdp)]
    near = pieces[: fsdp // 2]

    def landing(count):
        return [
            pltpu.VMEM(layer.shape, BF16),
            pltpu.VMEM((count, *w_bc.shape), BF16),
            pltpu.SemaphoreType.DMA((1 + count,)),
        ]

    early = call(
        functools.partial(early_kernel, len(near)), "project_early",
        shape((tokens, 2 * state), F32), (), hbm=(pinned(layer), *near), scratch=landing(len(near)),
    )
    layer_scr, w_scr, sems = landing(fsdp)
    kept, bc = call(
        functools.partial(project_kernel, len(near), fsdp), "project",
        [
            shape((2 * tokens + HALO, 2 * state), F32),
            shape((tokens, 2 * state), BF16),
        ],
        (), halo, early, conv_w, conv_b[None, :], hbm=(pinned(layer), *pieces),
        scratch=[layer_scr, w_scr, pltpu.VMEM((tokens + HALO, 2 * state), F32), sems],
    )
    bcs = [bc, toggled(bc, "ctx", 1)]
    def within(slot, i, *earlier):
        x_at, g_at, xa, ga = source(slot, i)
        return call(
            functools.partial(
                inside_kernel, counts[i], slot * heads + starts[i], starts[i], heads, x_at, g_at
            ),
            "inside",
            [shape((tokens, widths[i]), F32)] * 2 + [shape((tokens, tokens), F32), square, square]
            + [shape((8, LANES), F32)],
            (skip_scale,), xa, ga, after(bcs[slot], *earlier), step, cum, cumt,
        )

    inside = {(0, 0): within(0, 0)}
    swapped_g = toggled(after(swaps[2], bcs[1], inside[0, 0][2]), "ctx", 1)
    order = [(slot, i) for slot in range(2) for i in range(GROUPS)]
    states, received, earlier = [], [], [inside[0, 0][2]]
    for i in range(GROUPS):
        lanes = (starts[i], heads + starts[i])
        if i:
            scaled[1, i] = scale(1, i)
        wide = shape((state, widths[i]), BF16)
        first, p, q, s_first, d_second, decays = call(
            functools.partial(states_kernel, counts[i], lanes), "states",
            [wide] * 5 + [shape((8, widths[i]), F32)],
            (), *bcs, *scaled[0, i], *scaled[1, i], after(grow, *earlier),
            scratch=[pltpu.VMEM((2, state, widths[i]), F32)] * 2
            + [pltpu.VMEM((2, 1, widths[i]), F32)],
        )
        states.append((decays, p, s_first, d_second, q))
        received.append([first])
        earlier = [first]
        if i == 0:
            for key in order[1:GROUPS]:
                inside[key] = within(*key, first)
                earlier.append(inside[key][2])
            earlier.append(packs[0])
    waiting = order[GROUPS:]
    for hop in range(hops):
        moves = [(hop, hop + 1), (pairs - 1 - hop, pairs - 2 - hop)]
        moves = [(2 * a + i, 2 * b + i) for a, b in moves for i in range(2)]
        for i in range(GROUPS):
            value = received[i][-1]
            if hop:
                decays, p, _, _, q = states[i]
                value = call(
                    functools.partial(hop_kernel, hop), "hop", shape(value.shape, BF16), (),
                    after(value, *earlier), p, q, decays,
                )
                earlier = [value]
                if waiting and i == 0:
                    key = waiting.pop(0)
                    inside[key] = within(*key, *earlier)
                    earlier = [inside[key][2]]
            received[i].append(lax.ppermute(value, "ctx", moves))
    for key in waiting:
        inside[key] = within(*key, *earlier)

    arrays = [packs[0]]
    at = {(0, k): (0, k) for k in range(fsdp // 2)}
    message, bit = packs[1], fsdp // 2
    sent = [(0, k) for k in range(bit, fsdp)]
    while bit:
        arrays.append(toggled(message, "fsdp", bit))
        for j, (source_bits, owner_bits) in enumerate(sent):
            at[source_bits ^ bit, owner_bits ^ bit] = (len(arrays) - 1, j)
        bit //= 2
        if bit:
            sent = [key for key in sorted(at) if key[1] & bit and key[1] < 2 * bit]
            message = call(
                functools.partial(relay_kernel, [at[key] for key in sent]), "relay",
                shape((len(sent), tokens + HALO, rows), BF16), (), *arrays,
            )
    picks = [at[k, 0] for k in range(fsdp)]
    dbcs = call(inside_bc_kernel, "inside_bc", both_bc, (), *bcs, *[inside[key][2] for key in order])

    full = shape((tokens, width), BF16)
    finals, sends, us, ts, res = (), [], [], [], []
    for i in range(GROUPS):
        last = i == GROUPS - 1
        own_at, _, xa, ga = source(0, i)
        x_at, g_at, xb, gb = source(1, i)
        if i == 1:
            left = call(
                functools.partial(turn_kernel, picks), "turn",
                shape((rows, fsdp * (tokens + HALO)), BF16), (), after(arrays[0], *sends), *arrays[1:],
            )
        lanes = (starts[i], heads + starts[i])
        send_shapes = [shape((2, tokens, widths[i]), BF16)] if i else [flats[0]] * 2
        y, dx, *rest, dbc_own, dbc_other, u, t, re = call(
            functools.partial(
                across_kernel, counts[i], lanes, hops, len(finals) // 2, own_at, (x_at, g_at)
            ),
            "across",
            [full, full, *send_shapes]
            + [both_bc[0], shape((tokens, 2 * state), BF16 if last else F32)]
            + [square, square, shape((8, LANES), F32)],
            (), xa, ga, xb, gb, after(bcs[0], left) if i == 1 else bcs[0], bcs[1], *scaled[0, i],
            *scaled[1, i], step, grow, endw,
            *states[i][:4], *inside[0, i][:2], *inside[1, i][:2], *dbcs, *received[i][1:],
            hbm=finals, hbm_outs=2, aliases={0: 0, 1: 1} if finals else None,
            scratch=[pltpu.VMEM((state, widths[i]), BF16)] * 2
            + [pltpu.VMEM((2, state, widths[i]), BF16)] * 2
            + [pltpu.VMEM((2, 1, widths[i]), F32)] + [pltpu.VMEM((tokens, widths[i]), BF16)] * 2
            + [pltpu.SemaphoreType.DMA((2,))],
        )
        finals, dbcs = (y, dx), (dbc_own, dbc_other)
        sends += rest
        us.append(u)
        ts.append(t)
        res.append(re)

    raw_own, dbc_send, head_sums = call(
        steps_kernel, "steps",
        [turned, shape((tokens + heads, 2 * state), BF16), shape((8, LANES), F32)], (),
        sig, rate, step, grow, endw, *[inside[key][j] for j in (3, 4, 5) for key in order],
        *us, *ts, *res, dbcs[1],
    )
    dbc_ret = toggled(dbc_send, "ctx", 1)
    grad, rim_send, message = call(
        conv_back_kernel, "conv_back",
        [
            shape((tokens, 2 * state), F32),
            shape((8, 2 * state), F32),
            shape((tokens + HALO + 16, 2 * state), BF16),
        ],
        (), dbcs[0], dbc_ret, kept, conv_w, head_sums,
        scratch=[
            pltpu.VMEM((tokens + 2 * HALO, 2 * state), F32),
            pltpu.VMEM((8, 2 * state), F32),
        ],
    )
    rim = lax.ppermute(rim_send, "ctx", [(i + 1, i) for i in range(ctx - 1)])
    backs = [toggled(after(sends[0], dbc_ret), "ctx", 1)]

    rights = [message] + [toggled(message, "fsdp", k) for k in range(fsdp - 1, 0, -1)][::-1]
    terms = call(
        functools.partial(weight_kernel, fsdp), "weight",
        shape((ctx, chunk_rows + 16, 2 * state), BF16), (), left, after(message, *backs), *rights[1:],
    )
    backs += [toggled(after(a, dbc_ret), "ctx", 1) for a in sends[1:]]
    total, grad_cw, grad_cb, *per_head = call(
        functools.partial(reduce_kernel, heads), "reduce",
        [
            shape((ctx, chunk_rows, 2 * state), BF16),
            shape((taps, 2 * state), F32),
            shape((1, 2 * state), F32),
        ]
        + [shape((1, total_heads), F32)] * 3,
        (), after(exchanged(terms, "ctx"), rim, *backs[:-1]),
    )
    grad_weight = call(
        place_rows_kernel, "place_rows", shape((rows, 2 * state), F32), (), exchanged(total, "ctx")
    )
    grad_tokens = call(
        functools.partial(tokens_kernel, fsdp), "grad_tokens", shape((tokens, fsdp * rows), BF16),
        (), after(grad, total), rim, hbm=pieces,
        scratch=[pltpu.VMEM((fsdp, *w_bc.shape), BF16), pltpu.SemaphoreType.DMA((fsdp,))],
    )
    ssm_out, grad_values, grad_raw = call(
        join_kernel, "join", [full, full, shape((total_heads, tokens), F32)],
        (), raw_own, dbc_ret, *backs, hbm=finals, hbm_outs=2,
        aliases={0: 0, 1: 1}, scratch=[pltpu.SemaphoreType.DMA((2 * GROUPS,))],
    )
    return (
        ssm_out[None],
        grad_values[None],
        grad_tokens[None],
        grad_raw.T[None],
        grad_weight,
        grad_cw,
        grad_cb[0],
        *[a[0] for a in per_head],
    )


def solution(mesh):
    tokens = P("fsdp", "ctx", None)
    in_specs = (tokens, P("fsdp", None), P(), P(), tokens, tokens, P(), P(), P(), tokens)
    out_specs = (tokens, tokens, tokens, tokens, P("fsdp", None), P(), P(), P(), P(), P())
    return jax.shard_map(body, mesh=mesh, in_specs=in_specs, out_specs=out_specs, check_vma=False)
```

```python
import functools

import jax
import jax.numpy as jnp
from jax import lax
from jax.experimental import pallas as pl
from jax.experimental.pallas import tpu as pltpu
from jax.sharding import PartitionSpec as P

F32 = jnp.float32
BF16 = jnp.bfloat16
LANES = 128
HALO = 16
PARTS = (2, 2)
GROUPS = len(PARTS)
LIMIT = 16 * 1024 * 1024
HIGHEST = lax.Precision.HIGHEST
TN = ((0,), (0,))
NT = ((1,), (1,))


def dot(a, b, dims=((1,), (0,)), precision=None):
    return lax.dot_general(
        a, b, (dims, ((), ())), precision=precision, preferred_element_type=F32
    )


def shape(dims, dtype):
    return jax.ShapeDtypeStruct(dims, dtype)


def call(kernel, name, out_shape, smem, *operands, hbm=(), hbm_outs=0, scratch=(), aliases=None):
    single = not isinstance(out_shape, list)
    outs = [out_shape] if single else out_shape
    spaces = [pltpu.SMEM] * len(smem) + [pl.ANY] * len(hbm) + [pltpu.VMEM] * len(operands)
    out_spaces = [pltpu.HBM] * hbm_outs + [pltpu.VMEM] * (len(outs) - hbm_outs)
    result = pl.pallas_call(
        kernel,
        out_shape=outs,
        in_specs=[pl.BlockSpec(memory_space=a) for a in spaces],
        out_specs=[pl.BlockSpec(memory_space=a) for a in out_spaces],
        scratch_shapes=list(scratch),
        compiler_params=pltpu.CompilerParams(vmem_limit_bytes=LIMIT),
        input_output_aliases=aliases or {},
        name=name,
    )(*smem, *hbm, *operands)
    return result[0] if single else result


def copy_all(pairs, sems):
    copies = [pltpu.make_async_copy(a, b, sems.at[i]) for i, (a, b) in enumerate(pairs)]
    for copy in copies:
        copy.start()
    return copies


def side():
    return lax.rem(lax.axis_index("ctx"), 2)


def place():
    return lax.div(lax.axis_index("ctx"), 2)


def peer_columns(k, rows):
    return aligned((lax.axis_index("fsdp") ^ k) * rows, rows)


def aligned(at, size):
    return pl.ds(pl.multiple_of(at, LANES), size)


def triangle(n):
    rows = lax.broadcasted_iota(jnp.int32, (n, n), 0)
    cols = lax.broadcasted_iota(jnp.int32, (n, n), 1)
    return rows >= cols


def split(value):
    high = value.astype(BF16).astype(F32)
    return jnp.concatenate([high, value - high], 0).astype(BF16)


def tail_kernel(layer_ref, out_ref, sems):
    tokens = layer_ref.shape[0]
    for copy in copy_all([(layer_ref.at[tokens - HALO : tokens, :], out_ref)], sems):
        copy.wait()


def swap_kernel(x_ref, g_ref, out_ref, sems):
    width = out_ref.shape[1] // 2
    other = aligned((1 - side()) * width, width)
    pairs = [
        (x_ref.at[:, other], out_ref.at[:, :width]),
        (g_ref.at[:, other], out_ref.at[:, width:]),
    ]
    for copy in copy_all(pairs, sems):
        copy.wait()


def vectors_kernel(
    dt_ref, back_ref, bias_ref, alog_ref, step_ref, cum_ref, cumt_ref, grow_ref, endw_ref, sig_ref,
    rate_ref, turned, rows,
):
    n = back_ref.shape[1]
    heads = back_ref.shape[0] // 2
    r = side()
    mine = pl.ds(pl.multiple_of(r * heads, 8), heads)
    turned[...] = jnp.zeros_like(turned)
    turned[0:heads, :] = dt_ref[mine, :]
    turned[heads : 2 * heads, :] = back_ref[mine, :]
    rows[...] = jnp.zeros_like(rows)
    for i, ref in enumerate((bias_ref, alog_ref)):
        half = jnp.where(r == 0, ref[:, :heads], ref[:, heads:])
        rows[i : i + 1, 0:heads] = half
        rows[i : i + 1, heads : 2 * heads] = half
    raw = turned[...].T + rows[0:1, :]
    step = jnp.maximum(raw, 0.0) + jnp.log1p(jnp.exp(-jnp.abs(raw)))
    rate = jnp.exp(rows[1:2, :])
    log_decay = -step * rate
    lower = jnp.where(triangle(n), 1.0, 0.0).astype(F32)
    cum = dot(lower, log_decay, precision=HIGHEST)
    step_ref[...] = step
    cum_ref[...] = cum
    cumt_ref[...] = cum.T
    grow_ref[...] = jnp.exp(cum)
    endw_ref[...] = jnp.exp(cum[n - 1 : n, :] - cum)
    sig_ref[...] = jax.nn.sigmoid(raw)
    rate_ref[...] = jnp.broadcast_to(rate, rate_ref.shape)


def early_kernel(count, layer_ref, *refs):
    pieces = refs[:count]
    out_ref, layer_scr, w_scr, sems = refs[count:]
    copies = copy_all(
        [(layer_ref, layer_scr)] + [(pieces[k], w_scr.at[k]) for k in range(count)], sems
    )
    copies[0].wait()
    total = 0.0
    for k in range(count):
        copies[k + 1].wait()
        total += dot(layer_scr[:, peer_columns(k, w_scr.shape[1])], w_scr[k])
    out_ref[...] = total


def project_kernel(done, count, layer_ref, *refs):
    pieces = refs[:count]
    halo_ref, early_ref, cw_ref, cb_ref, kept_ref, bc_ref, layer_scr, w_scr, ext_scr, sems = refs[count:]
    copies = copy_all(
        [(layer_ref, layer_scr)] + [(pieces[k], w_scr.at[k]) for k in range(count)], sems
    )
    taps = cw_ref.shape[0]
    tokens = layer_ref.shape[0]
    copies[0].wait()
    total, rim = early_ref[...], 0.0
    for k in range(count):
        copies[k + 1].wait()
        at = peer_columns(k, w_scr.shape[1])
        rim += dot(halo_ref[:, at], w_scr[k])
        if k >= done:
            total += dot(layer_scr[:, at], w_scr[k])
    ext_scr[0:HALO, :] = rim
    ext_scr[HALO:, :] = total
    kept_ref[0 : HALO + tokens, :] = ext_scr[...]
    first = HALO - taps + 1
    pre = cb_ref[...] + cw_ref[0:1, :] * ext_scr[first : first + tokens, :]
    for k in range(1, taps):
        pre = pre + cw_ref[k : k + 1, :] * ext_scr[first + k : first + k + tokens, :]
    kept_ref[HALO + tokens :, :] = pre
    bc_ref[...] = (pre * jax.nn.sigmoid(pre)).astype(BF16)


def head_columns(at, h):
    first, more = at
    return aligned(first + side() * more + h * LANES, LANES)


def scale_kernel(heads, lane, x_at, g_at, x_ref, g_ref, step_ref, grow_ref, endw_ref, xe_ref, ge_ref):
    for h in range(heads):
        at = slice(h * LANES, (h + 1) * LANES)
        one = slice(lane + h, lane + h + 1)
        x = x_ref[:, head_columns(x_at, h)].astype(F32)
        g = g_ref[:, head_columns(g_at, h)].astype(F32)
        xe_ref[:, at] = (x * (step_ref[:, one] * endw_ref[:, one])).astype(BF16)
        ge_ref[:, at] = (g * grow_ref[:, one]).astype(BF16)


def widen(row, lane, heads):
    return jnp.concatenate(
        [jnp.broadcast_to(row[:, lane + h : lane + h + 1], (1, LANES)) for h in range(heads)], 1
    )


def states_kernel(
    heads, lanes, bc0_ref, bc1_ref, xe0_ref, ge0_ref, xe1_ref, ge1_ref, grow_ref,
    first_ref, p_ref, q_ref, sf_ref, ds_ref, dec_ref, s_scr, d_scr, dec_scr,
):
    n = grow_ref.shape[0]
    r = side()
    for slot, (bc_ref, xe_ref, ge_ref) in enumerate(
        ((bc0_ref, xe0_ref, ge0_ref), (bc1_ref, xe1_ref, ge1_ref))
    ):
        s_scr[slot] = dot(bc_ref[:, :LANES], xe_ref[...], TN)
        d_scr[slot] = dot(bc_ref[:, LANES:], ge_ref[...], TN)
        dec_scr[slot] = widen(grow_ref[n - 1 : n, :], lanes[slot], heads)
    dec_first, dec_second = dec_scr[r], dec_scr[1 - r]
    s_first, d_second = s_scr[r], d_scr[1 - r]
    sf_ref[...] = s_first.astype(BF16)
    ds_ref[...] = d_second.astype(BF16)
    p = (dec_second * s_first + s_scr[1 - r]).astype(BF16)
    q = (dec_first * d_second + d_scr[r]).astype(BF16)
    p_ref[...] = p
    q_ref[...] = q

    @pl.when(place() == 0)
    def _():
        first_ref[...] = p

    @pl.when(place() != 0)
    def _():
        first_ref[...] = q

    dec_ref[0:1, :] = dec_first * dec_second
    dec_ref[1:2, :] = dec_first
    dec_ref[2:3, :] = dec_second
    dec_ref[3:8, :] = jnp.zeros((5, dec_first.shape[1]), F32)


def hop_kernel(hop, received_ref, p_ref, q_ref, dec_ref, out_ref):
    carried = dec_ref[0:1, :] * received_ref[...].astype(F32)

    @pl.when(place() == hop)
    def _():
        out_ref[...] = (carried + p_ref[...].astype(F32)).astype(BF16)

    @pl.when(place() != hop)
    def _():
        out_ref[...] = (carried + q_ref[...].astype(F32)).astype(BF16)


def inside_kernel(
    heads, lane, skip_at, all_heads, x_at, g_at, skip_ref, x_ref, g_ref, bc_ref, step_ref, cum_ref,
    cumt_ref, y_ref, dx_ref, dscores_ref, gy_ref, ds_ref, gx_ref,
):
    n = step_ref.shape[0]
    mask = triangle(n)
    scores = jnp.where(mask, dot(bc_ref[:, LANES:], bc_ref[:, :LANES], NT), 0.0)
    gy_ref[...] = jnp.zeros_like(gy_ref)
    ds_ref[...] = jnp.zeros_like(ds_ref)
    gx_ref[...] = jnp.zeros_like(gx_ref)
    dscores = jnp.zeros((n, n), F32)
    for h in range(heads):
        at = slice(h * LANES, (h + 1) * LANES)
        one = slice(lane + h, lane + h + 1)
        step = step_ref[:, one]
        gap = cum_ref[:, one] - cumt_ref[one, :]
        decay = jnp.exp(jnp.where(mask, gap, 0.0))
        mixing = (scores * decay).astype(BF16)
        x = x_ref[:, head_columns(x_at, h)].astype(F32)
        g = g_ref[:, head_columns(g_at, h)]
        gf = g.astype(F32)
        xs = (x * step).astype(BF16)
        skip = skip_ref[side() * all_heads + skip_at + h]
        y = dot(mixing, xs)
        dxs = dot(mixing, g, TN)
        dscores += dot(g, xs, NT) * decay
        y_ref[:, at] = y + skip * x
        dx_ref[:, at] = dxs * step + skip * gf
        gy_ref[:, one] = jnp.sum(gf * y, axis=1, keepdims=True)
        ds_ref[:, one] = jnp.sum(x * dxs, axis=1, keepdims=True)
        gx_ref[0:1, one] = jnp.sum(jnp.sum(gf * x, axis=0, keepdims=True), axis=1, keepdims=True)
    dscores_ref[...] = jnp.where(mask, dscores, 0.0)


def inside_bc_kernel(bc0_ref, bc1_ref, *refs):
    parts, outs = refs[: 2 * GROUPS], refs[2 * GROUPS :]
    for slot, bc_ref in enumerate((bc0_ref, bc1_ref)):
        total = parts[slot * GROUPS][...]
        for i in range(1, GROUPS):
            total = total + parts[slot * GROUPS + i][...]
        ds = total.astype(BF16)
        outs[slot][:, :LANES] = dot(ds, bc_ref[:, LANES:], TN)
        outs[slot][:, LANES:] = dot(ds, bc_ref[:, :LANES])


def across_kernel(heads, lanes, hops, filled, own_at, columns, *refs):
    refs = refs[2 * filled :]
    across_block(heads, lanes, hops, own_at, columns, *refs)


def across_block(
    heads, lanes, hops, own_at, columns, x0_ref, g0_ref, x1_ref, g1_ref, bc0_ref, bc1_ref, xe0_ref,
    ge0_ref, xe1_ref, ge1_ref, step_ref, grow_ref, endw_ref, dec_ref, p_ref, sf_ref, ds_ref,
    y0_ref, dx0_ref, y1_ref, dx1_ref, dbc0_ref, dbc1_ref, *refs
):
    received = refs[:hops]
    (
        yf_ref, dxf_ref, ys_ref, dxs_ref, dbco0_ref, dbco1_ref, u_ref, t_ref, re_ref,
        e_in, r_in, e_scr, r_scr, n_scr, yo_ref, dxo_ref, sems,
    ) = refs[hops:]
    r, pos = side(), place()
    width = yo_ref.shape[1]
    e_in[...] = jnp.zeros_like(e_in)
    r_in[...] = jnp.zeros_like(r_in)
    for k in range(hops):

        @pl.when(pos - 1 == k)
        def _(k=k):
            e_in[...] = received[k][...]

        @pl.when(hops - 1 - pos == k)
        def _(k=k):
            r_in[...] = received[k][...]

    dec_pair, dec_first, dec_second = dec_ref[0:1, :], dec_ref[1:2, :], dec_ref[2:3, :]
    entering = e_in[...].astype(F32)
    later = r_in[...].astype(F32)
    middle = dec_first * entering + sf_ref[...].astype(F32)
    leaving = dec_pair * entering + p_ref[...].astype(F32)
    earlier = dec_second * later + ds_ref[...].astype(F32)
    e_scr[r] = e_in[...]
    e_scr[1 - r] = middle.astype(BF16)
    r_scr[1 - r] = r_in[...]
    r_scr[r] = earlier.astype(BF16)
    n_scr[1 - r] = jnp.sum(later * leaving, axis=0, keepdims=True)
    n_scr[r] = jnp.sum(earlier * middle, axis=0, keepdims=True)

    u_ref[...] = jnp.zeros_like(u_ref)
    t_ref[...] = jnp.zeros_like(t_ref)
    re_ref[...] = jnp.zeros_like(re_ref)
    for slot, (bc_ref, xe_ref, ge_ref, y_ref, dx_ref, dbc_ref, dbco_ref) in enumerate(
        (
            (bc0_ref, xe0_ref, ge0_ref, y0_ref, dx0_ref, dbc0_ref, dbco0_ref),
            (bc1_ref, xe1_ref, ge1_ref, y1_ref, dx1_ref, dbc1_ref, dbco1_ref),
        )
    ):
        e_all = e_scr[slot]
        r_all = r_scr[slot]
        db = dbc_ref[:, :LANES] + dot(xe_ref[...], r_all, NT)
        dc = dbc_ref[:, LANES:] + dot(ge_ref[...], e_all, NT)
        dbco_ref[:, :LANES] = db.astype(dbco_ref.dtype)
        dbco_ref[:, LANES:] = dc.astype(dbco_ref.dtype)
        ce_all = dot(bc_ref[:, LANES:], e_all)
        br_all = dot(bc_ref[:, :LANES], r_all)
        for h in range(heads):
            at = slice(h * LANES, (h + 1) * LANES)
            lane = lanes[slot] + h
            one = slice(lane, lane + 1)
            ce, br = ce_all[:, at], br_all[:, at]
            y = (y_ref[:, at] + grow_ref[:, one] * ce).astype(BF16)
            dx = (dx_ref[:, at] + (step_ref[:, one] * endw_ref[:, one]) * br).astype(BF16)
            if slot == 0:
                yo_ref[:, at] = y
                dxo_ref[:, at] = dx
                x = x0_ref[:, head_columns(own_at, h)].astype(F32)
                g = g0_ref[:, head_columns(own_at, h)].astype(F32)
            else:
                ys_ref[:, at] = y
                dxs_ref[:, at] = dx
                x = x1_ref[:, head_columns(columns[0], h)].astype(F32)
                g = g1_ref[:, head_columns(columns[1], h)].astype(F32)
            u_ref[:, one] = jnp.sum(g * ce, axis=1, keepdims=True)
            t_ref[:, one] = jnp.sum(x * br, axis=1, keepdims=True)
            re_ref[0:1, one] = jnp.sum(n_scr[slot][:, at], axis=1, keepdims=True)
        if slot == 0:
            final = aligned(own_at[0] + r * own_at[1], width)
            pairs = [(yo_ref, yf_ref.at[:, final]), (dxo_ref, dxf_ref.at[:, final])]
            copies = copy_all(pairs, sems)
    for copy in copies:
        copy.wait()


def steps_kernel(sig_ref, rate_ref, step_ref, grow_ref, endw_ref, *refs):
    count = 2 * GROUPS
    gys, dss, gxs = refs[:count], refs[count : 2 * count], refs[2 * count : 3 * count]
    refs = refs[3 * count :]
    us, ts, res = refs[:GROUPS], refs[GROUPS : 2 * GROUPS], refs[2 * GROUPS : 3 * GROUPS]
    dbc_ref, own_ref, send_ref, sums_ref = refs[3 * GROUPS :]

    def total(parts):
        value = parts[0][...]
        for a in parts[1:]:
            value = value + a[...]
        return value

    n = step_ref.shape[0]
    step = step_ref[...]
    ds = total(dss) + endw_ref[...] * total(ts)
    gy = total(gys) + grow_ref[...] * total(us)
    rate = rate_ref[0:1, :]
    last = lax.broadcasted_iota(jnp.int32, (n, LANES), 0) == n - 1
    dcum = gy - step * ds + jnp.where(last, total(res)[0:1, :], 0.0)
    lower = jnp.where(triangle(n), 1.0, 0.0).astype(F32)
    dlog = dot(lower, dcum, TN, precision=HIGHEST)
    draw = (ds - rate * dlog) * sig_ref[...]
    turned = draw.T
    heads = own_ref.shape[0]
    own_ref[...] = turned[:heads, :]
    both = split(turned[heads : 2 * heads, :])
    send_ref[0:n, :] = dbc_ref[...]
    send_ref[n:, :LANES] = both[:heads]
    send_ref[n:, LANES:] = both[heads:]
    sums_ref[0:1, :] = jnp.sum(draw, axis=0, keepdims=True)
    sums_ref[1:2, :] = jnp.sum(dlog * (-step * rate), axis=0, keepdims=True)
    sums_ref[2:3, :] = total(gxs)[0:1, :]
    sums_ref[3:8, :] = jnp.zeros((5, LANES), F32)


def conv_back_kernel(
    own_ref, ret_ref, kept_ref, cw_ref, heads_ref, grad_ref, rim_ref, message_ref, z_scr, sum_scr
):
    tokens = own_ref.shape[0]
    taps = cw_ref.shape[0]
    pre = kept_ref[HALO + tokens :, :]
    sig = jax.nn.sigmoid(pre)
    dconv = (own_ref[...] + ret_ref[0:tokens, :].astype(F32)) * sig * (1.0 + pre * (1.0 - sig))
    z_scr[...] = jnp.zeros_like(z_scr)
    z_scr[HALO : HALO + tokens, :] = dconv
    grad = cw_ref[0:1, :] * z_scr[taps - 1 : taps - 1 + tokens + HALO, :]
    for k in range(1, taps):
        grad = grad + cw_ref[k : k + 1, :] * z_scr[taps - 1 - k : taps - 1 - k + tokens + HALO, :]
    grad_ref[...] = grad[HALO:, :]
    rim_ref[...] = grad[HALO - 8 : HALO, :]
    first = HALO - taps + 1
    sum_scr[...] = jnp.zeros_like(sum_scr)
    for k in range(taps):
        sum_scr[k : k + 1, :] = jnp.sum(
            dconv * kept_ref[first + k : first + k + tokens, :], axis=0, keepdims=True
        )
    sum_scr[taps : taps + 1, :] = jnp.sum(dconv, axis=0, keepdims=True)
    sum_scr[5:8, aligned(side() * LANES, LANES)] = heads_ref[0:3, :]
    small = split(sum_scr[...])
    message_ref[0 : tokens + HALO, :] = grad.astype(BF16)
    message_ref[tokens + HALO :, :] = small


def pack_kernel(layer_ref, halo_ref, keep_ref, send_ref, sems):
    half, _, rows = keep_ref.shape
    pairs = []
    for k in range(2 * half):
        out = keep_ref.at[k] if k < half else send_ref.at[k - half]
        at = peer_columns(k, rows)
        pairs.append((halo_ref.at[:, at], out.at[0:HALO, :]))
        pairs.append((layer_ref.at[:, at], out.at[HALO:, :]))
    for copy in copy_all(pairs, sems):
        copy.wait()


def relay_kernel(picks, *refs):
    out_ref = refs[-1]
    for j, (ref, at) in enumerate(picks):
        out_ref[j] = refs[ref][at]


def turn_kernel(picks, *refs):
    out_ref = refs[-1]
    parts = [refs[ref].at[at] for ref, at in picks]
    tokens = parts[0].shape[0] - HALO
    for k, part in enumerate(parts):
        out_ref[:, k * tokens : (k + 1) * tokens] = part[HALO:, :].T
    halos = jnp.concatenate([part[0:HALO, :] for part in parts], 0)
    out_ref[:, len(parts) * tokens :] = halos.T


def weight_kernel(count, left_ref, *refs):
    rights, out_ref = refs[:count], refs[count]
    tokens = (left_ref.shape[1] // count) - HALO
    right = jnp.concatenate(
        [a[HALO : HALO + tokens, :] for a in rights] + [a[0:HALO, :] for a in rights], 0
    )
    at = tokens + HALO
    both = jnp.zeros((16, right.shape[1]), F32)
    for a in rights:
        both += a[at : at + 16, :].astype(F32)
    small = split(both[0:8, :] + both[8:16, :])
    chunk = out_ref.shape[1] - 16
    for k in range(out_ref.shape[0]):
        term = dot(left_ref[k * chunk : (k + 1) * chunk, :], right)
        out_ref[k, 0:chunk, :] = term.astype(BF16)
        out_ref[k, chunk:, :] = small


def reduce_kernel(heads, terms_ref, total_ref, cw_ref, cb_ref, *head_refs):
    chunk = total_ref.shape[1]
    total = terms_ref[0].astype(F32)
    for k in range(1, terms_ref.shape[0]):
        total = total + terms_ref[k].astype(F32)
    for k in range(total_ref.shape[0]):
        total_ref[k] = total[0:chunk].astype(BF16)
    small = total[chunk : chunk + 8] + total[chunk + 8 :]
    taps = cw_ref.shape[0]
    cw_ref[...] = small[0:taps, :]
    cb_ref[...] = small[taps : taps + 1, :]
    for i, ref in enumerate(head_refs):
        row = small[5 + i : 6 + i, :]
        ref[:, :heads] = row[:, :heads] + row[:, heads : 2 * heads]
        row = row[:, LANES:]
        ref[:, heads:] = row[:, :heads] + row[:, heads : 2 * heads]


def place_rows_kernel(parts_ref, out_ref):
    chunk = parts_ref.shape[1]
    for k in range(parts_ref.shape[0]):
        out_ref[k * chunk : (k + 1) * chunk, :] = parts_ref[k].astype(F32)


def tokens_kernel(count, *refs):
    pieces = refs[:count]
    grad_ref, rim_ref, out_ref, w_scr, sems = refs[count:]
    copies = copy_all([(pieces[k], w_scr.at[k]) for k in range(count)], sems)
    tail = rim_ref.shape[0]
    own = grad_ref[...]
    g = jnp.concatenate([own[:-tail], own[-tail:] + rim_ref[...]], 0).astype(BF16)
    rows = pieces[0].shape[0]
    for k in range(count):
        copies[k].wait()
        out_ref[:, peer_columns(k, rows)] = dot(g, w_scr[k], NT).astype(BF16)


def join_kernel(*refs):
    own_ref, back_ref = refs[2:4]
    backs = refs[4 : 4 + 2 * GROUPS]
    y_ref, dx_ref, raw_ref, sems = refs[4 + 2 * GROUPS :]
    r = side()
    at = (1 - r) * (y_ref.shape[1] // 2)
    pairs = []
    for i in range(GROUPS):
        y, dx = backs[2 * i : 2 * i + 2]
        columns = aligned(at, y.shape[1])
        at += y.shape[1]
        pairs.append((y, y_ref.at[:, columns]))
        pairs.append((dx, dx_ref.at[:, columns]))
    copies = copy_all(pairs, sems)
    heads = own_ref.shape[0]
    raw_ref[pl.ds(pl.multiple_of(r * heads, 8), heads), :] = own_ref[...]
    back = back_ref[back_ref.shape[0] - heads :, :].astype(F32)
    raw_ref[pl.ds(pl.multiple_of((1 - r) * heads, 8), heads), :] = back[:, :LANES] + back[:, LANES:]
    for copy in copies:
        copy.wait()


def pinned(x):
    return pltpu.with_memory_space_constraint(x, pltpu.HBM)


def toggled(x, axis, bits):
    size = lax.axis_size(axis)
    return lax.ppermute(x, axis, [(i, i ^ bits) for i in range(size)])


def exchanged(x, axis):
    return lax.all_to_all(x, axis, 0, 0)


def after(x, *others):
    return lax.optimization_barrier((x, *others))[0]


def body(layer_in, w_bc, conv_w, conv_b, ssm_in, dt_raw, dt_bias, a_log, skip_scale, grad_out):
    ctx, fsdp = lax.axis_size("ctx"), lax.axis_size("fsdp")
    layer, x, g, dt = layer_in[0], ssm_in[0], grad_out[0], dt_raw[0].T
    tokens, width = x.shape
    total_heads = dt_bias.shape[0]
    heads = total_heads // 2
    half = width // 2
    counts = [heads // part for part in PARTS]
    starts = [sum(counts[:i]) for i in range(GROUPS)]
    widths = [half // part for part in PARTS]
    ats = [sum(widths[:i]) for i in range(GROUPS)]
    state = w_bc.shape[1] // 2
    taps = conv_w.shape[0]
    rows = w_bc.shape[0]
    chunk_rows = rows // ctx
    pairs = ctx // 2
    hops = pairs - 1
    square = shape((tokens, LANES), F32)
    flats = [shape((tokens, a), BF16) for a in widths]
    turned = shape((heads, tokens), F32)
    both_bc = [shape((tokens, 2 * state), F32)] * 2

    tail = call(
        tail_kernel, "tail", shape((HALO, layer.shape[1]), BF16), (), hbm=(pinned(layer),),
        scratch=[pltpu.SemaphoreType.DMA((1,))],
    )
    halo = lax.ppermute(tail, "ctx", [(i, i + 1) for i in range(ctx - 1)])
    dt_back = toggled(dt, "ctx", 1)
    swap = call(
        swap_kernel, "swap", shape((tokens, width), BF16), (), hbm=(pinned(x), pinned(g)),
        scratch=[pltpu.SemaphoreType.DMA((2,))],
    )
    swapped = toggled(after(swap, halo, dt_back), "ctx", 1)

    step, cum, cumt, grow, endw, sig, rate = call(
        vectors_kernel, "vectors", [square] * 6 + [shape((8, LANES), F32)], (), dt, dt_back,
        dt_bias[None, :], a_log[None, :],
        scratch=[pltpu.VMEM((tokens, tokens), F32), pltpu.VMEM((8, LANES), F32)],
    )

    def source(slot, i):
        if slot == 0:
            return (ats[i], half), (ats[i], half), x, g
        return (ats[i], 0), (half + ats[i], 0), swapped, swapped

    def scale(slot, i):
        x_at, g_at, xa, ga = source(slot, i)
        return call(
            functools.partial(scale_kernel, counts[i], slot * heads + starts[i], x_at, g_at), "scale",
            [flats[i]] * 2, (), xa, ga, step, grow, endw,
        )

    scaled = {(0, i): scale(0, i) for i in range(GROUPS)}
    def landing(count):
        return [
            pltpu.VMEM(layer.shape, BF16),
            pltpu.VMEM((count, *w_bc.shape), BF16),
            pltpu.SemaphoreType.DMA((1 + count,)),
        ]

    parts = shape((fsdp // 2, tokens + HALO, rows), BF16)
    packs = call(
        pack_kernel, "pack", [parts, parts], (), hbm=(pinned(layer), halo),
        scratch=[pltpu.SemaphoreType.DMA((2 * fsdp,))],
    )
    far_bit = fsdp // 2
    far = [toggled(w_bc, "fsdp", far_bit)]
    near = [w_bc]
    while len(near) < far_bit:
        near += [toggled(a, "fsdp", len(near)) for a in near]
    early = call(
        functools.partial(early_kernel, len(near)), "project_early",
        shape((tokens, 2 * state), F32), (), hbm=(pinned(layer), after(near[0], packs[0]), *near[1:]),
        scratch=landing(len(near)),
    )
    far[0] = after(far[0], early, *[scaled[0, i][0] for i in range(GROUPS)])
    while len(far) < far_bit:
        far += [toggled(a, "fsdp", len(far)) for a in far]
    pieces = near + far
    layer_scr, w_scr, sems = landing(fsdp)
    kept, bc = call(
        functools.partial(project_kernel, len(near), fsdp), "project",
        [
            shape((2 * tokens + HALO, 2 * state), F32),
            shape((tokens, 2 * state), BF16),
        ],
        (), halo, early, conv_w, conv_b[None, :], hbm=(pinned(layer), *pieces),
        scratch=[layer_scr, w_scr, pltpu.VMEM((tokens + HALO, 2 * state), F32), sems],
    )
    bcs = [bc, toggled(bc, "ctx", 1)]
    def within(slot, i, *earlier):
        x_at, g_at, xa, ga = source(slot, i)
        return call(
            functools.partial(
                inside_kernel, counts[i], slot * heads + starts[i], starts[i], heads, x_at, g_at
            ),
            "inside",
            [shape((tokens, widths[i]), F32)] * 2 + [shape((tokens, tokens), F32), square, square]
            + [shape((8, LANES), F32)],
            (skip_scale,), xa, ga, after(bcs[slot], *earlier), step, cum, cumt,
        )

    order = [(slot, i) for slot in range(2) for i in range(GROUPS)]
    inside, states, received, earlier = {}, [], [], []
    for key in order[:GROUPS]:
        inside[key] = within(*key, *earlier)
        earlier = [inside[key][2]]
    for i in range(GROUPS):
        lanes = (starts[i], heads + starts[i])
        scaled[1, i] = scale(1, i)
        wide = shape((state, widths[i]), BF16)
        first, p, q, s_first, d_second, decays = call(
            functools.partial(states_kernel, counts[i], lanes), "states",
            [wide] * 5 + [shape((8, widths[i]), F32)],
            (), *bcs, *scaled[0, i], *scaled[1, i], after(grow, *earlier),
            scratch=[pltpu.VMEM((2, state, widths[i]), F32)] * 2
            + [pltpu.VMEM((2, 1, widths[i]), F32)],
        )
        states.append((decays, p, s_first, d_second, q))
        received.append([first])
        earlier = [first]
    for slot, i in order[GROUPS:]:
        inside[slot, i] = within(slot, i, *earlier)
        earlier = [inside[slot, i][2]]
    for hop in range(hops):
        moves = [(hop, hop + 1), (pairs - 1 - hop, pairs - 2 - hop)]
        moves = [(2 * a + i, 2 * b + i) for a, b in moves for i in range(2)]
        for i in range(GROUPS):
            value = received[i][-1]
            if hop:
                decays, p, _, _, q = states[i]
                value = call(
                    functools.partial(hop_kernel, hop), "hop", shape(value.shape, BF16), (),
                    after(value, *earlier), p, q, decays,
                )
                earlier = [value]
            received[i].append(lax.ppermute(value, "ctx", moves))
    arrays = [packs[0]]
    at = {(0, k): (0, k) for k in range(fsdp // 2)}
    message, bit = packs[1], fsdp // 2
    sent = [(0, k) for k in range(bit, fsdp)]
    while bit:
        arrays.append(toggled(message, "fsdp", bit))
        for j, (source_bits, owner_bits) in enumerate(sent):
            at[source_bits ^ bit, owner_bits ^ bit] = (len(arrays) - 1, j)
        bit //= 2
        if bit:
            sent = [key for key in sorted(at) if key[1] & bit and key[1] < 2 * bit]
            message = call(
                functools.partial(relay_kernel, [at[key] for key in sent]), "relay",
                shape((len(sent), tokens + HALO, rows), BF16), (), after(arrays[0], received[-1][0]),
                *arrays[1:],
            )
    picks = [at[k, 0] for k in range(fsdp)]
    dbcs = call(inside_bc_kernel, "inside_bc", both_bc, (), *bcs, *[inside[key][2] for key in order])

    full = shape((tokens, width), BF16)
    finals, sends, us, ts, res = (), [], [], [], []
    for i in range(GROUPS):
        last = i == GROUPS - 1
        own_at, _, xa, ga = source(0, i)
        x_at, g_at, xb, gb = source(1, i)
        if i == 1:
            left = call(
                functools.partial(turn_kernel, picks), "turn",
                shape((rows, fsdp * (tokens + HALO)), BF16), (), after(arrays[0], *sends), *arrays[1:],
            )
        lanes = (starts[i], heads + starts[i])
        y, dx, y_send, dx_send, dbc_own, dbc_other, u, t, re = call(
            functools.partial(
                across_kernel, counts[i], lanes, hops, len(finals) // 2, own_at, (x_at, g_at)
            ),
            "across",
            [full, full, flats[i], flats[i]]
            + [both_bc[0], shape((tokens, 2 * state), BF16 if last else F32)]
            + [square, square, shape((8, LANES), F32)],
            (), xa, ga, xb, gb, after(bcs[0], left) if i == 1 else bcs[0], bcs[1], *scaled[0, i],
            *scaled[1, i], step, grow, endw,
            *states[i][:4], *inside[0, i][:2], *inside[1, i][:2], *dbcs, *received[i][1:],
            hbm=finals, hbm_outs=2, aliases={0: 0, 1: 1} if finals else None,
            scratch=[pltpu.VMEM((state, widths[i]), BF16)] * 2
            + [pltpu.VMEM((2, state, widths[i]), BF16)] * 2
            + [pltpu.VMEM((2, 1, widths[i]), F32)] + [pltpu.VMEM((tokens, widths[i]), BF16)] * 2
            + [pltpu.SemaphoreType.DMA((2,))],
        )
        finals, dbcs = (y, dx), (dbc_own, dbc_other)
        sends += [y_send, dx_send]
        us.append(u)
        ts.append(t)
        res.append(re)

    raw_own, dbc_send, head_sums = call(
        steps_kernel, "steps",
        [turned, shape((tokens + heads, 2 * state), BF16), shape((8, LANES), F32)], (),
        sig, rate, step, grow, endw, *[inside[key][j] for j in (3, 4, 5) for key in order],
        *us, *ts, *res, dbcs[1],
    )
    dbc_ret = toggled(dbc_send, "ctx", 1)
    grad, rim_send, message = call(
        conv_back_kernel, "conv_back",
        [
            shape((tokens, 2 * state), F32),
            shape((8, 2 * state), F32),
            shape((tokens + HALO + 16, 2 * state), BF16),
        ],
        (), dbcs[0], dbc_ret, kept, conv_w, head_sums,
        scratch=[
            pltpu.VMEM((tokens + 2 * HALO, 2 * state), F32),
            pltpu.VMEM((8, 2 * state), F32),
        ],
    )
    rim = lax.ppermute(rim_send, "ctx", [(i + 1, i) for i in range(ctx - 1)])
    backs = [toggled(after(sends[0], dbc_ret), "ctx", 1)]

    rights = [message] + [toggled(message, "fsdp", k) for k in range(fsdp - 1, 0, -1)][::-1]
    terms = call(
        functools.partial(weight_kernel, fsdp), "weight",
        shape((ctx, chunk_rows + 16, 2 * state), BF16), (), left, after(message, *backs), *rights[1:],
    )
    backs += [toggled(after(a, terms), "ctx", 1) for a in sends[1:]]
    total, grad_cw, grad_cb, *per_head = call(
        functools.partial(reduce_kernel, heads), "reduce",
        [
            shape((ctx, chunk_rows, 2 * state), BF16),
            shape((taps, 2 * state), F32),
            shape((1, 2 * state), F32),
        ]
        + [shape((1, total_heads), F32)] * 3,
        (), after(exchanged(terms, "ctx"), rim, *backs[:-1]),
    )
    grad_weight = call(
        place_rows_kernel, "place_rows", shape((rows, 2 * state), F32), (), exchanged(total, "ctx")
    )
    grad_tokens = call(
        functools.partial(tokens_kernel, fsdp), "grad_tokens", shape((tokens, fsdp * rows), BF16),
        (), after(grad, total), rim, hbm=pieces,
        scratch=[pltpu.VMEM((fsdp, *w_bc.shape), BF16), pltpu.SemaphoreType.DMA((fsdp,))],
    )
    ssm_out, grad_values, grad_raw = call(
        join_kernel, "join", [full, full, shape((total_heads, tokens), F32)],
        (), raw_own, dbc_ret, *backs, hbm=finals, hbm_outs=2,
        aliases={0: 0, 1: 1}, scratch=[pltpu.SemaphoreType.DMA((2 * GROUPS,))],
    )
    return (
        ssm_out[None],
        grad_values[None],
        grad_tokens[None],
        grad_raw.T[None],
        grad_weight,
        grad_cw,
        grad_cb[0],
        *[a[0] for a in per_head],
    )


def solution(mesh):
    tokens = P("fsdp", "ctx", None)
    in_specs = (tokens, P("fsdp", None), P(), P(), tokens, tokens, P(), P(), P(), tokens)
    out_specs = (tokens, tokens, tokens, tokens, P("fsdp", None), P(), P(), P(), P(), P())
    return jax.shard_map(body, mesh=mesh, in_specs=in_specs, out_specs=out_specs, check_vma=False)
```

```python
import functools

import jax
import jax.numpy as jnp
from jax import lax
from jax.experimental import pallas as pl
from jax.experimental.pallas import tpu as pltpu
from jax.sharding import PartitionSpec as P

F32 = jnp.float32
BF16 = jnp.bfloat16
LANES = 128
HALO = 16
PARTS = (2, 2)
GROUPS = len(PARTS)
LIMIT = 16 * 1024 * 1024
HIGHEST = lax.Precision.HIGHEST
TN = ((0,), (0,))
NT = ((1,), (1,))


def dot(a, b, dims=((1,), (0,)), precision=None):
    return lax.dot_general(
        a, b, (dims, ((), ())), precision=precision, preferred_element_type=F32
    )


def shape(dims, dtype):
    return jax.ShapeDtypeStruct(dims, dtype)


def call(kernel, name, out_shape, smem, *operands, hbm=(), hbm_outs=0, scratch=(), aliases=None):
    single = not isinstance(out_shape, list)
    outs = [out_shape] if single else out_shape
    spaces = [pltpu.SMEM] * len(smem) + [pl.ANY] * len(hbm) + [pltpu.VMEM] * len(operands)
    out_spaces = [pltpu.HBM] * hbm_outs + [pltpu.VMEM] * (len(outs) - hbm_outs)
    result = pl.pallas_call(
        kernel,
        out_shape=outs,
        in_specs=[pl.BlockSpec(memory_space=a) for a in spaces],
        out_specs=[pl.BlockSpec(memory_space=a) for a in out_spaces],
        scratch_shapes=list(scratch),
        compiler_params=pltpu.CompilerParams(vmem_limit_bytes=LIMIT),
        input_output_aliases=aliases or {},
        name=name,
    )(*smem, *hbm, *operands)
    return result[0] if single else result


def copy_all(pairs, sems):
    copies = [pltpu.make_async_copy(a, b, sems.at[i]) for i, (a, b) in enumerate(pairs)]
    for copy in copies:
        copy.start()
    return copies


def side():
    return lax.rem(lax.axis_index("ctx"), 2)


def place():
    return lax.div(lax.axis_index("ctx"), 2)


def peer_columns(k, rows):
    return aligned((lax.axis_index("fsdp") ^ k) * rows, rows)


def aligned(at, size):
    return pl.ds(pl.multiple_of(at, LANES), size)


def triangle(n):
    rows = lax.broadcasted_iota(jnp.int32, (n, n), 0)
    cols = lax.broadcasted_iota(jnp.int32, (n, n), 1)
    return rows >= cols


def split(value):
    high = value.astype(BF16).astype(F32)
    return jnp.concatenate([high, value - high], 0).astype(BF16)


def tail_kernel(layer_ref, out_ref, sems):
    tokens = layer_ref.shape[0]
    for copy in copy_all([(layer_ref.at[tokens - HALO : tokens, :], out_ref)], sems):
        copy.wait()


def swap_kernel(x_ref, g_ref, out_ref, sems):
    width = out_ref.shape[1] // 2
    other = aligned((1 - side()) * width, width)
    pairs = [
        (x_ref.at[:, other], out_ref.at[:, :width]),
        (g_ref.at[:, other], out_ref.at[:, width:]),
    ]
    for copy in copy_all(pairs, sems):
        copy.wait()


def vectors_kernel(
    dt_ref, back_ref, bias_ref, alog_ref, step_ref, cum_ref, cumt_ref, grow_ref, endw_ref, sig_ref,
    rate_ref, turned, rows,
):
    n = back_ref.shape[1]
    heads = back_ref.shape[0] // 2
    r = side()
    mine = pl.ds(pl.multiple_of(r * heads, 8), heads)
    turned[...] = jnp.zeros_like(turned)
    turned[0:heads, :] = dt_ref[mine, :]
    turned[heads : 2 * heads, :] = back_ref[mine, :]
    rows[...] = jnp.zeros_like(rows)
    for i, ref in enumerate((bias_ref, alog_ref)):
        half = jnp.where(r == 0, ref[:, :heads], ref[:, heads:])
        rows[i : i + 1, 0:heads] = half
        rows[i : i + 1, heads : 2 * heads] = half
    raw = turned[...].T + rows[0:1, :]
    step = jnp.maximum(raw, 0.0) + jnp.log1p(jnp.exp(-jnp.abs(raw)))
    rate = jnp.exp(rows[1:2, :])
    log_decay = -step * rate
    lower = jnp.where(triangle(n), 1.0, 0.0).astype(F32)
    cum = dot(lower, log_decay, precision=HIGHEST)
    step_ref[...] = step
    cum_ref[...] = cum
    cumt_ref[...] = cum.T
    grow_ref[...] = jnp.exp(cum)
    endw_ref[...] = jnp.exp(cum[n - 1 : n, :] - cum)
    sig_ref[...] = jax.nn.sigmoid(raw)
    rate_ref[...] = jnp.broadcast_to(rate, rate_ref.shape)


def early_kernel(count, layer_ref, *refs):
    pieces = refs[:count]
    out_ref, layer_scr, w_scr, sems = refs[count:]
    copies = copy_all(
        [(layer_ref, layer_scr)] + [(pieces[k], w_scr.at[k]) for k in range(count)], sems
    )
    copies[0].wait()
    total = 0.0
    for k in range(count):
        copies[k + 1].wait()
        total += dot(layer_scr[:, peer_columns(k, w_scr.shape[1])], w_scr[k])
    out_ref[...] = total


def project_kernel(done, count, layer_ref, *refs):
    pieces = refs[:count]
    halo_ref, early_ref, cw_ref, cb_ref, kept_ref, bc_ref, layer_scr, w_scr, ext_scr, sems = refs[count:]
    copies = copy_all(
        [(layer_ref, layer_scr)] + [(pieces[k], w_scr.at[k]) for k in range(count)], sems
    )
    taps = cw_ref.shape[0]
    tokens = layer_ref.shape[0]
    copies[0].wait()
    total, rim = early_ref[...], 0.0
    for k in range(count):
        copies[k + 1].wait()
        at = peer_columns(k, w_scr.shape[1])
        rim += dot(halo_ref[:, at], w_scr[k])
        if k >= done:
            total += dot(layer_scr[:, at], w_scr[k])
    ext_scr[0:HALO, :] = rim
    ext_scr[HALO:, :] = total
    kept_ref[0 : HALO + tokens, :] = ext_scr[...]
    first = HALO - taps + 1
    pre = cb_ref[...] + cw_ref[0:1, :] * ext_scr[first : first + tokens, :]
    for k in range(1, taps):
        pre = pre + cw_ref[k : k + 1, :] * ext_scr[first + k : first + k + tokens, :]
    kept_ref[HALO + tokens :, :] = pre
    bc_ref[...] = (pre * jax.nn.sigmoid(pre)).astype(BF16)


def head_columns(at, h):
    first, more = at
    return aligned(first + side() * more + h * LANES, LANES)


def scale_kernel(heads, lane, x_at, g_at, x_ref, g_ref, step_ref, grow_ref, endw_ref, xe_ref, ge_ref):
    for h in range(heads):
        at = slice(h * LANES, (h + 1) * LANES)
        one = slice(lane + h, lane + h + 1)
        x = x_ref[:, head_columns(x_at, h)].astype(F32)
        g = g_ref[:, head_columns(g_at, h)].astype(F32)
        xe_ref[:, at] = (x * (step_ref[:, one] * endw_ref[:, one])).astype(BF16)
        ge_ref[:, at] = (g * grow_ref[:, one]).astype(BF16)


def widen(row, lane, heads):
    return jnp.concatenate(
        [jnp.broadcast_to(row[:, lane + h : lane + h + 1], (1, LANES)) for h in range(heads)], 1
    )


def states_kernel(
    heads, lanes, bc0_ref, bc1_ref, xe0_ref, ge0_ref, xe1_ref, ge1_ref, grow_ref,
    first_ref, p_ref, q_ref, sf_ref, ds_ref, dec_ref, s_scr, d_scr, dec_scr,
):
    n = grow_ref.shape[0]
    r = side()
    for slot, (bc_ref, xe_ref, ge_ref) in enumerate(
        ((bc0_ref, xe0_ref, ge0_ref), (bc1_ref, xe1_ref, ge1_ref))
    ):
        s_scr[slot] = dot(bc_ref[:, :LANES], xe_ref[...], TN)
        d_scr[slot] = dot(bc_ref[:, LANES:], ge_ref[...], TN)
        dec_scr[slot] = widen(grow_ref[n - 1 : n, :], lanes[slot], heads)
    dec_first, dec_second = dec_scr[r], dec_scr[1 - r]
    s_first, d_second = s_scr[r], d_scr[1 - r]
    sf_ref[...] = s_first.astype(BF16)
    ds_ref[...] = d_second.astype(BF16)
    p = (dec_second * s_first + s_scr[1 - r]).astype(BF16)
    q = (dec_first * d_second + d_scr[r]).astype(BF16)
    p_ref[...] = p
    q_ref[...] = q

    @pl.when(place() == 0)
    def _():
        first_ref[...] = p

    @pl.when(place() != 0)
    def _():
        first_ref[...] = q

    dec_ref[0:1, :] = dec_first * dec_second
    dec_ref[1:2, :] = dec_first
    dec_ref[2:3, :] = dec_second
    dec_ref[3:8, :] = jnp.zeros((5, dec_first.shape[1]), F32)


def hop_kernel(hop, received_ref, p_ref, q_ref, dec_ref, out_ref):
    carried = dec_ref[0:1, :] * received_ref[...].astype(F32)

    @pl.when(place() == hop)
    def _():
        out_ref[...] = (carried + p_ref[...].astype(F32)).astype(BF16)

    @pl.when(place() != hop)
    def _():
        out_ref[...] = (carried + q_ref[...].astype(F32)).astype(BF16)


def inside_kernel(
    heads, lane, skip_at, all_heads, x_at, g_at, skip_ref, x_ref, g_ref, bc_ref, step_ref, cum_ref,
    cumt_ref, y_ref, dx_ref, dscores_ref, gy_ref, ds_ref, gx_ref,
):
    n = step_ref.shape[0]
    mask = triangle(n)
    scores = jnp.where(mask, dot(bc_ref[:, LANES:], bc_ref[:, :LANES], NT), 0.0)
    gy_ref[...] = jnp.zeros_like(gy_ref)
    ds_ref[...] = jnp.zeros_like(ds_ref)
    gx_ref[...] = jnp.zeros_like(gx_ref)
    dscores = jnp.zeros((n, n), F32)
    for h in range(heads):
        at = slice(h * LANES, (h + 1) * LANES)
        one = slice(lane + h, lane + h + 1)
        step = step_ref[:, one]
        gap = cum_ref[:, one] - cumt_ref[one, :]
        decay = jnp.exp(jnp.where(mask, gap, 0.0))
        mixing = (scores * decay).astype(BF16)
        x = x_ref[:, head_columns(x_at, h)].astype(F32)
        g = g_ref[:, head_columns(g_at, h)]
        gf = g.astype(F32)
        xs = (x * step).astype(BF16)
        skip = skip_ref[side() * all_heads + skip_at + h]
        y = dot(mixing, xs)
        dxs = dot(mixing, g, TN)
        dscores += dot(g, xs, NT) * decay
        y_ref[:, at] = y + skip * x
        dx_ref[:, at] = dxs * step + skip * gf
        gy_ref[:, one] = jnp.sum(gf * y, axis=1, keepdims=True)
        ds_ref[:, one] = jnp.sum(x * dxs, axis=1, keepdims=True)
        gx_ref[0:1, one] = jnp.sum(jnp.sum(gf * x, axis=0, keepdims=True), axis=1, keepdims=True)
    dscores_ref[...] = jnp.where(mask, dscores, 0.0)


def inside_bc_kernel(bc0_ref, bc1_ref, *refs):
    parts, outs = refs[: 2 * GROUPS], refs[2 * GROUPS :]
    for slot, bc_ref in enumerate((bc0_ref, bc1_ref)):
        total = parts[slot * GROUPS][...]
        for i in range(1, GROUPS):
            total = total + parts[slot * GROUPS + i][...]
        ds = total.astype(BF16)
        outs[slot][:, :LANES] = dot(ds, bc_ref[:, LANES:], TN)
        outs[slot][:, LANES:] = dot(ds, bc_ref[:, :LANES])


def across_kernel(heads, lanes, hops, filled, own_at, columns, *refs):
    refs = refs[2 * filled :]
    across_block(heads, lanes, hops, own_at, columns, *refs)


def across_block(
    heads, lanes, hops, own_at, columns, x0_ref, g0_ref, x1_ref, g1_ref, bc0_ref, bc1_ref, xe0_ref,
    ge0_ref, xe1_ref, ge1_ref, step_ref, grow_ref, endw_ref, dec_ref, p_ref, sf_ref, ds_ref,
    y0_ref, dx0_ref, y1_ref, dx1_ref, dbc0_ref, dbc1_ref, *refs
):
    received = refs[:hops]
    (
        yf_ref, dxf_ref, ys_ref, dxs_ref, dbco0_ref, dbco1_ref, u_ref, t_ref, re_ref,
        e_in, r_in, e_scr, r_scr, n_scr, yo_ref, dxo_ref, sems,
    ) = refs[hops:]
    r, pos = side(), place()
    width = yo_ref.shape[1]
    e_in[...] = jnp.zeros_like(e_in)
    r_in[...] = jnp.zeros_like(r_in)
    for k in range(hops):

        @pl.when(pos - 1 == k)
        def _(k=k):
            e_in[...] = received[k][...]

        @pl.when(hops - 1 - pos == k)
        def _(k=k):
            r_in[...] = received[k][...]

    dec_pair, dec_first, dec_second = dec_ref[0:1, :], dec_ref[1:2, :], dec_ref[2:3, :]
    entering = e_in[...].astype(F32)
    later = r_in[...].astype(F32)
    middle = dec_first * entering + sf_ref[...].astype(F32)
    leaving = dec_pair * entering + p_ref[...].astype(F32)
    earlier = dec_second * later + ds_ref[...].astype(F32)
    e_scr[r] = e_in[...]
    e_scr[1 - r] = middle.astype(BF16)
    r_scr[1 - r] = r_in[...]
    r_scr[r] = earlier.astype(BF16)
    n_scr[1 - r] = jnp.sum(later * leaving, axis=0, keepdims=True)
    n_scr[r] = jnp.sum(earlier * middle, axis=0, keepdims=True)

    u_ref[...] = jnp.zeros_like(u_ref)
    t_ref[...] = jnp.zeros_like(t_ref)
    re_ref[...] = jnp.zeros_like(re_ref)
    for slot, (bc_ref, xe_ref, ge_ref, y_ref, dx_ref, dbc_ref, dbco_ref) in enumerate(
        (
            (bc0_ref, xe0_ref, ge0_ref, y0_ref, dx0_ref, dbc0_ref, dbco0_ref),
            (bc1_ref, xe1_ref, ge1_ref, y1_ref, dx1_ref, dbc1_ref, dbco1_ref),
        )
    ):
        e_all = e_scr[slot]
        r_all = r_scr[slot]
        db = dbc_ref[:, :LANES] + dot(xe_ref[...], r_all, NT)
        dc = dbc_ref[:, LANES:] + dot(ge_ref[...], e_all, NT)
        dbco_ref[:, :LANES] = db.astype(dbco_ref.dtype)
        dbco_ref[:, LANES:] = dc.astype(dbco_ref.dtype)
        ce_all = dot(bc_ref[:, LANES:], e_all)
        br_all = dot(bc_ref[:, :LANES], r_all)
        for h in range(heads):
            at = slice(h * LANES, (h + 1) * LANES)
            lane = lanes[slot] + h
            one = slice(lane, lane + 1)
            ce, br = ce_all[:, at], br_all[:, at]
            y = (y_ref[:, at] + grow_ref[:, one] * ce).astype(BF16)
            dx = (dx_ref[:, at] + (step_ref[:, one] * endw_ref[:, one]) * br).astype(BF16)
            if slot == 0:
                yo_ref[:, at] = y
                dxo_ref[:, at] = dx
                x = x0_ref[:, head_columns(own_at, h)].astype(F32)
                g = g0_ref[:, head_columns(own_at, h)].astype(F32)
            else:
                ys_ref[:, at] = y
                dxs_ref[:, at] = dx
                x = x1_ref[:, head_columns(columns[0], h)].astype(F32)
                g = g1_ref[:, head_columns(columns[1], h)].astype(F32)
            u_ref[:, one] = jnp.sum(g * ce, axis=1, keepdims=True)
            t_ref[:, one] = jnp.sum(x * br, axis=1, keepdims=True)
            re_ref[0:1, one] = jnp.sum(n_scr[slot][:, at], axis=1, keepdims=True)
        if slot == 0:
            final = aligned(own_at[0] + r * own_at[1], width)
            pairs = [(yo_ref, yf_ref.at[:, final]), (dxo_ref, dxf_ref.at[:, final])]
            copies = copy_all(pairs, sems)
    for copy in copies:
        copy.wait()


def steps_kernel(sig_ref, rate_ref, step_ref, grow_ref, endw_ref, *refs):
    count = 2 * GROUPS
    gys, dss, gxs = refs[:count], refs[count : 2 * count], refs[2 * count : 3 * count]
    refs = refs[3 * count :]
    us, ts, res = refs[:GROUPS], refs[GROUPS : 2 * GROUPS], refs[2 * GROUPS : 3 * GROUPS]
    dbc_ref, own_ref, send_ref, sums_ref = refs[3 * GROUPS :]

    def total(parts):
        value = parts[0][...]
        for a in parts[1:]:
            value = value + a[...]
        return value

    n = step_ref.shape[0]
    step = step_ref[...]
    ds = total(dss) + endw_ref[...] * total(ts)
    gy = total(gys) + grow_ref[...] * total(us)
    rate = rate_ref[0:1, :]
    last = lax.broadcasted_iota(jnp.int32, (n, LANES), 0) == n - 1
    dcum = gy - step * ds + jnp.where(last, total(res)[0:1, :], 0.0)
    lower = jnp.where(triangle(n), 1.0, 0.0).astype(F32)
    dlog = dot(lower, dcum, TN, precision=HIGHEST)
    draw = (ds - rate * dlog) * sig_ref[...]
    turned = draw.T
    heads = own_ref.shape[0]
    own_ref[...] = turned[:heads, :]
    both = split(turned[heads : 2 * heads, :])
    send_ref[0:n, :] = dbc_ref[...]
    send_ref[n:, :LANES] = both[:heads]
    send_ref[n:, LANES:] = both[heads:]
    sums_ref[0:1, :] = jnp.sum(draw, axis=0, keepdims=True)
    sums_ref[1:2, :] = jnp.sum(dlog * (-step * rate), axis=0, keepdims=True)
    sums_ref[2:3, :] = total(gxs)[0:1, :]
    sums_ref[3:8, :] = jnp.zeros((5, LANES), F32)


def conv_back_kernel(
    own_ref, ret_ref, kept_ref, cw_ref, heads_ref, grad_ref, raw_ref, rim_ref, message_ref, z_scr,
    sum_scr, grad_scr, raw_scr, sems,
):
    tokens = own_ref.shape[0]
    taps = cw_ref.shape[0]
    pre = kept_ref[HALO + tokens :, :]
    sig = jax.nn.sigmoid(pre)
    dconv = (own_ref[...] + ret_ref[0:tokens, :].astype(F32)) * sig * (1.0 + pre * (1.0 - sig))
    z_scr[...] = jnp.zeros_like(z_scr)
    z_scr[HALO : HALO + tokens, :] = dconv
    grad = cw_ref[0:1, :] * z_scr[taps - 1 : taps - 1 + tokens + HALO, :]
    for k in range(1, taps):
        grad = grad + cw_ref[k : k + 1, :] * z_scr[taps - 1 - k : taps - 1 - k + tokens + HALO, :]
    grad_scr[...] = grad[HALO:, :]
    raw = ret_ref[tokens:, :].astype(F32)
    raw_scr[...] = raw[:, :LANES] + raw[:, LANES:]
    copies = copy_all([(grad_scr, grad_ref), (raw_scr, raw_ref)], sems)
    rim_ref[...] = grad[HALO - 8 : HALO, :]
    first = HALO - taps + 1
    sum_scr[...] = jnp.zeros_like(sum_scr)
    for k in range(taps):
        sum_scr[k : k + 1, :] = jnp.sum(
            dconv * kept_ref[first + k : first + k + tokens, :], axis=0, keepdims=True
        )
    sum_scr[taps : taps + 1, :] = jnp.sum(dconv, axis=0, keepdims=True)
    sum_scr[5:8, aligned(side() * LANES, LANES)] = heads_ref[0:3, :]
    small = split(sum_scr[...])
    message_ref[0 : tokens + HALO, :] = grad.astype(BF16)
    message_ref[tokens + HALO :, :] = small
    for copy in copies:
        copy.wait()


def pack_kernel(layer_ref, halo_ref, keep_ref, send_ref, sems):
    half, _, rows = keep_ref.shape
    pairs = []
    for k in range(2 * half):
        out = keep_ref.at[k] if k < half else send_ref.at[k - half]
        at = peer_columns(k, rows)
        pairs.append((halo_ref.at[:, at], out.at[0:HALO, :]))
        pairs.append((layer_ref.at[:, at], out.at[HALO:, :]))
    for copy in copy_all(pairs, sems):
        copy.wait()


def relay_kernel(picks, *refs):
    out_ref = refs[-1]
    for j, (ref, at) in enumerate(picks):
        out_ref[j] = refs[ref][at]


def turn_kernel(picks, *refs):
    out_ref = refs[-1]
    parts = [refs[ref].at[at] for ref, at in picks]
    tokens = parts[0].shape[0] - HALO
    for k, part in enumerate(parts):
        out_ref[:, k * tokens : (k + 1) * tokens] = part[HALO:, :].T
    halos = jnp.concatenate([part[0:HALO, :] for part in parts], 0)
    out_ref[:, len(parts) * tokens :] = halos.T


def weight_kernel(count, left_ref, *refs):
    rights, out_ref = refs[:count], refs[count]
    tokens = (left_ref.shape[1] // count) - HALO
    right = jnp.concatenate(
        [a[HALO : HALO + tokens, :] for a in rights] + [a[0:HALO, :] for a in rights], 0
    )
    at = tokens + HALO
    both = jnp.zeros((16, right.shape[1]), F32)
    for a in rights:
        both += a[at : at + 16, :].astype(F32)
    small = split(both[0:8, :] + both[8:16, :])
    chunk = out_ref.shape[1] - 16
    for k in range(out_ref.shape[0]):
        term = dot(left_ref[k * chunk : (k + 1) * chunk, :], right)
        out_ref[k, 0:chunk, :] = term.astype(BF16)
        out_ref[k, chunk:, :] = small


def reduce_kernel(heads, terms_ref, total_ref, cw_ref, cb_ref, *head_refs):
    chunk = total_ref.shape[1]
    total = terms_ref[0].astype(F32)
    for k in range(1, terms_ref.shape[0]):
        total = total + terms_ref[k].astype(F32)
    for k in range(total_ref.shape[0]):
        total_ref[k] = total[0:chunk].astype(BF16)
    small = total[chunk : chunk + 8] + total[chunk + 8 :]
    taps = cw_ref.shape[0]
    cw_ref[...] = small[0:taps, :]
    cb_ref[...] = small[taps : taps + 1, :]
    for i, ref in enumerate(head_refs):
        row = small[5 + i : 6 + i, :]
        ref[:, :heads] = row[:, :heads] + row[:, heads : 2 * heads]
        row = row[:, LANES:]
        ref[:, heads:] = row[:, :heads] + row[:, heads : 2 * heads]


def place_rows_kernel(parts_ref, out_ref):
    chunk = parts_ref.shape[1]
    for k in range(parts_ref.shape[0]):
        out_ref[k * chunk : (k + 1) * chunk, :] = parts_ref[k].astype(F32)


def tokens_kernel(count, *refs):
    pieces = refs[:count]
    grad_ref, rim_ref, out_ref, w_scr, sems = refs[count:]
    copies = copy_all([(pieces[k], w_scr.at[k]) for k in range(count)], sems)
    tail = rim_ref.shape[0]
    own = grad_ref[...]
    g = jnp.concatenate([own[:-tail], own[-tail:] + rim_ref[...]], 0).astype(BF16)
    rows = pieces[0].shape[0]
    for k in range(count):
        copies[k].wait()
        out_ref[:, peer_columns(k, rows)] = dot(g, w_scr[k], NT).astype(BF16)


def join_kernel(*refs):
    own_ref, back_ref = refs[2:4]
    backs = refs[4 : 4 + 2 * GROUPS]
    y_ref, dx_ref, raw_ref, sems = refs[4 + 2 * GROUPS :]
    r = side()
    at = (1 - r) * (y_ref.shape[1] // 2)
    pairs = []
    for i in range(GROUPS):
        y, dx = backs[2 * i : 2 * i + 2]
        columns = aligned(at, y.shape[1])
        at += y.shape[1]
        pairs.append((y, y_ref.at[:, columns]))
        pairs.append((dx, dx_ref.at[:, columns]))
    copies = copy_all(pairs, sems)
    heads = own_ref.shape[0]
    raw_ref[pl.ds(pl.multiple_of(r * heads, 8), heads), :] = own_ref[...]
    raw_ref[pl.ds(pl.multiple_of((1 - r) * heads, 8), heads), :] = back_ref[...]
    for copy in copies:
        copy.wait()


def pinned(x):
    return pltpu.with_memory_space_constraint(x, pltpu.HBM)


def toggled(x, axis, bits):
    size = lax.axis_size(axis)
    return lax.ppermute(x, axis, [(i, i ^ bits) for i in range(size)])


def exchanged(x, axis):
    return lax.all_to_all(x, axis, 0, 0)


def after(x, *others):
    return lax.optimization_barrier((x, *others))[0]


def body(layer_in, w_bc, conv_w, conv_b, ssm_in, dt_raw, dt_bias, a_log, skip_scale, grad_out):
    ctx, fsdp = lax.axis_size("ctx"), lax.axis_size("fsdp")
    layer, x, g, dt = layer_in[0], ssm_in[0], grad_out[0], dt_raw[0].T
    tokens, width = x.shape
    total_heads = dt_bias.shape[0]
    heads = total_heads // 2
    half = width // 2
    counts = [heads // part for part in PARTS]
    starts = [sum(counts[:i]) for i in range(GROUPS)]
    widths = [half // part for part in PARTS]
    ats = [sum(widths[:i]) for i in range(GROUPS)]
    state = w_bc.shape[1] // 2
    taps = conv_w.shape[0]
    rows = w_bc.shape[0]
    chunk_rows = rows // ctx
    pairs = ctx // 2
    hops = pairs - 1
    square = shape((tokens, LANES), F32)
    flats = [shape((tokens, a), BF16) for a in widths]
    turned = shape((heads, tokens), F32)
    both_bc = [shape((tokens, 2 * state), F32)] * 2

    tail = call(
        tail_kernel, "tail", shape((HALO, layer.shape[1]), BF16), (), hbm=(pinned(layer),),
        scratch=[pltpu.SemaphoreType.DMA((1,))],
    )
    halo = lax.ppermute(tail, "ctx", [(i, i + 1) for i in range(ctx - 1)])
    dt_back = toggled(dt, "ctx", 1)
    swap = call(
        swap_kernel, "swap", shape((tokens, width), BF16), (), hbm=(pinned(x), pinned(g)),
        scratch=[pltpu.SemaphoreType.DMA((2,))],
    )
    swapped = toggled(after(swap, halo, dt_back), "ctx", 1)

    step, cum, cumt, grow, endw, sig, rate = call(
        vectors_kernel, "vectors", [square] * 6 + [shape((8, LANES), F32)], (), dt, dt_back,
        dt_bias[None, :], a_log[None, :],
        scratch=[pltpu.VMEM((tokens, tokens), F32), pltpu.VMEM((8, LANES), F32)],
    )

    def source(slot, i):
        if slot == 0:
            return (ats[i], half), (ats[i], half), x, g
        return (ats[i], 0), (half + ats[i], 0), swapped, swapped

    def scale(slot, i):
        x_at, g_at, xa, ga = source(slot, i)
        return call(
            functools.partial(scale_kernel, counts[i], slot * heads + starts[i], x_at, g_at), "scale",
            [flats[i]] * 2, (), xa, ga, step, grow, endw,
        )

    scaled = {(0, i): scale(0, i) for i in range(GROUPS)}
    def landing(count):
        return [
            pltpu.VMEM(layer.shape, BF16),
            pltpu.VMEM((count, *w_bc.shape), BF16),
            pltpu.SemaphoreType.DMA((1 + count,)),
        ]

    parts = shape((fsdp // 2, tokens + HALO, rows), BF16)
    packs = call(
        pack_kernel, "pack", [parts, parts], (), hbm=(pinned(layer), halo),
        scratch=[pltpu.SemaphoreType.DMA((2 * fsdp,))],
    )
    far_bit = fsdp // 2
    own = after(w_bc, swap)
    far = [toggled(own, "fsdp", far_bit)]
    near = [own]
    while len(near) < far_bit:
        near += [toggled(a, "fsdp", len(near)) for a in near]
    early = call(
        functools.partial(early_kernel, len(near)), "project_early",
        shape((tokens, 2 * state), F32), (), hbm=(pinned(layer), after(near[0], packs[0]), *near[1:]),
        scratch=landing(len(near)),
    )
    far[0] = after(far[0], early, *[scaled[0, i][0] for i in range(GROUPS)])
    while len(far) < far_bit:
        far += [toggled(a, "fsdp", len(far)) for a in far]
    pieces = near + far
    layer_scr, w_scr, sems = landing(fsdp)
    kept, bc = call(
        functools.partial(project_kernel, len(near), fsdp), "project",
        [
            shape((2 * tokens + HALO, 2 * state), F32),
            shape((tokens, 2 * state), BF16),
        ],
        (), halo, early, conv_w, conv_b[None, :], hbm=(pinned(layer), *pieces),
        scratch=[layer_scr, w_scr, pltpu.VMEM((tokens + HALO, 2 * state), F32), sems],
    )
    bcs = [bc, toggled(bc, "ctx", 1)]
    def within(slot, i, *earlier):
        x_at, g_at, xa, ga = source(slot, i)
        return call(
            functools.partial(
                inside_kernel, counts[i], slot * heads + starts[i], starts[i], heads, x_at, g_at
            ),
            "inside",
            [shape((tokens, widths[i]), F32)] * 2 + [shape((tokens, tokens), F32), square, square]
            + [shape((8, LANES), F32)],
            (skip_scale,), xa, ga, after(bcs[slot], *earlier), step, cum, cumt,
        )

    order = [(slot, i) for slot in range(2) for i in range(GROUPS)]
    inside, states, received, earlier = {}, [], [], []
    for key in order[:GROUPS]:
        inside[key] = within(*key, *earlier)
        earlier = [inside[key][2]]
    for i in range(GROUPS):
        lanes = (starts[i], heads + starts[i])
        scaled[1, i] = scale(1, i)
        wide = shape((state, widths[i]), BF16)
        first, p, q, s_first, d_second, decays = call(
            functools.partial(states_kernel, counts[i], lanes), "states",
            [wide] * 5 + [shape((8, widths[i]), F32)],
            (), *bcs, *scaled[0, i], *scaled[1, i], after(grow, *earlier),
            scratch=[pltpu.VMEM((2, state, widths[i]), F32)] * 2
            + [pltpu.VMEM((2, 1, widths[i]), F32)],
        )
        states.append((decays, p, s_first, d_second, q))
        received.append([first])
        earlier = [first]
    for slot, i in order[GROUPS:]:
        inside[slot, i] = within(slot, i, *earlier)
        earlier = [inside[slot, i][2]]
    for hop in range(hops):
        moves = [(hop, hop + 1), (pairs - 1 - hop, pairs - 2 - hop)]
        moves = [(2 * a + i, 2 * b + i) for a, b in moves for i in range(2)]
        for i in range(GROUPS):
            value = received[i][-1]
            if hop:
                decays, p, _, _, q = states[i]
                value = call(
                    functools.partial(hop_kernel, hop), "hop", shape(value.shape, BF16), (),
                    after(value, *earlier), p, q, decays,
                )
                earlier = [value]
            received[i].append(lax.ppermute(value, "ctx", moves))
    arrays = [packs[0]]
    at = {(0, k): (0, k) for k in range(fsdp // 2)}
    message, bit = packs[1], fsdp // 2
    sent = [(0, k) for k in range(bit, fsdp)]
    while bit:
        arrays.append(toggled(message, "fsdp", bit))
        for j, (source_bits, owner_bits) in enumerate(sent):
            at[source_bits ^ bit, owner_bits ^ bit] = (len(arrays) - 1, j)
        bit //= 2
        if bit:
            sent = [key for key in sorted(at) if key[1] & bit and key[1] < 2 * bit]
            message = call(
                functools.partial(relay_kernel, [at[key] for key in sent]), "relay",
                shape((len(sent), tokens + HALO, rows), BF16), (), after(arrays[0], received[-1][0]),
                *arrays[1:],
            )
    picks = [at[k, 0] for k in range(fsdp)]
    dbcs = call(inside_bc_kernel, "inside_bc", both_bc, (), *bcs, *[inside[key][2] for key in order])

    full = shape((tokens, width), BF16)
    finals, sends, us, ts, res = (), [], [], [], []
    for i in range(GROUPS):
        last = i == GROUPS - 1
        own_at, _, xa, ga = source(0, i)
        x_at, g_at, xb, gb = source(1, i)
        if i == 1:
            left = call(
                functools.partial(turn_kernel, picks), "turn",
                shape((rows, fsdp * (tokens + HALO)), BF16), (), after(arrays[0], *sends), *arrays[1:],
            )
        lanes = (starts[i], heads + starts[i])
        y, dx, y_send, dx_send, dbc_own, dbc_other, u, t, re = call(
            functools.partial(
                across_kernel, counts[i], lanes, hops, len(finals) // 2, own_at, (x_at, g_at)
            ),
            "across",
            [full, full, flats[i], flats[i]]
            + [both_bc[0], shape((tokens, 2 * state), BF16 if last else F32)]
            + [square, square, shape((8, LANES), F32)],
            (), xa, ga, xb, gb, after(bcs[0], left) if i == 1 else bcs[0], bcs[1], *scaled[0, i],
            *scaled[1, i], step, grow, endw,
            *states[i][:4], *inside[0, i][:2], *inside[1, i][:2], *dbcs, *received[i][1:],
            hbm=finals, hbm_outs=2, aliases={0: 0, 1: 1} if finals else None,
            scratch=[pltpu.VMEM((state, widths[i]), BF16)] * 2
            + [pltpu.VMEM((2, state, widths[i]), BF16)] * 2
            + [pltpu.VMEM((2, 1, widths[i]), F32)] + [pltpu.VMEM((tokens, widths[i]), BF16)] * 2
            + [pltpu.SemaphoreType.DMA((2,))],
        )
        finals, dbcs = (y, dx), (dbc_own, dbc_other)
        sends += [y_send, dx_send]
        us.append(u)
        ts.append(t)
        res.append(re)

    raw_own, dbc_send, head_sums = call(
        steps_kernel, "steps",
        [turned, shape((tokens + heads, 2 * state), BF16), shape((8, LANES), F32)], (),
        sig, rate, step, grow, endw, *[inside[key][j] for j in (3, 4, 5) for key in order],
        *us, *ts, *res, dbcs[1],
    )
    dbc_ret = toggled(dbc_send, "ctx", 1)
    backs = [toggled(sends[0], "ctx", 1)]
    grad, raw_back, rim_send, message = call(
        conv_back_kernel, "conv_back",
        [
            shape((tokens, 2 * state), F32),
            turned,
            shape((8, 2 * state), F32),
            shape((tokens + HALO + 16, 2 * state), BF16),
        ],
        (), after(dbcs[0], *backs), dbc_ret, kept, conv_w, head_sums, hbm_outs=2,
        scratch=[
            pltpu.VMEM((tokens + 2 * HALO, 2 * state), F32),
            pltpu.VMEM((8, 2 * state), F32),
            pltpu.VMEM((tokens, 2 * state), F32),
            pltpu.VMEM(turned.shape, F32),
            pltpu.SemaphoreType.DMA((2,)),
        ],
    )
    rim = lax.ppermute(rim_send, "ctx", [(i + 1, i) for i in range(ctx - 1)])
    backs.append(toggled(after(sends[1], dbc_ret), "ctx", 1))

    rights = [message] + [toggled(message, "fsdp", k) for k in range(fsdp - 1, 0, -1)][::-1]
    terms = call(
        functools.partial(weight_kernel, fsdp), "weight",
        shape((ctx, chunk_rows + 16, 2 * state), BF16), (), left, after(message, rim, *backs), *rights[1:],
    )
    backs += [toggled(after(a, terms), "ctx", 1) for a in sends[2:]]
    total, grad_cw, grad_cb, *per_head = call(
        functools.partial(reduce_kernel, heads), "reduce",
        [
            shape((ctx, chunk_rows, 2 * state), BF16),
            shape((taps, 2 * state), F32),
            shape((1, 2 * state), F32),
        ]
        + [shape((1, total_heads), F32)] * 3,
        (), after(exchanged(terms, "ctx"), *backs[:-1]),
    )
    grad_weight = call(
        place_rows_kernel, "place_rows", shape((rows, 2 * state), F32), (), exchanged(total, "ctx")
    )
    grad_tokens = call(
        functools.partial(tokens_kernel, fsdp), "grad_tokens", shape((tokens, fsdp * rows), BF16),
        (), after(grad, total), rim, hbm=pieces,
        scratch=[pltpu.VMEM((fsdp, *w_bc.shape), BF16), pltpu.SemaphoreType.DMA((fsdp,))],
    )
    ssm_out, grad_values, grad_raw = call(
        join_kernel, "join", [full, full, shape((total_heads, tokens), F32)],
        (), raw_own, raw_back, *backs, hbm=finals, hbm_outs=2,
        aliases={0: 0, 1: 1}, scratch=[pltpu.SemaphoreType.DMA((2 * GROUPS,))],
    )
    return (
        ssm_out[None],
        grad_values[None],
        grad_tokens[None],
        grad_raw.T[None],
        grad_weight,
        grad_cw,
        grad_cb[0],
        *[a[0] for a in per_head],
    )


def solution(mesh):
    tokens = P("fsdp", "ctx", None)
    in_specs = (tokens, P("fsdp", None), P(), P(), tokens, tokens, P(), P(), P(), tokens)
    out_specs = (tokens, tokens, tokens, tokens, P("fsdp", None), P(), P(), P(), P(), P())
    return jax.shard_map(body, mesh=mesh, in_specs=in_specs, out_specs=out_specs, check_vma=False)
```

```python
import functools

import jax
import jax.numpy as jnp
from jax import lax
from jax.experimental import pallas as pl
from jax.experimental.pallas import tpu as pltpu
from jax.sharding import PartitionSpec as P

F32 = jnp.float32
BF16 = jnp.bfloat16
LANES = 128
HALO = 16
PARTS = (2, 2)
GROUPS = len(PARTS)
LIMIT = 16 * 1024 * 1024
HIGHEST = lax.Precision.HIGHEST
TN = ((0,), (0,))
NT = ((1,), (1,))


def dot(a, b, dims=((1,), (0,)), precision=None):
    return lax.dot_general(
        a, b, (dims, ((), ())), precision=precision, preferred_element_type=F32
    )


def shape(dims, dtype):
    return jax.ShapeDtypeStruct(dims, dtype)


def call(kernel, name, out_shape, smem, *operands, hbm=(), hbm_outs=0, scratch=(), aliases=None):
    single = not isinstance(out_shape, list)
    outs = [out_shape] if single else out_shape
    spaces = [pltpu.SMEM] * len(smem) + [pl.ANY] * len(hbm) + [pltpu.VMEM] * len(operands)
    out_spaces = [pltpu.HBM] * hbm_outs + [pltpu.VMEM] * (len(outs) - hbm_outs)
    result = pl.pallas_call(
        kernel,
        out_shape=outs,
        in_specs=[pl.BlockSpec(memory_space=a) for a in spaces],
        out_specs=[pl.BlockSpec(memory_space=a) for a in out_spaces],
        scratch_shapes=list(scratch),
        compiler_params=pltpu.CompilerParams(vmem_limit_bytes=LIMIT),
        input_output_aliases=aliases or {},
        name=name,
    )(*smem, *hbm, *operands)
    return result[0] if single else result


def copy_all(pairs, sems):
    copies = [pltpu.make_async_copy(a, b, sems.at[i]) for i, (a, b) in enumerate(pairs)]
    for copy in copies:
        copy.start()
    return copies


def side():
    return lax.rem(lax.axis_index("ctx"), 2)


def place():
    return lax.div(lax.axis_index("ctx"), 2)


def peer_columns(k, rows):
    return aligned((lax.axis_index("fsdp") ^ k) * rows, rows)


def aligned(at, size):
    return pl.ds(pl.multiple_of(at, LANES), size)


def triangle(n):
    rows = lax.broadcasted_iota(jnp.int32, (n, n), 0)
    cols = lax.broadcasted_iota(jnp.int32, (n, n), 1)
    return rows >= cols


def split(value):
    high = value.astype(BF16).astype(F32)
    return jnp.concatenate([high, value - high], 0).astype(BF16)


def swap_kernel(layer_ref, x_ref, g_ref, halo_ref, first_ref, x_out_ref, g_out_ref, sems):
    width = x_out_ref.shape[1]
    tokens = layer_ref.shape[0]
    base = (1 - side()) * (2 * width)
    pairs = [
        (layer_ref.at[tokens - HALO : tokens, :], halo_ref),
        (x_ref.at[:, aligned(base, width)], first_ref.at[:, :width]),
        (g_ref.at[:, aligned(base, width)], first_ref.at[:, width:]),
        (x_ref.at[:, aligned(base + width, width)], x_out_ref),
        (g_ref.at[:, aligned(base + width, width)], g_out_ref),
    ]
    for copy in copy_all(pairs, sems):
        copy.wait()


def vectors_kernel(
    dt_ref, back_ref, bias_ref, alog_ref, step_ref, cum_ref, cumt_ref, grow_ref, endw_ref, sig_ref,
    rate_ref, turned, rows,
):
    n = back_ref.shape[1]
    heads = back_ref.shape[0] // 2
    r = side()
    mine = pl.ds(pl.multiple_of(r * heads, 8), heads)
    turned[...] = jnp.zeros_like(turned)
    turned[0:heads, :] = dt_ref[mine, :]
    turned[heads : 2 * heads, :] = back_ref[mine, :]
    rows[...] = jnp.zeros_like(rows)
    for i, ref in enumerate((bias_ref, alog_ref)):
        half = jnp.where(r == 0, ref[:, :heads], ref[:, heads:])
        rows[i : i + 1, 0:heads] = half
        rows[i : i + 1, heads : 2 * heads] = half
    raw = turned[...].T + rows[0:1, :]
    step = jnp.maximum(raw, 0.0) + jnp.log1p(jnp.exp(-jnp.abs(raw)))
    rate = jnp.exp(rows[1:2, :])
    log_decay = -step * rate
    lower = jnp.where(triangle(n), 1.0, 0.0).astype(F32)
    cum = dot(lower, log_decay, precision=HIGHEST)
    step_ref[...] = step
    cum_ref[...] = cum
    cumt_ref[...] = cum.T
    grow_ref[...] = jnp.exp(cum)
    endw_ref[...] = jnp.exp(cum[n - 1 : n, :] - cum)
    sig_ref[...] = jax.nn.sigmoid(raw)
    rate_ref[...] = jnp.broadcast_to(rate, rate_ref.shape)


def early_kernel(count, layer_ref, *refs):
    pieces = refs[:count]
    out_ref, layer_scr, w_scr, sems = refs[count:]
    copies = copy_all(
        [(layer_ref, layer_scr)] + [(pieces[k], w_scr.at[k]) for k in range(count)], sems
    )
    copies[0].wait()
    total = 0.0
    for k in range(count):
        copies[k + 1].wait()
        total += dot(layer_scr[:, peer_columns(k, w_scr.shape[1])], w_scr[k])
    out_ref[...] = total


def project_kernel(done, count, layer_ref, *refs):
    pieces = refs[:count]
    halo_ref, early_ref, cw_ref, cb_ref, kept_ref, bc_ref, layer_scr, w_scr, ext_scr, sems = refs[count:]
    copies = copy_all(
        [(layer_ref, layer_scr)] + [(pieces[k], w_scr.at[k]) for k in range(count)], sems
    )
    taps = cw_ref.shape[0]
    tokens = layer_ref.shape[0]
    copies[0].wait()
    total, rim = early_ref[...], 0.0
    for k in range(count):
        copies[k + 1].wait()
        at = peer_columns(k, w_scr.shape[1])
        rim += dot(halo_ref[:, at], w_scr[k])
        if k >= done:
            total += dot(layer_scr[:, at], w_scr[k])
    ext_scr[0:HALO, :] = rim
    ext_scr[HALO:, :] = total
    kept_ref[0 : HALO + tokens, :] = ext_scr[...]
    first = HALO - taps + 1
    pre = cb_ref[...] + cw_ref[0:1, :] * ext_scr[first : first + tokens, :]
    for k in range(1, taps):
        pre = pre + cw_ref[k : k + 1, :] * ext_scr[first + k : first + k + tokens, :]
    kept_ref[HALO + tokens :, :] = pre
    bc_ref[...] = (pre * jax.nn.sigmoid(pre)).astype(BF16)


def head_columns(at, h):
    first, more = at
    return aligned(first + side() * more + h * LANES, LANES)


def scale_kernel(heads, lane, x_at, g_at, x_ref, g_ref, step_ref, grow_ref, endw_ref, xe_ref, ge_ref):
    for h in range(heads):
        at = slice(h * LANES, (h + 1) * LANES)
        one = slice(lane + h, lane + h + 1)
        x = x_ref[:, head_columns(x_at, h)].astype(F32)
        g = g_ref[:, head_columns(g_at, h)].astype(F32)
        xe_ref[:, at] = (x * (step_ref[:, one] * endw_ref[:, one])).astype(BF16)
        ge_ref[:, at] = (g * grow_ref[:, one]).astype(BF16)


def widen(row, lane, heads):
    return jnp.concatenate(
        [jnp.broadcast_to(row[:, lane + h : lane + h + 1], (1, LANES)) for h in range(heads)], 1
    )


def states_kernel(
    heads, lanes, bc0_ref, bc1_ref, xe0_ref, ge0_ref, xe1_ref, ge1_ref, grow_ref,
    first_ref, p_ref, q_ref, sf_ref, ds_ref, dec_ref, s_scr, d_scr, dec_scr,
):
    n = grow_ref.shape[0]
    r = side()
    for slot, (bc_ref, xe_ref, ge_ref) in enumerate(
        ((bc0_ref, xe0_ref, ge0_ref), (bc1_ref, xe1_ref, ge1_ref))
    ):
        s_scr[slot] = dot(bc_ref[:, :LANES], xe_ref[...], TN)
        d_scr[slot] = dot(bc_ref[:, LANES:], ge_ref[...], TN)
        dec_scr[slot] = widen(grow_ref[n - 1 : n, :], lanes[slot], heads)
    dec_first, dec_second = dec_scr[r], dec_scr[1 - r]
    s_first, d_second = s_scr[r], d_scr[1 - r]
    sf_ref[...] = s_first.astype(BF16)
    ds_ref[...] = d_second.astype(BF16)
    p = (dec_second * s_first + s_scr[1 - r]).astype(BF16)
    q = (dec_first * d_second + d_scr[r]).astype(BF16)
    p_ref[...] = p
    q_ref[...] = q

    @pl.when(place() == 0)
    def _():
        first_ref[...] = p

    @pl.when(place() != 0)
    def _():
        first_ref[...] = q

    dec_ref[0:1, :] = dec_first * dec_second
    dec_ref[1:2, :] = dec_first
    dec_ref[2:3, :] = dec_second
    dec_ref[3:8, :] = jnp.zeros((5, dec_first.shape[1]), F32)


def hop_kernel(hop, received_ref, p_ref, q_ref, dec_ref, out_ref):
    carried = dec_ref[0:1, :] * received_ref[...].astype(F32)

    @pl.when(place() == hop)
    def _():
        out_ref[...] = (carried + p_ref[...].astype(F32)).astype(BF16)

    @pl.when(place() != hop)
    def _():
        out_ref[...] = (carried + q_ref[...].astype(F32)).astype(BF16)


def inside_kernel(
    heads, lane, skip_at, all_heads, x_at, g_at, skip_ref, x_ref, g_ref, bc_ref, step_ref, cum_ref,
    cumt_ref, y_ref, dx_ref, dscores_ref, gy_ref, ds_ref, gx_ref,
):
    n = step_ref.shape[0]
    mask = triangle(n)
    scores = jnp.where(mask, dot(bc_ref[:, LANES:], bc_ref[:, :LANES], NT), 0.0)
    gy_ref[...] = jnp.zeros_like(gy_ref)
    ds_ref[...] = jnp.zeros_like(ds_ref)
    gx_ref[...] = jnp.zeros_like(gx_ref)
    dscores = jnp.zeros((n, n), F32)
    for h in range(heads):
        at = slice(h * LANES, (h + 1) * LANES)
        one = slice(lane + h, lane + h + 1)
        step = step_ref[:, one]
        gap = cum_ref[:, one] - cumt_ref[one, :]
        decay = jnp.exp(jnp.where(mask, gap, 0.0))
        mixing = (scores * decay).astype(BF16)
        x = x_ref[:, head_columns(x_at, h)].astype(F32)
        g = g_ref[:, head_columns(g_at, h)]
        gf = g.astype(F32)
        xs = (x * step).astype(BF16)
        skip = skip_ref[side() * all_heads + skip_at + h]
        y = dot(mixing, xs)
        dxs = dot(mixing, g, TN)
        dscores += dot(g, xs, NT) * decay
        y_ref[:, at] = y + skip * x
        dx_ref[:, at] = dxs * step + skip * gf
        gy_ref[:, one] = jnp.sum(gf * y, axis=1, keepdims=True)
        ds_ref[:, one] = jnp.sum(x * dxs, axis=1, keepdims=True)
        gx_ref[0:1, one] = jnp.sum(jnp.sum(gf * x, axis=0, keepdims=True), axis=1, keepdims=True)
    dscores_ref[...] = jnp.where(mask, dscores, 0.0)


def inside_bc_kernel(bc0_ref, bc1_ref, *refs):
    parts, outs = refs[: 2 * GROUPS], refs[2 * GROUPS :]
    for slot, bc_ref in enumerate((bc0_ref, bc1_ref)):
        total = parts[slot * GROUPS][...]
        for i in range(1, GROUPS):
            total = total + parts[slot * GROUPS + i][...]
        ds = total.astype(BF16)
        outs[slot][:, :LANES] = dot(ds, bc_ref[:, LANES:], TN)
        outs[slot][:, LANES:] = dot(ds, bc_ref[:, :LANES])


def across_kernel(heads, lanes, hops, filled, own_at, columns, *refs):
    refs = refs[2 * filled :]
    across_block(heads, lanes, hops, own_at, columns, *refs)


def across_block(
    heads, lanes, hops, own_at, columns, x0_ref, g0_ref, x1_ref, g1_ref, bc0_ref, bc1_ref, xe0_ref,
    ge0_ref, xe1_ref, ge1_ref, step_ref, grow_ref, endw_ref, dec_ref, p_ref, sf_ref, ds_ref,
    y0_ref, dx0_ref, y1_ref, dx1_ref, dbc0_ref, dbc1_ref, *refs
):
    received = refs[:hops]
    (
        yf_ref, dxf_ref, ys_ref, dxs_ref, dbco0_ref, dbco1_ref, u_ref, t_ref, re_ref,
        e_in, r_in, e_scr, r_scr, n_scr, yo_ref, dxo_ref, sems,
    ) = refs[hops:]
    r, pos = side(), place()
    width = yo_ref.shape[1]
    e_in[...] = jnp.zeros_like(e_in)
    r_in[...] = jnp.zeros_like(r_in)
    for k in range(hops):

        @pl.when(pos - 1 == k)
        def _(k=k):
            e_in[...] = received[k][...]

        @pl.when(hops - 1 - pos == k)
        def _(k=k):
            r_in[...] = received[k][...]

    dec_pair, dec_first, dec_second = dec_ref[0:1, :], dec_ref[1:2, :], dec_ref[2:3, :]
    entering = e_in[...].astype(F32)
    later = r_in[...].astype(F32)
    middle = dec_first * entering + sf_ref[...].astype(F32)
    leaving = dec_pair * entering + p_ref[...].astype(F32)
    earlier = dec_second * later + ds_ref[...].astype(F32)
    e_scr[r] = e_in[...]
    e_scr[1 - r] = middle.astype(BF16)
    r_scr[1 - r] = r_in[...]
    r_scr[r] = earlier.astype(BF16)
    n_scr[1 - r] = jnp.sum(later * leaving, axis=0, keepdims=True)
    n_scr[r] = jnp.sum(earlier * middle, axis=0, keepdims=True)

    u_ref[...] = jnp.zeros_like(u_ref)
    t_ref[...] = jnp.zeros_like(t_ref)
    re_ref[...] = jnp.zeros_like(re_ref)
    for slot, (bc_ref, xe_ref, ge_ref, y_ref, dx_ref, dbc_ref, dbco_ref) in enumerate(
        (
            (bc0_ref, xe0_ref, ge0_ref, y0_ref, dx0_ref, dbc0_ref, dbco0_ref),
            (bc1_ref, xe1_ref, ge1_ref, y1_ref, dx1_ref, dbc1_ref, dbco1_ref),
        )
    ):
        e_all = e_scr[slot]
        r_all = r_scr[slot]
        db = dbc_ref[:, :LANES] + dot(xe_ref[...], r_all, NT)
        dc = dbc_ref[:, LANES:] + dot(ge_ref[...], e_all, NT)
        dbco_ref[:, :LANES] = db.astype(dbco_ref.dtype)
        dbco_ref[:, LANES:] = dc.astype(dbco_ref.dtype)
        ce_all = dot(bc_ref[:, LANES:], e_all)
        br_all = dot(bc_ref[:, :LANES], r_all)
        for h in range(heads):
            at = slice(h * LANES, (h + 1) * LANES)
            lane = lanes[slot] + h
            one = slice(lane, lane + 1)
            ce, br = ce_all[:, at], br_all[:, at]
            y = (y_ref[:, at] + grow_ref[:, one] * ce).astype(BF16)
            dx = (dx_ref[:, at] + (step_ref[:, one] * endw_ref[:, one]) * br).astype(BF16)
            if slot == 0:
                yo_ref[:, at] = y
                dxo_ref[:, at] = dx
                x = x0_ref[:, head_columns(own_at, h)].astype(F32)
                g = g0_ref[:, head_columns(own_at, h)].astype(F32)
            else:
                ys_ref[:, at] = y
                dxs_ref[:, at] = dx
                x = x1_ref[:, head_columns(columns[0], h)].astype(F32)
                g = g1_ref[:, head_columns(columns[1], h)].astype(F32)
            u_ref[:, one] = jnp.sum(g * ce, axis=1, keepdims=True)
            t_ref[:, one] = jnp.sum(x * br, axis=1, keepdims=True)
            re_ref[0:1, one] = jnp.sum(n_scr[slot][:, at], axis=1, keepdims=True)
        if slot == 0:
            final = aligned(own_at[0] + r * own_at[1], width)
            pairs = [(yo_ref, yf_ref.at[:, final]), (dxo_ref, dxf_ref.at[:, final])]
            copies = copy_all(pairs, sems)
    for copy in copies:
        copy.wait()


def steps_kernel(sig_ref, rate_ref, step_ref, grow_ref, endw_ref, *refs):
    count = 2 * GROUPS
    gys, dss, gxs = refs[:count], refs[count : 2 * count], refs[2 * count : 3 * count]
    refs = refs[3 * count :]
    us, ts, res = refs[:GROUPS], refs[GROUPS : 2 * GROUPS], refs[2 * GROUPS : 3 * GROUPS]
    dbc_ref, own_ref, send_ref, sums_ref = refs[3 * GROUPS :]

    def total(parts):
        value = parts[0][...]
        for a in parts[1:]:
            value = value + a[...]
        return value

    n = step_ref.shape[0]
    step = step_ref[...]
    ds = total(dss) + endw_ref[...] * total(ts)
    gy = total(gys) + grow_ref[...] * total(us)
    rate = rate_ref[0:1, :]
    last = lax.broadcasted_iota(jnp.int32, (n, LANES), 0) == n - 1
    dcum = gy - step * ds + jnp.where(last, total(res)[0:1, :], 0.0)
    lower = jnp.where(triangle(n), 1.0, 0.0).astype(F32)
    dlog = dot(lower, dcum, TN, precision=HIGHEST)
    draw = (ds - rate * dlog) * sig_ref[...]
    turned = draw.T
    heads = own_ref.shape[0]
    own_ref[...] = turned[:heads, :]
    both = split(turned[heads : 2 * heads, :])
    send_ref[0:n, :] = dbc_ref[...]
    send_ref[n:, :LANES] = both[:heads]
    send_ref[n:, LANES:] = both[heads:]
    sums_ref[0:1, :] = jnp.sum(draw, axis=0, keepdims=True)
    sums_ref[1:2, :] = jnp.sum(dlog * (-step * rate), axis=0, keepdims=True)
    sums_ref[2:3, :] = total(gxs)[0:1, :]
    sums_ref[3:8, :] = jnp.zeros((5, LANES), F32)


def conv_back_kernel(
    own_ref, ret_ref, kept_ref, cw_ref, heads_ref, grad_ref, raw_ref, rim_ref, message_ref, z_scr,
    sum_scr, grad_scr, raw_scr, sems,
):
    tokens = own_ref.shape[0]
    taps = cw_ref.shape[0]
    pre = kept_ref[HALO + tokens :, :]
    sig = jax.nn.sigmoid(pre)
    dconv = (own_ref[...] + ret_ref[0:tokens, :].astype(F32)) * sig * (1.0 + pre * (1.0 - sig))
    z_scr[...] = jnp.zeros_like(z_scr)
    z_scr[HALO : HALO + tokens, :] = dconv
    grad = cw_ref[0:1, :] * z_scr[taps - 1 : taps - 1 + tokens + HALO, :]
    for k in range(1, taps):
        grad = grad + cw_ref[k : k + 1, :] * z_scr[taps - 1 - k : taps - 1 - k + tokens + HALO, :]
    grad_scr[...] = grad[HALO:, :]
    raw = ret_ref[tokens:, :].astype(F32)
    raw_scr[...] = raw[:, :LANES] + raw[:, LANES:]
    copies = copy_all([(grad_scr, grad_ref), (raw_scr, raw_ref)], sems)
    rim_ref[...] = grad[HALO - 8 : HALO, :]
    first = HALO - taps + 1
    sum_scr[...] = jnp.zeros_like(sum_scr)
    for k in range(taps):
        sum_scr[k : k + 1, :] = jnp.sum(
            dconv * kept_ref[first + k : first + k + tokens, :], axis=0, keepdims=True
        )
    sum_scr[taps : taps + 1, :] = jnp.sum(dconv, axis=0, keepdims=True)
    sum_scr[5:8, aligned(side() * LANES, LANES)] = heads_ref[0:3, :]
    small = split(sum_scr[...])
    message_ref[0 : tokens + HALO, :] = grad.astype(BF16)
    message_ref[tokens + HALO :, :] = small
    for copy in copies:
        copy.wait()


def pack_kernel(layer_ref, halo_ref, keep_ref, send_ref, sems):
    half, _, rows = keep_ref.shape
    pairs = []
    for k in range(2 * half):
        out = keep_ref.at[k] if k < half else send_ref.at[k - half]
        at = peer_columns(k, rows)
        pairs.append((halo_ref.at[:, at], out.at[0:HALO, :]))
        pairs.append((layer_ref.at[:, at], out.at[HALO:, :]))
    for copy in copy_all(pairs, sems):
        copy.wait()


def relay_kernel(picks, *refs):
    out_ref = refs[-1]
    for j, (ref, at) in enumerate(picks):
        out_ref[j] = refs[ref][at]


def turn_kernel(picks, *refs):
    out_ref = refs[-1]
    parts = [refs[ref].at[at] for ref, at in picks]
    tokens = parts[0].shape[0] - HALO
    for k, part in enumerate(parts):
        out_ref[:, k * tokens : (k + 1) * tokens] = part[HALO:, :].T
    halos = jnp.concatenate([part[0:HALO, :] for part in parts], 0)
    out_ref[:, len(parts) * tokens :] = halos.T


def weight_kernel(count, left_ref, *refs):
    rights, out_ref = refs[:count], refs[count]
    tokens = (left_ref.shape[1] // count) - HALO
    right = jnp.concatenate(
        [a[HALO : HALO + tokens, :] for a in rights] + [a[0:HALO, :] for a in rights], 0
    )
    at = tokens + HALO
    both = jnp.zeros((16, right.shape[1]), F32)
    for a in rights:
        both += a[at : at + 16, :].astype(F32)
    small = split(both[0:8, :] + both[8:16, :])
    chunk = out_ref.shape[1] - 16
    for k in range(out_ref.shape[0]):
        term = dot(left_ref[k * chunk : (k + 1) * chunk, :], right)
        out_ref[k, 0:chunk, :] = term.astype(BF16)
        out_ref[k, chunk:, :] = small


def reduce_kernel(heads, terms_ref, total_ref, cw_ref, cb_ref, *head_refs):
    chunk = total_ref.shape[1]
    total = terms_ref[0].astype(F32)
    for k in range(1, terms_ref.shape[0]):
        total = total + terms_ref[k].astype(F32)
    for k in range(total_ref.shape[0]):
        total_ref[k] = total[0:chunk].astype(BF16)
    small = total[chunk : chunk + 8] + total[chunk + 8 :]
    taps = cw_ref.shape[0]
    cw_ref[...] = small[0:taps, :]
    cb_ref[...] = small[taps : taps + 1, :]
    for i, ref in enumerate(head_refs):
        row = small[5 + i : 6 + i, :]
        ref[:, :heads] = row[:, :heads] + row[:, heads : 2 * heads]
        row = row[:, LANES:]
        ref[:, heads:] = row[:, :heads] + row[:, heads : 2 * heads]


def place_rows_kernel(parts_ref, out_ref):
    chunk = parts_ref.shape[1]
    for k in range(parts_ref.shape[0]):
        out_ref[k * chunk : (k + 1) * chunk, :] = parts_ref[k].astype(F32)


def tokens_kernel(count, *refs):
    pieces = refs[:count]
    grad_ref, rim_ref, out_ref, w_scr, sems = refs[count:]
    copies = copy_all([(pieces[k], w_scr.at[k]) for k in range(count)], sems)
    tail = rim_ref.shape[0]
    own = grad_ref[...]
    g = jnp.concatenate([own[:-tail], own[-tail:] + rim_ref[...]], 0).astype(BF16)
    rows = pieces[0].shape[0]
    for k in range(count):
        copies[k].wait()
        out_ref[:, peer_columns(k, rows)] = dot(g, w_scr[k], NT).astype(BF16)


def join_kernel(*refs):
    own_ref, back_ref = refs[2:4]
    backs = refs[4 : 4 + 2 * GROUPS]
    y_ref, dx_ref, raw_ref, sems = refs[4 + 2 * GROUPS :]
    r = side()
    at = (1 - r) * (y_ref.shape[1] // 2)
    pairs = []
    for i in range(GROUPS):
        y, dx = backs[2 * i : 2 * i + 2]
        columns = aligned(at, y.shape[1])
        at += y.shape[1]
        pairs.append((y, y_ref.at[:, columns]))
        pairs.append((dx, dx_ref.at[:, columns]))
    copies = copy_all(pairs, sems)
    heads = own_ref.shape[0]
    raw_ref[pl.ds(pl.multiple_of(r * heads, 8), heads), :] = own_ref[...]
    raw_ref[pl.ds(pl.multiple_of((1 - r) * heads, 8), heads), :] = back_ref[...]
    for copy in copies:
        copy.wait()


def pinned(x):
    return pltpu.with_memory_space_constraint(x, pltpu.HBM)


def toggled(x, axis, bits):
    size = lax.axis_size(axis)
    return lax.ppermute(x, axis, [(i, i ^ bits) for i in range(size)])


def exchanged(x, axis):
    return lax.all_to_all(x, axis, 0, 0)


def after(x, *others):
    return lax.optimization_barrier((x, *others))[0]


def body(layer_in, w_bc, conv_w, conv_b, ssm_in, dt_raw, dt_bias, a_log, skip_scale, grad_out):
    ctx, fsdp = lax.axis_size("ctx"), lax.axis_size("fsdp")
    layer, x, g, dt = layer_in[0], ssm_in[0], grad_out[0], dt_raw[0].T
    tokens, width = x.shape
    total_heads = dt_bias.shape[0]
    heads = total_heads // 2
    half = width // 2
    counts = [heads // part for part in PARTS]
    starts = [sum(counts[:i]) for i in range(GROUPS)]
    widths = [half // part for part in PARTS]
    ats = [sum(widths[:i]) for i in range(GROUPS)]
    state = w_bc.shape[1] // 2
    taps = conv_w.shape[0]
    rows = w_bc.shape[0]
    chunk_rows = rows // ctx
    pairs = ctx // 2
    hops = pairs - 1
    square = shape((tokens, LANES), F32)
    flats = [shape((tokens, a), BF16) for a in widths]
    turned = shape((heads, tokens), F32)
    both_bc = [shape((tokens, 2 * state), F32)] * 2

    dt_back = toggled(dt, "ctx", 1)
    halo_send, *swaps = call(
        swap_kernel, "swap",
        [shape((HALO, layer.shape[1]), BF16), shape((tokens, half), BF16), flats[1], flats[1]], (),
        hbm=(pinned(layer), pinned(x), pinned(g)), scratch=[pltpu.SemaphoreType.DMA((5,))],
    )
    halo = lax.ppermute(halo_send, "ctx", [(i, i + 1) for i in range(ctx - 1)])
    swapped_first = toggled(after(swaps[0], dt_back), "ctx", 1)
    swapped_x = toggled(after(swaps[1], halo), "ctx", 1)

    step, cum, cumt, grow, endw, sig, rate = call(
        vectors_kernel, "vectors", [square] * 6 + [shape((8, LANES), F32)], (), dt, dt_back,
        dt_bias[None, :], a_log[None, :],
        scratch=[pltpu.VMEM((tokens, tokens), F32), pltpu.VMEM((8, LANES), F32)],
    )

    def source(slot, i):
        if slot == 0:
            return (ats[i], half), (ats[i], half), x, g
        if i == 0:
            return (0, 0), (widths[0], 0), swapped_first, swapped_first
        return (0, 0), (0, 0), swapped_x, swapped_g

    def scale(slot, i):
        x_at, g_at, xa, ga = source(slot, i)
        return call(
            functools.partial(scale_kernel, counts[i], slot * heads + starts[i], x_at, g_at), "scale",
            [flats[i]] * 2, (), xa, ga, step, grow, endw,
        )

    scaled = {(0, i): scale(0, i) for i in range(GROUPS)}
    scaled[1, 0] = scale(1, 0)
    def landing(count):
        return [
            pltpu.VMEM(layer.shape, BF16),
            pltpu.VMEM((count, *w_bc.shape), BF16),
            pltpu.SemaphoreType.DMA((1 + count,)),
        ]

    parts = shape((fsdp // 2, tokens + HALO, rows), BF16)
    packs = call(
        pack_kernel, "pack", [parts, parts], (), hbm=(pinned(layer), halo),
        scratch=[pltpu.SemaphoreType.DMA((2 * fsdp,))],
    )
    far_bit = fsdp // 2
    far = [toggled(w_bc, "fsdp", far_bit)]
    near = [w_bc]
    while len(near) < far_bit:
        near += [toggled(a, "fsdp", len(near)) for a in near]
    early = call(
        functools.partial(early_kernel, len(near)), "project_early",
        shape((tokens, 2 * state), F32), (), hbm=(pinned(layer), *near),
        scratch=landing(len(near)),
    )
    far[0] = after(
        far[0], early, halo, scaled[1, 0][0], *[scaled[0, i][0] for i in range(GROUPS)]
    )
    while len(far) < far_bit:
        far += [toggled(a, "fsdp", len(far)) for a in far]
    pieces = near + far
    layer_scr, w_scr, sems = landing(fsdp)
    kept, bc = call(
        functools.partial(project_kernel, len(near), fsdp), "project",
        [
            shape((2 * tokens + HALO, 2 * state), F32),
            shape((tokens, 2 * state), BF16),
        ],
        (), after(halo, packs[0]), early, conv_w, conv_b[None, :], hbm=(pinned(layer), *pieces),
        scratch=[layer_scr, w_scr, pltpu.VMEM((tokens + HALO, 2 * state), F32), sems],
    )
    bcs = [bc, toggled(bc, "ctx", 1)]
    def within(slot, i, *earlier):
        x_at, g_at, xa, ga = source(slot, i)
        return call(
            functools.partial(
                inside_kernel, counts[i], slot * heads + starts[i], starts[i], heads, x_at, g_at
            ),
            "inside",
            [shape((tokens, widths[i]), F32)] * 2 + [shape((tokens, tokens), F32), square, square]
            + [shape((8, LANES), F32)],
            (skip_scale,), xa, ga, after(bcs[slot], *earlier), step, cum, cumt,
        )

    order = [(slot, i) for slot in range(2) for i in range(GROUPS)]
    inside, states, received, earlier = {}, [], [], []
    inside[0, 0] = within(0, 0)
    swapped_g = toggled(after(swaps[2], bcs[1], inside[0, 0][2]), "ctx", 1)
    earlier = [inside[0, 0][2]]
    for i in range(GROUPS):
        lanes = (starts[i], heads + starts[i])
        if i:
            scaled[1, i] = scale(1, i)
        wide = shape((state, widths[i]), BF16)
        first, p, q, s_first, d_second, decays = call(
            functools.partial(states_kernel, counts[i], lanes), "states",
            [wide] * 5 + [shape((8, widths[i]), F32)],
            (), *bcs, *scaled[0, i], *scaled[1, i], after(grow, *earlier),
            scratch=[pltpu.VMEM((2, state, widths[i]), F32)] * 2
            + [pltpu.VMEM((2, 1, widths[i]), F32)],
        )
        states.append((decays, p, s_first, d_second, q))
        received.append([first])
        earlier = [first]
        if i == 0:
            for key in order[1:GROUPS]:
                inside[key] = within(*key, first)
                earlier.append(inside[key][2])
    waiting = order[GROUPS:]
    for hop in range(hops):
        moves = [(hop, hop + 1), (pairs - 1 - hop, pairs - 2 - hop)]
        moves = [(2 * a + i, 2 * b + i) for a, b in moves for i in range(2)]
        for i in range(GROUPS):
            value = received[i][-1]
            if hop:
                decays, p, _, _, q = states[i]
                value = call(
                    functools.partial(hop_kernel, hop), "hop", shape(value.shape, BF16), (),
                    after(value, *earlier), p, q, decays,
                )
                earlier = [value]
                if waiting and i == 0:
                    key = waiting.pop(0)
                    inside[key] = within(*key, *earlier)
                    earlier = [inside[key][2]]
            received[i].append(lax.ppermute(value, "ctx", moves))
    arrays = [packs[0]]
    at = {(0, k): (0, k) for k in range(fsdp // 2)}
    message, bit = packs[1], fsdp // 2
    sent = [(0, k) for k in range(bit, fsdp)]
    while bit:
        arrays.append(toggled(message, "fsdp", bit))
        for j, (source_bits, owner_bits) in enumerate(sent):
            at[source_bits ^ bit, owner_bits ^ bit] = (len(arrays) - 1, j)
        bit //= 2
        if bit:
            sent = [key for key in sorted(at) if key[1] & bit and key[1] < 2 * bit]
            message = call(
                functools.partial(relay_kernel, [at[key] for key in sent]), "relay",
                shape((len(sent), tokens + HALO, rows), BF16), (), after(arrays[0], received[-1][0]),
                *arrays[1:],
            )
    picks = [at[k, 0] for k in range(fsdp)]
    for key in waiting:
        inside[key] = within(*key, *earlier)
    dbcs = call(inside_bc_kernel, "inside_bc", both_bc, (), *bcs, *[inside[key][2] for key in order])

    full = shape((tokens, width), BF16)
    finals, sends, us, ts, res = (), [], [], [], []
    for i in range(GROUPS):
        last = i == GROUPS - 1
        own_at, _, xa, ga = source(0, i)
        x_at, g_at, xb, gb = source(1, i)
        if i == 1:
            left = call(
                functools.partial(turn_kernel, picks), "turn",
                shape((rows, fsdp * (tokens + HALO)), BF16), (), after(arrays[0], *sends), *arrays[1:],
            )
        lanes = (starts[i], heads + starts[i])
        y, dx, y_send, dx_send, dbc_own, dbc_other, u, t, re = call(
            functools.partial(
                across_kernel, counts[i], lanes, hops, len(finals) // 2, own_at, (x_at, g_at)
            ),
            "across",
            [full, full, flats[i], flats[i]]
            + [both_bc[0], shape((tokens, 2 * state), BF16 if last else F32)]
            + [square, square, shape((8, LANES), F32)],
            (), xa, ga, xb, gb, after(bcs[0], left) if i == 1 else bcs[0], bcs[1], *scaled[0, i],
            *scaled[1, i], step, grow, endw,
            *states[i][:4], *inside[0, i][:2], *inside[1, i][:2], *dbcs, *received[i][1:],
            hbm=finals, hbm_outs=2, aliases={0: 0, 1: 1} if finals else None,
            scratch=[pltpu.VMEM((state, widths[i]), BF16)] * 2
            + [pltpu.VMEM((2, state, widths[i]), BF16)] * 2
            + [pltpu.VMEM((2, 1, widths[i]), F32)] + [pltpu.VMEM((tokens, widths[i]), BF16)] * 2
            + [pltpu.SemaphoreType.DMA((2,))],
        )
        finals, dbcs = (y, dx), (dbc_own, dbc_other)
        sends += [y_send, dx_send]
        us.append(u)
        ts.append(t)
        res.append(re)

    raw_own, dbc_send, head_sums = call(
        steps_kernel, "steps",
        [turned, shape((tokens + heads, 2 * state), BF16), shape((8, LANES), F32)], (),
        sig, rate, step, grow, endw, *[inside[key][j] for j in (3, 4, 5) for key in order],
        *us, *ts, *res, dbcs[1],
    )
    dbc_ret = toggled(dbc_send, "ctx", 1)
    backs = [toggled(sends[0], "ctx", 1)]
    grad, raw_back, rim_send, message = call(
        conv_back_kernel, "conv_back",
        [
            shape((tokens, 2 * state), F32),
            turned,
            shape((8, 2 * state), F32),
            shape((tokens + HALO + 16, 2 * state), BF16),
        ],
        (), after(dbcs[0], *backs), dbc_ret, kept, conv_w, head_sums, hbm_outs=2,
        scratch=[
            pltpu.VMEM((tokens + 2 * HALO, 2 * state), F32),
            pltpu.VMEM((8, 2 * state), F32),
            pltpu.VMEM((tokens, 2 * state), F32),
            pltpu.VMEM(turned.shape, F32),
            pltpu.SemaphoreType.DMA((2,)),
        ],
    )
    rim = lax.ppermute(rim_send, "ctx", [(i + 1, i) for i in range(ctx - 1)])
    backs.append(toggled(after(sends[1], dbc_ret), "ctx", 1))

    rights = [message] + [toggled(message, "fsdp", k) for k in range(fsdp - 1, 0, -1)][::-1]
    terms = call(
        functools.partial(weight_kernel, fsdp), "weight",
        shape((ctx, chunk_rows + 16, 2 * state), BF16), (), left, after(message, rim, *backs), *rights[1:],
    )
    backs += [toggled(after(a, terms), "ctx", 1) for a in sends[2:]]
    total, grad_cw, grad_cb, *per_head = call(
        functools.partial(reduce_kernel, heads), "reduce",
        [
            shape((ctx, chunk_rows, 2 * state), BF16),
            shape((taps, 2 * state), F32),
            shape((1, 2 * state), F32),
        ]
        + [shape((1, total_heads), F32)] * 3,
        (), after(exchanged(terms, "ctx"), *backs[:-1]),
    )
    grad_weight = call(
        place_rows_kernel, "place_rows", shape((rows, 2 * state), F32), (), exchanged(total, "ctx")
    )
    grad_tokens = call(
        functools.partial(tokens_kernel, fsdp), "grad_tokens", shape((tokens, fsdp * rows), BF16),
        (), after(grad, total), rim, hbm=pieces,
        scratch=[pltpu.VMEM((fsdp, *w_bc.shape), BF16), pltpu.SemaphoreType.DMA((fsdp,))],
    )
    ssm_out, grad_values, grad_raw = call(
        join_kernel, "join", [full, full, shape((total_heads, tokens), F32)],
        (), raw_own, raw_back, *backs, hbm=finals, hbm_outs=2,
        aliases={0: 0, 1: 1}, scratch=[pltpu.SemaphoreType.DMA((2 * GROUPS,))],
    )
    return (
        ssm_out[None],
        grad_values[None],
        grad_tokens[None],
        grad_raw.T[None],
        grad_weight,
        grad_cw,
        grad_cb[0],
        *[a[0] for a in per_head],
    )


def solution(mesh):
    tokens = P("fsdp", "ctx", None)
    in_specs = (tokens, P("fsdp", None), P(), P(), tokens, tokens, P(), P(), P(), tokens)
    out_specs = (tokens, tokens, tokens, tokens, P("fsdp", None), P(), P(), P(), P(), P())
    return jax.shard_map(body, mesh=mesh, in_specs=in_specs, out_specs=out_specs, check_vma=False)
```

```python
import functools

import jax
import jax.numpy as jnp
from jax import lax
from jax.experimental import pallas as pl
from jax.experimental.pallas import tpu as pltpu
from jax.sharding import PartitionSpec as P

F32 = jnp.float32
BF16 = jnp.bfloat16
LANES = 128
HALO = 16
PARTS = (2, 2)
GROUPS = len(PARTS)
LIMIT = 16 * 1024 * 1024
HIGHEST = lax.Precision.HIGHEST
TN = ((0,), (0,))
NT = ((1,), (1,))


def dot(a, b, dims=((1,), (0,)), precision=None):
    return lax.dot_general(
        a, b, (dims, ((), ())), precision=precision, preferred_element_type=F32
    )


def shape(dims, dtype):
    return jax.ShapeDtypeStruct(dims, dtype)


def call(kernel, name, out_shape, smem, *operands, hbm=(), hbm_outs=0, scratch=(), aliases=None):
    single = not isinstance(out_shape, list)
    outs = [out_shape] if single else out_shape
    spaces = [pltpu.SMEM] * len(smem) + [pl.ANY] * len(hbm) + [pltpu.VMEM] * len(operands)
    out_spaces = [pltpu.HBM] * hbm_outs + [pltpu.VMEM] * (len(outs) - hbm_outs)
    result = pl.pallas_call(
        kernel,
        out_shape=outs,
        in_specs=[pl.BlockSpec(memory_space=a) for a in spaces],
        out_specs=[pl.BlockSpec(memory_space=a) for a in out_spaces],
        scratch_shapes=list(scratch),
        compiler_params=pltpu.CompilerParams(vmem_limit_bytes=LIMIT),
        input_output_aliases=aliases or {},
        name=name,
    )(*smem, *hbm, *operands)
    return result[0] if single else result


def copy_all(pairs, sems):
    copies = [pltpu.make_async_copy(a, b, sems.at[i]) for i, (a, b) in enumerate(pairs)]
    for copy in copies:
        copy.start()
    return copies


def side():
    return lax.rem(lax.axis_index("ctx"), 2)


def place():
    return lax.div(lax.axis_index("ctx"), 2)


def peer_columns(k, rows):
    return aligned((lax.axis_index("fsdp") ^ k) * rows, rows)


def aligned(at, size):
    return pl.ds(pl.multiple_of(at, LANES), size)


def triangle(n):
    rows = lax.broadcasted_iota(jnp.int32, (n, n), 0)
    cols = lax.broadcasted_iota(jnp.int32, (n, n), 1)
    return rows >= cols


def split(value):
    high = value.astype(BF16).astype(F32)
    return jnp.concatenate([high, value - high], 0).astype(BF16)


def swap_kernel(layer_ref, x_ref, g_ref, halo_ref, first_ref, x_out_ref, g_out_ref, sems):
    width = x_out_ref.shape[1]
    tokens = layer_ref.shape[0]
    base = (1 - side()) * (2 * width)
    pairs = [
        (layer_ref.at[tokens - HALO : tokens, :], halo_ref),
        (x_ref.at[:, aligned(base, width)], first_ref.at[:, :width]),
        (g_ref.at[:, aligned(base, width)], first_ref.at[:, width:]),
        (x_ref.at[:, aligned(base + width, width)], x_out_ref),
        (g_ref.at[:, aligned(base + width, width)], g_out_ref),
    ]
    for copy in copy_all(pairs, sems):
        copy.wait()


def vectors_kernel(
    dt_ref, back_ref, bias_ref, alog_ref, step_ref, cum_ref, cumt_ref, grow_ref, endw_ref, sig_ref,
    rate_ref, turned, rows,
):
    n = back_ref.shape[1]
    heads = back_ref.shape[0] // 2
    r = side()
    mine = pl.ds(pl.multiple_of(r * heads, 8), heads)
    turned[...] = jnp.zeros_like(turned)
    turned[0:heads, :] = dt_ref[mine, :]
    turned[heads : 2 * heads, :] = back_ref[mine, :]
    rows[...] = jnp.zeros_like(rows)
    for i, ref in enumerate((bias_ref, alog_ref)):
        half = jnp.where(r == 0, ref[:, :heads], ref[:, heads:])
        rows[i : i + 1, 0:heads] = half
        rows[i : i + 1, heads : 2 * heads] = half
    raw = turned[...].T + rows[0:1, :]
    step = jnp.maximum(raw, 0.0) + jnp.log1p(jnp.exp(-jnp.abs(raw)))
    rate = jnp.exp(rows[1:2, :])
    log_decay = -step * rate
    lower = jnp.where(triangle(n), 1.0, 0.0).astype(F32)
    cum = dot(lower, log_decay, precision=HIGHEST)
    step_ref[...] = step
    cum_ref[...] = cum
    cumt_ref[...] = cum.T
    grow_ref[...] = jnp.exp(cum)
    endw_ref[...] = jnp.exp(cum[n - 1 : n, :] - cum)
    sig_ref[...] = jax.nn.sigmoid(raw)
    rate_ref[...] = jnp.broadcast_to(rate, rate_ref.shape)


def early_kernel(count, layer_ref, *refs):
    pieces = refs[:count]
    out_ref, layer_scr, w_scr, sems = refs[count:]
    copies = copy_all(
        [(layer_ref, layer_scr)] + [(pieces[k], w_scr.at[k]) for k in range(count)], sems
    )
    copies[0].wait()
    total = 0.0
    for k in range(count):
        copies[k + 1].wait()
        total += dot(layer_scr[:, peer_columns(k, w_scr.shape[1])], w_scr[k])
    out_ref[...] = total


def project_kernel(done, count, layer_ref, *refs):
    pieces = refs[:count]
    halo_ref, early_ref, cw_ref, cb_ref, kept_ref, bc_ref, layer_scr, w_scr, ext_scr, sems = refs[count:]
    copies = copy_all(
        [(layer_ref, layer_scr)] + [(pieces[k], w_scr.at[k]) for k in range(count)], sems
    )
    taps = cw_ref.shape[0]
    tokens = layer_ref.shape[0]
    copies[0].wait()
    total, rim = early_ref[...], 0.0
    for k in range(count):
        copies[k + 1].wait()
        at = peer_columns(k, w_scr.shape[1])
        rim += dot(halo_ref[:, at], w_scr[k])
        if k >= done:
            total += dot(layer_scr[:, at], w_scr[k])
    ext_scr[0:HALO, :] = rim
    ext_scr[HALO:, :] = total
    kept_ref[0 : HALO + tokens, :] = ext_scr[...]
    first = HALO - taps + 1
    pre = cb_ref[...] + cw_ref[0:1, :] * ext_scr[first : first + tokens, :]
    for k in range(1, taps):
        pre = pre + cw_ref[k : k + 1, :] * ext_scr[first + k : first + k + tokens, :]
    kept_ref[HALO + tokens :, :] = pre
    bc_ref[...] = (pre * jax.nn.sigmoid(pre)).astype(BF16)


def head_columns(at, h):
    first, more = at
    return aligned(first + side() * more + h * LANES, LANES)


def scale_kernel(heads, lane, x_at, g_at, x_ref, g_ref, step_ref, grow_ref, endw_ref, xe_ref, ge_ref):
    for h in range(heads):
        at = slice(h * LANES, (h + 1) * LANES)
        one = slice(lane + h, lane + h + 1)
        x = x_ref[:, head_columns(x_at, h)].astype(F32)
        g = g_ref[:, head_columns(g_at, h)].astype(F32)
        xe_ref[:, at] = (x * (step_ref[:, one] * endw_ref[:, one])).astype(BF16)
        ge_ref[:, at] = (g * grow_ref[:, one]).astype(BF16)


def widen(row, lane, heads):
    return jnp.concatenate(
        [jnp.broadcast_to(row[:, lane + h : lane + h + 1], (1, LANES)) for h in range(heads)], 1
    )


def states_kernel(
    heads, lanes, bc0_ref, bc1_ref, xe0_ref, ge0_ref, xe1_ref, ge1_ref, grow_ref,
    first_ref, p_ref, q_ref, sf_ref, ds_ref, dec_ref, s_scr, d_scr, dec_scr,
):
    n = grow_ref.shape[0]
    r = side()
    for slot, (bc_ref, xe_ref, ge_ref) in enumerate(
        ((bc0_ref, xe0_ref, ge0_ref), (bc1_ref, xe1_ref, ge1_ref))
    ):
        s_scr[slot] = dot(bc_ref[:, :LANES], xe_ref[...], TN)
        d_scr[slot] = dot(bc_ref[:, LANES:], ge_ref[...], TN)
        dec_scr[slot] = widen(grow_ref[n - 1 : n, :], lanes[slot], heads)
    dec_first, dec_second = dec_scr[r], dec_scr[1 - r]
    s_first, d_second = s_scr[r], d_scr[1 - r]
    sf_ref[...] = s_first.astype(BF16)
    ds_ref[...] = d_second.astype(BF16)
    p = (dec_second * s_first + s_scr[1 - r]).astype(BF16)
    q = (dec_first * d_second + d_scr[r]).astype(BF16)
    p_ref[...] = p
    q_ref[...] = q

    @pl.when(place() == 0)
    def _():
        first_ref[...] = p

    @pl.when(place() != 0)
    def _():
        first_ref[...] = q

    dec_ref[0:1, :] = dec_first * dec_second
    dec_ref[1:2, :] = dec_first
    dec_ref[2:3, :] = dec_second
    dec_ref[3:8, :] = jnp.zeros((5, dec_first.shape[1]), F32)


def hop_kernel(hop, received_ref, p_ref, q_ref, dec_ref, out_ref):
    carried = dec_ref[0:1, :] * received_ref[...].astype(F32)

    @pl.when(place() == hop)
    def _():
        out_ref[...] = (carried + p_ref[...].astype(F32)).astype(BF16)

    @pl.when(place() != hop)
    def _():
        out_ref[...] = (carried + q_ref[...].astype(F32)).astype(BF16)


def inside_kernel(
    heads, lane, skip_at, all_heads, x_at, g_at, skip_ref, x_ref, g_ref, bc_ref, step_ref, cum_ref,
    cumt_ref, y_ref, dx_ref, dscores_ref, gy_ref, ds_ref, gx_ref,
):
    n = step_ref.shape[0]
    mask = triangle(n)
    scores = jnp.where(mask, dot(bc_ref[:, LANES:], bc_ref[:, :LANES], NT), 0.0)
    gy_ref[...] = jnp.zeros_like(gy_ref)
    ds_ref[...] = jnp.zeros_like(ds_ref)
    gx_ref[...] = jnp.zeros_like(gx_ref)
    dscores = jnp.zeros((n, n), F32)
    for h in range(heads):
        at = slice(h * LANES, (h + 1) * LANES)
        one = slice(lane + h, lane + h + 1)
        step = step_ref[:, one]
        gap = cum_ref[:, one] - cumt_ref[one, :]
        decay = jnp.exp(jnp.where(mask, gap, 0.0))
        mixing = (scores * decay).astype(BF16)
        x = x_ref[:, head_columns(x_at, h)].astype(F32)
        g = g_ref[:, head_columns(g_at, h)]
        gf = g.astype(F32)
        xs = (x * step).astype(BF16)
        skip = skip_ref[side() * all_heads + skip_at + h]
        y = dot(mixing, xs)
        dxs = dot(mixing, g, TN)
        dscores += dot(g, xs, NT) * decay
        y_ref[:, at] = y + skip * x
        dx_ref[:, at] = dxs * step + skip * gf
        gy_ref[:, one] = jnp.sum(gf * y, axis=1, keepdims=True)
        ds_ref[:, one] = jnp.sum(x * dxs, axis=1, keepdims=True)
        gx_ref[0:1, one] = jnp.sum(jnp.sum(gf * x, axis=0, keepdims=True), axis=1, keepdims=True)
    dscores_ref[...] = jnp.where(mask, dscores, 0.0)


def inside_bc_kernel(bc0_ref, bc1_ref, *refs):
    parts, outs = refs[: 2 * GROUPS], refs[2 * GROUPS :]
    for slot, bc_ref in enumerate((bc0_ref, bc1_ref)):
        total = parts[slot * GROUPS][...]
        for i in range(1, GROUPS):
            total = total + parts[slot * GROUPS + i][...]
        ds = total.astype(BF16)
        outs[slot][:, :LANES] = dot(ds, bc_ref[:, LANES:], TN)
        outs[slot][:, LANES:] = dot(ds, bc_ref[:, :LANES])


def across_kernel(heads, lanes, hops, filled, own_at, columns, *refs):
    refs = refs[2 * filled :]
    across_block(heads, lanes, hops, own_at, columns, *refs)


def across_block(
    heads, lanes, hops, own_at, columns, x0_ref, g0_ref, x1_ref, g1_ref, bc0_ref, bc1_ref, xe0_ref,
    ge0_ref, xe1_ref, ge1_ref, step_ref, grow_ref, endw_ref, dec_ref, p_ref, sf_ref, ds_ref,
    y0_ref, dx0_ref, y1_ref, dx1_ref, dbc0_ref, dbc1_ref, *refs
):
    received = refs[:hops]
    (
        yf_ref, dxf_ref, ys_ref, dxs_ref, dbco0_ref, dbco1_ref, u_ref, t_ref, re_ref,
        e_in, r_in, e_scr, r_scr, n_scr, yo_ref, dxo_ref, sems,
    ) = refs[hops:]
    r, pos = side(), place()
    width = yo_ref.shape[1]
    e_in[...] = jnp.zeros_like(e_in)
    r_in[...] = jnp.zeros_like(r_in)
    for k in range(hops):

        @pl.when(pos - 1 == k)
        def _(k=k):
            e_in[...] = received[k][...]

        @pl.when(hops - 1 - pos == k)
        def _(k=k):
            r_in[...] = received[k][...]

    dec_pair, dec_first, dec_second = dec_ref[0:1, :], dec_ref[1:2, :], dec_ref[2:3, :]
    entering = e_in[...].astype(F32)
    later = r_in[...].astype(F32)
    middle = dec_first * entering + sf_ref[...].astype(F32)
    leaving = dec_pair * entering + p_ref[...].astype(F32)
    earlier = dec_second * later + ds_ref[...].astype(F32)
    e_scr[r] = e_in[...]
    e_scr[1 - r] = middle.astype(BF16)
    r_scr[1 - r] = r_in[...]
    r_scr[r] = earlier.astype(BF16)
    n_scr[1 - r] = jnp.sum(later * leaving, axis=0, keepdims=True)
    n_scr[r] = jnp.sum(earlier * middle, axis=0, keepdims=True)

    u_ref[...] = jnp.zeros_like(u_ref)
    t_ref[...] = jnp.zeros_like(t_ref)
    re_ref[...] = jnp.zeros_like(re_ref)
    for slot, (bc_ref, xe_ref, ge_ref, y_ref, dx_ref, dbc_ref, dbco_ref) in enumerate(
        (
            (bc0_ref, xe0_ref, ge0_ref, y0_ref, dx0_ref, dbc0_ref, dbco0_ref),
            (bc1_ref, xe1_ref, ge1_ref, y1_ref, dx1_ref, dbc1_ref, dbco1_ref),
        )
    ):
        e_all = e_scr[slot]
        r_all = r_scr[slot]
        db = dbc_ref[:, :LANES] + dot(xe_ref[...], r_all, NT)
        dc = dbc_ref[:, LANES:] + dot(ge_ref[...], e_all, NT)
        dbco_ref[:, :LANES] = db.astype(dbco_ref.dtype)
        dbco_ref[:, LANES:] = dc.astype(dbco_ref.dtype)
        ce_all = dot(bc_ref[:, LANES:], e_all)
        br_all = dot(bc_ref[:, :LANES], r_all)
        for h in range(heads):
            at = slice(h * LANES, (h + 1) * LANES)
            lane = lanes[slot] + h
            one = slice(lane, lane + 1)
            ce, br = ce_all[:, at], br_all[:, at]
            y = (y_ref[:, at] + grow_ref[:, one] * ce).astype(BF16)
            dx = (dx_ref[:, at] + (step_ref[:, one] * endw_ref[:, one]) * br).astype(BF16)
            if slot == 0:
                yo_ref[:, at] = y
                dxo_ref[:, at] = dx
                x = x0_ref[:, head_columns(own_at, h)].astype(F32)
                g = g0_ref[:, head_columns(own_at, h)].astype(F32)
            else:
                ys_ref[:, at] = y
                dxs_ref[:, at] = dx
                x = x1_ref[:, head_columns(columns[0], h)].astype(F32)
                g = g1_ref[:, head_columns(columns[1], h)].astype(F32)
            u_ref[:, one] = jnp.sum(g * ce, axis=1, keepdims=True)
            t_ref[:, one] = jnp.sum(x * br, axis=1, keepdims=True)
            re_ref[0:1, one] = jnp.sum(n_scr[slot][:, at], axis=1, keepdims=True)
        if slot == 0:
            final = aligned(own_at[0] + r * own_at[1], width)
            pairs = [(yo_ref, yf_ref.at[:, final]), (dxo_ref, dxf_ref.at[:, final])]
            copies = copy_all(pairs, sems)
    for copy in copies:
        copy.wait()


def steps_kernel(sig_ref, rate_ref, step_ref, grow_ref, endw_ref, *refs):
    count = 2 * GROUPS
    gys, dss, gxs = refs[:count], refs[count : 2 * count], refs[2 * count : 3 * count]
    refs = refs[3 * count :]
    us, ts, res = refs[:GROUPS], refs[GROUPS : 2 * GROUPS], refs[2 * GROUPS : 3 * GROUPS]
    dbc_ref, own_ref, send_ref, sums_ref = refs[3 * GROUPS :]

    def total(parts):
        value = parts[0][...]
        for a in parts[1:]:
            value = value + a[...]
        return value

    n = step_ref.shape[0]
    step = step_ref[...]
    ds = total(dss) + endw_ref[...] * total(ts)
    gy = total(gys) + grow_ref[...] * total(us)
    rate = rate_ref[0:1, :]
    last = lax.broadcasted_iota(jnp.int32, (n, LANES), 0) == n - 1
    dcum = gy - step * ds + jnp.where(last, total(res)[0:1, :], 0.0)
    lower = jnp.where(triangle(n), 1.0, 0.0).astype(F32)
    dlog = dot(lower, dcum, TN, precision=HIGHEST)
    draw = (ds - rate * dlog) * sig_ref[...]
    turned = draw.T
    heads = own_ref.shape[0]
    own_ref[...] = turned[:heads, :]
    both = split(turned[heads : 2 * heads, :])
    send_ref[0:n, :] = dbc_ref[...]
    send_ref[n:, :LANES] = both[:heads]
    send_ref[n:, LANES:] = both[heads:]
    sums_ref[0:1, :] = jnp.sum(draw, axis=0, keepdims=True)
    sums_ref[1:2, :] = jnp.sum(dlog * (-step * rate), axis=0, keepdims=True)
    sums_ref[2:3, :] = total(gxs)[0:1, :]
    sums_ref[3:8, :] = jnp.zeros((5, LANES), F32)


def conv_back_kernel(
    own_ref, ret_ref, kept_ref, cw_ref, heads_ref, grad_ref, raw_ref, rim_ref, message_ref, z_scr,
    sum_scr, grad_scr, raw_scr, sems,
):
    tokens = own_ref.shape[0]
    taps = cw_ref.shape[0]
    pre = kept_ref[HALO + tokens :, :]
    sig = jax.nn.sigmoid(pre)
    dconv = (own_ref[...] + ret_ref[0:tokens, :].astype(F32)) * sig * (1.0 + pre * (1.0 - sig))
    z_scr[...] = jnp.zeros_like(z_scr)
    z_scr[HALO : HALO + tokens, :] = dconv
    grad = cw_ref[0:1, :] * z_scr[taps - 1 : taps - 1 + tokens + HALO, :]
    for k in range(1, taps):
        grad = grad + cw_ref[k : k + 1, :] * z_scr[taps - 1 - k : taps - 1 - k + tokens + HALO, :]
    grad_scr[...] = grad[HALO:, :]
    raw = ret_ref[tokens:, :].astype(F32)
    raw_scr[...] = raw[:, :LANES] + raw[:, LANES:]
    copies = copy_all([(grad_scr, grad_ref), (raw_scr, raw_ref)], sems)
    rim_ref[...] = grad[HALO - 8 : HALO, :]
    first = HALO - taps + 1
    sum_scr[...] = jnp.zeros_like(sum_scr)
    for k in range(taps):
        sum_scr[k : k + 1, :] = jnp.sum(
            dconv * kept_ref[first + k : first + k + tokens, :], axis=0, keepdims=True
        )
    sum_scr[taps : taps + 1, :] = jnp.sum(dconv, axis=0, keepdims=True)
    sum_scr[5:8, aligned(side() * LANES, LANES)] = heads_ref[0:3, :]
    small = split(sum_scr[...])
    message_ref[0 : tokens + HALO, :] = grad.astype(BF16)
    message_ref[tokens + HALO :, :] = small
    for copy in copies:
        copy.wait()


def pack_kernel(layer_ref, halo_ref, keep_ref, send_ref, sems):
    half, _, rows = keep_ref.shape
    pairs = []
    for k in range(2 * half):
        out = keep_ref.at[k] if k < half else send_ref.at[k - half]
        at = peer_columns(k, rows)
        pairs.append((halo_ref.at[:, at], out.at[0:HALO, :]))
        pairs.append((layer_ref.at[:, at], out.at[HALO:, :]))
    for copy in copy_all(pairs, sems):
        copy.wait()


def relay_kernel(picks, *refs):
    out_ref = refs[-1]
    for j, (ref, at) in enumerate(picks):
        out_ref[j] = refs[ref][at]


def turn_kernel(picks, *refs):
    out_ref = refs[-1]
    parts = [refs[ref].at[at] for ref, at in picks]
    tokens = parts[0].shape[0] - HALO
    for k, part in enumerate(parts):
        out_ref[:, k * tokens : (k + 1) * tokens] = part[HALO:, :].T
    halos = jnp.concatenate([part[0:HALO, :] for part in parts], 0)
    out_ref[:, len(parts) * tokens :] = halos.T


def weight_kernel(count, left_ref, *refs):
    rights, out_ref = refs[:count], refs[count]
    tokens = (left_ref.shape[1] // count) - HALO
    right = jnp.concatenate(
        [a[HALO : HALO + tokens, :] for a in rights] + [a[0:HALO, :] for a in rights], 0
    )
    at = tokens + HALO
    both = jnp.zeros((16, right.shape[1]), F32)
    for a in rights:
        both += a[at : at + 16, :].astype(F32)
    small = split(both[0:8, :] + both[8:16, :])
    chunk = out_ref.shape[1] - 16
    for k in range(out_ref.shape[0]):
        term = dot(left_ref[k * chunk : (k + 1) * chunk, :], right)
        out_ref[k, 0:chunk, :] = term.astype(BF16)
        out_ref[k, chunk:, :] = small


def reduce_kernel(heads, terms_ref, total_ref, cw_ref, cb_ref, *head_refs):
    chunk = total_ref.shape[1]
    total = terms_ref[0].astype(F32)
    for k in range(1, terms_ref.shape[0]):
        total = total + terms_ref[k].astype(F32)
    for k in range(total_ref.shape[0]):
        total_ref[k] = total[0:chunk].astype(BF16)
    small = total[chunk : chunk + 8] + total[chunk + 8 :]
    taps = cw_ref.shape[0]
    cw_ref[...] = small[0:taps, :]
    cb_ref[...] = small[taps : taps + 1, :]
    for i, ref in enumerate(head_refs):
        row = small[5 + i : 6 + i, :]
        ref[:, :heads] = row[:, :heads] + row[:, heads : 2 * heads]
        row = row[:, LANES:]
        ref[:, heads:] = row[:, :heads] + row[:, heads : 2 * heads]


def place_rows_kernel(parts_ref, out_ref):
    chunk = parts_ref.shape[1]
    for k in range(parts_ref.shape[0]):
        out_ref[k * chunk : (k + 1) * chunk, :] = parts_ref[k].astype(F32)


def tokens_kernel(count, *refs):
    pieces = refs[:count]
    grad_ref, rim_ref, out_ref, w_scr, sems = refs[count:]
    copies = copy_all([(pieces[k], w_scr.at[k]) for k in range(count)], sems)
    tail = rim_ref.shape[0]
    own = grad_ref[...]
    g = jnp.concatenate([own[:-tail], own[-tail:] + rim_ref[...]], 0).astype(BF16)
    rows = pieces[0].shape[0]
    for k in range(count):
        copies[k].wait()
        out_ref[:, peer_columns(k, rows)] = dot(g, w_scr[k], NT).astype(BF16)


def join_kernel(targets, *refs):
    blocks = refs[2 : 2 + len(targets)]
    *outs, sems = refs[2 + len(targets) :]
    half = outs[0].shape[1] // 2
    base = (1 - side()) * half
    pairs = []
    for block, (which, at) in zip(blocks, targets):
        pairs.append((block, outs[which].at[:, aligned(base + at, block.shape[1])]))
    for copy in copy_all(pairs, sems):
        copy.wait()


def join_steps_kernel(own_ref, back_ref, out_ref):
    heads = own_ref.shape[0]
    r = side()
    out_ref[pl.ds(pl.multiple_of(r * heads, 8), heads), :] = own_ref[...]
    out_ref[pl.ds(pl.multiple_of((1 - r) * heads, 8), heads), :] = back_ref[...]


def pinned(x):
    return pltpu.with_memory_space_constraint(x, pltpu.HBM)


def toggled(x, axis, bits):
    size = lax.axis_size(axis)
    return lax.ppermute(x, axis, [(i, i ^ bits) for i in range(size)])


def exchanged(x, axis):
    return lax.all_to_all(x, axis, 0, 0)


def after(x, *others):
    return lax.optimization_barrier((x, *others))[0]


def body(layer_in, w_bc, conv_w, conv_b, ssm_in, dt_raw, dt_bias, a_log, skip_scale, grad_out):
    ctx, fsdp = lax.axis_size("ctx"), lax.axis_size("fsdp")
    layer, x, g, dt = layer_in[0], ssm_in[0], grad_out[0], dt_raw[0].T
    tokens, width = x.shape
    total_heads = dt_bias.shape[0]
    heads = total_heads // 2
    half = width // 2
    counts = [heads // part for part in PARTS]
    starts = [sum(counts[:i]) for i in range(GROUPS)]
    widths = [half // part for part in PARTS]
    ats = [sum(widths[:i]) for i in range(GROUPS)]
    state = w_bc.shape[1] // 2
    taps = conv_w.shape[0]
    rows = w_bc.shape[0]
    chunk_rows = rows // ctx
    pairs = ctx // 2
    hops = pairs - 1
    square = shape((tokens, LANES), F32)
    flats = [shape((tokens, a), BF16) for a in widths]
    turned = shape((heads, tokens), F32)
    both_bc = [shape((tokens, 2 * state), F32)] * 2

    dt_back = toggled(dt, "ctx", 1)
    halo_send, *swaps = call(
        swap_kernel, "swap",
        [shape((HALO, layer.shape[1]), BF16), shape((tokens, half), BF16), flats[1], flats[1]], (),
        hbm=(pinned(layer), pinned(x), pinned(g)), scratch=[pltpu.SemaphoreType.DMA((5,))],
    )
    halo = lax.ppermute(halo_send, "ctx", [(i, i + 1) for i in range(ctx - 1)])
    swapped_first = toggled(after(swaps[0], dt_back), "ctx", 1)
    swapped_x = toggled(after(swaps[1], halo), "ctx", 1)

    step, cum, cumt, grow, endw, sig, rate = call(
        vectors_kernel, "vectors", [square] * 6 + [shape((8, LANES), F32)], (), dt, dt_back,
        dt_bias[None, :], a_log[None, :],
        scratch=[pltpu.VMEM((tokens, tokens), F32), pltpu.VMEM((8, LANES), F32)],
    )

    def source(slot, i):
        if slot == 0:
            return (ats[i], half), (ats[i], half), x, g
        if i == 0:
            return (0, 0), (widths[0], 0), swapped_first, swapped_first
        return (0, 0), (0, 0), swapped_x, swapped_g

    def scale(slot, i):
        x_at, g_at, xa, ga = source(slot, i)
        return call(
            functools.partial(scale_kernel, counts[i], slot * heads + starts[i], x_at, g_at), "scale",
            [flats[i]] * 2, (), xa, ga, step, grow, endw,
        )

    scaled = {(0, i): scale(0, i) for i in range(GROUPS)}
    scaled[1, 0] = scale(1, 0)
    def landing(count):
        return [
            pltpu.VMEM(layer.shape, BF16),
            pltpu.VMEM((count, *w_bc.shape), BF16),
            pltpu.SemaphoreType.DMA((1 + count,)),
        ]

    parts = shape((fsdp // 2, tokens + HALO, rows), BF16)
    packs = call(
        pack_kernel, "pack", [parts, parts], (), hbm=(pinned(layer), halo),
        scratch=[pltpu.SemaphoreType.DMA((2 * fsdp,))],
    )
    far_bit = fsdp // 2
    far = [toggled(w_bc, "fsdp", far_bit)]
    near = [w_bc]
    while len(near) < far_bit:
        near += [toggled(a, "fsdp", len(near)) for a in near]
    early = call(
        functools.partial(early_kernel, len(near)), "project_early",
        shape((tokens, 2 * state), F32), (), hbm=(pinned(layer), *near),
        scratch=landing(len(near)),
    )
    far[0] = after(
        far[0], early, halo, scaled[1, 0][0], *[scaled[0, i][0] for i in range(GROUPS)]
    )
    while len(far) < far_bit:
        far += [toggled(a, "fsdp", len(far)) for a in far]
    pieces = near + far
    layer_scr, w_scr, sems = landing(fsdp)
    kept, bc = call(
        functools.partial(project_kernel, len(near), fsdp), "project",
        [
            shape((2 * tokens + HALO, 2 * state), F32),
            shape((tokens, 2 * state), BF16),
        ],
        (), after(halo, packs[0]), early, conv_w, conv_b[None, :], hbm=(pinned(layer), *pieces),
        scratch=[layer_scr, w_scr, pltpu.VMEM((tokens + HALO, 2 * state), F32), sems],
    )
    bcs = [bc, toggled(bc, "ctx", 1)]
    def within(slot, i, *earlier):
        x_at, g_at, xa, ga = source(slot, i)
        return call(
            functools.partial(
                inside_kernel, counts[i], slot * heads + starts[i], starts[i], heads, x_at, g_at
            ),
            "inside",
            [shape((tokens, widths[i]), F32)] * 2 + [shape((tokens, tokens), F32), square, square]
            + [shape((8, LANES), F32)],
            (skip_scale,), xa, ga, after(bcs[slot], *earlier), step, cum, cumt,
        )

    order = [(slot, i) for slot in range(2) for i in range(GROUPS)]
    inside, states, received, earlier = {}, [], [], []
    inside[0, 0] = within(0, 0)
    swapped_g = toggled(after(swaps[2], bcs[1], inside[0, 0][2]), "ctx", 1)
    earlier = [inside[0, 0][2]]
    for i in range(GROUPS):
        lanes = (starts[i], heads + starts[i])
        if i:
            scaled[1, i] = scale(1, i)
        wide = shape((state, widths[i]), BF16)
        first, p, q, s_first, d_second, decays = call(
            functools.partial(states_kernel, counts[i], lanes), "states",
            [wide] * 5 + [shape((8, widths[i]), F32)],
            (), *bcs, *scaled[0, i], *scaled[1, i], after(grow, *earlier),
            scratch=[pltpu.VMEM((2, state, widths[i]), F32)] * 2
            + [pltpu.VMEM((2, 1, widths[i]), F32)],
        )
        states.append((decays, p, s_first, d_second, q))
        received.append([first])
        earlier = [first]
        if i == 0:
            for key in order[1:GROUPS]:
                inside[key] = within(*key, first)
                earlier.append(inside[key][2])
    waiting = order[GROUPS:]
    for hop in range(hops):
        moves = [(hop, hop + 1), (pairs - 1 - hop, pairs - 2 - hop)]
        moves = [(2 * a + i, 2 * b + i) for a, b in moves for i in range(2)]
        for i in range(GROUPS):
            value = received[i][-1]
            if hop:
                decays, p, _, _, q = states[i]
                value = call(
                    functools.partial(hop_kernel, hop), "hop", shape(value.shape, BF16), (),
                    after(value, *earlier), p, q, decays,
                )
                earlier = [value]
                if waiting and i == 0:
                    key = waiting.pop(0)
                    inside[key] = within(*key, *earlier)
                    earlier = [inside[key][2]]
            received[i].append(lax.ppermute(value, "ctx", moves))
    arrays = [packs[0]]
    at = {(0, k): (0, k) for k in range(fsdp // 2)}
    message, bit = packs[1], fsdp // 2
    sent = [(0, k) for k in range(bit, fsdp)]
    while bit:
        arrays.append(toggled(message, "fsdp", bit))
        for j, (source_bits, owner_bits) in enumerate(sent):
            at[source_bits ^ bit, owner_bits ^ bit] = (len(arrays) - 1, j)
        bit //= 2
        if bit:
            sent = [key for key in sorted(at) if key[1] & bit and key[1] < 2 * bit]
            message = call(
                functools.partial(relay_kernel, [at[key] for key in sent]), "relay",
                shape((len(sent), tokens + HALO, rows), BF16), (), after(arrays[0], received[-1][0]),
                *arrays[1:],
            )
    picks = [at[k, 0] for k in range(fsdp)]
    for key in waiting:
        inside[key] = within(*key, *earlier)
    dbcs = call(inside_bc_kernel, "inside_bc", both_bc, (), *bcs, *[inside[key][2] for key in order])

    full = shape((tokens, width), BF16)
    finals, sends, us, ts, res = (), [], [], [], []
    for i in range(GROUPS):
        last = i == GROUPS - 1
        own_at, _, xa, ga = source(0, i)
        x_at, g_at, xb, gb = source(1, i)
        if i == 1:
            left = call(
                functools.partial(turn_kernel, picks), "turn",
                shape((rows, fsdp * (tokens + HALO)), BF16), (), after(arrays[0], *sends), *arrays[1:],
            )
        lanes = (starts[i], heads + starts[i])
        y, dx, y_send, dx_send, dbc_own, dbc_other, u, t, re = call(
            functools.partial(
                across_kernel, counts[i], lanes, hops, len(finals) // 2, own_at, (x_at, g_at)
            ),
            "across",
            [full, full, flats[i], flats[i]]
            + [both_bc[0], shape((tokens, 2 * state), BF16 if last else F32)]
            + [square, square, shape((8, LANES), F32)],
            (), xa, ga, xb, gb, after(bcs[0], left) if i == 1 else bcs[0], bcs[1], *scaled[0, i],
            *scaled[1, i], step, grow, endw,
            *states[i][:4], *inside[0, i][:2], *inside[1, i][:2], *dbcs, *received[i][1:],
            hbm=finals, hbm_outs=2, aliases={0: 0, 1: 1} if finals else None,
            scratch=[pltpu.VMEM((state, widths[i]), BF16)] * 2
            + [pltpu.VMEM((2, state, widths[i]), BF16)] * 2
            + [pltpu.VMEM((2, 1, widths[i]), F32)] + [pltpu.VMEM((tokens, widths[i]), BF16)] * 2
            + [pltpu.SemaphoreType.DMA((2,))],
        )
        finals, dbcs = (y, dx), (dbc_own, dbc_other)
        sends += [y_send, dx_send]
        us.append(u)
        ts.append(t)
        res.append(re)

    raw_own, dbc_send, head_sums = call(
        steps_kernel, "steps",
        [turned, shape((tokens + heads, 2 * state), BF16), shape((8, LANES), F32)], (),
        sig, rate, step, grow, endw, *[inside[key][j] for j in (3, 4, 5) for key in order],
        *us, *ts, *res, dbcs[1],
    )
    dbc_ret = toggled(dbc_send, "ctx", 1)
    backs = [toggled(sends[0], "ctx", 1)]
    grad, raw_back, rim_send, message = call(
        conv_back_kernel, "conv_back",
        [
            shape((tokens, 2 * state), F32),
            turned,
            shape((8, 2 * state), F32),
            shape((tokens + HALO + 16, 2 * state), BF16),
        ],
        (), after(dbcs[0], *backs), dbc_ret, kept, conv_w, head_sums, hbm_outs=2,
        scratch=[
            pltpu.VMEM((tokens + 2 * HALO, 2 * state), F32),
            pltpu.VMEM((8, 2 * state), F32),
            pltpu.VMEM((tokens, 2 * state), F32),
            pltpu.VMEM(turned.shape, F32),
            pltpu.SemaphoreType.DMA((2,)),
        ],
    )
    rim = lax.ppermute(rim_send, "ctx", [(i + 1, i) for i in range(ctx - 1)])
    backs.append(toggled(after(sends[1], dbc_ret), "ctx", 1))

    rights = [message] + [toggled(message, "fsdp", k) for k in range(fsdp - 1, 0, -1)][::-1]
    terms = call(
        functools.partial(weight_kernel, fsdp), "weight",
        shape((ctx, chunk_rows + 16, 2 * state), BF16), (), left, after(message, *backs), *rights[1:],
    )
    backs += [toggled(after(a, terms), "ctx", 1) for a in sends[2:]]
    total, grad_cw, grad_cb, *per_head = call(
        functools.partial(reduce_kernel, heads), "reduce",
        [
            shape((ctx, chunk_rows, 2 * state), BF16),
            shape((taps, 2 * state), F32),
            shape((1, 2 * state), F32),
        ]
        + [shape((1, total_heads), F32)] * 3,
        (), after(exchanged(terms, "ctx"), rim, *backs[:-1]),
    )
    grad_weight = call(
        place_rows_kernel, "place_rows", shape((rows, 2 * state), F32), (), exchanged(total, "ctx")
    )
    grad_tokens = call(
        functools.partial(tokens_kernel, fsdp), "grad_tokens", shape((tokens, fsdp * rows), BF16),
        (), after(grad, total), rim, hbm=pieces,
        scratch=[pltpu.VMEM((fsdp, *w_bc.shape), BF16), pltpu.SemaphoreType.DMA((fsdp,))],
    )
    grad_raw = call(
        join_steps_kernel, "join_steps", shape((total_heads, tokens), F32), (), raw_own,
        after(raw_back, total),
    )
    targets = [(k % 2, ats[k // 2]) for k in range(2 * GROUPS)]

    def join(arrays, which, blocks):
        return call(
            functools.partial(join_kernel, [targets[k] for k in which]), "join", [full, full], (),
            *blocks, hbm=arrays, hbm_outs=2, aliases={0: 0, 1: 1},
            scratch=[pltpu.SemaphoreType.DMA((len(which),))],
        )

    early_backs = range(2 * GROUPS - 1)
    finals = join(finals, early_backs, [after(backs[0], total), *backs[1:-1]])
    ssm_out, grad_values = join(
        finals, [2 * GROUPS - 1], [after(backs[-1], grad_tokens, finals[0], grad_raw)]
    )
    return (
        ssm_out[None],
        grad_values[None],
        grad_tokens[None],
        grad_raw.T[None],
        grad_weight,
        grad_cw,
        grad_cb[0],
        *[a[0] for a in per_head],
    )


def solution(mesh):
    tokens = P("fsdp", "ctx", None)
    in_specs = (tokens, P("fsdp", None), P(), P(), tokens, tokens, P(), P(), P(), tokens)
    out_specs = (tokens, tokens, tokens, tokens, P("fsdp", None), P(), P(), P(), P(), P())
    return jax.shard_map(body, mesh=mesh, in_specs=in_specs, out_specs=out_specs, check_vma=False)
```

```python
import functools

import jax
import jax.numpy as jnp
from jax import lax
from jax.experimental import pallas as pl
from jax.experimental.pallas import tpu as pltpu
from jax.sharding import PartitionSpec as P

F32 = jnp.float32
BF16 = jnp.bfloat16
LANES = 128
HALO = 16
PARTS = (2, 2)
GROUPS = len(PARTS)
LIMIT = 16 * 1024 * 1024
HIGHEST = lax.Precision.HIGHEST
TN = ((0,), (0,))
NT = ((1,), (1,))


def dot(a, b, dims=((1,), (0,)), precision=None):
    return lax.dot_general(
        a, b, (dims, ((), ())), precision=precision, preferred_element_type=F32
    )


def shape(dims, dtype):
    return jax.ShapeDtypeStruct(dims, dtype)


def call(kernel, name, out_shape, smem, *operands, hbm=(), hbm_outs=0, scratch=(), aliases=None):
    single = not isinstance(out_shape, list)
    outs = [out_shape] if single else out_shape
    spaces = [pltpu.SMEM] * len(smem) + [pl.ANY] * len(hbm) + [pltpu.VMEM] * len(operands)
    out_spaces = [pltpu.HBM] * hbm_outs + [pltpu.VMEM] * (len(outs) - hbm_outs)
    result = pl.pallas_call(
        kernel,
        out_shape=outs,
        in_specs=[pl.BlockSpec(memory_space=a) for a in spaces],
        out_specs=[pl.BlockSpec(memory_space=a) for a in out_spaces],
        scratch_shapes=list(scratch),
        compiler_params=pltpu.CompilerParams(vmem_limit_bytes=LIMIT),
        input_output_aliases=aliases or {},
        name=name,
    )(*smem, *hbm, *operands)
    return result[0] if single else result


def copy_all(pairs, sems):
    copies = [pltpu.make_async_copy(a, b, sems.at[i]) for i, (a, b) in enumerate(pairs)]
    for copy in copies:
        copy.start()
    return copies


def side():
    return lax.rem(lax.axis_index("ctx"), 2)


def place():
    return lax.div(lax.axis_index("ctx"), 2)


def peer_columns(k, rows):
    return aligned((lax.axis_index("fsdp") ^ k) * rows, rows)


def aligned(at, size):
    return pl.ds(pl.multiple_of(at, LANES), size)


def triangle(n):
    rows = lax.broadcasted_iota(jnp.int32, (n, n), 0)
    cols = lax.broadcasted_iota(jnp.int32, (n, n), 1)
    return rows >= cols


def split(value):
    high = value.astype(BF16).astype(F32)
    return jnp.concatenate([high, value - high], 0).astype(BF16)


def swap_kernel(layer_ref, x_ref, g_ref, halo_ref, first_ref, x_out_ref, g_out_ref, sems):
    width = x_out_ref.shape[1]
    tokens = layer_ref.shape[0]
    base = (1 - side()) * (2 * width)
    pairs = [
        (layer_ref.at[tokens - HALO : tokens, :], halo_ref),
        (x_ref.at[:, aligned(base, width)], first_ref.at[:, :width]),
        (g_ref.at[:, aligned(base, width)], first_ref.at[:, width:]),
        (x_ref.at[:, aligned(base + width, width)], x_out_ref),
        (g_ref.at[:, aligned(base + width, width)], g_out_ref),
    ]
    for copy in copy_all(pairs, sems):
        copy.wait()


def vectors_kernel(
    dt_ref, back_ref, bias_ref, alog_ref, step_ref, cum_ref, cumt_ref, grow_ref, endw_ref, sig_ref,
    rate_ref, turned, rows,
):
    n = back_ref.shape[1]
    heads = back_ref.shape[0] // 2
    r = side()
    mine = pl.ds(pl.multiple_of(r * heads, 8), heads)
    turned[...] = jnp.zeros_like(turned)
    turned[0:heads, :] = dt_ref[mine, :]
    turned[heads : 2 * heads, :] = back_ref[mine, :]
    rows[...] = jnp.zeros_like(rows)
    for i, ref in enumerate((bias_ref, alog_ref)):
        half = jnp.where(r == 0, ref[:, :heads], ref[:, heads:])
        rows[i : i + 1, 0:heads] = half
        rows[i : i + 1, heads : 2 * heads] = half
    raw = turned[...].T + rows[0:1, :]
    step = jnp.maximum(raw, 0.0) + jnp.log1p(jnp.exp(-jnp.abs(raw)))
    rate = jnp.exp(rows[1:2, :])
    log_decay = -step * rate
    lower = jnp.where(triangle(n), 1.0, 0.0).astype(F32)
    cum = dot(lower, log_decay, precision=HIGHEST)
    step_ref[...] = step
    cum_ref[...] = cum
    cumt_ref[...] = cum.T
    grow_ref[...] = jnp.exp(cum)
    endw_ref[...] = jnp.exp(cum[n - 1 : n, :] - cum)
    sig_ref[...] = jax.nn.sigmoid(raw)
    rate_ref[...] = jnp.broadcast_to(rate, rate_ref.shape)


def early_kernel(count, layer_ref, *refs):
    pieces = refs[:count]
    out_ref, layer_scr, w_scr, sems = refs[count:]
    copies = copy_all(
        [(layer_ref, layer_scr)] + [(pieces[k], w_scr.at[k]) for k in range(count)], sems
    )
    copies[0].wait()
    total = 0.0
    for k in range(count):
        copies[k + 1].wait()
        total += dot(layer_scr[:, peer_columns(k, w_scr.shape[1])], w_scr[k])
    out_ref[...] = total


def project_kernel(done, count, layer_ref, *refs):
    pieces = refs[:count]
    halo_ref, early_ref, cw_ref, cb_ref, kept_ref, bc_ref, layer_scr, w_scr, ext_scr, sems = refs[count:]
    copies = copy_all(
        [(layer_ref, layer_scr)] + [(pieces[k], w_scr.at[k]) for k in range(count)], sems
    )
    taps = cw_ref.shape[0]
    tokens = layer_ref.shape[0]
    copies[0].wait()
    total, rim = early_ref[...], 0.0
    for k in range(count):
        copies[k + 1].wait()
        at = peer_columns(k, w_scr.shape[1])
        rim += dot(halo_ref[:, at], w_scr[k])
        if k >= done:
            total += dot(layer_scr[:, at], w_scr[k])
    ext_scr[0:HALO, :] = rim
    ext_scr[HALO:, :] = total
    kept_ref[0 : HALO + tokens, :] = ext_scr[...]
    first = HALO - taps + 1
    pre = cb_ref[...] + cw_ref[0:1, :] * ext_scr[first : first + tokens, :]
    for k in range(1, taps):
        pre = pre + cw_ref[k : k + 1, :] * ext_scr[first + k : first + k + tokens, :]
    kept_ref[HALO + tokens :, :] = pre
    bc_ref[...] = (pre * jax.nn.sigmoid(pre)).astype(BF16)


def head_columns(at, h):
    first, more = at
    return aligned(first + side() * more + h * LANES, LANES)


def scale_kernel(heads, lane, x_at, g_at, x_ref, g_ref, step_ref, grow_ref, endw_ref, xe_ref, ge_ref):
    for h in range(heads):
        at = slice(h * LANES, (h + 1) * LANES)
        one = slice(lane + h, lane + h + 1)
        x = x_ref[:, head_columns(x_at, h)].astype(F32)
        g = g_ref[:, head_columns(g_at, h)].astype(F32)
        xe_ref[:, at] = (x * (step_ref[:, one] * endw_ref[:, one])).astype(BF16)
        ge_ref[:, at] = (g * grow_ref[:, one]).astype(BF16)


def widen(row, lane, heads):
    return jnp.concatenate(
        [jnp.broadcast_to(row[:, lane + h : lane + h + 1], (1, LANES)) for h in range(heads)], 1
    )


def states_kernel(
    heads, lanes, bc0_ref, bc1_ref, xe0_ref, ge0_ref, xe1_ref, ge1_ref, grow_ref,
    first_ref, p_ref, q_ref, sf_ref, ds_ref, dec_ref, s_scr, d_scr, dec_scr,
):
    n = grow_ref.shape[0]
    r = side()
    for slot, (bc_ref, xe_ref, ge_ref) in enumerate(
        ((bc0_ref, xe0_ref, ge0_ref), (bc1_ref, xe1_ref, ge1_ref))
    ):
        s_scr[slot] = dot(bc_ref[:, :LANES], xe_ref[...], TN)
        d_scr[slot] = dot(bc_ref[:, LANES:], ge_ref[...], TN)
        dec_scr[slot] = widen(grow_ref[n - 1 : n, :], lanes[slot], heads)
    dec_first, dec_second = dec_scr[r], dec_scr[1 - r]
    s_first, d_second = s_scr[r], d_scr[1 - r]
    sf_ref[...] = s_first.astype(BF16)
    ds_ref[...] = d_second.astype(BF16)
    p = (dec_second * s_first + s_scr[1 - r]).astype(BF16)
    q = (dec_first * d_second + d_scr[r]).astype(BF16)
    p_ref[...] = p
    q_ref[...] = q

    @pl.when(place() == 0)
    def _():
        first_ref[...] = p

    @pl.when(place() != 0)
    def _():
        first_ref[...] = q

    dec_ref[0:1, :] = dec_first * dec_second
    dec_ref[1:2, :] = dec_first
    dec_ref[2:3, :] = dec_second
    dec_ref[3:8, :] = jnp.zeros((5, dec_first.shape[1]), F32)


def hop_kernel(hop, received_ref, p_ref, q_ref, dec_ref, out_ref):
    carried = dec_ref[0:1, :] * received_ref[...].astype(F32)

    @pl.when(place() == hop)
    def _():
        out_ref[...] = (carried + p_ref[...].astype(F32)).astype(BF16)

    @pl.when(place() != hop)
    def _():
        out_ref[...] = (carried + q_ref[...].astype(F32)).astype(BF16)


def inside_kernel(
    heads, lane, skip_at, all_heads, x_at, g_at, skip_ref, x_ref, g_ref, bc_ref, step_ref, cum_ref,
    cumt_ref, y_ref, dx_ref, dscores_ref, gy_ref, ds_ref, gx_ref,
):
    n = step_ref.shape[0]
    mask = triangle(n)
    scores = jnp.where(mask, dot(bc_ref[:, LANES:], bc_ref[:, :LANES], NT), 0.0)
    gy_ref[...] = jnp.zeros_like(gy_ref)
    ds_ref[...] = jnp.zeros_like(ds_ref)
    gx_ref[...] = jnp.zeros_like(gx_ref)
    dscores = jnp.zeros((n, n), F32)
    for h in range(heads):
        at = slice(h * LANES, (h + 1) * LANES)
        one = slice(lane + h, lane + h + 1)
        step = step_ref[:, one]
        gap = cum_ref[:, one] - cumt_ref[one, :]
        decay = jnp.exp(jnp.where(mask, gap, 0.0))
        mixing = (scores * decay).astype(BF16)
        x = x_ref[:, head_columns(x_at, h)].astype(F32)
        g = g_ref[:, head_columns(g_at, h)]
        gf = g.astype(F32)
        xs = (x * step).astype(BF16)
        skip = skip_ref[side() * all_heads + skip_at + h]
        y = dot(mixing, xs)
        dxs = dot(mixing, g, TN)
        dscores += dot(g, xs, NT) * decay
        y_ref[:, at] = y + skip * x
        dx_ref[:, at] = dxs * step + skip * gf
        gy_ref[:, one] = jnp.sum(gf * y, axis=1, keepdims=True)
        ds_ref[:, one] = jnp.sum(x * dxs, axis=1, keepdims=True)
        gx_ref[0:1, one] = jnp.sum(jnp.sum(gf * x, axis=0, keepdims=True), axis=1, keepdims=True)
    dscores_ref[...] = jnp.where(mask, dscores, 0.0)


def inside_bc_kernel(bc0_ref, bc1_ref, *refs):
    parts, outs = refs[: 2 * GROUPS], refs[2 * GROUPS :]
    for slot, bc_ref in enumerate((bc0_ref, bc1_ref)):
        total = parts[slot * GROUPS][...]
        for i in range(1, GROUPS):
            total = total + parts[slot * GROUPS + i][...]
        ds = total.astype(BF16)
        outs[slot][:, :LANES] = dot(ds, bc_ref[:, LANES:], TN)
        outs[slot][:, LANES:] = dot(ds, bc_ref[:, :LANES])


def enter_kernel(
    hops, xe0_ref, ge0_ref, xe1_ref, ge1_ref, dec_ref, p_ref, sf_ref, ds_ref, dbc0_ref, dbc1_ref, *refs
):
    received = refs[:hops]
    e_ref, r_ref, n_ref, dbco0_ref, dbco1_ref, e_in, r_in = refs[hops:]
    r, pos = side(), place()
    e_in[...] = jnp.zeros_like(e_in)
    r_in[...] = jnp.zeros_like(r_in)
    for k in range(hops):

        @pl.when(pos - 1 == k)
        def _(k=k):
            e_in[...] = received[k][...]

        @pl.when(hops - 1 - pos == k)
        def _(k=k):
            r_in[...] = received[k][...]

    dec_pair, dec_first, dec_second = dec_ref[0:1, :], dec_ref[1:2, :], dec_ref[2:3, :]
    entering = e_in[...].astype(F32)
    later = r_in[...].astype(F32)
    middle = dec_first * entering + sf_ref[...].astype(F32)
    leaving = dec_pair * entering + p_ref[...].astype(F32)
    earlier = dec_second * later + ds_ref[...].astype(F32)
    e_ref[r] = e_in[...]
    e_ref[1 - r] = middle.astype(BF16)
    r_ref[1 - r] = r_in[...]
    r_ref[r] = earlier.astype(BF16)
    n_ref[1 - r] = jnp.sum(later * leaving, axis=0, keepdims=True)
    n_ref[r] = jnp.sum(earlier * middle, axis=0, keepdims=True)
    for slot, (xe_ref, ge_ref, dbc_ref, dbco_ref) in enumerate(
        ((xe0_ref, ge0_ref, dbc0_ref, dbco0_ref), (xe1_ref, ge1_ref, dbc1_ref, dbco1_ref))
    ):
        db = dbc_ref[:, :LANES] + dot(xe_ref[...], r_ref[slot], NT)
        dc = dbc_ref[:, LANES:] + dot(ge_ref[...], e_ref[slot], NT)
        dbco_ref[:, :LANES] = db.astype(dbco_ref.dtype)
        dbco_ref[:, LANES:] = dc.astype(dbco_ref.dtype)


def across_kernel(heads, lanes, filled, own_at, columns, *refs):
    refs = refs[2 * filled :]
    across_block(heads, lanes, own_at, columns, *refs)


def across_block(
    heads, lanes, own_at, columns, x0_ref, g0_ref, x1_ref, g1_ref, bc0_ref, bc1_ref, step_ref,
    grow_ref, endw_ref, e_ref, r_ref, n_ref, y0_ref, dx0_ref, y1_ref, dx1_ref, yf_ref, dxf_ref,
    ys_ref, dxs_ref, u_ref, t_ref, re_ref, yo_ref, dxo_ref, sems
):
    r = side()
    width, cut = yo_ref.shape[1], ys_ref.shape[1]
    u_ref[...] = jnp.zeros_like(u_ref)
    t_ref[...] = jnp.zeros_like(t_ref)
    re_ref[...] = jnp.zeros_like(re_ref)
    for slot, (bc_ref, y_ref, dx_ref) in enumerate(
        ((bc0_ref, y0_ref, dx0_ref), (bc1_ref, y1_ref, dx1_ref))
    ):
        e_all = e_ref[slot]
        r_all = r_ref[slot]
        ce_all = dot(bc_ref[:, LANES:], e_all)
        br_all = dot(bc_ref[:, :LANES], r_all)
        for h in range(heads):
            at = slice(h * LANES, (h + 1) * LANES)
            lane = lanes[slot] + h
            one = slice(lane, lane + 1)
            ce, br = ce_all[:, at], br_all[:, at]
            y = (y_ref[:, at] + grow_ref[:, one] * ce).astype(BF16)
            dx = (dx_ref[:, at] + (step_ref[:, one] * endw_ref[:, one]) * br).astype(BF16)
            if slot == 0:
                yo_ref[:, at] = y
                dxo_ref[:, at] = dx
                x = x0_ref[:, head_columns(own_at, h)].astype(F32)
                g = g0_ref[:, head_columns(own_at, h)].astype(F32)
            else:
                first = h * LANES
                if first < cut:
                    ys_ref[:, at] = y
                else:
                    dxs_ref[:, first - cut : first - cut + LANES] = y
                dxs_ref[:, first + width - cut : first + width - cut + LANES] = dx
                x = x1_ref[:, head_columns(columns[0], h)].astype(F32)
                g = g1_ref[:, head_columns(columns[1], h)].astype(F32)
            u_ref[:, one] = jnp.sum(g * ce, axis=1, keepdims=True)
            t_ref[:, one] = jnp.sum(x * br, axis=1, keepdims=True)
            re_ref[0:1, one] = jnp.sum(n_ref[slot][:, at], axis=1, keepdims=True)
        if slot == 0:
            final = aligned(own_at[0] + r * own_at[1], width)
            pairs = [(yo_ref, yf_ref.at[:, final]), (dxo_ref, dxf_ref.at[:, final])]
            copies = copy_all(pairs, sems)
    for copy in copies:
        copy.wait()


def steps_kernel(sig_ref, rate_ref, step_ref, grow_ref, endw_ref, *refs):
    count = 2 * GROUPS
    gys, dss, gxs = refs[:count], refs[count : 2 * count], refs[2 * count : 3 * count]
    refs = refs[3 * count :]
    us, ts, res = refs[:GROUPS], refs[GROUPS : 2 * GROUPS], refs[2 * GROUPS : 3 * GROUPS]
    own_ref, send_ref, sums_ref = refs[3 * GROUPS :]

    def total(parts):
        value = parts[0][...]
        for a in parts[1:]:
            value = value + a[...]
        return value

    n = step_ref.shape[0]
    step = step_ref[...]
    ds = total(dss) + endw_ref[...] * total(ts)
    gy = total(gys) + grow_ref[...] * total(us)
    rate = rate_ref[0:1, :]
    last = lax.broadcasted_iota(jnp.int32, (n, LANES), 0) == n - 1
    dcum = gy - step * ds + jnp.where(last, total(res)[0:1, :], 0.0)
    lower = jnp.where(triangle(n), 1.0, 0.0).astype(F32)
    dlog = dot(lower, dcum, TN, precision=HIGHEST)
    draw = (ds - rate * dlog) * sig_ref[...]
    turned = draw.T
    heads = own_ref.shape[0]
    own_ref[...] = turned[:heads, :]
    send_ref[...] = turned[heads : 2 * heads, :]
    sums_ref[0:1, :] = jnp.sum(draw, axis=0, keepdims=True)
    sums_ref[1:2, :] = jnp.sum(dlog * (-step * rate), axis=0, keepdims=True)
    sums_ref[2:3, :] = total(gxs)[0:1, :]
    sums_ref[3:8, :] = jnp.zeros((5, LANES), F32)


def conv_back_kernel(
    own_ref, ret_ref, kept_ref, cw_ref, heads_ref, grad_ref, rim_ref, message_ref, z_scr, sum_scr,
):
    tokens = own_ref.shape[0]
    taps = cw_ref.shape[0]
    pre = kept_ref[HALO + tokens :, :]
    sig = jax.nn.sigmoid(pre)
    dconv = (own_ref[...] + ret_ref[...].astype(F32)) * sig * (1.0 + pre * (1.0 - sig))
    z_scr[...] = jnp.zeros_like(z_scr)
    z_scr[HALO : HALO + tokens, :] = dconv
    grad = cw_ref[0:1, :] * z_scr[taps - 1 : taps - 1 + tokens + HALO, :]
    for k in range(1, taps):
        grad = grad + cw_ref[k : k + 1, :] * z_scr[taps - 1 - k : taps - 1 - k + tokens + HALO, :]
    grad_ref[...] = grad[HALO:, :]
    rim_ref[...] = grad[HALO - 8 : HALO, :]
    first = HALO - taps + 1
    sum_scr[...] = jnp.zeros_like(sum_scr)
    for k in range(taps):
        sum_scr[k : k + 1, :] = jnp.sum(
            dconv * kept_ref[first + k : first + k + tokens, :], axis=0, keepdims=True
        )
    sum_scr[taps : taps + 1, :] = jnp.sum(dconv, axis=0, keepdims=True)
    sum_scr[5:8, aligned(side() * LANES, LANES)] = heads_ref[0:3, :]
    small = split(sum_scr[...])
    message_ref[0 : tokens + HALO, :] = grad.astype(BF16)
    message_ref[tokens + HALO :, :] = small


def pack_kernel(layer_ref, halo_ref, keep_ref, send_ref, sems):
    half, _, rows = keep_ref.shape
    pairs = []
    for k in range(2 * half):
        out = keep_ref.at[k] if k < half else send_ref.at[k - half]
        at = peer_columns(k, rows)
        pairs.append((halo_ref.at[:, at], out.at[0:HALO, :]))
        pairs.append((layer_ref.at[:, at], out.at[HALO:, :]))
    for copy in copy_all(pairs, sems):
        copy.wait()


def relay_kernel(picks, *refs):
    out_ref = refs[-1]
    for j, (ref, at) in enumerate(picks):
        out_ref[j] = refs[ref][at]


def turn_kernel(picks, *refs):
    out_ref = refs[-1]
    parts = [refs[ref].at[at] for ref, at in picks]
    tokens = parts[0].shape[0] - HALO
    for k, part in enumerate(parts):
        out_ref[:, k * tokens : (k + 1) * tokens] = part[HALO:, :].T
    halos = jnp.concatenate([part[0:HALO, :] for part in parts], 0)
    out_ref[:, len(parts) * tokens :] = halos.T


def weight_kernel(count, left_ref, *refs):
    rights, out_ref = refs[:count], refs[count]
    tokens = (left_ref.shape[1] // count) - HALO
    right = jnp.concatenate(
        [a[HALO : HALO + tokens, :] for a in rights] + [a[0:HALO, :] for a in rights], 0
    )
    at = tokens + HALO
    both = jnp.zeros((16, right.shape[1]), F32)
    for a in rights:
        both += a[at : at + 16, :].astype(F32)
    small = split(both[0:8, :] + both[8:16, :])
    chunk = out_ref.shape[1] - 16
    for k in range(out_ref.shape[0]):
        term = dot(left_ref[k * chunk : (k + 1) * chunk, :], right)
        out_ref[k, 0:chunk, :] = term.astype(BF16)
        out_ref[k, chunk:, :] = small


def reduce_kernel(heads, terms_ref, total_ref, cw_ref, cb_ref, *head_refs):
    chunk = total_ref.shape[1]
    total = terms_ref[0].astype(F32)
    for k in range(1, terms_ref.shape[0]):
        total = total + terms_ref[k].astype(F32)
    for k in range(total_ref.shape[0]):
        total_ref[k] = total[0:chunk].astype(BF16)
    small = total[chunk : chunk + 8] + total[chunk + 8 :]
    taps = cw_ref.shape[0]
    cw_ref[...] = small[0:taps, :]
    cb_ref[...] = small[taps : taps + 1, :]
    for i, ref in enumerate(head_refs):
        row = small[5 + i : 6 + i, :]
        ref[:, :heads] = row[:, :heads] + row[:, heads : 2 * heads]
        row = row[:, LANES:]
        ref[:, heads:] = row[:, :heads] + row[:, heads : 2 * heads]


def place_rows_kernel(parts_ref, out_ref):
    chunk = parts_ref.shape[1]
    for k in range(parts_ref.shape[0]):
        out_ref[k * chunk : (k + 1) * chunk, :] = parts_ref[k].astype(F32)


def tokens_kernel(count, *refs):
    pieces = refs[:count]
    grad_ref, rim_ref, out_ref, w_scr, sems = refs[count:]
    copies = copy_all([(pieces[k], w_scr.at[k]) for k in range(count)], sems)
    tail = rim_ref.shape[0]
    own = grad_ref[...]
    g = jnp.concatenate([own[:-tail], own[-tail:] + rim_ref[...]], 0).astype(BF16)
    rows = pieces[0].shape[0]
    for k in range(count):
        copies[k].wait()
        out_ref[:, peer_columns(k, rows)] = dot(g, w_scr[k], NT).astype(BF16)


def join_kernel(targets, *refs):
    blocks = refs[2 : 2 + len(targets)]
    *outs, sems = refs[2 + len(targets) :]
    half = outs[0].shape[1] // 2
    base = (1 - side()) * half
    pairs = []
    for block, pieces in zip(blocks, targets):
        for first, width, which, at in pieces:
            pairs.append((block.at[:, first : first + width], outs[which].at[:, aligned(base + at, width)]))
    for copy in copy_all(pairs, sems):
        copy.wait()


def join_steps_kernel(own_ref, back_ref, out_ref):
    heads = own_ref.shape[0]
    r = side()
    out_ref[pl.ds(pl.multiple_of(r * heads, 8), heads), :] = own_ref[...]
    out_ref[pl.ds(pl.multiple_of((1 - r) * heads, 8), heads), :] = back_ref[...]


def pinned(x):
    return pltpu.with_memory_space_constraint(x, pltpu.HBM)


def toggled(x, axis, bits):
    size = lax.axis_size(axis)
    return lax.ppermute(x, axis, [(i, i ^ bits) for i in range(size)])


def exchanged(x, axis):
    return lax.all_to_all(x, axis, 0, 0)


def after(x, *others):
    return lax.optimization_barrier((x, *others))[0]


def body(layer_in, w_bc, conv_w, conv_b, ssm_in, dt_raw, dt_bias, a_log, skip_scale, grad_out):
    ctx, fsdp = lax.axis_size("ctx"), lax.axis_size("fsdp")
    layer, x, g, dt = layer_in[0], ssm_in[0], grad_out[0], dt_raw[0].T
    tokens, width = x.shape
    total_heads = dt_bias.shape[0]
    heads = total_heads // 2
    half = width // 2
    counts = [heads // part for part in PARTS]
    starts = [sum(counts[:i]) for i in range(GROUPS)]
    widths = [half // part for part in PARTS]
    ats = [sum(widths[:i]) for i in range(GROUPS)]
    state = w_bc.shape[1] // 2
    taps = conv_w.shape[0]
    rows = w_bc.shape[0]
    chunk_rows = rows // ctx
    pairs = ctx // 2
    hops = pairs - 1
    square = shape((tokens, LANES), F32)
    flats = [shape((tokens, a), BF16) for a in widths]
    turned = shape((heads, tokens), F32)
    both_bc = [shape((tokens, 2 * state), F32)] * 2

    dt_back = toggled(dt, "ctx", 1)
    halo_send, *swaps = call(
        swap_kernel, "swap",
        [shape((HALO, layer.shape[1]), BF16), shape((tokens, half), BF16), flats[1], flats[1]], (),
        hbm=(pinned(layer), pinned(x), pinned(g)), scratch=[pltpu.SemaphoreType.DMA((5,))],
    )
    halo = lax.ppermute(halo_send, "ctx", [(i, i + 1) for i in range(ctx - 1)])
    swapped_first = toggled(after(swaps[0], dt_back), "ctx", 1)
    swapped_x = toggled(after(swaps[1], halo), "ctx", 1)

    step, cum, cumt, grow, endw, sig, rate = call(
        vectors_kernel, "vectors", [square] * 6 + [shape((8, LANES), F32)], (), dt, dt_back,
        dt_bias[None, :], a_log[None, :],
        scratch=[pltpu.VMEM((tokens, tokens), F32), pltpu.VMEM((8, LANES), F32)],
    )

    def source(slot, i):
        if slot == 0:
            return (ats[i], half), (ats[i], half), x, g
        if i == 0:
            return (0, 0), (widths[0], 0), swapped_first, swapped_first
        return (0, 0), (0, 0), swapped_x, swapped_g

    def scale(slot, i):
        x_at, g_at, xa, ga = source(slot, i)
        return call(
            functools.partial(scale_kernel, counts[i], slot * heads + starts[i], x_at, g_at), "scale",
            [flats[i]] * 2, (), xa, ga, step, grow, endw,
        )

    scaled = {(0, i): scale(0, i) for i in range(GROUPS)}
    scaled[1, 0] = scale(1, 0)
    def landing(count):
        return [
            pltpu.VMEM(layer.shape, BF16),
            pltpu.VMEM((count, *w_bc.shape), BF16),
            pltpu.SemaphoreType.DMA((1 + count,)),
        ]

    parts = shape((fsdp // 2, tokens + HALO, rows), BF16)
    packs = call(
        pack_kernel, "pack", [parts, parts], (), hbm=(pinned(layer), halo),
        scratch=[pltpu.SemaphoreType.DMA((2 * fsdp,))],
    )
    far_bit = fsdp // 2
    far = [toggled(w_bc, "fsdp", far_bit)]
    near = [w_bc]
    while len(near) < far_bit:
        near += [toggled(a, "fsdp", len(near)) for a in near]
    early = call(
        functools.partial(early_kernel, len(near)), "project_early",
        shape((tokens, 2 * state), F32), (), hbm=(pinned(layer), *near),
        scratch=landing(len(near)),
    )
    far[0] = after(
        far[0], early, halo, scaled[1, 0][0], *[scaled[0, i][0] for i in range(GROUPS)]
    )
    while len(far) < far_bit:
        far += [toggled(a, "fsdp", len(far)) for a in far]
    pieces = near + far
    layer_scr, w_scr, sems = landing(fsdp)
    kept, bc = call(
        functools.partial(project_kernel, len(near), fsdp), "project",
        [
            shape((2 * tokens + HALO, 2 * state), F32),
            shape((tokens, 2 * state), BF16),
        ],
        (), after(halo, packs[0]), early, conv_w, conv_b[None, :], hbm=(pinned(layer), *pieces),
        scratch=[layer_scr, w_scr, pltpu.VMEM((tokens + HALO, 2 * state), F32), sems],
    )
    bcs = [bc, toggled(bc, "ctx", 1)]
    def within(slot, i, *earlier):
        x_at, g_at, xa, ga = source(slot, i)
        return call(
            functools.partial(
                inside_kernel, counts[i], slot * heads + starts[i], starts[i], heads, x_at, g_at
            ),
            "inside",
            [shape((tokens, widths[i]), F32)] * 2 + [shape((tokens, tokens), F32), square, square]
            + [shape((8, LANES), F32)],
            (skip_scale,), xa, ga, after(bcs[slot], *earlier), step, cum, cumt,
        )

    order = [(slot, i) for slot in range(2) for i in range(GROUPS)]
    inside, states, received, earlier = {}, [], [], []
    inside[0, 0] = within(0, 0)
    swapped_g = toggled(after(swaps[2], bcs[1], inside[0, 0][2]), "ctx", 1)
    earlier = [inside[0, 0][2]]
    for i in range(GROUPS):
        lanes = (starts[i], heads + starts[i])
        if i:
            scaled[1, i] = scale(1, i)
        wide = shape((state, widths[i]), BF16)
        first, p, q, s_first, d_second, decays = call(
            functools.partial(states_kernel, counts[i], lanes), "states",
            [wide] * 5 + [shape((8, widths[i]), F32)],
            (), *bcs, *scaled[0, i], *scaled[1, i], after(grow, *earlier),
            scratch=[pltpu.VMEM((2, state, widths[i]), F32)] * 2
            + [pltpu.VMEM((2, 1, widths[i]), F32)],
        )
        states.append((decays, p, s_first, d_second, q))
        received.append([first])
        earlier = [first]
        if i == 0:
            for key in order[1:GROUPS]:
                inside[key] = within(*key, first)
                earlier.append(inside[key][2])
    waiting = order[GROUPS:]
    for hop in range(hops):
        moves = [(hop, hop + 1), (pairs - 1 - hop, pairs - 2 - hop)]
        moves = [(2 * a + i, 2 * b + i) for a, b in moves for i in range(2)]
        for i in range(GROUPS):
            value = received[i][-1]
            if hop:
                decays, p, _, _, q = states[i]
                value = call(
                    functools.partial(hop_kernel, hop), "hop", shape(value.shape, BF16), (),
                    after(value, *earlier), p, q, decays,
                )
                earlier = [value]
                if waiting and i == 0:
                    key = waiting.pop(0)
                    inside[key] = within(*key, *earlier)
                    earlier = [inside[key][2]]
            received[i].append(lax.ppermute(value, "ctx", moves))
    arrays = [packs[0]]
    at = {(0, k): (0, k) for k in range(fsdp // 2)}
    message, bit = packs[1], fsdp // 2
    sent = [(0, k) for k in range(bit, fsdp)]
    while bit:
        arrays.append(toggled(message, "fsdp", bit))
        for j, (source_bits, owner_bits) in enumerate(sent):
            at[source_bits ^ bit, owner_bits ^ bit] = (len(arrays) - 1, j)
        bit //= 2
        if bit:
            sent = [key for key in sorted(at) if key[1] & bit and key[1] < 2 * bit]
            message = call(
                functools.partial(relay_kernel, [at[key] for key in sent]), "relay",
                shape((len(sent), tokens + HALO, rows), BF16), (), after(arrays[0], received[-1][0]),
                *arrays[1:],
            )
    picks = [at[k, 0] for k in range(fsdp)]
    for key in waiting:
        inside[key] = within(*key, *earlier)
    dbcs = call(inside_bc_kernel, "inside_bc", both_bc, (), *bcs, *[inside[key][2] for key in order])

    full = shape((tokens, width), BF16)
    finals, sends, us, ts, res = (), [], [], [], []
    cuts = [widths[0] // 2, *widths[1:]]
    returns = [
        (shape((tokens, cut), BF16), shape((tokens, 2 * w - cut), BF16)) for cut, w in zip(cuts, widths)
    ]
    for i in range(GROUPS):
        last = i == GROUPS - 1
        own_at, _, xa, ga = source(0, i)
        x_at, g_at, xb, gb = source(1, i)
        if i == 1:
            backs = [toggled(sends[0], "ctx", 1)]
            left = call(
                functools.partial(turn_kernel, picks), "turn",
                shape((rows, fsdp * (tokens + HALO)), BF16), (), after(arrays[0], *sends, *backs),
                *arrays[1:],
            )
        lanes = (starts[i], heads + starts[i])
        pair = [shape((2, state, widths[i]), BF16)] * 2
        *both, n, dbc_own, dbc_other = call(
            functools.partial(enter_kernel, hops), "enter",
            [*pair, shape((2, 1, widths[i]), F32), both_bc[0]]
            + [shape((tokens, 2 * state), BF16 if last else F32)],
            (), after(scaled[0, i][0], *sends), scaled[0, i][1], *scaled[1, i], *states[i][:4], *dbcs,
            *received[i][1:],
            scratch=[pltpu.VMEM((state, widths[i]), BF16)] * 2,
        )
        dbcs = (dbc_own, dbc_other)
        if last:
            dbc_ret = toggled(dbc_other, "ctx", 1)
        y, dx, y_send, dx_send, u, t, re = call(
            functools.partial(
                across_kernel, counts[i], lanes, len(finals) // 2, own_at, (x_at, g_at)
            ),
            "across", [full, full, *returns[i], square, square, shape((8, LANES), F32)],
            (), xa, ga, xb, gb, after(bcs[0], left) if i == 1 else bcs[0], bcs[1], step, grow, endw,
            *both, n, *inside[0, i][:2], *inside[1, i][:2],
            hbm=finals, hbm_outs=2, aliases={0: 0, 1: 1} if finals else None,
            scratch=[pltpu.VMEM((tokens, widths[i]), BF16)] * 2 + [pltpu.SemaphoreType.DMA((2,))],
        )
        finals = (y, dx)
        sends += [y_send, dx_send]
        us.append(u)
        ts.append(t)
        res.append(re)

    raw_own, raw_send, head_sums = call(
        steps_kernel, "steps", [turned, turned, shape((8, LANES), F32)], (),
        sig, rate, step, grow, endw, *[inside[key][j] for j in (3, 4, 5) for key in order],
        *us, *ts, *res,
    )
    raw_back = toggled(raw_send, "ctx", 1)
    grad, rim_send, message = call(
        conv_back_kernel, "conv_back",
        [
            shape((tokens, 2 * state), F32),
            shape((8, 2 * state), F32),
            shape((tokens + HALO + 16, 2 * state), BF16),
        ],
        (), after(dbcs[0], *backs), dbc_ret, kept, conv_w, head_sums,
        scratch=[
            pltpu.VMEM((tokens + 2 * HALO, 2 * state), F32),
            pltpu.VMEM((8, 2 * state), F32),
        ],
    )
    rim = lax.ppermute(rim_send, "ctx", [(i + 1, i) for i in range(ctx - 1)])
    backs.append(toggled(after(sends[1], dbc_ret, head_sums), "ctx", 1))

    rights = [message] + [toggled(message, "fsdp", k) for k in range(fsdp - 1, 0, -1)][::-1]
    terms = call(
        functools.partial(weight_kernel, fsdp), "weight",
        shape((ctx, chunk_rows + 16, 2 * state), BF16), (), left, after(message, *backs), *rights[1:],
    )
    backs += [toggled(after(a, terms), "ctx", 1) for a in sends[2:]]
    total, grad_cw, grad_cb, *per_head = call(
        functools.partial(reduce_kernel, heads), "reduce",
        [
            shape((ctx, chunk_rows, 2 * state), BF16),
            shape((taps, 2 * state), F32),
            shape((1, 2 * state), F32),
        ]
        + [shape((1, total_heads), F32)] * 3,
        (), after(exchanged(terms, "ctx"), rim, raw_back, *backs[:-1]),
    )
    grad_weight = call(
        place_rows_kernel, "place_rows", shape((rows, 2 * state), F32), (), exchanged(total, "ctx")
    )
    grad_tokens = call(
        functools.partial(tokens_kernel, fsdp), "grad_tokens", shape((tokens, fsdp * rows), BF16),
        (), after(grad, total), rim, hbm=pieces,
        scratch=[pltpu.VMEM((fsdp, *w_bc.shape), BF16), pltpu.SemaphoreType.DMA((fsdp,))],
    )
    grad_raw = call(
        join_steps_kernel, "join_steps", shape((total_heads, tokens), F32), (), raw_own,
        after(raw_back, total),
    )
    targets = []
    for at, cut, w in zip(ats, cuts, widths):
        rest = [(0, w - cut, 0, at + cut)] if cut < w else []
        targets += [[(0, cut, 0, at)], [*rest, (w - cut, w, 1, at)]]

    def join(arrays, which, blocks):
        return call(
            functools.partial(join_kernel, [targets[k] for k in which]), "join", [full, full], (),
            *blocks, hbm=arrays, hbm_outs=2, aliases={0: 0, 1: 1},
            scratch=[pltpu.SemaphoreType.DMA((2 * len(which),))],
        )

    early_backs = range(2 * GROUPS - 1)
    finals = join(finals, early_backs, [after(backs[0], total), *backs[1:-1]])
    ssm_out, grad_values = join(
        finals, [2 * GROUPS - 1], [after(backs[-1], grad_tokens, finals[0], grad_raw)]
    )
    return (
        ssm_out[None],
        grad_values[None],
        grad_tokens[None],
        grad_raw.T[None],
        grad_weight,
        grad_cw,
        grad_cb[0],
        *[a[0] for a in per_head],
    )


def solution(mesh):
    tokens = P("fsdp", "ctx", None)
    in_specs = (tokens, P("fsdp", None), P(), P(), tokens, tokens, P(), P(), P(), tokens)
    out_specs = (tokens, tokens, tokens, tokens, P("fsdp", None), P(), P(), P(), P(), P())
    return jax.shard_map(body, mesh=mesh, in_specs=in_specs, out_specs=out_specs, check_vma=False)
```

```python
import functools

import jax
import jax.numpy as jnp
from jax import lax
from jax.experimental import pallas as pl
from jax.experimental.pallas import tpu as pltpu
from jax.sharding import PartitionSpec as P

F32 = jnp.float32
BF16 = jnp.bfloat16
LANES = 128
HALO = 16
PARTS = (2, 2)
GROUPS = len(PARTS)
LIMIT = 16 * 1024 * 1024
HIGHEST = lax.Precision.HIGHEST
TN = ((0,), (0,))
NT = ((1,), (1,))


def dot(a, b, dims=((1,), (0,)), precision=None):
    return lax.dot_general(
        a, b, (dims, ((), ())), precision=precision, preferred_element_type=F32
    )


def shape(dims, dtype):
    return jax.ShapeDtypeStruct(dims, dtype)


def call(kernel, name, out_shape, smem, *operands, hbm=(), hbm_outs=0, scratch=(), aliases=None):
    single = not isinstance(out_shape, list)
    outs = [out_shape] if single else out_shape
    spaces = [pltpu.SMEM] * len(smem) + [pl.ANY] * len(hbm) + [pltpu.VMEM] * len(operands)
    out_spaces = [pltpu.HBM] * hbm_outs + [pltpu.VMEM] * (len(outs) - hbm_outs)
    result = pl.pallas_call(
        kernel,
        out_shape=outs,
        in_specs=[pl.BlockSpec(memory_space=a) for a in spaces],
        out_specs=[pl.BlockSpec(memory_space=a) for a in out_spaces],
        scratch_shapes=list(scratch),
        compiler_params=pltpu.CompilerParams(vmem_limit_bytes=LIMIT),
        input_output_aliases=aliases or {},
        name=name,
    )(*smem, *hbm, *operands)
    return result[0] if single else result


def copy_all(pairs, sems):
    copies = [pltpu.make_async_copy(a, b, sems.at[i]) for i, (a, b) in enumerate(pairs)]
    for copy in copies:
        copy.start()
    return copies


def side():
    return lax.rem(lax.axis_index("ctx"), 2)


def place():
    return lax.div(lax.axis_index("ctx"), 2)


def peer_columns(k, rows):
    return aligned((lax.axis_index("fsdp") ^ k) * rows, rows)


def aligned(at, size):
    return pl.ds(pl.multiple_of(at, LANES), size)


def triangle(n):
    rows = lax.broadcasted_iota(jnp.int32, (n, n), 0)
    cols = lax.broadcasted_iota(jnp.int32, (n, n), 1)
    return rows >= cols


def split(value):
    high = value.astype(BF16).astype(F32)
    return jnp.concatenate([high, value - high], 0).astype(BF16)


def swap_kernel(layer_ref, x_ref, g_ref, halo_ref, first_ref, x_out_ref, g_out_ref, sems):
    width = x_out_ref.shape[1]
    tokens = layer_ref.shape[0]
    base = (1 - side()) * (2 * width)
    pairs = [
        (layer_ref.at[tokens - HALO : tokens, :], halo_ref),
        (x_ref.at[:, aligned(base, width)], first_ref.at[:, :width]),
        (g_ref.at[:, aligned(base, width)], first_ref.at[:, width:]),
        (x_ref.at[:, aligned(base + width, width)], x_out_ref),
        (g_ref.at[:, aligned(base + width, width)], g_out_ref),
    ]
    for copy in copy_all(pairs, sems):
        copy.wait()


def vectors_kernel(
    dt_ref, back_ref, bias_ref, alog_ref, step_ref, cum_ref, cumt_ref, grow_ref, endw_ref, sig_ref,
    rate_ref, turned, rows,
):
    n = back_ref.shape[1]
    heads = back_ref.shape[0] // 2
    r = side()
    mine = pl.ds(pl.multiple_of(r * heads, 8), heads)
    turned[...] = jnp.zeros_like(turned)
    turned[0:heads, :] = dt_ref[mine, :]
    turned[heads : 2 * heads, :] = back_ref[mine, :]
    rows[...] = jnp.zeros_like(rows)
    for i, ref in enumerate((bias_ref, alog_ref)):
        half = jnp.where(r == 0, ref[:, :heads], ref[:, heads:])
        rows[i : i + 1, 0:heads] = half
        rows[i : i + 1, heads : 2 * heads] = half
    raw = turned[...].T + rows[0:1, :]
    step = jnp.maximum(raw, 0.0) + jnp.log1p(jnp.exp(-jnp.abs(raw)))
    rate = jnp.exp(rows[1:2, :])
    log_decay = -step * rate
    lower = jnp.where(triangle(n), 1.0, 0.0).astype(F32)
    cum = dot(lower, log_decay, precision=HIGHEST)
    step_ref[...] = step
    cum_ref[...] = cum
    cumt_ref[...] = cum.T
    grow_ref[...] = jnp.exp(cum)
    endw_ref[...] = jnp.exp(cum[n - 1 : n, :] - cum)
    sig_ref[...] = jax.nn.sigmoid(raw)
    rate_ref[...] = jnp.broadcast_to(rate, rate_ref.shape)


def early_kernel(count, layer_ref, *refs):
    pieces = refs[:count]
    out_ref, layer_scr, w_scr, sems = refs[count:]
    copies = copy_all(
        [(layer_ref, layer_scr)] + [(pieces[k], w_scr.at[k]) for k in range(count)], sems
    )
    copies[0].wait()
    total = 0.0
    for k in range(count):
        copies[k + 1].wait()
        total += dot(layer_scr[:, peer_columns(k, w_scr.shape[1])], w_scr[k])
    out_ref[...] = total


def project_kernel(done, count, layer_ref, *refs):
    pieces = refs[:count]
    halo_ref, early_ref, cw_ref, cb_ref, kept_ref, bc_ref, layer_scr, w_scr, ext_scr, sems = refs[count:]
    copies = copy_all(
        [(layer_ref, layer_scr)] + [(pieces[k], w_scr.at[k]) for k in range(count)], sems
    )
    taps = cw_ref.shape[0]
    tokens = layer_ref.shape[0]
    copies[0].wait()
    total, rim = early_ref[...], 0.0
    for k in range(count):
        copies[k + 1].wait()
        at = peer_columns(k, w_scr.shape[1])
        rim += dot(halo_ref[:, at], w_scr[k])
        if k >= done:
            total += dot(layer_scr[:, at], w_scr[k])
    ext_scr[0:HALO, :] = rim
    ext_scr[HALO:, :] = total
    kept_ref[0 : HALO + tokens, :] = ext_scr[...]
    first = HALO - taps + 1
    pre = cb_ref[...] + cw_ref[0:1, :] * ext_scr[first : first + tokens, :]
    for k in range(1, taps):
        pre = pre + cw_ref[k : k + 1, :] * ext_scr[first + k : first + k + tokens, :]
    kept_ref[HALO + tokens :, :] = pre
    bc_ref[...] = (pre * jax.nn.sigmoid(pre)).astype(BF16)


def head_columns(at, h):
    first, more = at
    return aligned(first + side() * more + h * LANES, LANES)


def scale_kernel(heads, lane, x_at, g_at, x_ref, g_ref, step_ref, grow_ref, endw_ref, xe_ref, ge_ref):
    for h in range(heads):
        at = slice(h * LANES, (h + 1) * LANES)
        one = slice(lane + h, lane + h + 1)
        x = x_ref[:, head_columns(x_at, h)].astype(F32)
        g = g_ref[:, head_columns(g_at, h)].astype(F32)
        xe_ref[:, at] = (x * (step_ref[:, one] * endw_ref[:, one])).astype(BF16)
        ge_ref[:, at] = (g * grow_ref[:, one]).astype(BF16)


def widen(row, lane, heads):
    return jnp.concatenate(
        [jnp.broadcast_to(row[:, lane + h : lane + h + 1], (1, LANES)) for h in range(heads)], 1
    )


def states_kernel(
    heads, lanes, bc0_ref, bc1_ref, xe0_ref, ge0_ref, xe1_ref, ge1_ref, grow_ref,
    first_ref, p_ref, q_ref, sf_ref, ds_ref, dec_ref, s_scr, d_scr, dec_scr,
):
    n = grow_ref.shape[0]
    r = side()
    for slot, (bc_ref, xe_ref, ge_ref) in enumerate(
        ((bc0_ref, xe0_ref, ge0_ref), (bc1_ref, xe1_ref, ge1_ref))
    ):
        s_scr[slot] = dot(bc_ref[:, :LANES], xe_ref[...], TN)
        d_scr[slot] = dot(bc_ref[:, LANES:], ge_ref[...], TN)
        dec_scr[slot] = widen(grow_ref[n - 1 : n, :], lanes[slot], heads)
    dec_first, dec_second = dec_scr[r], dec_scr[1 - r]
    s_first, d_second = s_scr[r], d_scr[1 - r]
    sf_ref[...] = s_first.astype(BF16)
    ds_ref[...] = d_second.astype(BF16)
    p = (dec_second * s_first + s_scr[1 - r]).astype(BF16)
    q = (dec_first * d_second + d_scr[r]).astype(BF16)
    p_ref[...] = p
    q_ref[...] = q

    @pl.when(place() == 0)
    def _():
        first_ref[...] = p

    @pl.when(place() != 0)
    def _():
        first_ref[...] = q

    dec_ref[0:1, :] = dec_first * dec_second
    dec_ref[1:2, :] = dec_first
    dec_ref[2:3, :] = dec_second
    dec_ref[3:8, :] = jnp.zeros((5, dec_first.shape[1]), F32)


def hop_kernel(hop, received_ref, p_ref, q_ref, dec_ref, out_ref):
    carried = dec_ref[0:1, :] * received_ref[...].astype(F32)

    @pl.when(place() == hop)
    def _():
        out_ref[...] = (carried + p_ref[...].astype(F32)).astype(BF16)

    @pl.when(place() != hop)
    def _():
        out_ref[...] = (carried + q_ref[...].astype(F32)).astype(BF16)


def inside_kernel(
    heads, lane, skip_at, all_heads, x_at, g_at, skip_ref, x_ref, g_ref, bc_ref, step_ref, cum_ref,
    cumt_ref, y_ref, dx_ref, dscores_ref, gy_ref, ds_ref, gx_ref,
):
    n = step_ref.shape[0]
    mask = triangle(n)
    scores = jnp.where(mask, dot(bc_ref[:, LANES:], bc_ref[:, :LANES], NT), 0.0)
    gy_ref[...] = jnp.zeros_like(gy_ref)
    ds_ref[...] = jnp.zeros_like(ds_ref)
    gx_ref[...] = jnp.zeros_like(gx_ref)
    dscores = jnp.zeros((n, n), F32)
    for h in range(heads):
        at = slice(h * LANES, (h + 1) * LANES)
        one = slice(lane + h, lane + h + 1)
        step = step_ref[:, one]
        gap = cum_ref[:, one] - cumt_ref[one, :]
        decay = jnp.exp(jnp.where(mask, gap, 0.0))
        mixing = (scores * decay).astype(BF16)
        x = x_ref[:, head_columns(x_at, h)].astype(F32)
        g = g_ref[:, head_columns(g_at, h)]
        gf = g.astype(F32)
        xs = (x * step).astype(BF16)
        skip = skip_ref[side() * all_heads + skip_at + h]
        y = dot(mixing, xs)
        dxs = dot(mixing, g, TN)
        dscores += dot(g, xs, NT) * decay
        y_ref[:, at] = y + skip * x
        dx_ref[:, at] = dxs * step + skip * gf
        gy_ref[:, one] = jnp.sum(gf * y, axis=1, keepdims=True)
        ds_ref[:, one] = jnp.sum(x * dxs, axis=1, keepdims=True)
        gx_ref[0:1, one] = jnp.sum(jnp.sum(gf * x, axis=0, keepdims=True), axis=1, keepdims=True)
    dscores_ref[...] = jnp.where(mask, dscores, 0.0)


def inside_bc_kernel(bc0_ref, bc1_ref, *refs):
    parts, outs = refs[: 2 * GROUPS], refs[2 * GROUPS :]
    for slot, bc_ref in enumerate((bc0_ref, bc1_ref)):
        total = parts[slot * GROUPS][...]
        for i in range(1, GROUPS):
            total = total + parts[slot * GROUPS + i][...]
        ds = total.astype(BF16)
        outs[slot][:, :LANES] = dot(ds, bc_ref[:, LANES:], TN)
        outs[slot][:, LANES:] = dot(ds, bc_ref[:, :LANES])


def enter_kernel(
    hops, xe0_ref, ge0_ref, xe1_ref, ge1_ref, dec_ref, p_ref, sf_ref, ds_ref, dbc0_ref, dbc1_ref, *refs
):
    received = refs[:hops]
    e_ref, r_ref, n_ref, dbco0_ref, dbco1_ref, e_in, r_in = refs[hops:]
    r, pos = side(), place()
    e_in[...] = jnp.zeros_like(e_in)
    r_in[...] = jnp.zeros_like(r_in)
    for k in range(hops):

        @pl.when(pos - 1 == k)
        def _(k=k):
            e_in[...] = received[k][...]

        @pl.when(hops - 1 - pos == k)
        def _(k=k):
            r_in[...] = received[k][...]

    dec_pair, dec_first, dec_second = dec_ref[0:1, :], dec_ref[1:2, :], dec_ref[2:3, :]
    entering = e_in[...].astype(F32)
    later = r_in[...].astype(F32)
    middle = dec_first * entering + sf_ref[...].astype(F32)
    leaving = dec_pair * entering + p_ref[...].astype(F32)
    earlier = dec_second * later + ds_ref[...].astype(F32)
    e_ref[r] = e_in[...]
    e_ref[1 - r] = middle.astype(BF16)
    r_ref[1 - r] = r_in[...]
    r_ref[r] = earlier.astype(BF16)
    n_ref[1 - r] = jnp.sum(later * leaving, axis=0, keepdims=True)
    n_ref[r] = jnp.sum(earlier * middle, axis=0, keepdims=True)
    for slot, (xe_ref, ge_ref, dbc_ref, dbco_ref) in enumerate(
        ((xe0_ref, ge0_ref, dbc0_ref, dbco0_ref), (xe1_ref, ge1_ref, dbc1_ref, dbco1_ref))
    ):
        db = dbc_ref[:, :LANES] + dot(xe_ref[...], r_ref[slot], NT)
        dc = dbc_ref[:, LANES:] + dot(ge_ref[...], e_ref[slot], NT)
        dbco_ref[:, :LANES] = db.astype(dbco_ref.dtype)
        dbco_ref[:, LANES:] = dc.astype(dbco_ref.dtype)


def across_kernel(heads, lanes, filled, own_at, columns, *refs):
    refs = refs[2 * filled :]
    across_block(heads, lanes, own_at, columns, *refs)


def across_block(
    heads, lanes, own_at, columns, x0_ref, g0_ref, x1_ref, g1_ref, bc0_ref, bc1_ref, step_ref,
    grow_ref, endw_ref, e_ref, r_ref, n_ref, y0_ref, dx0_ref, y1_ref, dx1_ref, yf_ref, dxf_ref,
    ys_ref, dxs_ref, u_ref, t_ref, re_ref, yo_ref, dxo_ref, sems
):
    r = side()
    width, cut = yo_ref.shape[1], ys_ref.shape[1]
    u_ref[...] = jnp.zeros_like(u_ref)
    t_ref[...] = jnp.zeros_like(t_ref)
    re_ref[...] = jnp.zeros_like(re_ref)
    for slot, (bc_ref, y_ref, dx_ref) in enumerate(
        ((bc0_ref, y0_ref, dx0_ref), (bc1_ref, y1_ref, dx1_ref))
    ):
        e_all = e_ref[slot]
        r_all = r_ref[slot]
        ce_all = dot(bc_ref[:, LANES:], e_all)
        br_all = dot(bc_ref[:, :LANES], r_all)
        for h in range(heads):
            at = slice(h * LANES, (h + 1) * LANES)
            lane = lanes[slot] + h
            one = slice(lane, lane + 1)
            ce, br = ce_all[:, at], br_all[:, at]
            y = (y_ref[:, at] + grow_ref[:, one] * ce).astype(BF16)
            dx = (dx_ref[:, at] + (step_ref[:, one] * endw_ref[:, one]) * br).astype(BF16)
            if slot == 0:
                yo_ref[:, at] = y
                dxo_ref[:, at] = dx
                x = x0_ref[:, head_columns(own_at, h)].astype(F32)
                g = g0_ref[:, head_columns(own_at, h)].astype(F32)
            else:
                first = h * LANES
                if first < cut:
                    ys_ref[:, at] = y
                else:
                    dxs_ref[:, first - cut : first - cut + LANES] = y
                dxs_ref[:, first + width - cut : first + width - cut + LANES] = dx
                x = x1_ref[:, head_columns(columns[0], h)].astype(F32)
                g = g1_ref[:, head_columns(columns[1], h)].astype(F32)
            u_ref[:, one] = jnp.sum(g * ce, axis=1, keepdims=True)
            t_ref[:, one] = jnp.sum(x * br, axis=1, keepdims=True)
            re_ref[0:1, one] = jnp.sum(n_ref[slot][:, at], axis=1, keepdims=True)
        if slot == 0:
            final = aligned(own_at[0] + r * own_at[1], width)
            pairs = [(yo_ref, yf_ref.at[:, final]), (dxo_ref, dxf_ref.at[:, final])]
            copies = copy_all(pairs, sems)
    for copy in copies:
        copy.wait()


def steps_kernel(sig_ref, rate_ref, step_ref, grow_ref, endw_ref, *refs):
    count = 2 * GROUPS
    gys, dss, gxs = refs[:count], refs[count : 2 * count], refs[2 * count : 3 * count]
    refs = refs[3 * count :]
    us, ts, res = refs[:GROUPS], refs[GROUPS : 2 * GROUPS], refs[2 * GROUPS : 3 * GROUPS]
    own_ref, send_ref, sums_ref = refs[3 * GROUPS :]

    def total(parts):
        value = parts[0][...]
        for a in parts[1:]:
            value = value + a[...]
        return value

    n = step_ref.shape[0]
    step = step_ref[...]
    ds = total(dss) + endw_ref[...] * total(ts)
    gy = total(gys) + grow_ref[...] * total(us)
    rate = rate_ref[0:1, :]
    last = lax.broadcasted_iota(jnp.int32, (n, LANES), 0) == n - 1
    dcum = gy - step * ds + jnp.where(last, total(res)[0:1, :], 0.0)
    lower = jnp.where(triangle(n), 1.0, 0.0).astype(F32)
    dlog = dot(lower, dcum, TN, precision=HIGHEST)
    draw = (ds - rate * dlog) * sig_ref[...]
    turned = draw.T
    heads = own_ref.shape[0]
    own_ref[...] = turned[:heads, :]
    send_ref[...] = turned[heads : 2 * heads, :]
    sums_ref[0:1, :] = jnp.sum(draw, axis=0, keepdims=True)
    sums_ref[1:2, :] = jnp.sum(dlog * (-step * rate), axis=0, keepdims=True)
    sums_ref[2:3, :] = total(gxs)[0:1, :]
    sums_ref[3:8, :] = jnp.zeros((5, LANES), F32)


def conv_back_kernel(
    own_ref, ret_ref, kept_ref, cw_ref, heads_ref, grad_ref, rim_ref, message_ref, z_scr, sum_scr,
    grad_scr, sems,
):
    tokens = own_ref.shape[0]
    taps = cw_ref.shape[0]
    pre = kept_ref[HALO + tokens :, :]
    sig = jax.nn.sigmoid(pre)
    dconv = (own_ref[...] + ret_ref[...].astype(F32)) * sig * (1.0 + pre * (1.0 - sig))
    z_scr[...] = jnp.zeros_like(z_scr)
    z_scr[HALO : HALO + tokens, :] = dconv
    grad = cw_ref[0:1, :] * z_scr[taps - 1 : taps - 1 + tokens + HALO, :]
    for k in range(1, taps):
        grad = grad + cw_ref[k : k + 1, :] * z_scr[taps - 1 - k : taps - 1 - k + tokens + HALO, :]
    grad_scr[...] = grad[HALO:, :]
    copies = copy_all([(grad_scr, grad_ref)], sems)
    rim_ref[...] = grad[HALO - 8 : HALO, :]
    first = HALO - taps + 1
    sum_scr[...] = jnp.zeros_like(sum_scr)
    for k in range(taps):
        sum_scr[k : k + 1, :] = jnp.sum(
            dconv * kept_ref[first + k : first + k + tokens, :], axis=0, keepdims=True
        )
    sum_scr[taps : taps + 1, :] = jnp.sum(dconv, axis=0, keepdims=True)
    sum_scr[5:8, aligned(side() * LANES, LANES)] = heads_ref[0:3, :]
    small = split(sum_scr[...])
    message_ref[0 : tokens + HALO, :] = grad.astype(BF16)
    message_ref[tokens + HALO :, :] = small
    for copy in copies:
        copy.wait()


def pack_kernel(layer_ref, halo_ref, keep_ref, send_ref, sems):
    half, _, rows = keep_ref.shape
    pairs = []
    for k in range(2 * half):
        out = keep_ref.at[k] if k < half else send_ref.at[k - half]
        at = peer_columns(k, rows)
        pairs.append((halo_ref.at[:, at], out.at[0:HALO, :]))
        pairs.append((layer_ref.at[:, at], out.at[HALO:, :]))
    for copy in copy_all(pairs, sems):
        copy.wait()


def relay_kernel(picks, *refs):
    out_ref = refs[-1]
    for j, (ref, at) in enumerate(picks):
        out_ref[j] = refs[ref][at]


def turn_kernel(picks, *refs):
    out_ref = refs[-1]
    parts = [refs[ref].at[at] for ref, at in picks]
    tokens = parts[0].shape[0] - HALO
    for k, part in enumerate(parts):
        out_ref[:, k * tokens : (k + 1) * tokens] = part[HALO:, :].T
    halos = jnp.concatenate([part[0:HALO, :] for part in parts], 0)
    out_ref[:, len(parts) * tokens :] = halos.T


def weight_kernel(count, left_ref, *refs):
    rights, out_ref = refs[:count], refs[count]
    tokens = (left_ref.shape[1] // count) - HALO
    right = jnp.concatenate(
        [a[HALO : HALO + tokens, :] for a in rights] + [a[0:HALO, :] for a in rights], 0
    )
    at = tokens + HALO
    both = jnp.zeros((16, right.shape[1]), F32)
    for a in rights:
        both += a[at : at + 16, :].astype(F32)
    small = split(both[0:8, :] + both[8:16, :])
    chunk = out_ref.shape[1] - 16
    for k in range(out_ref.shape[0]):
        term = dot(left_ref[k * chunk : (k + 1) * chunk, :], right)
        out_ref[k, 0:chunk, :] = term.astype(BF16)
        out_ref[k, chunk:, :] = small


def reduce_kernel(heads, terms_ref, total_ref, cw_ref, cb_ref, *head_refs):
    chunk = total_ref.shape[1]
    total = terms_ref[0].astype(F32)
    for k in range(1, terms_ref.shape[0]):
        total = total + terms_ref[k].astype(F32)
    for k in range(total_ref.shape[0]):
        total_ref[k] = total[0:chunk].astype(BF16)
    small = total[chunk : chunk + 8] + total[chunk + 8 :]
    taps = cw_ref.shape[0]
    cw_ref[...] = small[0:taps, :]
    cb_ref[...] = small[taps : taps + 1, :]
    for i, ref in enumerate(head_refs):
        row = small[5 + i : 6 + i, :]
        ref[:, :heads] = row[:, :heads] + row[:, heads : 2 * heads]
        row = row[:, LANES:]
        ref[:, heads:] = row[:, :heads] + row[:, heads : 2 * heads]


def place_rows_kernel(parts_ref, out_ref):
    chunk = parts_ref.shape[1]
    for k in range(parts_ref.shape[0]):
        out_ref[k * chunk : (k + 1) * chunk, :] = parts_ref[k].astype(F32)


def tokens_kernel(count, *refs):
    pieces = refs[:count]
    grad_ref, rim_ref, out_ref, w_scr, sems = refs[count:]
    copies = copy_all([(pieces[k], w_scr.at[k]) for k in range(count)], sems)
    tail = rim_ref.shape[0]
    own = grad_ref[...]
    g = jnp.concatenate([own[:-tail], own[-tail:] + rim_ref[...]], 0).astype(BF16)
    rows = pieces[0].shape[0]
    for k in range(count):
        copies[k].wait()
        out_ref[:, peer_columns(k, rows)] = dot(g, w_scr[k], NT).astype(BF16)


def join_kernel(targets, *refs):
    blocks = refs[2 : 2 + len(targets)]
    *outs, sems = refs[2 + len(targets) :]
    half = outs[0].shape[1] // 2
    base = (1 - side()) * half
    pairs = []
    for block, pieces in zip(blocks, targets):
        for first, width, which, at in pieces:
            pairs.append((block.at[:, first : first + width], outs[which].at[:, aligned(base + at, width)]))
    for copy in copy_all(pairs, sems):
        copy.wait()


def join_steps_kernel(own_ref, back_ref, out_ref):
    heads = own_ref.shape[0]
    r = side()
    out_ref[pl.ds(pl.multiple_of(r * heads, 8), heads), :] = own_ref[...]
    out_ref[pl.ds(pl.multiple_of((1 - r) * heads, 8), heads), :] = back_ref[...]


def pinned(x):
    return pltpu.with_memory_space_constraint(x, pltpu.HBM)


def toggled(x, axis, bits):
    size = lax.axis_size(axis)
    return lax.ppermute(x, axis, [(i, i ^ bits) for i in range(size)])


def exchanged(x, axis):
    return lax.all_to_all(x, axis, 0, 0)


def after(x, *others):
    return lax.optimization_barrier((x, *others))[0]


def body(layer_in, w_bc, conv_w, conv_b, ssm_in, dt_raw, dt_bias, a_log, skip_scale, grad_out):
    ctx, fsdp = lax.axis_size("ctx"), lax.axis_size("fsdp")
    layer, x, g, dt = layer_in[0], ssm_in[0], grad_out[0], dt_raw[0].T
    tokens, width = x.shape
    total_heads = dt_bias.shape[0]
    heads = total_heads // 2
    half = width // 2
    counts = [heads // part for part in PARTS]
    starts = [sum(counts[:i]) for i in range(GROUPS)]
    widths = [half // part for part in PARTS]
    ats = [sum(widths[:i]) for i in range(GROUPS)]
    state = w_bc.shape[1] // 2
    taps = conv_w.shape[0]
    rows = w_bc.shape[0]
    chunk_rows = rows // ctx
    pairs = ctx // 2
    hops = pairs - 1
    square = shape((tokens, LANES), F32)
    flats = [shape((tokens, a), BF16) for a in widths]
    turned = shape((heads, tokens), F32)
    both_bc = [shape((tokens, 2 * state), F32)] * 2

    dt_back = toggled(dt, "ctx", 1)
    halo_send, *swaps = call(
        swap_kernel, "swap",
        [shape((HALO, layer.shape[1]), BF16), shape((tokens, half), BF16), flats[1], flats[1]], (),
        hbm=(pinned(layer), pinned(x), pinned(g)), scratch=[pltpu.SemaphoreType.DMA((5,))],
    )
    halo = lax.ppermute(halo_send, "ctx", [(i, i + 1) for i in range(ctx - 1)])
    swapped_first = toggled(after(swaps[0], dt_back), "ctx", 1)
    swapped_x = toggled(after(swaps[1], halo), "ctx", 1)

    step, cum, cumt, grow, endw, sig, rate = call(
        vectors_kernel, "vectors", [square] * 6 + [shape((8, LANES), F32)], (), dt, dt_back,
        dt_bias[None, :], a_log[None, :],
        scratch=[pltpu.VMEM((tokens, tokens), F32), pltpu.VMEM((8, LANES), F32)],
    )

    def source(slot, i):
        if slot == 0:
            return (ats[i], half), (ats[i], half), x, g
        if i == 0:
            return (0, 0), (widths[0], 0), swapped_first, swapped_first
        return (0, 0), (0, 0), swapped_x, swapped_g

    def scale(slot, i):
        x_at, g_at, xa, ga = source(slot, i)
        return call(
            functools.partial(scale_kernel, counts[i], slot * heads + starts[i], x_at, g_at), "scale",
            [flats[i]] * 2, (), xa, ga, step, grow, endw,
        )

    scaled = {(0, i): scale(0, i) for i in range(GROUPS)}
    scaled[1, 0] = scale(1, 0)
    def landing(count):
        return [
            pltpu.VMEM(layer.shape, BF16),
            pltpu.VMEM((count, *w_bc.shape), BF16),
            pltpu.SemaphoreType.DMA((1 + count,)),
        ]

    parts = shape((fsdp // 2, tokens + HALO, rows), BF16)
    packs = call(
        pack_kernel, "pack", [parts, parts], (), hbm=(pinned(layer), halo),
        scratch=[pltpu.SemaphoreType.DMA((2 * fsdp,))],
    )
    far_bit = fsdp // 2
    far = [toggled(w_bc, "fsdp", far_bit)]
    near = [w_bc]
    while len(near) < far_bit:
        near += [toggled(a, "fsdp", len(near)) for a in near]
    early = call(
        functools.partial(early_kernel, len(near)), "project_early",
        shape((tokens, 2 * state), F32), (), hbm=(pinned(layer), *near),
        scratch=landing(len(near)),
    )
    far[0] = after(
        far[0], early, halo, scaled[1, 0][0], *[scaled[0, i][0] for i in range(GROUPS)]
    )
    while len(far) < far_bit:
        far += [toggled(a, "fsdp", len(far)) for a in far]
    pieces = near + far
    layer_scr, w_scr, sems = landing(fsdp)
    kept, bc = call(
        functools.partial(project_kernel, len(near), fsdp), "project",
        [
            shape((2 * tokens + HALO, 2 * state), F32),
            shape((tokens, 2 * state), BF16),
        ],
        (), after(halo, packs[0]), early, conv_w, conv_b[None, :], hbm=(pinned(layer), *pieces),
        scratch=[layer_scr, w_scr, pltpu.VMEM((tokens + HALO, 2 * state), F32), sems],
    )
    bcs = [bc, toggled(bc, "ctx", 1)]
    def within(slot, i, *earlier):
        x_at, g_at, xa, ga = source(slot, i)
        return call(
            functools.partial(
                inside_kernel, counts[i], slot * heads + starts[i], starts[i], heads, x_at, g_at
            ),
            "inside",
            [shape((tokens, widths[i]), F32)] * 2 + [shape((tokens, tokens), F32), square, square]
            + [shape((8, LANES), F32)],
            (skip_scale,), xa, ga, after(bcs[slot], *earlier), step, cum, cumt,
        )

    order = [(slot, i) for slot in range(2) for i in range(GROUPS)]
    inside, states, received, earlier = {}, [], [], []
    inside[0, 0] = within(0, 0)
    swapped_g = toggled(after(swaps[2], bcs[1], inside[0, 0][2]), "ctx", 1)
    earlier = [inside[0, 0][2]]
    for i in range(GROUPS):
        lanes = (starts[i], heads + starts[i])
        if i:
            scaled[1, i] = scale(1, i)
        wide = shape((state, widths[i]), BF16)
        first, p, q, s_first, d_second, decays = call(
            functools.partial(states_kernel, counts[i], lanes), "states",
            [wide] * 5 + [shape((8, widths[i]), F32)],
            (), *bcs, *scaled[0, i], *scaled[1, i], after(grow, *earlier),
            scratch=[pltpu.VMEM((2, state, widths[i]), F32)] * 2
            + [pltpu.VMEM((2, 1, widths[i]), F32)],
        )
        states.append((decays, p, s_first, d_second, q))
        received.append([first])
        earlier = [first]
        if i == 0:
            for key in order[1:GROUPS]:
                inside[key] = within(*key, first)
                earlier.append(inside[key][2])
    waiting = order[GROUPS:]
    for hop in range(hops):
        moves = [(hop, hop + 1), (pairs - 1 - hop, pairs - 2 - hop)]
        moves = [(2 * a + i, 2 * b + i) for a, b in moves for i in range(2)]
        for i in range(GROUPS):
            value = received[i][-1]
            if hop:
                decays, p, _, _, q = states[i]
                value = call(
                    functools.partial(hop_kernel, hop), "hop", shape(value.shape, BF16), (),
                    after(value, *earlier), p, q, decays,
                )
                earlier = [value]
                if waiting and i == 0:
                    key = waiting.pop(0)
                    inside[key] = within(*key, *earlier)
                    earlier = [inside[key][2]]
            received[i].append(lax.ppermute(value, "ctx", moves))
    arrays = [packs[0]]
    at = {(0, k): (0, k) for k in range(fsdp // 2)}
    message, bit = packs[1], fsdp // 2
    sent = [(0, k) for k in range(bit, fsdp)]
    while bit:
        arrays.append(toggled(message, "fsdp", bit))
        for j, (source_bits, owner_bits) in enumerate(sent):
            at[source_bits ^ bit, owner_bits ^ bit] = (len(arrays) - 1, j)
        bit //= 2
        if bit:
            sent = [key for key in sorted(at) if key[1] & bit and key[1] < 2 * bit]
            message = call(
                functools.partial(relay_kernel, [at[key] for key in sent]), "relay",
                shape((len(sent), tokens + HALO, rows), BF16), (), after(arrays[0], received[-1][0]),
                *arrays[1:],
            )
    picks = [at[k, 0] for k in range(fsdp)]
    for key in waiting:
        inside[key] = within(*key, *earlier)
    dbcs = call(inside_bc_kernel, "inside_bc", both_bc, (), *bcs, *[inside[key][2] for key in order])

    full = shape((tokens, width), BF16)
    finals, sends, us, ts, res = (), [], [], [], []
    cuts = [widths[0] // 2, *widths[1:]]
    returns = [
        (shape((tokens, cut), BF16), shape((tokens, 2 * w - cut), BF16)) for cut, w in zip(cuts, widths)
    ]
    for i in range(GROUPS):
        last = i == GROUPS - 1
        own_at, _, xa, ga = source(0, i)
        x_at, g_at, xb, gb = source(1, i)
        if i == 1:
            backs = [toggled(sends[0], "ctx", 1)]
            left = call(
                functools.partial(turn_kernel, picks), "turn",
                shape((rows, fsdp * (tokens + HALO)), BF16), (), after(arrays[0], *sends, *backs),
                *arrays[1:],
            )
        lanes = (starts[i], heads + starts[i])
        pair = [shape((2, state, widths[i]), BF16)] * 2
        *both, n, dbc_own, dbc_other = call(
            functools.partial(enter_kernel, hops), "enter",
            [*pair, shape((2, 1, widths[i]), F32), both_bc[0]]
            + [shape((tokens, 2 * state), BF16 if last else F32)],
            (), after(scaled[0, i][0], *sends), scaled[0, i][1], *scaled[1, i], *states[i][:4], *dbcs,
            *received[i][1:],
            scratch=[pltpu.VMEM((state, widths[i]), BF16)] * 2,
        )
        dbcs = (dbc_own, dbc_other)
        if last:
            dbc_ret = toggled(dbc_other, "ctx", 1)
        y, dx, y_send, dx_send, u, t, re = call(
            functools.partial(
                across_kernel, counts[i], lanes, len(finals) // 2, own_at, (x_at, g_at)
            ),
            "across", [full, full, *returns[i], square, square, shape((8, LANES), F32)],
            (), xa, ga, xb, gb, after(bcs[0], left) if i == 1 else bcs[0], bcs[1], step, grow, endw,
            *both, n, *inside[0, i][:2], *inside[1, i][:2],
            hbm=finals, hbm_outs=2, aliases={0: 0, 1: 1} if finals else None,
            scratch=[pltpu.VMEM((tokens, widths[i]), BF16)] * 2 + [pltpu.SemaphoreType.DMA((2,))],
        )
        finals = (y, dx)
        sends += [y_send, dx_send]
        us.append(u)
        ts.append(t)
        res.append(re)

    raw_own, raw_send, head_sums = call(
        steps_kernel, "steps", [turned, turned, shape((8, LANES), F32)], (),
        sig, rate, step, grow, endw, *[inside[key][j] for j in (3, 4, 5) for key in order],
        *us, *ts, *res,
    )
    raw_back = toggled(raw_send, "ctx", 1)
    grad, rim_send, message = call(
        conv_back_kernel, "conv_back",
        [
            pltpu.HBM((tokens, 2 * state), F32),
            shape((8, 2 * state), F32),
            shape((tokens + HALO + 16, 2 * state), BF16),
        ],
        (), after(dbcs[0], *backs), dbc_ret, kept, conv_w, head_sums, hbm_outs=1,
        scratch=[
            pltpu.VMEM((tokens + 2 * HALO, 2 * state), F32),
            pltpu.VMEM((8, 2 * state), F32),
            pltpu.VMEM((tokens, 2 * state), F32),
            pltpu.SemaphoreType.DMA((1,)),
        ],
    )
    rim = lax.ppermute(rim_send, "ctx", [(i + 1, i) for i in range(ctx - 1)])
    backs.append(toggled(after(sends[1], dbc_ret, head_sums), "ctx", 1))

    rights = [message] + [toggled(message, "fsdp", k) for k in range(fsdp - 1, 0, -1)][::-1]
    terms = call(
        functools.partial(weight_kernel, fsdp), "weight",
        shape((ctx, chunk_rows + 16, 2 * state), BF16), (), left, after(message, *backs), *rights[1:],
    )
    backs += [toggled(after(a, terms), "ctx", 1) for a in sends[2:]]
    total, grad_cw, grad_cb, *per_head = call(
        functools.partial(reduce_kernel, heads), "reduce",
        [
            shape((ctx, chunk_rows, 2 * state), BF16),
            shape((taps, 2 * state), F32),
            shape((1, 2 * state), F32),
        ]
        + [shape((1, total_heads), F32)] * 3,
        (), after(exchanged(terms, "ctx"), rim, raw_back, *backs[:-1]),
    )
    grad_weight = call(
        place_rows_kernel, "place_rows", shape((rows, 2 * state), F32), (), exchanged(total, "ctx")
    )
    grad_tokens = call(
        functools.partial(tokens_kernel, fsdp), "grad_tokens", shape((tokens, fsdp * rows), BF16),
        (), after(grad, total), rim, hbm=pieces,
        scratch=[pltpu.VMEM((fsdp, *w_bc.shape), BF16), pltpu.SemaphoreType.DMA((fsdp,))],
    )
    grad_raw = call(
        join_steps_kernel, "join_steps", shape((total_heads, tokens), F32), (), raw_own,
        after(raw_back, total),
    )
    targets = []
    for at, cut, w in zip(ats, cuts, widths):
        rest = [(0, w - cut, 0, at + cut)] if cut < w else []
        targets += [[(0, cut, 0, at)], [*rest, (w - cut, w, 1, at)]]

    def join(arrays, which, blocks):
        return call(
            functools.partial(join_kernel, [targets[k] for k in which]), "join", [full, full], (),
            *blocks, hbm=arrays, hbm_outs=2, aliases={0: 0, 1: 1},
            scratch=[pltpu.SemaphoreType.DMA((2 * len(which),))],
        )

    early_backs = range(2 * GROUPS - 1)
    finals = join(finals, early_backs, [after(backs[0], total), *backs[1:-1]])
    ssm_out, grad_values = join(
        finals, [2 * GROUPS - 1], [after(backs[-1], grad_tokens, finals[0], grad_raw)]
    )
    return (
        ssm_out[None],
        grad_values[None],
        grad_tokens[None],
        grad_raw.T[None],
        grad_weight,
        grad_cw,
        grad_cb[0],
        *[a[0] for a in per_head],
    )


def solution(mesh):
    tokens = P("fsdp", "ctx", None)
    in_specs = (tokens, P("fsdp", None), P(), P(), tokens, tokens, P(), P(), P(), tokens)
    out_specs = (tokens, tokens, tokens, tokens, P("fsdp", None), P(), P(), P(), P(), P())
    return jax.shard_map(body, mesh=mesh, in_specs=in_specs, out_specs=out_specs, check_vma=False)
```
